32 devices in a mesh: seq: 4 (over y, x), fsdp: 8 (over z, core).
Axes of the slice: x: 2, y: 2, z: 4, core: 2. Of those that a mesh axis runs over, the one named last changes fastest.
Arguments:
- tokens: bfloat16 [2, 3072, 1600], P(None, ('seq', 'fsdp')), may hold values from -6 to 6
- cotangent: bfloat16 [2, 3072, 1600], P(None, ('seq', 'fsdp')), may hold values from -6 to 6
- route: int32 [2, 3072], P(None, 'seq'), may hold values from 0 to 767, as said below
- lengths: int32 [2, 8, 3], P(None, 'fsdp'), may hold values from 1 to 336, as said below
- gain_in: float32 [1600], replicated, may hold values from 0.5 to 1.5
- w_qkv: bfloat16 [1600, 2240], P('fsdp'), may hold values from -0.15625 to 0.15625
- w_mix_in: bfloat16 [1600, 6400], P('fsdp'), may hold values from -0.15625 to 0.15625
- w_x: bfloat16 [3200, 132], P('fsdp'), may hold values from -0.109375 to 0.109375
- w_dt: bfloat16 [3200, 100], P('fsdp'), may hold values from -0.625 to 0.625
- w_small: bfloat16 [3200, 23], P('fsdp'), may hold values from -10 to 3, as said below
- gain_att: float32 [1600], replicated, may hold values from 0.5 to 1.5
- gain_ssm: float32 [3200], replicated, may hold values from 0.5 to 1.5
- w_out_att: bfloat16 [1600, 1600], P('fsdp'), may hold values from -0.15625 to 0.15625
- w_out_ssm: bfloat16 [3200, 1600], P('fsdp'), may hold values from -0.109375 to 0.109375
- gain_ffn: float32 [1600], replicated, may hold values from 0.5 to 1.5
- w_gate: bfloat16 [1600, 5504], P('fsdp'), may hold values from -0.15625 to 0.15625
- w_up: bfloat16 [1600, 5504], P('fsdp'), may hold values from -0.15625 to 0.15625
- w_down: bfloat16 [5504, 1600], P('fsdp'), may hold values from -0.078125 to 0.078125
Outputs:
- output: bfloat16 [2, 3072, 1600], P(None, ('seq', 'fsdp'))
- grad_tokens: bfloat16 [2, 3072, 1600], P(None, ('seq', 'fsdp'))
- grad_gain_in: float32 [1600], replicated
- grad_w_qkv: float32 [1600, 2240], P('fsdp', 'seq')
- grad_w_mix_in: float32 [1600, 6400], P('fsdp', 'seq')
- grad_w_x: float32 [3200, 132], P('fsdp', 'seq')
- grad_w_dt: float32 [3200, 100], P('fsdp', 'seq')
- grad_w_small: float32 [3200, 23], P('fsdp')
- grad_dt_bias: float32 [3200], P('fsdp')
- grad_gain_att: float32 [1600], replicated
- grad_gain_ssm: float32 [3200], replicated
- grad_w_out_att: float32 [1600, 1600], P('fsdp', 'seq')
- grad_w_out_ssm: float32 [3200, 1600], P('fsdp', 'seq')
- grad_gain_ffn: float32 [1600], replicated
- grad_w_gate: float32 [1600, 5504], P('fsdp', 'seq')
- grad_w_up: float32 [1600, 5504], P('fsdp', 'seq')
- grad_w_down: float32 [5504, 1600], P('fsdp', 'seq')
- rms: float32 [6], replicated
The draws below stay inside these ranges and needn't reach their ends.
Inputs may be any that keep to these rules, and one draw needn't show every extreme that they name: For each micro-batch and seq index, route maps the 768 rows of that slice one to one onto 0 to 767; of each run of 96 given rows, exactly 12 have route // 96 equal to each fsdp index. The 3 lengths of a pack sum to 384; one of them is 336. `w_small`: columns hold conv_w, conv_b, dt_bias, skip_d and log_a in this order.
All inputs are finite; a program needn't handle non-finite values.
Results may differ from the reference program's by a relative error of at most 0.02.
Values may be sent and summed in bfloat16 or wider, within the bound.
A program may use at most 448 MiB of HBM per device.

```python
import jax
import jax.numpy as jnp
from jax import lax

D = 1600
HEADS = 25
KV_HEADS = 5
HEAD = 64
INNER = 3200
STATE = 16
CONV = 4
DT_RANK = 100
FF = 5504
TOK = 96
MICRO = 2
SEQS = 3
SCAN_BLOCK = 16
ATT = 1600
KV_WIDTH = 320
SHORTS = 48
LONGEST = 336
ROWS = 3072
N_SEQ = 4
N_FSDP = 8


def draw_route(key, part):
    key = jax.random.fold_in(key, 11)
    per_peer = TOK // N_FSDP
    row_groups = MICRO * N_SEQ * N_FSDP
    src_keys = jax.random.split(jax.random.fold_in(key, 1), row_groups)
    dst_keys = jax.random.split(jax.random.fold_in(key, 2), row_groups)
    src_order = jax.vmap(lambda sub_key: jax.random.permutation(sub_key, TOK))(src_keys).reshape(MICRO, N_SEQ, N_FSDP, TOK)
    dst_order = jax.vmap(lambda sub_key: jax.random.permutation(sub_key, TOK))(dst_keys).reshape(MICRO, N_SEQ, N_FSDP * TOK)
    source = jnp.arange(N_FSDP, dtype=jnp.int32)[None, None, :, None]
    target_dev = (src_order // per_peer + source) % N_FSDP
    arrival = source * per_peer + src_order % per_peer
    flat_index = (target_dev * TOK + arrival).reshape(MICRO, N_SEQ, N_FSDP * TOK)
    dest_slot = jnp.take_along_axis(dst_order, flat_index, axis=2)
    routed = target_dev.reshape(MICRO, N_SEQ, N_FSDP * TOK) * TOK + dest_slot
    return routed.reshape(MICRO, N_SEQ * N_FSDP * TOK).astype(jnp.int32)


def draw_lengths(key, part):
    key = jax.random.fold_in(key, 12)
    pack_count = MICRO * N_FSDP
    first_short = jax.random.randint(jax.random.fold_in(key, 1), (pack_count,), 1, SHORTS)
    table = jnp.stack([jnp.full((pack_count,), LONGEST, jnp.int32), first_short, SHORTS - first_short], axis=1)
    order_keys = jax.random.split(jax.random.fold_in(key, 2), pack_count)
    placing = jax.vmap(lambda sub_key: jax.random.permutation(sub_key, 3))(order_keys)
    return jnp.take_along_axis(table, placing, axis=1).reshape(MICRO, N_FSDP, SEQS).astype(jnp.int32)


def draw_w_small(key, part):
    key = jax.random.fold_in(key, 13)
    taps = jnp.clip(0.5 * jax.random.normal(jax.random.fold_in(key, 1), (INNER, CONV), jnp.float32), -2.0, 2.0)
    conv_bias = jnp.clip(0.2 * jax.random.normal(jax.random.fold_in(key, 2), (INNER, 1), jnp.float32), -0.8, 0.8)
    dt_top = -2.3
    dt_target = jnp.exp(jax.random.uniform(jax.random.fold_in(key, 3), (INNER, 1), jnp.float32, -9.2, dt_top))
    dt_bias = jnp.log(jnp.expm1(dt_target))
    skip_d = jax.random.uniform(jax.random.fold_in(key, 4), (INNER, 1), jnp.float32, 0.5, 1.5)
    log_a = jax.random.uniform(jax.random.fold_in(key, 5), (INNER, STATE), jnp.float32, 0.0, 2.77)
    return jnp.concatenate([taps, conv_bias, dt_bias, skip_d, log_a], axis=1).astype(jnp.bfloat16)


def level_of(own_key, dims, cuts, least, top_value):
    def one(axis_at, parts):
        heights = jax.random.uniform(jax.random.fold_in(jax.random.fold_in(own_key, 6), axis_at), (parts,), jnp.float32, least / len(cuts), top_value / len(cuts))
        return jnp.repeat(jnp.exp(heights), dims[axis_at] // parts).reshape((-1,) + (1,) * (len(dims) - axis_at - 1))

    loudness = one(*cuts[0])
    for cut in cuts[1:]:
        loudness = loudness * one(*cut)
    return loudness


def scatter_about(key, shape, deviation, bound, cuts=(), kind=jnp.bfloat16):
    entries = deviation * jax.random.normal(key, shape, jnp.float32)
    if cuts:
        entries = entries * level_of(key, shape, cuts, -0.22, 0.18)
    return jnp.clip(entries, -bound, bound).astype(kind)


def setup_inputs(seed: int = 0) -> dict:
    streams_of = jax.random.split(jax.random.key(seed), 19)
    tokens = scatter_about(streams_of[0], (MICRO, ROWS, D), 1.0, 6.0, ((1, 32),))
    cotangent = scatter_about(streams_of[1], (MICRO, ROWS, D), 1.0, 6.0, ((1, 32),))
    route = draw_route(jax.random.fold_in(streams_of[18], 71), 0)
    lengths = draw_lengths(jax.random.fold_in(streams_of[18], 71), 0)
    gain_in = jnp.clip(1.0 + 0.1 * jax.random.normal(streams_of[4], (D,), jnp.float32), 0.5, 1.5)
    w_qkv = scatter_about(streams_of[5], (D, ATT + 2 * KV_WIDTH), D ** -0.5, 0.15625, ((0, 8),))
    w_mix_in = scatter_about(streams_of[6], (D, 2 * INNER), D ** -0.5, 0.15625, ((0, 8),))
    w_x = scatter_about(streams_of[7], (INNER, DT_RANK + 2 * STATE), INNER ** -0.5, 0.109375, ((0, 8),))
    w_dt = scatter_about(streams_of[8], (INNER, DT_RANK), DT_RANK ** -0.5, 0.625, ((0, 8),))
    w_small = draw_w_small(jax.random.fold_in(streams_of[18], 71), 0)
    gain_att = jnp.clip(1.0 + 0.1 * jax.random.normal(streams_of[10], (ATT,), jnp.float32), 0.5, 1.5)
    gain_ssm = jnp.clip(1.0 + 0.1 * jax.random.normal(streams_of[11], (INNER,), jnp.float32), 0.5, 1.5)
    w_out_att = scatter_about(streams_of[12], (ATT, D), ATT ** -0.5, 0.15625, ((0, 8),))
    w_out_ssm = scatter_about(streams_of[13], (INNER, D), INNER ** -0.5, 0.109375, ((0, 8),))
    gain_ffn = jnp.clip(1.0 + 0.1 * jax.random.normal(streams_of[14], (D,), jnp.float32), 0.5, 1.5)
    w_gate = scatter_about(streams_of[15], (D, FF), D ** -0.5, 0.15625, ((0, 8),))
    w_up = scatter_about(streams_of[16], (D, FF), D ** -0.5, 0.15625, ((0, 8),))
    w_down = scatter_about(streams_of[17], (FF, D), FF ** -0.5, 0.078125, ((0, 8),))
    return dict(tokens=tokens, cotangent=cotangent, route=route, lengths=lengths, gain_in=gain_in, w_qkv=w_qkv, w_mix_in=w_mix_in, w_x=w_x, w_dt=w_dt, w_small=w_small, gain_att=gain_att, gain_ssm=gain_ssm, w_out_att=w_out_att, w_out_ssm=w_out_ssm, gain_ffn=gain_ffn, w_gate=w_gate, w_up=w_up, w_down=w_down)


EPS = 1e-05
PRECISE = lax.Precision.HIGHEST

@jax.custom_vjp
def low(v):
    return lax.optimization_barrier(v.astype(jnp.bfloat16)).astype(jnp.float32)

@jax.custom_vjp
def low_back(v):
    return v

def low_keep(v):
    return (low(v), None)

def low_pass(kept, grad):
    return (grad,)

def back_keep(v):
    return (v, None)

def back_low(kept, grad):
    return (low(grad),)
low.defvjp(low_keep, low_pass)
low_back.defvjp(back_keep, back_low)

def matmul(left_op, right_op):
    return jnp.dot(left_op, right_op, precision=PRECISE, preferred_element_type=jnp.float32)

def rms_scale(row_vals, gain_vec):
    return row_vals * lax.rsqrt(lax.optimization_barrier(jnp.mean(row_vals * row_vals, axis=-1, keepdims=True)) + EPS) * gain_vec

def seq_layout(seq_lens, span_len):
    places = jnp.arange(span_len, dtype=jnp.int32)
    seq_ends = jnp.cumsum(seq_lens).astype(jnp.int32)
    segment = lax.optimization_barrier(jnp.sum((places[:, None] >= seq_ends[None, :]).astype(jnp.int32), axis=1))
    starts = (seq_ends - seq_lens).astype(jnp.int32)
    picked = (segment[:, None] == jnp.arange(seq_lens.shape[0], dtype=jnp.int32)[None, :]).astype(jnp.int32)
    position = places - lax.optimization_barrier(jnp.sum(picked * starts[None, :], axis=1))
    return (segment, position)

def attention(qkv_rows, segment, position):
    span_len = qkv_rows.shape[0]
    groups = HEADS // KV_HEADS
    queries = qkv_rows[:, :ATT].reshape(span_len, KV_HEADS, groups, HEAD)
    all_keys = qkv_rows[:, ATT:ATT + KV_WIDTH].reshape(span_len, KV_HEADS, HEAD)
    all_values = qkv_rows[:, ATT + KV_WIDTH:].reshape(span_len, KV_HEADS, HEAD)
    raw_scores = jnp.einsum('tkgd,ukd->kgtu', queries, all_keys, precision=PRECISE)
    scores = low_back(raw_scores * 0.125)
    visible = (segment[:, None] == segment[None, :]) & (position[None, :] <= position[:, None])
    masked = jnp.where(visible, scores, -1e+30)
    row_top = lax.optimization_barrier(jnp.max(masked, axis=-1, keepdims=True))
    exp_terms = jnp.exp(masked - row_top)
    softmax_p = low(exp_terms / lax.optimization_barrier(jnp.sum(exp_terms, axis=-1, keepdims=True)))
    context = jnp.einsum('kgtu,ukd->tkgd', softmax_p, all_values, precision=PRECISE)
    return low_back(context.reshape(span_len, ATT))

def ssm_scan(inner_u, step_dt, in_b, out_c, decay_a, keep_mask):

    def one_block(carry_state, pieces):

        def one_step(state_now, piece_now):
            u_now, dt_now, b_now, c_now, keep_now = piece_now
            state_now = keep_now * jnp.exp(dt_now[:, None] * decay_a) * state_now + (dt_now * u_now)[:, None] * b_now[None, :]
            return (state_now, lax.optimization_barrier(jnp.sum(state_now * c_now[None, :], axis=1)))
        return lax.scan(one_step, carry_state, pieces)
    span_len = inner_u.shape[0]
    shaped = tuple((member.reshape((span_len // SCAN_BLOCK, SCAN_BLOCK) + member.shape[1:]) for member in (inner_u, step_dt, in_b, out_c, keep_mask)))
    final_state, core_rows = lax.scan(jax.checkpoint(one_block), jnp.zeros((INNER, STATE), jnp.float32), shaped)
    return (core_rows.reshape(span_len, INNER), final_state)

def squares(row_vals):
    return jnp.sum(row_vals * row_vals)

def layer(x_rows, segment, position, params):
    gain_in, w_qkv, w_mix_in, w_x, w_dt, w_small, gain_att, gain_ssm, w_out_att, w_out_ssm, gain_ffn, w_gate, w_up, w_down = params
    span_len = x_rows.shape[0]
    normed = low(rms_scale(x_rows, gain_in))
    qkv_rows = low(low_back(matmul(normed, w_qkv)))
    context = attention(qkv_rows, segment, position)
    mixed = low(low_back(matmul(normed, w_mix_in)))
    inner_x = mixed[:, :INNER]
    gate_z = mixed[:, INNER:]
    conv_w = w_small[:, :CONV]
    conv_b = w_small[:, CONV]
    dt_bias = w_small[:, CONV + 1]
    skip_d = w_small[:, CONV + 2]
    log_a = w_small[:, CONV + 3:]
    conv_sum = conv_b[None, :] + jnp.zeros_like(inner_x)
    for tap_idx in range(CONV):
        shifted = jnp.pad(inner_x, ((tap_idx, 0), (0, 0)))[:span_len]
        conv_sum = conv_sum + conv_w[:, tap_idx][None, :] * shifted * (position >= tap_idx).astype(jnp.float32)[:, None]
    inner_u = jax.nn.silu(conv_sum)
    projected = low(low_back(matmul(low(inner_u), w_x)))
    dt_in = projected[:, :DT_RANK]
    in_b = projected[:, DT_RANK:DT_RANK + STATE]
    out_c = projected[:, DT_RANK + STATE:]
    dt_lin = low_back(lax.dot_general(dt_in, w_dt, (((1,), (1,)), ((), ())), precision=PRECISE, preferred_element_type=jnp.float32))
    step_dt = jax.nn.softplus(dt_lin + dt_bias[None, :])
    decay_a = -jnp.exp(log_a)
    keep_mask = (position > 0).astype(jnp.float32)
    core, final_state = ssm_scan(inner_u, step_dt, in_b, out_c, decay_a, keep_mask)
    ssm_out = (core + skip_d[None, :] * inner_u) * jax.nn.silu(gate_z)
    branch_att = low(rms_scale(context, gain_att))
    branch_ssm = low(rms_scale(ssm_out, gain_ssm))
    mixer_out = low_back(0.5 * (matmul(branch_att, w_out_att) + matmul(branch_ssm, w_out_ssm)))
    hidden = x_rows + mixer_out
    ffn_in = low(rms_scale(hidden, gain_ffn))
    gate_proj = low_back(matmul(ffn_in, w_gate))
    up_proj = low_back(matmul(ffn_in, w_up))
    act_low = low(jax.nn.silu(gate_proj) * up_proj)
    ffn_out = low_back(matmul(act_low, w_down))
    result = hidden + ffn_out
    sums = jnp.stack([squares(x_rows), squares(context), squares(ssm_out), squares(mixer_out), squares(ffn_out), squares(result)])
    return (result, sums)

def reference(tokens, cotangent, route, lengths, gain_in, w_qkv, w_mix_in, w_x, w_dt, w_small, gain_att, gain_ssm, w_out_att, w_out_ssm, gain_ffn, w_gate, w_up, w_down):
    row_total = tokens.shape[1]
    slab = N_FSDP * TOK
    base = (jnp.arange(row_total, dtype=jnp.int32) // slab * slab).astype(jnp.int32)
    owner = (route + base[None, :]).astype(jnp.int32)

    def to_owner(given):
        placed = jax.vmap(lambda values_in, index_row: jnp.zeros_like(values_in).at[index_row].set(values_in))(given, owner)
        placed = placed.reshape(MICRO, N_SEQ, N_FSDP, TOK, D).transpose(0, 2, 1, 3, 4)
        return placed.reshape(MICRO * N_FSDP, N_SEQ * TOK, D)

    def to_given(packs):
        placed = packs.reshape(MICRO, N_FSDP, N_SEQ, TOK, D).transpose(0, 2, 1, 3, 4).reshape(MICRO, row_total, D)
        return jax.vmap(lambda values_in, index_row: jnp.take(values_in, index_row, axis=0))(placed, owner)
    x_packs = to_owner(tokens.astype(jnp.float32))
    cot_packs = to_owner(cotangent.astype(jnp.float32))
    segments, positions = jax.vmap(lambda seq_lens: seq_layout(seq_lens, N_SEQ * TOK))(lengths.reshape(MICRO * N_FSDP, SEQS))
    params = tuple((param.astype(jnp.float32) for param in (gain_in, w_qkv, w_mix_in, w_x, w_dt, w_small, gain_att, gain_ssm, w_out_att, w_out_ssm, gain_ffn, w_gate, w_up, w_down)))

    def forward(x_all, param_set):

        def per_pack(totals, pieces):
            x_rows, segment, position = pieces
            result, sums = jax.checkpoint(layer)(x_rows, segment, position, param_set)
            return (totals + sums, result)
        totals, results = lax.scan(per_pack, jnp.zeros((6,), jnp.float32), (x_all, segments, positions))
        return (results, totals)
    results, pullback, totals = jax.vjp(forward, x_packs, params, has_aux=True)
    grad_x, grad_params = pullback(cot_packs)
    grad_list = tuple(grad_params)
    widths = jnp.array([D, ATT, INNER, D, D, D], jnp.float32)
    rms = jnp.sqrt(totals / (widths * (MICRO * row_total)))
    output = to_given(results).astype(jnp.bfloat16)
    grad_tokens = to_given(grad_x).astype(jnp.bfloat16)
    return (output, grad_tokens) + grad_list[:6] + (grad_list[5][:, CONV + 1],) + grad_list[6:] + (rms,)
```

```python
from functools import partial

import jax
import jax.numpy as jnp
from jax import lax
from jax.experimental import pallas as pl
from jax.experimental.pallas import tpu as pltpu
from jax.sharding import PartitionSpec as P

D = 1600
HEADS = 25
KV_HEADS = 5
HEAD = 64
INNER = 3200
STATE = 16
CONV = 4
DT_RANK = 100
MICRO = 2
ATT = 1600
KV_WIDTH = 320
PROJ = DT_RANK + 2 * STATE
PROJ_PAD = 144
LANES = 128
EPS = 1e-05
BF = jnp.bfloat16
F32 = jnp.float32


def dot(left_op, right_op, left_dim, right_dim):
    return lax.dot_general(
        left_op, right_op, (((left_dim,), (right_dim,)), ((), ())), preferred_element_type=F32
    )


def rms_scale(row_vals, gain_vec):
    return (
        row_vals * lax.rsqrt(jnp.mean(row_vals * row_vals, axis=-1, keepdims=True) + EPS) * gain_vec
    )


def seq_layout(seq_lens, span_len):
    places = jnp.arange(span_len, dtype=jnp.int32)
    seq_ends = jnp.cumsum(seq_lens)
    segment = jnp.sum((places[:, None] >= seq_ends[None, :]).astype(jnp.int32), axis=1)
    starts = seq_ends - seq_lens
    picked = (segment[:, None] == jnp.arange(seq_lens.shape[0], dtype=jnp.int32)[None, :]).astype(
        jnp.int32
    )
    position = places - jnp.sum(picked * starts[None, :], axis=1)
    return (segment, position)


def swap(array, k):
    size = lax.axis_size("seq")
    return lax.ppermute(array, "seq", [(i, i ^ k) for i in range(size)])


def pick(blocks, at):
    return lax.dynamic_index_in_dim(blocks, at, 0, keepdims=False)


def seq_deal(blocks):
    size, here = lax.axis_size("seq"), lax.axis_index("seq")
    out = blocks
    for k in range(1, size):
        there = here ^ k
        out = lax.dynamic_update_index_in_dim(out, swap(pick(blocks, there), k), there, 0)
    return out


def seq_gather(block):
    size, here = lax.axis_size("seq"), lax.axis_index("seq")
    out = lax.dynamic_update_index_in_dim(
        jnp.zeros((size,) + block.shape, block.dtype), block, here, 0
    )
    for k in range(1, size):
        out = lax.dynamic_update_index_in_dim(out, swap(block, k), here ^ k, 0)
    return out


def seq_scatter(blocks):
    size, here = lax.axis_size("seq"), lax.axis_index("seq")
    total = pick(blocks, here).astype(F32)
    for k in range(1, size):
        total = total + swap(pick(blocks, here ^ k).astype(BF), k).astype(F32)
    return total


def seq_sum(array):
    return jnp.sum(seq_gather(array).astype(F32), axis=0)


def routing(route_rows, tok_rows):
    fsdp_count, fsdp_rank = lax.axis_size("fsdp"), lax.axis_index("fsdp")
    micro = route_rows.shape[0]
    per_peer = tok_rows // fsdp_count
    target_dev = (route_rows // tok_rows).reshape(micro, fsdp_count, tok_rows)
    target_slot = (route_rows % tok_rows).reshape(micro, fsdp_count, tok_rows)
    steps = jnp.arange(tok_rows, dtype=jnp.int32)
    same = target_dev[:, :, :, None] == target_dev[:, :, None, :]
    earlier = steps[None, :] < steps[:, None]
    rank = jnp.sum((same & earlier).astype(jnp.int32), axis=3)
    my_dev = lax.dynamic_index_in_dim(target_dev, fsdp_rank, 1, keepdims=False)
    my_rank = lax.dynamic_index_in_dim(rank, fsdp_rank, 1, keepdims=False)
    micros = jnp.arange(micro, dtype=jnp.int32)
    send_at = (my_dev * micro + micros[:, None]) * per_peer + my_rank
    ranks = jnp.arange(per_peer, dtype=jnp.int32)
    mine = (target_dev == fsdp_rank)[:, :, None, :] & (rank[:, :, None, :] == ranks[:, None])
    slot = jnp.sum(mine.astype(jnp.int32) * target_slot[:, :, None, :], axis=3)
    land_at = (micros[:, None, None] * tok_rows + slot).transpose(1, 0, 2).reshape(-1)
    rows = jnp.arange(micro * tok_rows, dtype=jnp.int32)
    send_hot = (rows[:, None] == send_at.reshape(-1)[None, :]).astype(BF)
    land_hot = (rows[:, None] == land_at[None, :]).astype(BF)
    return send_hot, land_hot


def exchange(rows):
    return lax.all_to_all(rows, "fsdp", split_axis=0, concat_axis=0, tiled=True)


def bring(rows, send_hot, land_hot):
    sent = dot(send_hot, rows, 1, 0).astype(BF)
    return dot(land_hot, exchange(sent), 1, 0).astype(BF)


def give(rows, send_hot, land_hot):
    sent = dot(land_hot, rows, 0, 0).astype(BF)
    return dot(send_hot, exchange(sent), 0, 0).astype(BF)


def lane_groups(channels, most=4):
    tiles, out, first = channels // LANES, [], 0
    while first < tiles:
        count = min(most, tiles - first)
        out.append((first, count))
        first += count
    return out


def scan_kernel(groups, steps, dtm_ref, dtu_ref, b_ref, c_ref, a_ref, core_ref):
    place = lax.broadcasted_iota(jnp.int32, (8, LANES), 0)
    for first, count in groups:
        spans = [pl.ds((first + i) * LANES, LANES) for i in range(count)]
        rates = [a_ref[:, span] for span in spans]

        def block(k, held):
            held = list(held)
            base = pl.multiple_of(k * 8, 8)
            rows = pl.ds(base, 8)
            dts = [dtm_ref[rows, span] for span in spans]
            dus = [dtu_ref[rows, span] for span in spans]
            ys = [jnp.zeros((8, LANES), F32)] * count
            for j in range(8):
                b_now, c_now = b_ref[base + j], c_ref[base + j]
                for i in range(count):
                    decay = jnp.exp(dts[i][j : j + 1] * rates[i])
                    held[i] = decay * held[i] + dus[i][j : j + 1] * b_now
                    y = jnp.sum(held[i] * c_now, axis=0, keepdims=True)
                    ys[i] = jnp.where(place == j, y, ys[i])
            for i, span in enumerate(spans):
                core_ref[rows, span] = ys[i]
            return tuple(held)

        zero = jnp.zeros((STATE, LANES), F32)
        lax.fori_loop(0, steps // 8, block, (zero,) * count)


def scan_back_kernel(
    groups,
    steps,
    dtm_ref,
    dtu_ref,
    dcore_ref,
    b_ref,
    c_ref,
    a_ref,
    ddtu_ref,
    ddt_ref,
    da_ref,
    db_ref,
    dc_ref,
    hs,
    acc_b,
    acc_c,
):
    place = lax.broadcasted_iota(jnp.int32, (8, LANES), 0)
    zero = jnp.zeros((STATE, LANES), F32)
    for at, (first, count) in enumerate(groups):
        spans = [pl.ds((first + i) * LANES, LANES) for i in range(count)]
        slots = [pl.ds(i * LANES, LANES) for i in range(count)]
        rates = [a_ref[:, span] for span in spans]
        for slot in slots:
            hs[0, :, slot] = zero

        def block(k, held):
            held = list(held)
            base = pl.multiple_of(k * 8, 8)
            rows = pl.ds(base, 8)
            dts = [dtm_ref[rows, span] for span in spans]
            dus = [dtu_ref[rows, span] for span in spans]
            for j in range(8):
                b_now = b_ref[base + j]
                for i in range(count):
                    decay = jnp.exp(dts[i][j : j + 1] * rates[i])
                    held[i] = decay * held[i] + dus[i][j : j + 1] * b_now
                    hs[base + j + 1, :, slots[i]] = held[i]
            return tuple(held)

        lax.fori_loop(0, steps // 8, block, (zero,) * count)

        def back(k, carry):
            carry = list(carry)
            base = pl.multiple_of(steps - 8 - k * 8, 8)
            rows = pl.ds(base, 8)
            dts = [dtm_ref[rows, span] for span in spans]
            dus = [dtu_ref[rows, span] for span in spans]
            dys = [dcore_ref[rows, span] for span in spans]
            out_u = [jnp.zeros((8, LANES), F32)] * count
            out_t = [jnp.zeros((8, LANES), F32)] * count
            for j in reversed(range(8)):
                t = base + j
                b_now, c_now = b_ref[t], c_ref[t]
                sum_b = sum_c = zero
                for i in range(count):
                    later, rate_sum = carry[i]
                    dt, du, dy = dts[i][j : j + 1], dus[i][j : j + 1], dys[i][j : j + 1]
                    g = later + dy * c_now
                    sum_c = sum_c + hs[t + 1, :, slots[i]] * dy
                    sum_b = sum_b + g * du
                    through = g * jnp.exp(dt * rates[i])
                    moved = through * hs[t, :, slots[i]]
                    to_u = jnp.sum(g * b_now, axis=0, keepdims=True)
                    to_t = jnp.sum(moved * rates[i], axis=0, keepdims=True)
                    out_u[i] = jnp.where(place == j, to_u, out_u[i])
                    out_t[i] = jnp.where(place == j, to_t, out_t[i])
                    carry[i] = (through, rate_sum + moved * dt)
                if at == 0:
                    acc_b[t] = sum_b
                    acc_c[t] = sum_c
                else:
                    acc_b[t] = acc_b[t] + sum_b
                    acc_c[t] = acc_c[t] + sum_c
            for i, span in enumerate(spans):
                ddtu_ref[rows, span] = out_u[i]
                ddt_ref[rows, span] = out_t[i]
            return tuple(carry)

        ends = lax.fori_loop(0, steps // 8, back, ((zero, zero),) * count)
        for i, span in enumerate(spans):
            da_ref[:, span] = ends[i][1]
    ones = jnp.ones((8, LANES), F32)
    for acc, out in ((acc_b, db_ref), (acc_c, dc_ref)):
        out[...] = lax.dot_general(
            ones,
            acc[...].reshape(steps * STATE, LANES),
            (((1,), (1,)), ((), ())),
            precision=lax.Precision.HIGHEST,
            preferred_element_type=F32,
        )


VMEM_BYTES = 60 * 2**20


def scan_forward(dtm, dtu, b_wide, c_wide, rates):
    steps, channels = dtm.shape
    return pl.pallas_call(
        partial(scan_kernel, lane_groups(channels), steps),
        out_shape=jax.ShapeDtypeStruct((steps, channels), F32),
        in_specs=[pl.BlockSpec(memory_space=pltpu.VMEM)] * 5,
        out_specs=pl.BlockSpec(memory_space=pltpu.VMEM),
        compiler_params=pltpu.CompilerParams(vmem_limit_bytes=VMEM_BYTES),
        cost_estimate=pl.CostEstimate(
            flops=16 * steps * channels * STATE,
            bytes_accessed=40_000_000,
            transcendentals=steps * channels * STATE,
        ),
        name="scan_forward",
    )(dtm, dtu, b_wide, c_wide, rates)


def scan_backward(dtm, dtu, dcore, b_wide, c_wide, rates):
    steps, channels = dtm.shape
    groups = lane_groups(channels)
    rows = jax.ShapeDtypeStruct((steps, channels), F32)
    flat = jax.ShapeDtypeStruct((8, steps * STATE), F32)
    ddtu, ddt, da, db, dc = pl.pallas_call(
        partial(scan_back_kernel, groups, steps),
        out_shape=[rows, rows, jax.ShapeDtypeStruct((STATE, channels), F32), flat, flat],
        in_specs=[pl.BlockSpec(memory_space=pltpu.VMEM)] * 6,
        out_specs=[pl.BlockSpec(memory_space=pltpu.VMEM)] * 5,
        scratch_shapes=[
            pltpu.VMEM((steps + 1, STATE, groups[0][1] * LANES), F32),
            pltpu.VMEM((steps, STATE, LANES), F32),
            pltpu.VMEM((steps, STATE, LANES), F32),
        ],
        compiler_params=pltpu.CompilerParams(vmem_limit_bytes=VMEM_BYTES),
        cost_estimate=pl.CostEstimate(
            flops=40 * steps * channels * STATE,
            bytes_accessed=100_000_000,
            transcendentals=2 * steps * channels * STATE,
        ),
        name="scan_backward",
    )(dtm, dtu, dcore, b_wide, c_wide, rates)
    return ddtu, ddt, da, db[0].reshape(steps, STATE), dc[0].reshape(steps, STATE)


def conv_act(position, inner, tap_weights, tap_bias):
    row_count = inner.shape[0]
    ext_rows = jnp.pad(inner, ((CONV - 1, 0), (0, 0)))
    conv_sum = tap_bias[None, :] + jnp.zeros(inner.shape, F32)
    for tap_idx in range(CONV):
        shifted = ext_rows[CONV - 1 - tap_idx : CONV - 1 - tap_idx + row_count]
        conv_sum = (
            conv_sum
            + tap_weights[:, tap_idx][None, :]
            * shifted
            * (position >= tap_idx).astype(F32)[:, None]
        )
    return jax.nn.silu(conv_sum)


def gate_mix(core, inner_u, skip_d, gate_z):
    return (core + skip_d[None, :] * inner_u) * jax.nn.silu(gate_z)


def swiglu(gate_proj, up_proj):
    return jax.nn.silu(gate_proj) * up_proj


def squares(row_vals):
    return jnp.sum(row_vals * row_vals)


def local(
    tokens,
    cotangent,
    route,
    lengths,
    gain_in,
    w_qkv,
    w_mix_in,
    w_x,
    w_dt,
    w_small,
    gain_att,
    gain_ssm,
    w_out_att,
    w_out_ssm,
    gain_ffn,
    w_gate,
    w_up,
    w_down,
):
    S, N = lax.axis_size("seq"), lax.axis_size("fsdp")
    s = lax.axis_index("seq")
    micro, tok = tokens.shape[:2]
    pack = tok * S
    rows_d = gain_in.shape[0] // N
    ff = w_gate.shape[1]
    ch_piece, ff_piece = INNER // (N * S), ff // (N * S)
    ch = -(-INNER // (S * LANES)) * LANES
    ffs = -(-ff // (S * LANES)) * LANES
    cols = D // S
    groups = HEADS // KV_HEADS
    first_heads = [(HEADS * i + S - 1) // S for i in range(S + 1)]
    head_counts = [first_heads[i + 1] - first_heads[i] for i in range(S)]
    most = max(head_counts)
    width = most * HEAD
    first_head = jnp.array(first_heads, jnp.int32)[s]
    head_live = jnp.arange(most) < jnp.array(head_counts, jnp.int32)[s]
    live = jnp.repeat(head_live, HEAD).astype(F32)[None, :]
    in_low = (first_head + jnp.arange(most)) // groups <= s

    def gather(shard):
        return lax.all_gather(shard, "fsdp", axis=0, tiled=True)

    def scatter(whole):
        rows, wide = whole.shape[0] // N, whole.shape[1]
        fill = -rows % 8
        whole = whole.astype(BF)
        if fill:
            whole = jnp.pad(whole.reshape(N, rows, wide), ((0, 0), (0, fill), (0, 0)))
            whole = whole.reshape(N * (rows + fill), wide)
        return lax.psum_scatter(whole, "fsdp", scatter_dimension=0, tiled=True)[:rows]

    def part(shard, axis, chunks, wide):
        shape = shard.shape
        piece = shape[axis] // (chunks * S)
        shaped = shard.reshape(shape[:axis] + (chunks, S, piece) + shape[axis + 1 :])
        picked = lax.dynamic_index_in_dim(shaped, s, axis + 1, keepdims=False)
        fill = [(0, 0)] * picked.ndim
        fill[axis + 1] = (0, wide - piece)
        return jnp.pad(picked, fill).reshape(
            shape[:axis] + (chunks * wide,) + shape[axis + 1 :]
        )

    def span(array, axis, start, size):
        return lax.dynamic_slice_in_dim(array, start, size, axis)

    send_hot, land_hot = routing(route, tok)
    x_own = bring(tokens.reshape(micro * tok, D), send_hot, land_hot)
    x_own = x_own.reshape(micro, tok, D)
    q_start = first_head * HEAD
    mix_parts = part(w_mix_in, 1, 2 * N, ch // N)
    small_shard = jnp.concatenate(
        [w_x, w_dt, w_small, jnp.zeros((w_x.shape[0], 1), BF)], axis=1
    )
    w_in = gather(
        jnp.concatenate(
            [
                span(w_qkv, 1, q_start, width),
                span(w_qkv, 1, ATT + s * HEAD, 2 * HEAD),
                span(w_qkv, 1, ATT + KV_WIDTH + s * HEAD, 2 * HEAD),
                mix_parts,
            ],
            axis=1,
        )
    )
    w_small_part = gather(part(small_shard, 0, 1, ch // N))
    w_out_part = gather(part(w_out_ssm, 0, 1, ch // N))
    w_att_cols = gather(span(w_out_att, 1, s * cols, cols))
    w_gu = gather(jnp.concatenate([part(w_gate, 1, N, ffs // N), part(w_up, 1, N, ffs // N)], axis=1))
    w_down_part = gather(part(w_down, 0, 1, ffs // N))
    cot_own = bring(cotangent.reshape(micro * tok, D), send_hot, land_hot)
    cot_own = cot_own.reshape(micro, tok, D)

    w_att_pad = jnp.pad(w_att_cols, ((0, width), (0, 0)))
    w_att_part = (
        seq_deal(jnp.stack([w_att_pad[h * HEAD : h * HEAD + width] for h in first_heads[:S]]))
        .transpose(1, 0, 2)
        .reshape(width, D)
    )

    w_x_part = jnp.pad(w_small_part[:, :PROJ], ((0, 0), (0, PROJ_PAD - PROJ)))
    w_dt_part = w_small_part[:, PROJ : PROJ + DT_RANK]
    small_par = w_small_part[:, PROJ + DT_RANK : PROJ + DT_RANK + CONV + 3 + STATE].astype(F32)
    conv_w = small_par[:, :CONV]
    conv_b = small_par[:, CONV]
    dt_bias = small_par[:, CONV + 1]
    skip_d = small_par[:, CONV + 2]
    decay_a = -jnp.exp(small_par[:, CONV + 3 :])
    rates = decay_a.T
    gain_att_part = span(jnp.pad(gain_att, (0, width)), 0, q_start, width)
    gain_ssm_part = part(gain_ssm, 0, N, ch // N)

    def to_pack(block):
        return seq_gather(block).reshape(pack, block.shape[-1])

    def to_own(partial_rows):
        return seq_scatter(partial_rows.reshape(S, tok, partial_rows.shape[-1]))

    stats = jnp.zeros((6,), F32)
    gains = [jnp.zeros((n,), F32) for n in (D, width, ch, D)]
    kept = []
    results = []
    for m in range(micro):
        segment, position = seq_layout(lengths[m, 0], pack)
        visible = (segment[:, None] == segment[None, :]) & (position[None, :] <= position[:, None])
        x_mine = x_own[m].astype(F32)
        x_pack = to_pack(x_own[m]).astype(F32)
        normed_low = rms_scale(x_pack, gain_in).astype(BF)
        opened = dot(normed_low, w_in, 1, 0).astype(BF)
        q = opened[:, :width].reshape(pack, most, HEAD)
        kv = opened[:, width : width + 4 * HEAD].reshape(pack, 4, HEAD)
        pick_low = in_low[None, :, None]
        keys = jnp.where(pick_low, kv[:, 0:1], kv[:, 1:2])
        values = jnp.where(pick_low, kv[:, 2:3], kv[:, 3:4])
        scores = jnp.einsum("thd,uhd->htu", q, keys, preferred_element_type=F32) * 0.125
        masked = jnp.where(visible, scores, -1e30)
        row_top = jnp.max(masked, axis=-1, keepdims=True)
        exp_terms = jnp.exp(masked - row_top)
        row_total = jnp.sum(exp_terms, axis=-1, keepdims=True)
        probs = exp_terms / row_total
        context = (
            jnp.einsum("htu,uhd->thd", probs.astype(BF), values, preferred_element_type=F32)
        ).reshape(pack, width) * live
        at = width + 4 * HEAD
        inner = opened[:, at : at + ch].astype(F32)
        gate_z = opened[:, at + ch :].astype(F32)
        inner_u, conv_back = jax.vjp(partial(conv_act, position), inner, conv_w, conv_b)
        u_low = inner_u.astype(BF)
        projected = seq_sum(dot(w_x_part, u_low, 0, 1).astype(BF)).astype(BF)
        dt_in = projected[:DT_RANK]
        in_b = projected[DT_RANK : DT_RANK + STATE].astype(F32)
        out_c = projected[DT_RANK + STATE : PROJ].astype(F32)
        dt_lin = dot(dt_in, w_dt_part, 0, 1) + dt_bias[None, :]
        step_dt = jax.nn.softplus(dt_lin)
        dtm = jnp.where((position > 0)[:, None], step_dt, 1e30)
        dtu = step_dt * inner_u
        b_wide = jnp.broadcast_to(in_b.T[:, :, None], (pack, STATE, LANES))
        c_wide = jnp.broadcast_to(out_c.T[:, :, None], (pack, STATE, LANES))
        core = scan_forward(dtm, dtu, b_wide, c_wide, rates)
        ssm_out, gate_back = jax.vjp(gate_mix, core, inner_u, skip_d, gate_z)
        row_sums = jnp.stack(
            [jnp.sum(context * context, axis=1), jnp.sum(ssm_out * ssm_out, axis=1)]
        )
        row_sums = seq_sum(row_sums)
        scale_att = lax.rsqrt(row_sums[0] / ATT + EPS)[:, None]
        scale_ssm = lax.rsqrt(row_sums[1] / INNER + EPS)[:, None]
        att_low = (context * scale_att * gain_att_part).astype(BF)
        ssm_low = (ssm_out * scale_ssm * gain_ssm_part).astype(BF)
        mixer_out = to_own(
            0.5 * (dot(att_low, w_att_part, 1, 0) + dot(ssm_low, w_out_part, 1, 0))
        )
        hidden = x_mine + mixer_out
        ffn_in, ffn_norm_back = jax.vjp(rms_scale, hidden, gain_ffn)
        ffn_low = to_pack(ffn_in.astype(BF))
        gate_proj = dot(ffn_low, w_gu[:, :ffs], 1, 0)
        up_proj = dot(ffn_low, w_gu[:, ffs:], 1, 0)
        act_val, act_back = jax.vjp(swiglu, gate_proj, up_proj)
        act_low = act_val.astype(BF)
        ffn_out = to_own(dot(act_low, w_down_part, 1, 0))
        result = hidden + ffn_out
        results.append(result.astype(BF))
        here = lax.dynamic_slice_in_dim(row_sums, s * tok, tok, 1)
        stats = stats + jnp.stack(
            [
                squares(x_mine),
                jnp.sum(here[0]),
                jnp.sum(here[1]),
                squares(mixer_out),
                squares(ffn_out),
                squares(result),
            ]
        )
        cot_mine = cot_own[m].astype(F32)
        cot_low = to_pack(cot_own[m])
        d_act = dot(cot_low, w_down_part, 1, 1)
        d_gate, d_up = act_back(d_act)
        dgu_low = jnp.concatenate([d_gate, d_up], axis=1).astype(BF)
        d_ffn_in = to_own(dot(dgu_low, w_gu, 1, 1))
        d_hidden_norm, d_gain_ffn = ffn_norm_back(d_ffn_in)
        d_hidden = cot_mine + d_hidden_norm
        dmix_low = to_pack(d_hidden.astype(BF))
        d_att = 0.5 * dot(dmix_low, w_att_part, 1, 1) * live
        d_ssm = lax.optimization_barrier(0.5 * dot(dmix_low, w_out_part, 1, 1))
        d_gain_att = jnp.sum(d_att * context * scale_att, axis=0)
        d_gain_ssm = jnp.sum(d_ssm * ssm_out * scale_ssm, axis=0)
        t_att = d_att * gain_att_part
        t_ssm = d_ssm * gain_ssm_part
        back_sums = seq_sum(
            jnp.stack([jnp.sum(t_att * context, axis=1), jnp.sum(t_ssm * ssm_out, axis=1)])
        )
        d_context = (
            t_att * scale_att - context * scale_att**3 * (back_sums[0] / ATT)[:, None]
        ) * live
        d_ssm_out = t_ssm * scale_ssm - ssm_out * scale_ssm**3 * (back_sums[1] / INNER)[:, None]
        d_core, d_u_gate, d_skip, d_gate_z = gate_back(d_ssm_out)
        ddtu, ddt, d_rates, d_in_b, d_out_c = scan_backward(
            dtm, dtu, d_core, b_wide, c_wide, rates
        )
        d_decay = d_rates.T
        d_step = ddt + ddtu * inner_u
        d_lin = d_step * jax.nn.sigmoid(dt_lin)
        d_dt_bias = jnp.sum(d_lin, axis=0)
        ddt_low = d_lin.astype(BF)
        dproj = jnp.concatenate(
            [
                dot(w_dt_part, ddt_low, 0, 1),
                d_in_b.T,
                d_out_c.T,
                jnp.zeros((PROJ_PAD - PROJ, pack), F32),
            ],
            axis=0,
        )
        dproj_low = seq_sum(dproj.astype(BF)).astype(BF)
        d_inner_u = d_u_gate + ddtu * step_dt + dot(dproj_low, w_x_part, 0, 1)
        d_inner, d_conv_w, d_conv_b = conv_back(d_inner_u)
        small_grad = jnp.concatenate(
            [d_conv_w, d_conv_b[:, None], d_dt_bias[:, None], d_skip[:, None], d_decay * decay_a],
            axis=1,
        )
        dctx_low = d_context.astype(BF).reshape(pack, most, HEAD)
        d_values = jnp.einsum(
            "htu,thd->uhd", probs.astype(BF), dctx_low, preferred_element_type=F32
        )
        d_probs = jnp.einsum("thd,uhd->htu", dctx_low, values, preferred_element_type=F32)
        dscore_low = (
            probs * (d_probs - jnp.sum(probs * d_probs, axis=-1, keepdims=True))
        ).astype(BF)
        d_q = jnp.einsum("htu,uhd->thd", dscore_low, keys, preferred_element_type=F32) * 0.125
        d_keys = jnp.einsum("htu,thd->uhd", dscore_low, q, preferred_element_type=F32) * 0.125
        low_part, high_part = pick_low, ~pick_low

        def kv_sum(d_heads):
            return [
                jnp.sum(jnp.where(low_part, d_heads, 0.0), axis=1),
                jnp.sum(jnp.where(high_part, d_heads, 0.0), axis=1),
            ]

        d_opened = jnp.concatenate(
            [d_q.reshape(pack, width)] + kv_sum(d_keys) + kv_sum(d_values) + [d_inner, d_gate_z],
            axis=1,
        ).astype(BF)
        d_normed = to_own(dot(d_opened, w_in, 1, 1))
        _, norm_back = jax.vjp(rms_scale, x_mine, gain_in)
        d_x_norm, d_gain_in = norm_back(d_normed)
        d_x = d_hidden + d_x_norm
        gains = [
            a + b for a, b in zip(gains, (d_gain_in, d_gain_att, d_gain_ssm, d_gain_ffn))
        ]
        kept.append(
            dict(
                act=act_low,
                cot=cot_low,
                ffn=ffn_low,
                dgu=dgu_low,
                att=att_low,
                ssm=ssm_low,
                dmix=dmix_low,
                u=u_low,
                dproj=dproj_low,
                dt_in=dt_in,
                ddt=ddt_low,
                normed=normed_low,
                opened=d_opened,
                small=small_grad,
                dx=d_x.astype(BF),
            )
        )

    def both(name, axis=0):
        return jnp.concatenate([one[name] for one in kept], axis=axis)

    g_down = scatter(dot(both("act"), both("cot"), 0, 0))
    g_gu = scatter(dot(both("ffn"), both("dgu"), 0, 0))
    g_att_rows = (0.5 * dot(both("att"), both("dmix"), 0, 0)).astype(BF)
    g_att_blocks = seq_deal(g_att_rows.reshape(width, S, cols).transpose(1, 0, 2))
    g_att_whole = jnp.concatenate(
        [g_att_blocks[i, : head_counts[i] * HEAD] for i in range(S)], axis=0
    )
    g_att = scatter(g_att_whole).astype(F32)
    g_ssm = scatter(0.5 * dot(both("ssm"), both("dmix"), 0, 0))
    g_xdt = jnp.concatenate(
        [
            dot(both("u"), both("dproj", 1), 0, 1)[:, :PROJ],
            dot(both("ddt"), both("dt_in", 1), 0, 1),
            kept[0]["small"] + kept[1]["small"],
            jnp.zeros((ch, 1), F32),
        ],
        axis=1,
    )
    g_xdt = scatter(g_xdt)
    g_in = scatter(dot(both("normed"), both("opened"), 0, 0))

    def rows_back(shard):
        blocks = seq_deal(shard.reshape(shard.shape[0], S, cols).transpose(1, 0, 2))
        return blocks.reshape(S * shard.shape[0], cols).astype(F32)

    def cols_back(shard, chunks, piece):
        rows = shard.shape[0]
        blocks = shard.reshape(rows, S, chunks // S, -1)[..., :piece].transpose(1, 0, 2, 3)
        got = seq_deal(blocks)
        return got.transpose(1, 2, 0, 3).reshape(rows, chunks * piece).astype(F32)

    out_down = rows_back(g_down[:ff_piece])
    out_ssm = rows_back(g_ssm[:ch_piece])
    out_gate = cols_back(g_gu[:, :ffs], N, ff_piece)
    out_up = cols_back(g_gu[:, ffs:], N, ff_piece)
    at = width + 4 * HEAD
    out_mix = cols_back(g_in[:, at:], 2 * N, ch_piece)
    kv_at = jnp.zeros((rows_d, 2 * KV_WIDTH), BF)
    kv_at = lax.dynamic_update_slice_in_dim(kv_at, g_in[:, width : width + 2 * HEAD], s * HEAD, 1)
    kv_at = lax.dynamic_update_slice_in_dim(
        kv_at, g_in[:, width + 2 * HEAD : at], KV_WIDTH + s * HEAD, 1
    )
    q_at = jnp.zeros((rows_d, ATT + width), BF)
    q_live = jnp.where(live > 0, g_in[:, :width], 0)
    q_at = lax.dynamic_update_slice_in_dim(q_at, q_live, q_start, 1)
    qkv_at = jnp.concatenate([q_at[:, :ATT], kv_at], axis=1)
    out_qkv = seq_scatter(qkv_at.reshape(rows_d, S, -1).transpose(1, 0, 2))
    small_all = seq_gather(g_xdt[:ch_piece]).reshape(-1, g_xdt.shape[1]).astype(F32)
    out_x = span(small_all[:, :PROJ], 1, s * (PROJ // S), PROJ // S)
    out_dt = span(small_all[:, PROJ : PROJ + DT_RANK], 1, s * (DT_RANK // S), DT_RANK // S)
    out_small = small_all[:, PROJ + DT_RANK : PROJ + DT_RANK + CONV + 3 + STATE]

    att_at = lax.dynamic_update_slice_in_dim(
        jnp.zeros((ATT + width,), F32), gains[1] * live[0], q_start, 0
    )[:ATT]
    ssm_at = lax.dynamic_update_index_in_dim(
        jnp.zeros((N, S, ch_piece), F32), gains[2].reshape(N, -1)[:, :ch_piece], s, 1
    ).reshape(INNER)
    sums = lax.psum(
        jnp.concatenate([gains[0], att_at, ssm_at, gains[3], stats]), ("seq", "fsdp")
    )
    ends = [0, D, D + ATT, D + ATT + INNER, D + ATT + INNER + D, D + ATT + INNER + D + 6]
    g_gain_in, g_gain_att, g_gain_ssm, g_gain_ffn, stat_sum = [
        sums[a:b] for a, b in zip(ends[:-1], ends[1:])
    ]
    widths = jnp.array([D, ATT, INNER, D, D, D], F32)
    rms = jnp.sqrt(stat_sum / (widths * (micro * pack * N)))
    outputs = give(jnp.concatenate(results, axis=0), send_hot, land_hot)
    input_grads = give(both("dx"), send_hot, land_hot)
    return (
        outputs.reshape(tokens.shape),
        input_grads.reshape(tokens.shape),
        g_gain_in,
        out_qkv,
        out_mix,
        out_x,
        out_dt,
        out_small,
        out_small[:, CONV + 1],
        g_gain_att,
        g_gain_ssm,
        g_att,
        out_ssm,
        g_gain_ffn,
        out_gate,
        out_up,
        out_down,
        rms,
    )


def solution(mesh):
    rows = P(None, ("seq", "fsdp"), None)
    shard = P("fsdp", None)
    both = P("fsdp", "seq")
    placed = (rows, rows, P(None, "seq"), P(None, "fsdp", None), P())
    placed += (shard,) * 5 + (P(), P(), shard, shard, P(), shard, shard, shard)
    return jax.shard_map(
        local,
        mesh=mesh,
        in_specs=placed,
        out_specs=(
            rows,
            rows,
            P(),
            both,
            both,
            both,
            both,
            shard,
            P("fsdp"),
            P(),
            P(),
            both,
            both,
            P(),
            both,
            both,
            both,
            P(),
        ),
        check_vma=False,
    )
```

```python
from functools import partial

import jax
import jax.numpy as jnp
import numpy as np
from jax import lax
from jax.experimental import pallas as pl
from jax.experimental.pallas import tpu as pltpu
from jax.sharding import PartitionSpec as P

D = 1600
HEADS = 25
KV_HEADS = 5
HEAD = 64
INNER = 3200
STATE = 16
CONV = 4
DT_RANK = 100
MICRO = 2
ATT = 1600
KV_WIDTH = 320
PROJ = DT_RANK + 2 * STATE
PROJ_PAD = 144
LANES = 128
EPS = 1e-05
BF = jnp.bfloat16
F32 = jnp.float32


def dot(left_op, right_op, left_dim, right_dim):
    return lax.dot_general(
        left_op, right_op, (((left_dim,), (right_dim,)), ((), ())), preferred_element_type=F32
    )


def rms_scale(row_vals, gain_vec):
    return (
        row_vals * lax.rsqrt(jnp.mean(row_vals * row_vals, axis=-1, keepdims=True) + EPS) * gain_vec
    )


def seq_layout(seq_lens, span_len):
    places = jnp.arange(span_len, dtype=jnp.int32)
    seq_ends = jnp.cumsum(seq_lens)
    segment = jnp.sum((places[:, None] >= seq_ends[None, :]).astype(jnp.int32), axis=1)
    starts = seq_ends - seq_lens
    picked = (segment[:, None] == jnp.arange(seq_lens.shape[0], dtype=jnp.int32)[None, :]).astype(
        jnp.int32
    )
    position = places - jnp.sum(picked * starts[None, :], axis=1)
    return (segment, position)


def swap(array, k):
    size = lax.axis_size("seq")
    return lax.ppermute(array, "seq", [(i, i ^ k) for i in range(size)])


def pick(blocks, at):
    return lax.dynamic_index_in_dim(blocks, at, 0, keepdims=False)


def seq_deal(blocks):
    size, here = lax.axis_size("seq"), lax.axis_index("seq")
    out = blocks
    for k in range(1, size):
        there = here ^ k
        out = lax.dynamic_update_index_in_dim(out, swap(pick(blocks, there), k), there, 0)
    return out


def seq_gather(block):
    size, here = lax.axis_size("seq"), lax.axis_index("seq")
    out = lax.dynamic_update_index_in_dim(
        jnp.zeros((size,) + block.shape, block.dtype), block, here, 0
    )
    for k in range(1, size):
        out = lax.dynamic_update_index_in_dim(out, swap(block, k), here ^ k, 0)
    return out


def seq_scatter(blocks):
    size, here = lax.axis_size("seq"), lax.axis_index("seq")
    total = pick(blocks, here).astype(F32)
    for k in range(1, size):
        total = total + swap(pick(blocks, here ^ k).astype(BF), k).astype(F32)
    return total


def seq_sum(array):
    return jnp.sum(seq_gather(array).astype(F32), axis=0)


def routing(route_rows, tok_rows):
    fsdp_count, fsdp_rank = lax.axis_size("fsdp"), lax.axis_index("fsdp")
    micro = route_rows.shape[0]
    per_peer = tok_rows // fsdp_count
    target_dev = (route_rows // tok_rows).reshape(micro, fsdp_count, tok_rows)
    target_slot = (route_rows % tok_rows).reshape(micro, fsdp_count, tok_rows)
    steps = jnp.arange(tok_rows, dtype=jnp.int32)
    same = target_dev[:, :, :, None] == target_dev[:, :, None, :]
    earlier = steps[None, :] < steps[:, None]
    rank = jnp.sum((same & earlier).astype(jnp.int32), axis=3)
    my_dev = lax.dynamic_index_in_dim(target_dev, fsdp_rank, 1, keepdims=False)
    my_rank = lax.dynamic_index_in_dim(rank, fsdp_rank, 1, keepdims=False)
    micros = jnp.arange(micro, dtype=jnp.int32)
    send_at = (my_dev * micro + micros[:, None]) * per_peer + my_rank
    ranks = jnp.arange(per_peer, dtype=jnp.int32)
    mine = (target_dev == fsdp_rank)[:, :, None, :] & (rank[:, :, None, :] == ranks[:, None])
    slot = jnp.sum(mine.astype(jnp.int32) * target_slot[:, :, None, :], axis=3)
    land_at = (micros[:, None, None] * tok_rows + slot).transpose(1, 0, 2).reshape(-1)
    rows = jnp.arange(micro * tok_rows, dtype=jnp.int32)
    send_hot = (rows[:, None] == send_at.reshape(-1)[None, :]).astype(BF)
    land_hot = (rows[:, None] == land_at[None, :]).astype(BF)
    return send_hot, land_hot


def exchange(rows):
    return lax.all_to_all(rows, "fsdp", split_axis=0, concat_axis=0, tiled=True)


def bring(rows, send_hot, land_hot):
    sent = dot(send_hot, rows, 1, 0).astype(BF)
    return dot(land_hot, exchange(sent), 1, 0).astype(BF)


def give(rows, send_hot, land_hot):
    sent = dot(land_hot, rows, 0, 0).astype(BF)
    return dot(send_hot, exchange(sent), 0, 0).astype(BF)


def lane_groups(channels, most=4):
    tiles, out, first = channels // LANES, [], 0
    while first < tiles:
        count = min(most, tiles - first)
        out.append((first, count))
        first += count
    return out


def scan_kernel(groups, steps, dtm_ref, dtu_ref, b_ref, c_ref, a_ref, core_ref):
    place = lax.broadcasted_iota(jnp.int32, (8, LANES), 0)
    for first, count in groups:
        spans = [pl.ds((first + i) * LANES, LANES) for i in range(count)]
        rates = [a_ref[:, span] for span in spans]

        def block(k, held):
            held = list(held)
            base = pl.multiple_of(k * 8, 8)
            rows = pl.ds(base, 8)
            dts = [dtm_ref[rows, span] for span in spans]
            dus = [dtu_ref[rows, span] for span in spans]
            ys = [jnp.zeros((8, LANES), F32)] * count
            for j in range(8):
                b_now, c_now = b_ref[base + j], c_ref[base + j]
                for i in range(count):
                    decay = jnp.exp(dts[i][j : j + 1] * rates[i])
                    held[i] = decay * held[i] + dus[i][j : j + 1] * b_now
                    y = jnp.sum(held[i] * c_now, axis=0, keepdims=True)
                    ys[i] = jnp.where(place == j, y, ys[i])
            for i, span in enumerate(spans):
                core_ref[rows, span] = ys[i]
            return tuple(held)

        zero = jnp.zeros((STATE, LANES), F32)
        lax.fori_loop(0, steps // 8, block, (zero,) * count)


def scan_back_kernel(
    groups,
    steps,
    dtm_ref,
    dtu_ref,
    dcore_ref,
    b_ref,
    c_ref,
    a_ref,
    ddtu_ref,
    ddt_ref,
    da_ref,
    db_ref,
    dc_ref,
    hs,
    acc_b,
    acc_c,
):
    place = lax.broadcasted_iota(jnp.int32, (8, LANES), 0)
    zero = jnp.zeros((STATE, LANES), F32)
    for at, (first, count) in enumerate(groups):
        spans = [pl.ds((first + i) * LANES, LANES) for i in range(count)]
        slots = [pl.ds(i * LANES, LANES) for i in range(count)]
        rates = [a_ref[:, span] for span in spans]
        for slot in slots:
            hs[0, :, slot] = zero

        def block(k, held):
            held = list(held)
            base = pl.multiple_of(k * 8, 8)
            rows = pl.ds(base, 8)
            dts = [dtm_ref[rows, span] for span in spans]
            dus = [dtu_ref[rows, span] for span in spans]
            for j in range(8):
                b_now = b_ref[base + j]
                for i in range(count):
                    decay = jnp.exp(dts[i][j : j + 1] * rates[i])
                    held[i] = decay * held[i] + dus[i][j : j + 1] * b_now
                    hs[base + j + 1, :, slots[i]] = held[i]
            return tuple(held)

        lax.fori_loop(0, steps // 8, block, (zero,) * count)

        def back(k, carry):
            carry = list(carry)
            base = pl.multiple_of(steps - 8 - k * 8, 8)
            rows = pl.ds(base, 8)
            dts = [dtm_ref[rows, span] for span in spans]
            dus = [dtu_ref[rows, span] for span in spans]
            dys = [dcore_ref[rows, span] for span in spans]
            out_u = [jnp.zeros((8, LANES), F32)] * count
            out_t = [jnp.zeros((8, LANES), F32)] * count
            for j in reversed(range(8)):
                t = base + j
                b_now, c_now = b_ref[t], c_ref[t]
                sum_b = sum_c = zero
                for i in range(count):
                    later, rate_sum = carry[i]
                    dt, du, dy = dts[i][j : j + 1], dus[i][j : j + 1], dys[i][j : j + 1]
                    g = later + dy * c_now
                    sum_c = sum_c + hs[t + 1, :, slots[i]] * dy
                    sum_b = sum_b + g * du
                    through = g * jnp.exp(dt * rates[i])
                    moved = through * hs[t, :, slots[i]]
                    to_u = jnp.sum(g * b_now, axis=0, keepdims=True)
                    to_t = jnp.sum(moved * rates[i], axis=0, keepdims=True)
                    out_u[i] = jnp.where(place == j, to_u, out_u[i])
                    out_t[i] = jnp.where(place == j, to_t, out_t[i])
                    carry[i] = (through, rate_sum + moved * dt)
                if at == 0:
                    acc_b[t] = sum_b
                    acc_c[t] = sum_c
                else:
                    acc_b[t] = acc_b[t] + sum_b
                    acc_c[t] = acc_c[t] + sum_c
            for i, span in enumerate(spans):
                ddtu_ref[rows, span] = out_u[i]
                ddt_ref[rows, span] = out_t[i]
            return tuple(carry)

        ends = lax.fori_loop(0, steps // 8, back, ((zero, zero),) * count)
        for i, span in enumerate(spans):
            da_ref[:, span] = ends[i][1]
    ones = jnp.ones((8, LANES), F32)
    for acc, out in ((acc_b, db_ref), (acc_c, dc_ref)):
        out[...] = lax.dot_general(
            ones,
            acc[...].reshape(steps * STATE, LANES),
            (((1,), (1,)), ((), ())),
            precision=lax.Precision.HIGHEST,
            preferred_element_type=F32,
        )


VMEM_BYTES = 60 * 2**20


def scan_forward(dtm, dtu, b_wide, c_wide, rates):
    steps, channels = dtm.shape
    return pl.pallas_call(
        partial(scan_kernel, lane_groups(channels), steps),
        out_shape=jax.ShapeDtypeStruct((steps, channels), F32),
        in_specs=[pl.BlockSpec(memory_space=pltpu.VMEM)] * 5,
        out_specs=pl.BlockSpec(memory_space=pltpu.VMEM),
        compiler_params=pltpu.CompilerParams(vmem_limit_bytes=VMEM_BYTES),
        cost_estimate=pl.CostEstimate(
            flops=16 * steps * channels * STATE,
            bytes_accessed=40_000_000,
            transcendentals=steps * channels * STATE,
        ),
        name="scan_forward",
    )(dtm, dtu, b_wide, c_wide, rates)


def scan_backward(dtm, dtu, dcore, b_wide, c_wide, rates):
    steps, channels = dtm.shape
    groups = lane_groups(channels)
    rows = jax.ShapeDtypeStruct((steps, channels), F32)
    flat = jax.ShapeDtypeStruct((8, steps * STATE), F32)
    ddtu, ddt, da, db, dc = pl.pallas_call(
        partial(scan_back_kernel, groups, steps),
        out_shape=[rows, rows, jax.ShapeDtypeStruct((STATE, channels), F32), flat, flat],
        in_specs=[pl.BlockSpec(memory_space=pltpu.VMEM)] * 6,
        out_specs=[pl.BlockSpec(memory_space=pltpu.VMEM)] * 5,
        scratch_shapes=[
            pltpu.VMEM((steps + 1, STATE, groups[0][1] * LANES), F32),
            pltpu.VMEM((steps, STATE, LANES), F32),
            pltpu.VMEM((steps, STATE, LANES), F32),
        ],
        compiler_params=pltpu.CompilerParams(vmem_limit_bytes=VMEM_BYTES),
        cost_estimate=pl.CostEstimate(
            flops=40 * steps * channels * STATE,
            bytes_accessed=100_000_000,
            transcendentals=2 * steps * channels * STATE,
        ),
        name="scan_backward",
    )(dtm, dtu, dcore, b_wide, c_wide, rates)
    return ddtu, ddt, da, db[0].reshape(steps, STATE), dc[0].reshape(steps, STATE)


def regroup_kernel(plan, source_count, out_count, *refs):
    sources = refs[:source_count]
    maps = refs[source_count : len(refs) - out_count]
    outs = refs[len(refs) - out_count :]
    for out, block, tile, wide, terms in plan:
        at = pl.ds(tile * LANES, wide)
        total = None
        for source, which, low, high in terms:
            held = sources[source]
            held = held[..., low:high] if len(held.shape) == 2 else held[which[1], :, low:high]
            wanted = maps[which[0]][:, at] - low
            places = lax.broadcasted_iota(jnp.int32, (high - low, wide), 0)
            hot = (places == wanted).astype(F32).astype(BF)
            term = dot(held, hot, 1, 0)
            total = term if total is None else total + term
        ref = outs[out]
        if total is None:
            total = jnp.zeros((ref.shape[-2], wide), F32)
        if len(ref.shape) == 2:
            ref[:, at] = total.astype(ref.dtype)
        else:
            ref[block, :, at] = total.astype(ref.dtype)


def regroup(sources, outs, moves, here):
    plan, maps = [], []
    tables = []
    for source, from_block, out, block, table in moves:
        maps.append(jnp.asarray(table)[here][None] if len(table) > 1 else jnp.asarray(table))
        tables.append((source, from_block, out, block, table))
    for out, shape in enumerate(outs):
        for block in range(shape.shape[0] if len(shape.shape) == 3 else 1):
            for tile in range(-(-shape.shape[-1] // LANES)):
                wide = min(LANES, shape.shape[-1] - tile * LANES)
                terms = []
                for which, (source, from_block, to, to_block, table) in enumerate(tables):
                    used = table[:, tile * LANES : tile * LANES + wide]
                    if (to, to_block) != (out, block) or not (used >= 0).any():
                        continue
                    low = int(used[used >= 0].min()) // LANES * LANES
                    high = min(-(-(int(used.max()) + 1) // LANES) * LANES, sources[source].shape[-1])
                    terms.append((source, (which, from_block), low, high))
                plan.append((out, block, tile, wide, tuple(terms)))
    vmem = pl.BlockSpec(memory_space=pltpu.VMEM)
    return pl.pallas_call(
        partial(regroup_kernel, plan, len(sources), len(outs)),
        out_shape=list(outs),
        in_specs=[vmem] * (len(sources) + len(maps)),
        out_specs=[vmem] * len(outs),
        compiler_params=pltpu.CompilerParams(vmem_limit_bytes=VMEM_BYTES),
        name="regroup",
    )(*sources, *maps)


def pieces_table(chunks, size, piece, wide, start=0):
    at = np.arange(chunks * wide)
    chunk, place = at // wide, at % wide
    count = size // piece
    table = start + chunk * size + place + piece * np.arange(count)[:, None]
    return np.where(place < piece, table, -1).astype(np.int32)


def run_table(starts, count):
    return (np.asarray(starts)[:, None] + np.arange(count)).astype(np.int32)


def placed(table, at, width):
    out = np.full((table.shape[0], width), -1, np.int32)
    out[:, at : at + table.shape[1]] = table
    return out


def meet(peers):
    barrier = pltpu.get_barrier_semaphore()
    for peer in peers:
        pl.semaphore_signal(barrier, inc=1, device_id=peer, device_id_type=pl.DeviceIdType.MESH)
    pl.semaphore_wait(barrier, len(peers))


def deal_kernel(count, size, *refs):
    sources, outs = refs[:count], refs[count : 2 * count]
    own_sem, send_sem, recv_sem = refs[2 * count :]
    here, row = lax.axis_index("seq"), lax.axis_index("fsdp")
    others = [lax.rem(here + k, size) for k in range(1, size)]
    meet([(there, row) for there in others])
    copies = []
    for i, (source, out) in enumerate(zip(sources, outs)):
        copies.append(pltpu.make_async_copy(source.at[here], out.at[here], own_sem.at[i]))
        copies[-1].start()
        for k, there in enumerate(others):
            at = i * (size - 1) + k
            copies.append(
                pltpu.make_async_remote_copy(
                    src_ref=source.at[there],
                    dst_ref=out.at[here],
                    send_sem=send_sem.at[at],
                    recv_sem=recv_sem.at[at],
                    device_id=(there, row),
                    device_id_type=pl.DeviceIdType.MESH,
                )
            )
            copies[-1].start()
    for copy in copies:
        copy.wait()


def deal(arrays, collective_id):
    size, count = lax.axis_size("seq"), len(arrays)
    hbm = pl.BlockSpec(memory_space=pl.ANY)
    return pl.pallas_call(
        partial(deal_kernel, count, size),
        out_shape=[jax.ShapeDtypeStruct(a.shape, a.dtype) for a in arrays],
        in_specs=[hbm] * count,
        out_specs=[hbm] * count,
        scratch_shapes=[
            pltpu.SemaphoreType.DMA((count,)),
            pltpu.SemaphoreType.DMA((count * (size - 1),)),
            pltpu.SemaphoreType.DMA((count * (size - 1),)),
        ],
        compiler_params=pltpu.CompilerParams(collective_id=collective_id, has_side_effects=True),
        cost_estimate=pl.CostEstimate(
            flops=0, bytes_accessed=sum(a.size for a in arrays), transcendentals=0
        ),
        name="deal",
    )(*arrays)


def total_kernel(sizes, in_ref, out_ref, one, two, send_sem, recv_sem, send_two, recv_two):
    seq, fsdp = lax.axis_index("seq"), lax.axis_index("fsdp")
    across = [lax.rem(seq + k, sizes[0]) for k in range(1, sizes[0])]
    along = [lax.rem(fsdp + k, sizes[1]) for k in range(1, sizes[1])]
    meet([(there, fsdp) for there in across] + [(seq, there) for there in along])

    def spread(slots, me, devices, send, recv):
        copies = []
        for k, device in enumerate(devices):
            copies.append(
                pltpu.make_async_remote_copy(
                    src_ref=slots.at[me],
                    dst_ref=slots.at[me],
                    send_sem=send.at[k],
                    recv_sem=recv.at[k],
                    device_id=device,
                    device_id_type=pl.DeviceIdType.MESH,
                )
            )
            copies[-1].start()
        for copy in copies:
            copy.wait()
        total = slots[0]
        for i in range(1, slots.shape[0]):
            total = total + slots[i]
        return total

    one[seq] = in_ref[...]
    two[fsdp] = spread(one, seq, [(there, fsdp) for there in across], send_sem, recv_sem)
    out_ref[...] = spread(two, fsdp, [(seq, there) for there in along], send_two, recv_two)


def total_of(block, collective_id):
    sizes = (lax.axis_size("seq"), lax.axis_size("fsdp"))
    vmem = pl.BlockSpec(memory_space=pltpu.VMEM)
    return pl.pallas_call(
        partial(total_kernel, sizes),
        out_shape=jax.ShapeDtypeStruct(block.shape, block.dtype),
        in_specs=[vmem],
        out_specs=vmem,
        scratch_shapes=[pltpu.VMEM((n,) + block.shape, F32) for n in sizes]
        + [pltpu.SemaphoreType.DMA((n - 1,)) for n in sizes for _ in range(2)],
        compiler_params=pltpu.CompilerParams(collective_id=collective_id, has_side_effects=True),
        name="total",
    )(block)


def remote(source, target, send, recv, device):
    return pltpu.make_async_remote_copy(
        src_ref=source,
        dst_ref=target,
        send_sem=send,
        recv_sem=recv,
        device_id=device,
        device_id_type=pl.DeviceIdType.MESH,
    )


def block_rows(size, tok, m, d):
    return pl.ds(pl.multiple_of((m * size + d) * tok, tok), tok)


def spread_rows(size, tok, micro, own, whole, own_sem, send_sem, recv_sem, first):
    here, row = lax.axis_index("seq"), lax.axis_index("fsdp")
    copies = []
    for m in range(micro):
        source, target = own.at[pl.ds(m * tok, tok)], whole.at[block_rows(size, tok, m, here)]
        for k in range(1, size):
            at = first + m * (size - 1) + k - 1
            there = (lax.rem(here + k, size), row)
            copies.append(remote(source, target, send_sem.at[at], recv_sem.at[at], there))
        at = first // (size - 1) + m
        copies.append(pltpu.make_async_copy(source, target, own_sem.at[at]))
    for copy in copies:
        copy.start()
    return copies


def pack_peers(size):
    here, row = lax.axis_index("seq"), lax.axis_index("fsdp")
    return [(lax.rem(here + k, size), row) for k in range(1, size)]


def gather_kernel(size, tok, micro, count, *refs):
    owns, wholes = refs[:count], refs[count : 2 * count]
    own_sem, send_sem, recv_sem = refs[2 * count :]
    meet(pack_peers(size))
    copies = []
    for i in range(count):
        first = i * micro * (size - 1)
        copies += spread_rows(
            size, tok, micro, owns[i], wholes[i], own_sem, send_sem, recv_sem, first
        )
    for copy in copies:
        copy.wait()


def gather_rows(arrays, micro, collective_id):
    size, count = lax.axis_size("seq"), len(arrays)
    tok = arrays[0].shape[0] // micro
    hbm = pl.BlockSpec(memory_space=pl.ANY)
    links = count * micro * (size - 1)
    return pl.pallas_call(
        partial(gather_kernel, size, tok, micro, count),
        out_shape=[jax.ShapeDtypeStruct((a.shape[0] * size, a.shape[1]), a.dtype) for a in arrays],
        in_specs=[hbm] * count,
        out_specs=[hbm] * count,
        scratch_shapes=[
            pltpu.SemaphoreType.DMA((count * micro,)),
            pltpu.SemaphoreType.DMA((links,)),
            pltpu.SemaphoreType.DMA((links,)),
        ],
        compiler_params=pltpu.CompilerParams(collective_id=collective_id, has_side_effects=True),
        name="gather_rows",
    )(*arrays)


def spans_of(width, most=512):
    return [(low, min(low + most, width)) for low in range(0, width, most)]


def mixer_kernel(size, tok, micro, *refs):
    contexts, ssm_outs = refs[:micro], refs[micro : 2 * micro]
    sums_ref, x_ref, gain_att, gain_ssm, gain_ffn, w_att, w_ssm = refs[2 * micro : 2 * micro + 7]
    att, ssm, scale_att, scale_ssm, hidden, mixer, ffn = refs[2 * micro + 7 : 2 * micro + 14]
    sums, sent, got, ffn_own, sums_send, sums_recv, send, recv, own_sem, ffn_send, ffn_recv = refs[
        2 * micro + 14 :
    ]
    here, row = lax.axis_index("seq"), lax.axis_index("fsdp")
    peers = pack_peers(size)
    meet(peers)
    sums[here] = sums_ref[...]
    copies = [
        remote(sums.at[here], sums.at[here], sums_send.at[k], sums_recv.at[k], peer)
        for k, peer in enumerate(peers)
    ]
    for copy in copies:
        copy.start()
    for copy in copies:
        copy.wait()
    total = sums[0]
    for i in range(1, size):
        total = total + sums[i]
    place = lax.broadcasted_iota(jnp.int32, (8, LANES), 0)
    for kind, scale, width in ((0, scale_att, ATT), (1, scale_ssm, INNER)):
        column = lax.dot_general(
            total,
            (place == kind).astype(F32),
            (((0,), (0,)), ((), ())),
            precision=lax.Precision.HIGHEST,
            preferred_element_type=F32,
        )
        scale[...] = lax.rsqrt(column / width + EPS)
    pack = size * tok
    for m in range(micro):
        rows = pl.ds(m * pack, pack)
        att[rows] = (contexts[m][...] * scale_att[rows, :1] * gain_att[...]).astype(BF)
        ssm[rows] = (ssm_outs[m][...] * scale_ssm[rows, :1] * gain_ssm[...]).astype(BF)

    def product(d, low, high):
        left = [jnp.concatenate([ref[block_rows(size, tok, m, d)] for m in range(micro)]) for ref in (att, ssm)]
        return 0.5 * (
            dot(left[0], w_att[:, low:high], 1, 0) + dot(left[1], w_ssm[:, low:high], 1, 0)
        )

    copies = []
    for k, peer in enumerate(peers):
        for low, high in spans_of(D):
            sent[k, :, low:high] = product(peer[0], low, high).astype(BF)
        copies.append(remote(sent.at[k], got.at[k], send.at[k], recv.at[k], peer))
        copies[-1].start()
    for low, high in spans_of(D):
        mixer[:, low:high] = product(here, low, high)
    for copy in copies:
        copy.wait()
    for m in range(micro):
        rows = pl.ds(m * tok, tok)
        out = mixer[rows]
        for k in range(size - 1):
            out = out + got[k, rows].astype(F32)
        mixer[rows] = out
        whole = x_ref[rows].astype(F32) + out
        hidden[rows] = whole
        scale = lax.rsqrt(jnp.mean(whole * whole, axis=-1, keepdims=True) + EPS)
        ffn_own[rows] = (whole * scale * gain_ffn[...]).astype(BF)
    for copy in spread_rows(size, tok, micro, ffn_own, ffn, own_sem, ffn_send, ffn_recv, 0):
        copy.wait()


def mixer_rows(contexts, ssm_outs, sums, x_own, gains, w_att, w_ssm, collective_id):
    size, micro = lax.axis_size("seq"), len(contexts)
    own = x_own.shape[0]
    rows, tok = own * size, own // micro
    vmem, hbm = pl.BlockSpec(memory_space=pltpu.VMEM), pl.BlockSpec(memory_space=pl.ANY)
    shape = jax.ShapeDtypeStruct
    dma = pltpu.SemaphoreType.DMA
    return pl.pallas_call(
        partial(mixer_kernel, size, tok, micro),
        out_shape=[
            shape((rows, w_att.shape[0]), BF),
            shape((rows, w_ssm.shape[0]), BF),
            shape((rows, LANES), F32),
            shape((rows, LANES), F32),
            shape((own, D), F32),
            shape((own, D), F32),
            shape((rows, D), BF),
        ],
        in_specs=[vmem] * (2 * micro + 7),
        out_specs=[vmem] * 6 + [hbm],
        scratch_shapes=[
            pltpu.VMEM((size,) + sums.shape, F32),
            pltpu.VMEM((size - 1, own, D), BF),
            pltpu.VMEM((size - 1, own, D), BF),
            pltpu.VMEM((own, D), BF),
            dma((size - 1,)),
            dma((size - 1,)),
            dma((size - 1,)),
            dma((size - 1,)),
            dma((micro,)),
            dma((micro * (size - 1),)),
            dma((micro * (size - 1),)),
        ],
        compiler_params=pltpu.CompilerParams(
            collective_id=collective_id, has_side_effects=True, vmem_limit_bytes=VMEM_BYTES
        ),
        name="mixer_rows",
    )(*contexts, *ssm_outs, sums, x_own, *gains, w_att, w_ssm)


def ffn_kernel(size, tok, micro, *refs):
    ffn, cot, hidden, cot_own, gain, w_gu, w_down = refs[:7]
    act, dgu, down, d_hidden, d_gain, dmix = refs[7:13]
    sent, got, dmix_own, send, recv, own_sem, dmix_send, dmix_recv = refs[13:]
    here, row = lax.axis_index("seq"), lax.axis_index("fsdp")
    wide = w_down.shape[0]
    meet(pack_peers(size))

    def copy_of(k):
        return remote(
            sent.at[k], got.at[k], send.at[k], recv.at[k], (lax.rem(here + k + 1, size), row)
        )

    def block(k, carry):
        d = lax.rem(here + k + 1, size)
        spots = [block_rows(size, tok, m, d) for m in range(micro)]
        rows_in = jnp.concatenate([ffn[spot] for spot in spots])
        cots = jnp.concatenate([cot[spot] for spot in spots])
        for low, high in spans_of(wide):
            gate = dot(rows_in, w_gu[:, low:high], 1, 0)
            up = dot(rows_in, w_gu[:, wide + low : wide + high], 1, 0)
            d_act = dot(cots, w_down[low:high, :], 1, 1)
            sig = 1.0 / (1.0 + jnp.exp(-gate))
            silu = gate * sig
            pieces = (
                (act, low, silu * up),
                (dgu, low, d_act * up * (sig * (1.0 + gate - silu))),
                (dgu, wide + low, d_act * silu),
            )
            for ref, at, values in pieces:
                values = values.astype(BF)
                for m, spot in enumerate(spots):
                    ref[spot, at : at + high - low] = values[m * tok : (m + 1) * tok]
        d_all = jnp.concatenate([dgu[spot] for spot in spots])
        for low, high in spans_of(D):
            sent[k, :, low:high] = dot(d_all, w_gu[low:high, :], 1, 1).astype(BF)

        @pl.when(k < size - 1)
        def _():
            copy_of(k).start()

        acts = jnp.concatenate([act[spot] for spot in spots])
        for low, high in spans_of(D):
            down[d, :, low:high] = dot(acts, w_down[:, low:high], 1, 0).astype(BF)
        return carry

    lax.fori_loop(0, size, block, 0)
    for k in range(size - 1):
        copy_of(k).wait()
    gain_sum = jnp.zeros((1, D), F32)
    for m in range(micro):
        rows = pl.ds(m * tok, tok)
        d_in = sent[size - 1, rows].astype(F32)
        for k in range(size - 1):
            d_in = d_in + got[k, rows].astype(F32)
        whole = hidden[rows]
        scale = lax.rsqrt(jnp.mean(whole * whole, axis=-1, keepdims=True) + EPS)
        normal = whole * scale
        gain_sum = gain_sum + jnp.sum(d_in * normal, axis=0, keepdims=True)
        scaled = d_in * gain[...]
        inward = jnp.mean(scaled * normal, axis=-1, keepdims=True)
        out = cot_own[rows].astype(F32) + scale * (scaled - normal * inward)
        d_hidden[rows] = out
        dmix_own[rows] = out.astype(BF)
    d_gain[...] = gain_sum
    for copy in spread_rows(size, tok, micro, dmix_own, dmix, own_sem, dmix_send, dmix_recv, 0):
        copy.wait()


def ffn_rows(ffn, cot, hidden, cot_own, gain, w_gu, w_down, micro, collective_id):
    size = lax.axis_size("seq")
    own, rows = hidden.shape[0], ffn.shape[0]
    wide = w_down.shape[0]
    tok = own // micro
    vmem, hbm = pl.BlockSpec(memory_space=pltpu.VMEM), pl.BlockSpec(memory_space=pl.ANY)
    shape = jax.ShapeDtypeStruct
    dma = pltpu.SemaphoreType.DMA
    return pl.pallas_call(
        partial(ffn_kernel, size, tok, micro),
        out_shape=[
            shape((rows, wide), BF),
            shape((rows, 2 * wide), BF),
            shape((size, own, D), BF),
            shape((own, D), F32),
            shape((1, D), F32),
            shape((rows, D), BF),
        ],
        in_specs=[vmem] * 7,
        out_specs=[vmem] * 5 + [hbm],
        scratch_shapes=[
            pltpu.VMEM((size, own, D), BF),
            pltpu.VMEM((size - 1, own, D), BF),
            pltpu.VMEM((own, D), BF),
            dma((size - 1,)),
            dma((size - 1,)),
            dma((micro,)),
            dma((micro * (size - 1),)),
            dma((micro * (size - 1),)),
        ],
        compiler_params=pltpu.CompilerParams(
            collective_id=collective_id, has_side_effects=True, vmem_limit_bytes=VMEM_BYTES
        ),
        name="ffn_rows",
    )(ffn, cot, hidden, cot_own, gain, w_gu, w_down)


def conv_act(position, inner, tap_weights, tap_bias):
    row_count = inner.shape[0]
    ext_rows = jnp.pad(inner, ((CONV - 1, 0), (0, 0)))
    conv_sum = tap_bias[None, :] + jnp.zeros(inner.shape, F32)
    for tap_idx in range(CONV):
        shifted = ext_rows[CONV - 1 - tap_idx : CONV - 1 - tap_idx + row_count]
        conv_sum = (
            conv_sum
            + tap_weights[:, tap_idx][None, :]
            * shifted
            * (position >= tap_idx).astype(F32)[:, None]
        )
    return jax.nn.silu(conv_sum)


def gate_mix(core, inner_u, skip_d, gate_z):
    return (core + skip_d[None, :] * inner_u) * jax.nn.silu(gate_z)


def swiglu(gate_proj, up_proj):
    return jax.nn.silu(gate_proj) * up_proj


def squares(row_vals):
    return jnp.sum(row_vals * row_vals)


def local(
    tokens,
    cotangent,
    route,
    lengths,
    gain_in,
    w_qkv,
    w_mix_in,
    w_x,
    w_dt,
    w_small,
    gain_att,
    gain_ssm,
    w_out_att,
    w_out_ssm,
    gain_ffn,
    w_gate,
    w_up,
    w_down,
):
    S, N = lax.axis_size("seq"), lax.axis_size("fsdp")
    s = lax.axis_index("seq")
    micro, tok = tokens.shape[:2]
    pack = tok * S
    rows_d = gain_in.shape[0] // N
    ff = w_gate.shape[1]
    ch_piece, ff_piece = INNER // (N * S), ff // (N * S)
    ch = -(-INNER // (S * LANES)) * LANES
    ffs = -(-ff // (S * LANES)) * LANES
    cols = D // S
    groups = HEADS // KV_HEADS
    first_heads = [(HEADS * i + S - 1) // S for i in range(S + 1)]
    head_counts = [first_heads[i + 1] - first_heads[i] for i in range(S)]
    most = max(head_counts)
    width = most * HEAD
    first_head = jnp.array(first_heads, jnp.int32)[s]
    head_live = jnp.arange(most) < jnp.array(head_counts, jnp.int32)[s]
    live = jnp.repeat(head_live, HEAD).astype(F32)[None, :]
    in_low = (first_head + jnp.arange(most)) // groups <= s

    def gather(shard):
        return lax.all_gather(shard, "fsdp", axis=0, tiled=True)

    def scatter(whole):
        rows, wide = whole.shape[0] // N, whole.shape[1]
        fill = -rows % 8
        whole = whole.astype(BF)
        if fill:
            whole = jnp.pad(whole.reshape(N, rows, wide), ((0, 0), (0, fill), (0, 0)))
            whole = whole.reshape(N * (rows + fill), wide)
        return lax.psum_scatter(whole, "fsdp", scatter_dimension=0, tiled=True)[:rows]

    def part(shard, axis, chunks, wide):
        shape = shard.shape
        piece = shape[axis] // (chunks * S)
        shaped = shard.reshape(shape[:axis] + (chunks, S, piece) + shape[axis + 1 :])
        picked = lax.dynamic_index_in_dim(shaped, s, axis + 1, keepdims=False)
        fill = [(0, 0)] * picked.ndim
        fill[axis + 1] = (0, wide - piece)
        return jnp.pad(picked, fill).reshape(
            shape[:axis] + (chunks * wide,) + shape[axis + 1 :]
        )

    def span(array, axis, start, size):
        return lax.dynamic_slice_in_dim(array, start, size, axis)

    send_hot, land_hot = routing(route, tok)
    x_own = bring(tokens.reshape(micro * tok, D), send_hot, land_hot)
    q_start = first_head * HEAD
    chw, ffw = ch // N, ffs // N
    q_starts = [h * HEAD for h in first_heads[:S]]
    kv_starts = [ATT + HEAD * i for i in range(S)]
    at_k, at_v, at_q = 2 * ch, 2 * ch + 2 * HEAD, 2 * ch + 4 * HEAD
    at_att = at_q + width
    in_wide = at_att + cols
    mix_table = pieces_table(2 * N, INNER // N, ch_piece, chw)
    in_part = regroup(
        [w_mix_in, jnp.pad(w_qkv, ((0, 0), (0, -w_qkv.shape[1] % LANES))), w_out_att],
        [jax.ShapeDtypeStruct((rows_d, in_wide), BF)],
        [
            (0, None, 0, 0, placed(mix_table, 0, in_wide)),
            (1, None, 0, 0, placed(run_table(kv_starts, 2 * HEAD), at_k, in_wide)),
            (1, None, 0, 0, placed(run_table([a + KV_WIDTH for a in kv_starts], 2 * HEAD), at_v, in_wide)),
            (2, None, 0, 0, placed(run_table([cols * i for i in range(S)], cols), at_att, in_wide)),
            (1, None, 0, 0, placed(run_table(q_starts, width), at_q, in_wide)),
        ],
        s,
    )[0]
    small_part = part(
        jnp.concatenate([w_x, w_dt, w_small, jnp.zeros((w_x.shape[0], 1), BF)], axis=1), 0, 1, chw
    )
    small_wide = small_part.shape[1]
    gathered_in = gather(
        jnp.concatenate([in_part, jnp.pad(small_part, ((0, rows_d - chw), (0, 0)))], axis=1)
    )
    cot_own = bring(cotangent.reshape(micro * tok, D), send_hot, land_hot)
    x_rows = gather_rows([x_own], micro, 3)[0]
    cot_own, x_rows = lax.optimization_barrier((cot_own, x_rows))
    cot_rows = gather_rows([cot_own], micro, 6)[0]
    gathered_in, x_rows, cot_rows = lax.optimization_barrier((gathered_in, x_rows, cot_rows))
    out_piece, gathered_in = lax.optimization_barrier((part(w_out_ssm, 0, 1, chw), gathered_in))
    w_out_part = gather(out_piece)
    w_in = gathered_in[:, :at_att]
    w_att_cols = gathered_in[:, at_att:in_wide]
    w_small_part = (
        gathered_in[:, in_wide:].reshape(N, rows_d, small_wide)[:, :chw].reshape(ch, small_wide)
    )
    ff_table = pieces_table(N, ff // N, ff_piece, ffw)
    gu_part = regroup(
        [w_gate, w_up],
        [jax.ShapeDtypeStruct((rows_d, 2 * ffs), BF)],
        [
            (0, None, 0, 0, placed(ff_table, 0, 2 * ffs)),
            (1, None, 0, 0, placed(ff_table, ffs, 2 * ffs)),
        ],
        s,
    )[0]

    w_att_pad = jnp.pad(w_att_cols, ((0, width), (0, 0)))
    w_att_part = (
        seq_deal(jnp.stack([w_att_pad[h * HEAD : h * HEAD + width] for h in first_heads[:S]]))
        .transpose(1, 0, 2)
        .reshape(width, D)
    )

    w_x_part = jnp.pad(w_small_part[:, :PROJ], ((0, 0), (0, PROJ_PAD - PROJ)))
    w_dt_part = w_small_part[:, PROJ : PROJ + DT_RANK]
    small_par = w_small_part[:, PROJ + DT_RANK : PROJ + DT_RANK + CONV + 3 + STATE].astype(F32)
    conv_w = small_par[:, :CONV]
    conv_b = small_par[:, CONV]
    dt_bias = small_par[:, CONV + 1]
    skip_d = small_par[:, CONV + 2]
    decay_a = -jnp.exp(small_par[:, CONV + 3 :])
    rates = decay_a.T
    gain_att_part = span(jnp.pad(gain_att, (0, width)), 0, q_start, width)
    gain_ssm_part = part(gain_ssm, 0, N, ch // N)

    def to_pack(block):
        return seq_gather(block).reshape(pack, block.shape[-1])

    def to_own(partial_rows):
        return seq_scatter(partial_rows.reshape(S, tok, partial_rows.shape[-1]))

    def opening(m):
        x_pack = x_rows[m * pack : (m + 1) * pack].astype(F32)
        normed_low = rms_scale(x_pack, gain_in).astype(BF)
        return normed_low, dot(normed_low, w_in, 1, 0).astype(BF)

    def first_half(m, normed_low, opened):
        segment, position = seq_layout(lengths[m, 0], pack)
        visible = (segment[:, None] == segment[None, :]) & (position[None, :] <= position[:, None])
        q = opened[:, at_q:].reshape(pack, most, HEAD)
        kv = opened[:, at_k:at_q].reshape(pack, 4, HEAD)
        pick_low = in_low[None, :, None]
        keys = jnp.where(pick_low, kv[:, 0:1], kv[:, 1:2])
        values = jnp.where(pick_low, kv[:, 2:3], kv[:, 3:4])
        scores = jnp.einsum("thd,uhd->htu", q, keys, preferred_element_type=F32) * 0.125
        masked = jnp.where(visible, scores, -1e30)
        row_top = jnp.max(masked, axis=-1, keepdims=True)
        exp_terms = jnp.exp(masked - row_top)
        row_total = jnp.sum(exp_terms, axis=-1, keepdims=True)
        probs = exp_terms / row_total
        context = (
            jnp.einsum("htu,uhd->thd", probs.astype(BF), values, preferred_element_type=F32)
        ).reshape(pack, width) * live
        inner = opened[:, :ch].astype(F32)
        gate_z = opened[:, ch : 2 * ch].astype(F32)
        inner_u, conv_back = jax.vjp(partial(conv_act, position), inner, conv_w, conv_b)
        u_low = inner_u.astype(BF)
        projected = seq_sum(dot(w_x_part, u_low, 0, 1).astype(BF)).astype(BF)
        dt_in = projected[:DT_RANK]
        in_b = projected[DT_RANK : DT_RANK + STATE].astype(F32)
        out_c = projected[DT_RANK + STATE : PROJ].astype(F32)
        dt_lin = dot(dt_in, w_dt_part, 0, 1) + dt_bias[None, :]
        step_dt = jax.nn.softplus(dt_lin)
        dtm = jnp.where((position > 0)[:, None], step_dt, 1e30)
        dtu = step_dt * inner_u
        b_wide = jnp.broadcast_to(in_b.T[:, :, None], (pack, STATE, LANES))
        c_wide = jnp.broadcast_to(out_c.T[:, :, None], (pack, STATE, LANES))
        core = scan_forward(dtm, dtu, b_wide, c_wide, rates)
        ssm_out, gate_back = jax.vjp(gate_mix, core, inner_u, skip_d, gate_z)
        row_sums = jnp.stack(
            [jnp.sum(context * context, axis=1), jnp.sum(ssm_out * ssm_out, axis=1)]
        )
        return dict(
            position=position,
            normed=normed_low,
            q=q,
            keys=keys,
            values=values,
            probs=probs,
            context=context,
            inner_u=inner_u,
            conv_back=conv_back,
            u=u_low,
            dt_in=dt_in,
            dt_lin=dt_lin,
            step_dt=step_dt,
            scan=(dtm, dtu, b_wide, c_wide),
            ssm_out=ssm_out,
            gate_back=gate_back,
            row_sums=row_sums,
        )

    def second_half(h):
        context, ssm_out = h["context"], h["ssm_out"]
        scale_att, scale_ssm, dmix_low = h["scale_att"], h["scale_ssm"], h["dmix"]
        d_att = 0.5 * dot(dmix_low, w_att_part, 1, 1) * live
        d_ssm = lax.optimization_barrier(0.5 * dot(dmix_low, w_out_part, 1, 1))
        d_gain_att = jnp.sum(d_att * context * scale_att, axis=0)
        d_gain_ssm = jnp.sum(d_ssm * ssm_out * scale_ssm, axis=0)
        t_att = d_att * gain_att_part
        t_ssm = d_ssm * gain_ssm_part
        back_sums = seq_sum(
            jnp.stack([jnp.sum(t_att * context, axis=1), jnp.sum(t_ssm * ssm_out, axis=1)])
        )
        d_context = (
            t_att * scale_att - context * scale_att**3 * (back_sums[0] / ATT)[:, None]
        ) * live
        d_ssm_out = t_ssm * scale_ssm - ssm_out * scale_ssm**3 * (back_sums[1] / INNER)[:, None]
        d_core, d_u_gate, d_skip, d_gate_z = h["gate_back"](d_ssm_out)
        h.update(
            d_core=d_core,
            d_u_gate=d_u_gate,
            d_skip=d_skip,
            d_gate_z=d_gate_z,
            d_context=d_context.astype(BF),
            gains=(d_gain_att, d_gain_ssm),
        )

    def attention_half(h):
        probs, keys, values, q = h["probs"], h["keys"], h["values"], h["q"]
        dctx_low = h["d_context"].reshape(pack, most, HEAD)
        d_values = jnp.einsum(
            "htu,thd->uhd", probs.astype(BF), dctx_low, preferred_element_type=F32
        )
        d_probs = jnp.einsum("thd,uhd->htu", dctx_low, values, preferred_element_type=F32)
        dscore_low = (
            probs * (d_probs - jnp.sum(probs * d_probs, axis=-1, keepdims=True))
        ).astype(BF)
        d_q = jnp.einsum("htu,uhd->thd", dscore_low, keys, preferred_element_type=F32) * 0.125
        d_keys = jnp.einsum("htu,thd->uhd", dscore_low, q, preferred_element_type=F32) * 0.125
        pick_low = in_low[None, :, None]

        def kv_sum(d_heads):
            return [
                jnp.sum(jnp.where(pick_low, d_heads, 0.0), axis=1),
                jnp.sum(jnp.where(pick_low, 0.0, d_heads), axis=1),
            ]

        d_rest = jnp.concatenate(
            [h["d_gate_z"]]
            + kv_sum(d_keys)
            + kv_sum(d_values)
            + [d_q.reshape(pack, width), jnp.zeros((pack, cols), F32)],
            axis=1,
        ).astype(BF)
        h.update(d_rest=d_rest, d_normed=dot(d_rest, gathered_in[:, ch:in_wide], 1, 1))

    def third_half(h):
        dtm, dtu, b_wide, c_wide = h["scan"]
        ddtu, ddt, d_rates, d_in_b, d_out_c = scan_backward(
            dtm, dtu, h["d_core"], b_wide, c_wide, rates
        )
        d_lin = (ddt + ddtu * h["inner_u"]) * jax.nn.sigmoid(h["dt_lin"])
        d_dt_bias = jnp.sum(d_lin, axis=0)
        ddt_low = d_lin.astype(BF)
        dproj = jnp.concatenate(
            [
                dot(w_dt_part, ddt_low, 0, 1),
                d_in_b.T,
                d_out_c.T,
                jnp.zeros((PROJ_PAD - PROJ, pack), F32),
            ],
            axis=0,
        )
        dproj_low = seq_sum(dproj.astype(BF)).astype(BF)
        d_inner_u = h["d_u_gate"] + ddtu * h["step_dt"] + dot(dproj_low, w_x_part, 0, 1)
        d_inner, d_conv_w, d_conv_b = h["conv_back"](d_inner_u)
        d_inner_low = d_inner.astype(BF)
        small = [d_conv_w, d_conv_b[:, None], d_dt_bias[:, None], h["d_skip"][:, None]]
        small_grad = jnp.concatenate(small + [d_rates.T * decay_a], axis=1)
        h.update(ddt=ddt_low, dproj=dproj_low, d_inner=d_inner_low, small=small_grad)

    def last_half(h):
        d_normed = to_own(h["d_normed"] + dot(h["d_inner"], w_in[:, :ch], 1, 1))
        _, norm_back = jax.vjp(rms_scale, h["x_mine"], gain_in)
        d_x_norm, d_gain_in = norm_back(d_normed)
        h.update(d_gain_in=d_gain_in, dx=(h["d_hidden"] + d_x_norm).astype(BF))

    def both(name, axis=0):
        return jnp.concatenate([one[name] for one in halves], axis=axis)

    def hold(names, *extra):
        held = [[one[name] for name in names] for one in halves]
        held, extra = lax.optimization_barrier((held, extra))
        for one, values in zip(halves, held):
            one.update(zip(names, values))
        return extra

    def by_shard(whole):
        return whole.astype(BF).reshape(N, whole.shape[0] // N, whole.shape[1])

    opened = [opening(m) for m in range(micro)]
    opened, gu_part, down_part = lax.optimization_barrier(
        (opened, gu_part, part(w_down, 0, 1, ffw))
    )
    w_gu, w_down_part = gather(gu_part), gather(down_part)
    halves = [first_half(m, *opened[m]) for m in range(micro)]
    sums = jnp.concatenate([one["row_sums"] for one in halves], axis=1)
    att_low, ssm_low, scale_att, scale_ssm, hidden, mixer_out, ffn_low = mixer_rows(
        [one["context"] for one in halves],
        [one["ssm_out"] for one in halves],
        jnp.pad(sums, ((0, 6), (0, 0))),
        x_own,
        (gain_att_part[None], gain_ssm_part[None], gain_ffn[None]),
        w_att_part,
        w_out_part,
        4,
    )
    act_low, dgu_low, down_parts, d_hidden, d_gain_ffn, dmix_low = ffn_rows(
        ffn_low, cot_rows, hidden, cot_own, gain_ffn[None], w_gu, w_down_part, micro, 5
    )
    gu_whole = dot(ffn_low, dgu_low, 0, 0).astype(BF)
    down_whole = dot(act_low, cot_rows, 0, 0).astype(BF)
    dmix_low, gu_whole, down_whole = lax.optimization_barrier((dmix_low, gu_whole, down_whole))
    for m, half in enumerate(halves):
        rows = slice(m * pack, (m + 1) * pack)
        mine = slice(m * tok, (m + 1) * tok)
        half.update(
            scale_att=scale_att[rows, :1],
            scale_ssm=scale_ssm[rows, :1],
            dmix=dmix_low[rows],
            x_mine=x_own[mine].astype(F32),
            d_hidden=d_hidden[mine],
        )
    r_gu, r_down = scatter(gu_whole), scatter(down_whole)
    for half in halves:
        second_half(half)
    ssm_whole = (0.5 * dot(ssm_low, dmix_low, 0, 0)).astype(BF)
    g_att_rows = (0.5 * dot(att_low, dmix_low, 0, 0)).astype(BF)
    g_att_blocks = seq_deal(g_att_rows.reshape(width, S, cols).transpose(1, 0, 2))
    g_att_whole = jnp.concatenate(
        [g_att_blocks[i, : head_counts[i] * HEAD] for i in range(S)], axis=0
    )
    for half in halves:
        attention_half(half)
    halves[0]["d_rest"], r_gu = lax.optimization_barrier((halves[0]["d_rest"], r_gu))
    rest_whole = dot(both("normed"), both("d_rest"), 0, 0).astype(BF)
    rest_whole = lax.dynamic_update_slice(rest_whole, g_att_whole, (0, at_att - ch))
    r_down, ssm_whole, rest_whole = hold(["d_core"], r_down, ssm_whole, rest_whole)
    r_ssm, r_rest = scatter(ssm_whole), scatter(rest_whole)
    for half in halves:
        third_half(half)
    r_ssm, r_rest = hold(["d_inner"], r_ssm, r_rest)
    for half in halves:
        last_half(half)
    small_whole = jnp.concatenate(
        [
            dot(both("u"), both("dproj", 1), 0, 1)[:, :PROJ],
            dot(both("ddt"), both("dt_in", 1), 0, 1),
            halves[0]["small"] + halves[1]["small"],
            jnp.zeros((ch, 1), F32),
        ],
        axis=1,
    )
    last_whole = dot(both("normed"), both("d_inner"), 0, 0).astype(BF)
    (small_whole, last_whole) = hold(["dx"], small_whole, last_whole)
    r_small, r_last = scatter(small_whole), scatter(last_whole)
    input_grads = give(both("dx"), send_hot, land_hot)

    per = N // S
    gate_take = np.concatenate(
        [np.arange(ff_piece) + ffw * i for i in range(per)]
    )
    half_wide = -(-per * ff_piece // LANES) * LANES
    moves = []
    for d in range(S):
        for i in range(2):
            table = gate_take[None] + d * per * ffw + i * ffs
            moves.append((0, None, 0, d, placed(table, i * half_wide, 2 * half_wide)))
        moves.append((1, None, 1, d, run_table([d * cols], cols)))
        moves.append((2, None, 2, d, run_table([d * cols], cols)))
    blocks = regroup(
        [r_gu, r_ssm, r_down],
        [
            jax.ShapeDtypeStruct((S, rows_d, 2 * half_wide), BF),
            jax.ShapeDtypeStruct((S, r_ssm.shape[0], cols), BF),
            jax.ShapeDtypeStruct((S, r_down.shape[0], cols), BF),
        ],
        moves,
        s,
    )
    blocks, _ = lax.optimization_barrier((list(blocks), last_whole))
    gu_got, ssm_got, down_got, ffn_got = deal(blocks + [down_parts], 0)
    ffn_out = jnp.sum(ffn_got.astype(F32), axis=0)
    result = hidden + ffn_out
    outputs = give(result.astype(BF), send_hot, land_hot)
    out_ssm = ssm_got[:, :ch_piece].reshape(S * ch_piece, cols).astype(F32)
    out_down = down_got[:, :ff_piece].reshape(S * ff_piece, cols).astype(F32)
    ff_mine, mix_mine = ff // S, 2 * INNER // S
    moves = []
    at = np.arange(ff_mine)
    for source in range(S):
        chunk, inside = at // (S * ff_piece), at % (S * ff_piece)
        table = np.where(
            inside // ff_piece == source, chunk * ff_piece + inside % ff_piece, -1
        )[None].astype(np.int32)
        moves.append((0, source, 0, 0, table))
        moves.append((0, source, 1, 0, np.where(table >= 0, table + half_wide, -1)))
    out_gate, out_up = regroup(
        [gu_got], [jax.ShapeDtypeStruct((rows_d, ff_mine), F32)] * 2, moves, s
    )

    qkv_wide = (ATT + 2 * KV_WIDTH) // S
    mix_slot = -(-mix_mine // S // LANES) * LANES
    at = np.arange(mix_mine // S)
    moves = []
    starts = np.array(q_starts)[:, None]
    counts = np.array(head_counts)[:, None] * HEAD
    for d in range(S):
        chunk = at // ch_piece + d * (2 * N // S)
        table = chunk * chw + at % ch_piece
        wide = mix_slot + qkv_wide
        inner_part = np.where(chunk < N, table, -1)[None].astype(np.int32)
        gate_part = np.where(chunk >= N, table - ch, -1)[None].astype(np.int32)
        moves.append((0, None, 0, d, placed(inner_part, 0, wide)))
        moves.append((1, None, 0, d, placed(gate_part, 0, wide)))
        column = np.arange(qkv_wide)[None] + d * qkv_wide
        from_q = np.where(
            (column >= starts) & (column < starts + counts), column - starts + at_q - ch, -1
        )
        base = np.array(kv_starts)[:, None]
        from_k = np.where(
            (column >= base) & (column < base + 2 * HEAD), column - base + at_k - ch, -1
        )
        base = base + KV_WIDTH
        from_v = np.where(
            (column >= base) & (column < base + 2 * HEAD), column - base + at_v - ch, -1
        )
        table = np.maximum(np.maximum(from_q, from_k), from_v).astype(np.int32)
        moves.append((1, None, 0, d, placed(table, mix_slot, wide)))
    in_blocks = regroup(
        [r_last, r_rest], [jax.ShapeDtypeStruct((S, rows_d, wide), BF)], moves, s
    )[0]
    in_got, small_got = deal(
        [in_blocks, jnp.broadcast_to(r_small, (S,) + r_small.shape)], 1
    )
    moves = []
    at = np.arange(mix_mine)
    for source in range(S):
        chunk, inside = at // (S * ch_piece), at % (S * ch_piece)
        table = np.where(
            inside // ch_piece == source, chunk * ch_piece + inside % ch_piece, -1
        )[None].astype(np.int32)
        moves.append((0, source, 0, 0, table))
        moves.append((0, source, 1, 0, run_table([mix_slot], qkv_wide)))
    out_mix, out_qkv = regroup(
        [in_got],
        [
            jax.ShapeDtypeStruct((rows_d, mix_mine), F32),
            jax.ShapeDtypeStruct((rows_d, qkv_wide), F32),
        ],
        moves,
        s,
    )
    g_att = r_rest[:, at_att - ch :].astype(F32)
    small_all = small_got[:, :ch_piece].reshape(S * ch_piece, small_wide).astype(F32)
    out_x = span(small_all[:, :PROJ], 1, s * (PROJ // S), PROJ // S)
    out_dt = span(small_all[:, PROJ : PROJ + DT_RANK], 1, s * (DT_RANK // S), DT_RANK // S)
    out_small = small_all[:, PROJ + DT_RANK : PROJ + DT_RANK + CONV + 3 + STATE]

    def added(values):
        total = values[0]
        for further in values[1:]:
            total = total + further
        return total

    d_gain_att, d_gain_ssm = [added([one["gains"][i] for one in halves]) for i in range(2)]
    att_at = lax.dynamic_update_slice_in_dim(
        jnp.zeros((ATT + width,), F32), d_gain_att * live[0], q_start, 0
    )[:ATT]
    ssm_at = lax.dynamic_update_index_in_dim(
        jnp.zeros((N, S, ch_piece), F32), d_gain_ssm.reshape(N, -1)[:, :ch_piece], s, 1
    ).reshape(INNER)
    d_gain_in = added([one["d_gain_in"] for one in halves])
    stats = jnp.stack(
        [
            squares(x_own.astype(F32)),
            jnp.sum(sums[0]),
            jnp.sum(sums[1]),
            squares(mixer_out),
            squares(ffn_out),
            squares(result),
        ]
    )
    ends = np.cumsum([0, D, ATT, INNER, D, 6])
    line = jnp.concatenate([d_gain_in, att_at, ssm_at, d_gain_ffn[0], stats])
    sums = total_of(jnp.pad(line, (0, -line.shape[0] % 1024)).reshape(-1, LANES), 2).reshape(-1)
    g_gain_in, g_gain_att, g_gain_ssm, g_gain_ffn, stat_sum = [
        sums[a:b] for a, b in zip(ends[:-1], ends[1:])
    ]
    widths = jnp.array([D, ATT, INNER, D, D, D], F32)
    rms = jnp.sqrt(stat_sum / (widths * (micro * pack * N)))
    return (
        outputs.reshape(tokens.shape),
        input_grads.reshape(tokens.shape),
        g_gain_in,
        out_qkv,
        out_mix,
        out_x,
        out_dt,
        out_small,
        out_small[:, CONV + 1],
        g_gain_att,
        g_gain_ssm,
        g_att,
        out_ssm,
        g_gain_ffn,
        out_gate,
        out_up,
        out_down,
        rms,
    )


def solution(mesh):
    rows = P(None, ("seq", "fsdp"), None)
    shard = P("fsdp", None)
    both = P("fsdp", "seq")
    placed = (rows, rows, P(None, "seq"), P(None, "fsdp", None), P())
    placed += (shard,) * 5 + (P(), P(), shard, shard, P(), shard, shard, shard)
    return jax.shard_map(
        local,
        mesh=mesh,
        in_specs=placed,
        out_specs=(
            rows,
            rows,
            P(),
            both,
            both,
            both,
            both,
            shard,
            P("fsdp"),
            P(),
            P(),
            both,
            both,
            P(),
            both,
            both,
            both,
            P(),
        ),
        check_vma=False,
    )
```

```python
from functools import partial

import jax
import jax.numpy as jnp
import numpy as np
from jax import lax
from jax.experimental import pallas as pl
from jax.experimental.pallas import tpu as pltpu
from jax.sharding import PartitionSpec as P

D = 1600
HEADS = 25
KV_HEADS = 5
HEAD = 64
INNER = 3200
STATE = 16
CONV = 4
DT_RANK = 100
MICRO = 2
ATT = 1600
KV_WIDTH = 320
PROJ = DT_RANK + 2 * STATE
PROJ_PAD = 144
LANES = 128
EPS = 1e-05
BF = jnp.bfloat16
F32 = jnp.float32


def dot(left_op, right_op, left_dim, right_dim):
    return lax.dot_general(
        left_op, right_op, (((left_dim,), (right_dim,)), ((), ())), preferred_element_type=F32
    )


def rms_scale(row_vals, gain_vec):
    return (
        row_vals * lax.rsqrt(jnp.mean(row_vals * row_vals, axis=-1, keepdims=True) + EPS) * gain_vec
    )


def seq_layout(seq_lens, span_len):
    places = jnp.arange(span_len, dtype=jnp.int32)
    seq_ends = jnp.cumsum(seq_lens)
    segment = jnp.sum((places[:, None] >= seq_ends[None, :]).astype(jnp.int32), axis=1)
    starts = seq_ends - seq_lens
    picked = (segment[:, None] == jnp.arange(seq_lens.shape[0], dtype=jnp.int32)[None, :]).astype(
        jnp.int32
    )
    position = places - jnp.sum(picked * starts[None, :], axis=1)
    return (segment, position)


def swap(array, k):
    size = lax.axis_size("seq")
    return lax.ppermute(array, "seq", [(i, i ^ k) for i in range(size)])


def pick(blocks, at):
    return lax.dynamic_index_in_dim(blocks, at, 0, keepdims=False)


def seq_deal(blocks):
    size, here = lax.axis_size("seq"), lax.axis_index("seq")
    out = blocks
    for k in range(1, size):
        there = here ^ k
        out = lax.dynamic_update_index_in_dim(out, swap(pick(blocks, there), k), there, 0)
    return out


def seq_gather(block):
    size, here = lax.axis_size("seq"), lax.axis_index("seq")
    out = lax.dynamic_update_index_in_dim(
        jnp.zeros((size,) + block.shape, block.dtype), block, here, 0
    )
    for k in range(1, size):
        out = lax.dynamic_update_index_in_dim(out, swap(block, k), here ^ k, 0)
    return out


def seq_scatter(blocks):
    size, here = lax.axis_size("seq"), lax.axis_index("seq")
    total = pick(blocks, here).astype(F32)
    for k in range(1, size):
        total = total + swap(pick(blocks, here ^ k).astype(BF), k).astype(F32)
    return total


def seq_sum(array):
    return jnp.sum(seq_gather(array).astype(F32), axis=0)


def routing(route_rows, tok_rows):
    fsdp_count, fsdp_rank = lax.axis_size("fsdp"), lax.axis_index("fsdp")
    micro = route_rows.shape[0]
    per_peer = tok_rows // fsdp_count
    target_dev = (route_rows // tok_rows).reshape(micro, fsdp_count, tok_rows)
    target_slot = (route_rows % tok_rows).reshape(micro, fsdp_count, tok_rows)
    steps = jnp.arange(tok_rows, dtype=jnp.int32)
    same = target_dev[:, :, :, None] == target_dev[:, :, None, :]
    earlier = steps[None, :] < steps[:, None]
    rank = jnp.sum((same & earlier).astype(jnp.int32), axis=3)
    my_dev = lax.dynamic_index_in_dim(target_dev, fsdp_rank, 1, keepdims=False)
    my_rank = lax.dynamic_index_in_dim(rank, fsdp_rank, 1, keepdims=False)
    micros = jnp.arange(micro, dtype=jnp.int32)
    send_at = (my_dev * micro + micros[:, None]) * per_peer + my_rank
    ranks = jnp.arange(per_peer, dtype=jnp.int32)
    mine = (target_dev == fsdp_rank)[:, :, None, :] & (rank[:, :, None, :] == ranks[:, None])
    slot = jnp.sum(mine.astype(jnp.int32) * target_slot[:, :, None, :], axis=3)
    land_at = (micros[:, None, None] * tok_rows + slot).transpose(1, 0, 2).reshape(-1)
    rows = jnp.arange(micro * tok_rows, dtype=jnp.int32)
    send_hot = (rows[:, None] == send_at.reshape(-1)[None, :]).astype(BF)
    land_hot = (rows[:, None] == land_at[None, :]).astype(BF)
    return send_hot, land_hot


def exchange(rows):
    return lax.all_to_all(rows, "fsdp", split_axis=0, concat_axis=0, tiled=True)


def bring(rows, send_hot, land_hot):
    sent = dot(send_hot, rows, 1, 0).astype(BF)
    return dot(land_hot, exchange(sent), 1, 0).astype(BF)


def give(rows, send_hot, land_hot):
    sent = dot(land_hot, rows, 0, 0).astype(BF)
    return dot(send_hot, exchange(sent), 0, 0).astype(BF)


def meet(peers):
    barrier = pltpu.get_barrier_semaphore()
    for peer in peers:
        pl.semaphore_signal(barrier, inc=1, device_id=peer, device_id_type=pl.DeviceIdType.MESH)
    pl.semaphore_wait(barrier, len(peers))


def remote(source, target, send, recv, device):
    return pltpu.make_async_remote_copy(
        src_ref=source,
        dst_ref=target,
        send_sem=send,
        recv_sem=recv,
        device_id=device,
        device_id_type=pl.DeviceIdType.MESH,
    )


def pack_peers(size):
    here, row = lax.axis_index("seq"), lax.axis_index("fsdp")
    return [(lax.rem(here + k, size), row) for k in range(1, size)]


def start_deal(source, out, size, own_sem, send_sem, recv_sem, first=0, start=True):
    here, row = lax.axis_index("seq"), lax.axis_index("fsdp")
    copies = [pltpu.make_async_copy(source.at[here], out.at[here], own_sem)]
    for k in range(1, size):
        there = lax.rem(here + k, size)
        copies.append(
            remote(
                source.at[there],
                out.at[here],
                send_sem.at[first + k - 1],
                recv_sem.at[first + k - 1],
                (there, row),
            )
        )
    if start:
        for copy in copies:
            copy.start()
    return copies


def deal_sems(size, count=1):
    links = pltpu.SemaphoreType.DMA((count * (size - 1),))
    return [pltpu.SemaphoreType.DMA((count,)), links, links]


VMEM_BYTES = 60 * 2**20
VMEM = pl.BlockSpec(memory_space=pltpu.VMEM)
HBM = pl.BlockSpec(memory_space=pl.ANY)
SHAPE = jax.ShapeDtypeStruct


def lane_groups(channels, most=4):
    tiles, out, first = channels // LANES, [], 0
    while first < tiles:
        count = min(most, tiles - first)
        out.append((first, count))
        first += count
    return out


def sigmoid(v):
    return 1.0 / (1.0 + jnp.exp(-v))


def softplus(v):
    return jnp.maximum(v, 0.0) + jnp.log1p(jnp.exp(-jnp.abs(v)))


def steps_of(lin_ref, u_ref, position_ref, dtm, dtu):
    step = softplus(lin_ref[...])
    dtu[...] = step * u_ref[...]
    dtm[...] = jnp.where(position_ref[...] > 0, step, 1e30)


def both_of(ref, t):
    row = ref[t].astype(F32)
    return row[:STATE], row[STATE:]


def scan_kernel(size, groups, *refs):
    u_ref, lin_ref, bc_ref, a_ref, position_ref, gate_ref, skip_ref, held = refs[:8]
    core, out, sums, got, dtm, dtu, own_sem, held_send, held_recv = refs[8:]
    steps = u_ref.shape[0]

    def copies(start):
        return start_deal(held, got, size, own_sem.at[0], held_send, held_recv, start=start)

    @pl.when(pl.program_id(0) == 0)
    def _():
        meet(pack_peers(size))
        copies(True)

    steps_of(lin_ref, u_ref, position_ref, dtm, dtu)
    place = lax.broadcasted_iota(jnp.int32, (8, LANES), 0)
    for first, count in groups:
        spans = [pl.ds((first + i) * LANES, LANES) for i in range(count)]
        rates = [a_ref[:, span] for span in spans]

        def block(k, held):
            held = list(held)
            rows = pl.ds(pl.multiple_of(k * 8, 8), 8)
            dts = [dtm[rows, span] for span in spans]
            dus = [dtu[rows, span] for span in spans]
            ys = [jnp.zeros((8, LANES), F32)] * count
            for j in range(8):
                b_now, c_now = both_of(bc_ref, k * 8 + j)
                for i in range(count):
                    decay = jnp.exp(dts[i][j : j + 1] * rates[i])
                    held[i] = decay * held[i] + dus[i][j : j + 1] * b_now
                    y = jnp.sum(held[i] * c_now, axis=0, keepdims=True)
                    ys[i] = jnp.where(place == j, y, ys[i])
            for i, span in enumerate(spans):
                core[rows, span] = ys[i]
            return tuple(held)

        zero = jnp.zeros((STATE, LANES), F32)
        lax.fori_loop(0, steps // 8, block, (zero,) * count)
    gate = gate_ref[...].astype(F32)
    result = (core[...] + skip_ref[...] * u_ref[...]) * (gate * sigmoid(gate))
    out[...] = result
    sums[...] = row_sums(result * result)

    @pl.when(pl.program_id(0) == pl.num_programs(0) - 1)
    def _():
        for copy in copies(False):
            copy.wait()


def row_sums(values):
    return lax.dot_general(
        jnp.ones((8, values.shape[1]), F32),
        values,
        (((1,), (1,)), ((), ())),
        precision=lax.Precision.HIGHEST,
        preferred_element_type=F32,
    )


def scan_forward(u, lin, bc, rates, position, opened, skip, held, micro, collective_id):
    size = lax.axis_size("seq")
    rows, channels = u.shape
    steps = rows // micro
    block = pl.BlockSpec((steps, channels), lambda m: (m, 0))
    lane = pl.BlockSpec((8, steps), lambda m: (0, m))
    return pl.pallas_call(
        partial(scan_kernel, size, lane_groups(channels)),
        grid=(micro,),
        out_shape=[SHAPE((rows, channels), F32)] * 2
        + [SHAPE((8, rows), F32), SHAPE(held.shape, held.dtype)],
        in_specs=[
            block,
            block,
            pl.BlockSpec((steps, 2 * STATE, LANES), lambda m: (m, 0, 0)),
            pl.BlockSpec(rates.shape, lambda m: (0, 0)),
            pl.BlockSpec((steps, 1), lambda m: (m, 0)),
            pl.BlockSpec((steps, channels), lambda m: (m, 1)),
            pl.BlockSpec((1, channels), lambda m: (0, 0)),
            HBM,
        ],
        out_specs=[block, block, lane, HBM],
        scratch_shapes=[pltpu.VMEM((steps, channels), F32)] * 2 + deal_sems(size),
        compiler_params=pltpu.CompilerParams(
            collective_id=collective_id, has_side_effects=True, vmem_limit_bytes=VMEM_BYTES
        ),
        name="scan_forward",
    )(u, lin, bc, rates, position, opened, skip, held)


def scan_back_kernel(size, count, groups, *refs):
    dcore_ref, u_ref, lin_ref, bc_ref, a_ref, position_ref, skip_ref = refs[:7]
    helds, refs = refs[7 : 7 + count], refs[7 + count :]
    du_ref, dlin_ref, bias_ref, da_ref, db_ref, dc_ref = refs[:6]
    gots, refs = refs[6 : 6 + count], refs[6 + count :]
    dtm, dtu, ddtu, ddt, hs, acc_b, acc_c, own_sem, held_send, held_recv = refs
    steps = u_ref.shape[0]

    def copies():
        out = []
        for i, (held, got) in enumerate(zip(helds, gots)):
            out += start_deal(
                held, got, size, own_sem.at[i], held_send, held_recv, i * (size - 1), start=False
            )
        return out

    @pl.when(pl.program_id(0) == 0)
    def _():
        meet(pack_peers(size))
        for copy in copies():
            copy.start()

    steps_of(lin_ref, u_ref, position_ref, dtm, dtu)
    place = lax.broadcasted_iota(jnp.int32, (8, LANES), 0)
    zero = jnp.zeros((STATE, LANES), F32)
    for at, (first, count) in enumerate(groups):
        spans = [pl.ds((first + i) * LANES, LANES) for i in range(count)]
        slots = [pl.ds(i * LANES, LANES) for i in range(count)]
        rates = [a_ref[:, span] for span in spans]
        for slot in slots:
            hs[0, :, slot] = zero

        def block(k, held):
            held = list(held)
            base = pl.multiple_of(k * 8, 8)
            rows = pl.ds(base, 8)
            dts = [dtm[rows, span] for span in spans]
            dus = [dtu[rows, span] for span in spans]
            for j in range(8):
                b_now, _ = both_of(bc_ref, base + j)
                for i in range(count):
                    decay = jnp.exp(dts[i][j : j + 1] * rates[i])
                    held[i] = decay * held[i] + dus[i][j : j + 1] * b_now
                    hs[base + j + 1, :, slots[i]] = held[i]
            return tuple(held)

        lax.fori_loop(0, steps // 8, block, (zero,) * count)

        def back(k, carry):
            carry = list(carry)
            block_at = steps // 8 - 1 - k
            base = pl.multiple_of(block_at * 8, 8)
            rows = pl.ds(base, 8)
            dts = [dtm[rows, span] for span in spans]
            dus = [dtu[rows, span] for span in spans]
            dys = [dcore_ref[rows, span] for span in spans]
            out_u = [jnp.zeros((8, LANES), F32)] * count
            out_t = [jnp.zeros((8, LANES), F32)] * count
            for j in reversed(range(8)):
                t = base + j
                b_now, c_now = both_of(bc_ref, t)
                sum_b = sum_c = zero
                for i in range(count):
                    later, rate_sum = carry[i]
                    dt, du, dy = dts[i][j : j + 1], dus[i][j : j + 1], dys[i][j : j + 1]
                    g = later + dy * c_now
                    sum_c = sum_c + hs[t + 1, :, slots[i]] * dy
                    sum_b = sum_b + g * du
                    through = g * jnp.exp(dt * rates[i])
                    moved = through * hs[t, :, slots[i]]
                    to_u = jnp.sum(g * b_now, axis=0, keepdims=True)
                    to_t = jnp.sum(moved * rates[i], axis=0, keepdims=True)
                    out_u[i] = jnp.where(place == j, to_u, out_u[i])
                    out_t[i] = jnp.where(place == j, to_t, out_t[i])
                    carry[i] = (through, rate_sum + moved * dt)
                if at == 0:
                    acc_b[t] = sum_b
                    acc_c[t] = sum_c
                else:
                    acc_b[t] = acc_b[t] + sum_b
                    acc_c[t] = acc_c[t] + sum_c
            for i, span in enumerate(spans):
                ddtu[rows, span] = out_u[i]
                ddt[rows, span] = out_t[i]
            return tuple(carry)

        ends = lax.fori_loop(0, steps // 8, back, ((zero, zero),) * count)
        for i, span in enumerate(spans):
            da_ref[:, span] = ends[i][1]
    for acc, out in ((acc_b, db_ref), (acc_c, dc_ref)):
        out[...] = row_sums(acc[...].reshape(steps * STATE, LANES))
    lin = lin_ref[...]
    to_step = ddtu[...]
    du_ref[...] = dcore_ref[...] * skip_ref[...] + to_step * softplus(lin)
    d_lin = (ddt[...] + to_step * u_ref[...]) * sigmoid(lin)
    dlin_ref[...] = d_lin.astype(BF)
    bias_ref[...] = jnp.sum(d_lin, axis=0, keepdims=True)

    @pl.when(pl.program_id(0) == pl.num_programs(0) - 1)
    def _():
        for copy in copies():
            copy.wait()


def scan_backward(dcore, u, lin, bc, rates, position, skip, helds, micro, collective_id):
    size = lax.axis_size("seq")
    rows, channels = u.shape
    steps = rows // micro
    groups = lane_groups(channels)
    block = pl.BlockSpec((steps, channels), lambda m: (m, 0))
    rate = pl.BlockSpec(rates.shape, lambda m: (0, 0))
    line = pl.BlockSpec((1, channels), lambda m: (0, 0))
    flat = pl.BlockSpec((None, 8, steps * STATE), lambda m: (m, 0, 0))
    wide = pltpu.VMEM((steps, channels), F32)
    du, dlin, bias, da, db, dc, *gots = pl.pallas_call(
        partial(scan_back_kernel, size, len(helds), groups),
        grid=(micro,),
        out_shape=[
            SHAPE((rows, channels), F32),
            SHAPE((rows, channels), BF),
            SHAPE((micro, 1, channels), F32),
            SHAPE((micro, STATE, channels), F32),
            SHAPE((micro, 8, steps * STATE), F32),
            SHAPE((micro, 8, steps * STATE), F32),
        ]
        + [SHAPE(held.shape, held.dtype) for held in helds],
        in_specs=[
            block,
            block,
            block,
            pl.BlockSpec((steps, 2 * STATE, LANES), lambda m: (m, 0, 0)),
            rate,
            pl.BlockSpec((steps, 1), lambda m: (m, 0)),
            line,
        ]
        + [HBM] * len(helds),
        out_specs=[
            block,
            block,
            pl.BlockSpec((None, 1, channels), lambda m: (m, 0, 0)),
            pl.BlockSpec((None, STATE, channels), lambda m: (m, 0, 0)),
            flat,
            flat,
        ]
        + [HBM] * len(helds),
        scratch_shapes=[wide] * 4
        + [
            pltpu.VMEM((steps + 1, STATE, groups[0][1] * LANES), F32),
            pltpu.VMEM((steps, STATE, LANES), F32),
            pltpu.VMEM((steps, STATE, LANES), F32),
        ]
        + deal_sems(size, len(helds)),
        compiler_params=pltpu.CompilerParams(
            collective_id=collective_id, has_side_effects=True, vmem_limit_bytes=VMEM_BYTES
        ),
        name="scan_backward",
    )(dcore, u, lin, bc, rates, position, skip, *helds)
    return (
        du,
        dlin,
        jnp.sum(bias[:, 0], axis=0),
        jnp.sum(da, axis=0),
        db[:, 0].reshape(rows, STATE),
        dc[:, 0].reshape(rows, STATE),
        gots,
    )


def regroup_kernel(plan, source_count, out_count, *refs):
    sources = refs[:source_count]
    maps = refs[source_count : len(refs) - out_count]
    outs = refs[len(refs) - out_count :]
    for out, block, tile, wide, terms in plan:
        at = pl.ds(tile * LANES, wide)
        total = None
        for source, which, low, high in terms:
            held = sources[source]
            held = held[..., low:high] if len(held.shape) == 2 else held[which[1], :, low:high]
            wanted = maps[which[0]][:, at] - low
            places = lax.broadcasted_iota(jnp.int32, (high - low, wide), 0)
            hot = (places == wanted).astype(F32).astype(BF)
            term = dot(held, hot, 1, 0)
            total = term if total is None else total + term
        ref = outs[out]
        if total is None:
            total = jnp.zeros((ref.shape[-2], wide), F32)
        if len(ref.shape) == 2:
            ref[:, at] = total.astype(ref.dtype)
        else:
            ref[block, :, at] = total.astype(ref.dtype)


def regroup(sources, outs, moves, here):
    plan, maps = [], []
    tables = []
    for source, from_block, out, block, table in moves:
        maps.append(jnp.asarray(table)[here][None] if len(table) > 1 else jnp.asarray(table))
        tables.append((source, from_block, out, block, table))
    for out, shape in enumerate(outs):
        for block in range(shape.shape[0] if len(shape.shape) == 3 else 1):
            for tile in range(-(-shape.shape[-1] // LANES)):
                wide = min(LANES, shape.shape[-1] - tile * LANES)
                terms = []
                for which, (source, from_block, to, to_block, table) in enumerate(tables):
                    used = table[:, tile * LANES : tile * LANES + wide]
                    if (to, to_block) != (out, block) or not (used >= 0).any():
                        continue
                    low = int(used[used >= 0].min()) // LANES * LANES
                    high = min(-(-(int(used.max()) + 1) // LANES) * LANES, sources[source].shape[-1])
                    terms.append((source, (which, from_block), low, high))
                plan.append((out, block, tile, wide, tuple(terms)))
    vmem = pl.BlockSpec(memory_space=pltpu.VMEM)
    return pl.pallas_call(
        partial(regroup_kernel, plan, len(sources), len(outs)),
        out_shape=list(outs),
        in_specs=[vmem] * (len(sources) + len(maps)),
        out_specs=[vmem] * len(outs),
        compiler_params=pltpu.CompilerParams(vmem_limit_bytes=VMEM_BYTES),
        name="regroup",
    )(*sources, *maps)


def pieces_table(chunks, size, piece, wide, start=0):
    at = np.arange(chunks * wide)
    chunk, place = at // wide, at % wide
    count = size // piece
    table = start + chunk * size + place + piece * np.arange(count)[:, None]
    return np.where(place < piece, table, -1).astype(np.int32)


def run_table(starts, count):
    return (np.asarray(starts)[:, None] + np.arange(count)).astype(np.int32)


def placed(table, at, width):
    out = np.full((table.shape[0], width), -1, np.int32)
    out[:, at : at + table.shape[1]] = table
    return out


def deal_kernel(count, size, *refs):
    sources, outs = refs[:count], refs[count : 2 * count]
    own_sem, send_sem, recv_sem = refs[2 * count :]
    meet(pack_peers(size))
    copies = []
    for i, (source, out) in enumerate(zip(sources, outs)):
        copies += start_deal(
            source, out, size, own_sem.at[i], send_sem, recv_sem, i * (size - 1)
        )
    for copy in copies:
        copy.wait()


def deal(arrays, collective_id):
    size, count = lax.axis_size("seq"), len(arrays)
    hbm = pl.BlockSpec(memory_space=pl.ANY)
    return pl.pallas_call(
        partial(deal_kernel, count, size),
        out_shape=[jax.ShapeDtypeStruct(a.shape, a.dtype) for a in arrays],
        in_specs=[hbm] * count,
        out_specs=[hbm] * count,
        scratch_shapes=deal_sems(size, count),
        compiler_params=pltpu.CompilerParams(collective_id=collective_id, has_side_effects=True),
        cost_estimate=pl.CostEstimate(
            flops=0, bytes_accessed=1024, transcendentals=0
        ),
        name="deal",
    )(*arrays)


def spread(slots, me, devices, send, recv):
    copies = []
    for k, device in enumerate(devices):
        copies.append(remote(slots.at[me], slots.at[me], send.at[k], recv.at[k], device))
        copies[-1].start()
    for copy in copies:
        copy.wait()
    total = slots[0]
    for i in range(1, slots.shape[0]):
        total = total + slots[i]
    return total


def last_kernel(sizes, count, *refs):
    sources, in_ref = refs[:count], refs[count]
    outs, out_ref = refs[count + 1 : 2 * count + 1], refs[2 * count + 1]
    one, two, send_one, recv_one, send_two, recv_two, own_sem, send_sem, recv_sem = refs[
        2 * count + 2 :
    ]
    seq, fsdp = lax.axis_index("seq"), lax.axis_index("fsdp")
    across = [(lax.rem(seq + k, sizes[0]), fsdp) for k in range(1, sizes[0])]
    along = [(seq, lax.rem(fsdp + k, sizes[1])) for k in range(1, sizes[1])]
    meet(across + along)
    one[seq] = in_ref[...]
    two[fsdp] = spread(one, seq, across, send_one, recv_one)
    copies = []
    for i, (source, out) in enumerate(zip(sources, outs)):
        copies += start_deal(
            source, out, sizes[0], own_sem.at[i], send_sem, recv_sem, i * (sizes[0] - 1)
        )
    out_ref[...] = spread(two, fsdp, along, send_two, recv_two)
    for copy in copies:
        copy.wait()


def last_exchange(arrays, block, collective_id):
    sizes, count = (lax.axis_size("seq"), lax.axis_size("fsdp")), len(arrays)
    return pl.pallas_call(
        partial(last_kernel, sizes, count),
        out_shape=[SHAPE(a.shape, a.dtype) for a in arrays] + [SHAPE(block.shape, block.dtype)],
        in_specs=[HBM] * count + [VMEM],
        out_specs=[HBM] * count + [VMEM],
        scratch_shapes=[pltpu.VMEM((n,) + block.shape, F32) for n in sizes]
        + [pltpu.SemaphoreType.DMA((n - 1,)) for n in sizes for _ in range(2)]
        + deal_sems(sizes[0], count),
        compiler_params=pltpu.CompilerParams(collective_id=collective_id, has_side_effects=True),
        name="last_exchange",
    )(*arrays, block)


def block_rows(size, tok, m, d):
    return pl.ds(pl.multiple_of((m * size + d) * tok, tok), tok)


def spread_rows(size, tok, micro, own, whole, own_sem, send_sem, recv_sem, first):
    here, row = lax.axis_index("seq"), lax.axis_index("fsdp")
    copies = []
    for m in range(micro):
        source, target = own.at[pl.ds(m * tok, tok)], whole.at[block_rows(size, tok, m, here)]
        for k in range(1, size):
            at = first + m * (size - 1) + k - 1
            there = (lax.rem(here + k, size), row)
            copies.append(remote(source, target, send_sem.at[at], recv_sem.at[at], there))
        at = first // (size - 1) + m
        copies.append(pltpu.make_async_copy(source, target, own_sem.at[at]))
    for copy in copies:
        copy.start()
    return copies


def gather_kernel(size, tok, micro, count, *refs):
    owns, wholes = refs[:count], refs[count : 2 * count]
    own_sem, send_sem, recv_sem = refs[2 * count :]
    meet(pack_peers(size))
    copies = []
    for i in range(count):
        first = i * micro * (size - 1)
        copies += spread_rows(
            size, tok, micro, owns[i], wholes[i], own_sem, send_sem, recv_sem, first
        )
    for copy in copies:
        copy.wait()


def gather_rows(arrays, micro, collective_id):
    size, count = lax.axis_size("seq"), len(arrays)
    tok = arrays[0].shape[0] // micro
    hbm = pl.BlockSpec(memory_space=pl.ANY)
    links = count * micro * (size - 1)
    return pl.pallas_call(
        partial(gather_kernel, size, tok, micro, count),
        out_shape=[jax.ShapeDtypeStruct((a.shape[0] * size, a.shape[1]), a.dtype) for a in arrays],
        in_specs=[hbm] * count,
        out_specs=[hbm] * count,
        scratch_shapes=[
            pltpu.SemaphoreType.DMA((count * micro,)),
            pltpu.SemaphoreType.DMA((links,)),
            pltpu.SemaphoreType.DMA((links,)),
        ],
        compiler_params=pltpu.CompilerParams(collective_id=collective_id, has_side_effects=True),
        name="gather_rows",
    )(*arrays)


def spans_of(width, most=512):
    return [(low, min(low + most, width)) for low in range(0, width, most)]


def joined(blocks, out):
    wide = blocks.shape[2]
    for i in range(blocks.shape[0]):
        out[:, i * wide : (i + 1) * wide] = blocks[i]
    return out


def mixer_kernel(size, tok, micro, *refs):
    context, ssm_out, sums_ref, x_ref, gain_att, gain_ssm, gain_ffn, w_att, w_ssm = refs[:9]
    att, ssm, scale_att, scale_ssm, hidden, mixer, ffn = refs[9:16]
    sums, sent, got, ffn_own, sums_send, sums_recv, send, recv, own_sem, ffn_send, ffn_recv = refs[
        16:-1
    ]
    w_att = joined(w_att, refs[-1])
    here, row = lax.axis_index("seq"), lax.axis_index("fsdp")
    peers = pack_peers(size)
    meet(peers)
    sums[here] = sums_ref[...]
    copies = [
        remote(sums.at[here], sums.at[here], sums_send.at[k], sums_recv.at[k], peer)
        for k, peer in enumerate(peers)
    ]
    for copy in copies:
        copy.start()
    for copy in copies:
        copy.wait()
    total = sums[0]
    for i in range(1, size):
        total = total + sums[i]
    place = lax.broadcasted_iota(jnp.int32, (8, LANES), 0)
    for kind, scale, width in ((0, scale_att, ATT), (1, scale_ssm, INNER)):
        column = lax.dot_general(
            total,
            (place == kind).astype(F32),
            (((0,), (0,)), ((), ())),
            precision=lax.Precision.HIGHEST,
            preferred_element_type=F32,
        )
        scale[...] = lax.rsqrt(column / width + EPS)
    att[...] = (context[...] * scale_att[:, :1] * gain_att[...]).astype(BF)
    ssm[...] = (ssm_out[...] * scale_ssm[:, :1] * gain_ssm[...]).astype(BF)

    def product(d, low, high):
        left = [jnp.concatenate([ref[block_rows(size, tok, m, d)] for m in range(micro)]) for ref in (att, ssm)]
        return 0.5 * (
            dot(left[0], w_att[:, low:high], 1, 0) + dot(left[1], w_ssm[:, low:high], 1, 0)
        )

    copies = []
    for k, peer in enumerate(peers):
        for low, high in spans_of(D):
            sent[k, :, low:high] = product(peer[0], low, high).astype(BF)
        copies.append(remote(sent.at[k], got.at[k], send.at[k], recv.at[k], peer))
        copies[-1].start()
    for low, high in spans_of(D):
        mixer[:, low:high] = product(here, low, high)
    for copy in copies:
        copy.wait()
    for m in range(micro):
        rows = pl.ds(m * tok, tok)
        out = mixer[rows]
        for k in range(size - 1):
            out = out + got[k, rows].astype(F32)
        mixer[rows] = out
        whole = x_ref[rows].astype(F32) + out
        hidden[rows] = whole
        scale = lax.rsqrt(jnp.mean(whole * whole, axis=-1, keepdims=True) + EPS)
        ffn_own[rows] = (whole * scale * gain_ffn[...]).astype(BF)
    for copy in spread_rows(size, tok, micro, ffn_own, ffn, own_sem, ffn_send, ffn_recv, 0):
        copy.wait()


def mixer_rows(context, ssm_out, sums, x_own, gains, w_att, w_ssm, micro, collective_id):
    size = lax.axis_size("seq")
    own = x_own.shape[0]
    rows, tok = own * size, own // micro
    vmem, hbm = pl.BlockSpec(memory_space=pltpu.VMEM), pl.BlockSpec(memory_space=pl.ANY)
    shape = jax.ShapeDtypeStruct
    dma = pltpu.SemaphoreType.DMA
    return pl.pallas_call(
        partial(mixer_kernel, size, tok, micro),
        out_shape=[
            shape((rows, w_att.shape[1]), BF),
            shape((rows, w_ssm.shape[0]), BF),
            shape((rows, LANES), F32),
            shape((rows, LANES), F32),
            shape((own, D), F32),
            shape((own, D), F32),
            shape((rows, D), BF),
        ],
        in_specs=[vmem] * 9,
        out_specs=[vmem] * 6 + [hbm],
        scratch_shapes=[
            pltpu.VMEM((size,) + sums.shape, F32),
            pltpu.VMEM((size - 1, own, D), BF),
            pltpu.VMEM((size - 1, own, D), BF),
            pltpu.VMEM((own, D), BF),
            dma((size - 1,)),
            dma((size - 1,)),
            dma((size - 1,)),
            dma((size - 1,)),
            dma((micro,)),
            dma((micro * (size - 1),)),
            dma((micro * (size - 1),)),
            pltpu.VMEM((w_att.shape[1], D), BF),
        ],
        compiler_params=pltpu.CompilerParams(
            collective_id=collective_id, has_side_effects=True, vmem_limit_bytes=VMEM_BYTES
        ),
        name="mixer_rows",
    )(context, ssm_out, sums, x_own, *gains, w_att, w_ssm)


def ffn_kernel(size, tok, micro, *refs):
    ffn, cot, hidden, cot_own, gain, w_gu, w_down = refs[:7]
    act, dgu, down, d_hidden, d_gain, dmix = refs[7:13]
    sent, got, dmix_own, send, recv, own_sem, dmix_send, dmix_recv = refs[13:]
    here, row = lax.axis_index("seq"), lax.axis_index("fsdp")
    wide = w_down.shape[0]
    meet(pack_peers(size))

    def copy_of(k):
        return remote(
            sent.at[k], got.at[k], send.at[k], recv.at[k], (lax.rem(here + k + 1, size), row)
        )

    def block(k, carry):
        d = lax.rem(here + k + 1, size)
        spots = [block_rows(size, tok, m, d) for m in range(micro)]
        rows_in = jnp.concatenate([ffn[spot] for spot in spots])
        cots = jnp.concatenate([cot[spot] for spot in spots])
        for low, high in spans_of(wide):
            gate = dot(rows_in, w_gu[:, low:high], 1, 0)
            up = dot(rows_in, w_gu[:, wide + low : wide + high], 1, 0)
            d_act = dot(cots, w_down[low:high, :], 1, 1)
            sig = 1.0 / (1.0 + jnp.exp(-gate))
            silu = gate * sig
            pieces = (
                (act, low, silu * up),
                (dgu, low, d_act * up * (sig * (1.0 + gate - silu))),
                (dgu, wide + low, d_act * silu),
            )
            for ref, at, values in pieces:
                values = values.astype(BF)
                for m, spot in enumerate(spots):
                    ref[spot, at : at + high - low] = values[m * tok : (m + 1) * tok]
        d_all = jnp.concatenate([dgu[spot] for spot in spots])
        for low, high in spans_of(D):
            sent[k, :, low:high] = dot(d_all, w_gu[low:high, :], 1, 1).astype(BF)

        @pl.when(k < size - 1)
        def _():
            copy_of(k).start()

        acts = jnp.concatenate([act[spot] for spot in spots])
        for low, high in spans_of(D):
            down[d, :, low:high] = dot(acts, w_down[:, low:high], 1, 0).astype(BF)
        return carry

    lax.fori_loop(0, size, block, 0)
    for k in range(size - 1):
        copy_of(k).wait()
    gain_sum = jnp.zeros((1, D), F32)
    for m in range(micro):
        rows = pl.ds(m * tok, tok)
        d_in = sent[size - 1, rows].astype(F32)
        for k in range(size - 1):
            d_in = d_in + got[k, rows].astype(F32)
        whole = hidden[rows]
        scale = lax.rsqrt(jnp.mean(whole * whole, axis=-1, keepdims=True) + EPS)
        normal = whole * scale
        gain_sum = gain_sum + jnp.sum(d_in * normal, axis=0, keepdims=True)
        scaled = d_in * gain[...]
        inward = jnp.mean(scaled * normal, axis=-1, keepdims=True)
        out = cot_own[rows].astype(F32) + scale * (scaled - normal * inward)
        d_hidden[rows] = out
        dmix_own[rows] = out.astype(BF)
    d_gain[...] = gain_sum
    for copy in spread_rows(size, tok, micro, dmix_own, dmix, own_sem, dmix_send, dmix_recv, 0):
        copy.wait()


def ffn_rows(ffn, cot, hidden, cot_own, gain, w_gu, w_down, micro, collective_id):
    size = lax.axis_size("seq")
    own, rows = hidden.shape[0], ffn.shape[0]
    wide = w_down.shape[0]
    tok = own // micro
    vmem, hbm = pl.BlockSpec(memory_space=pltpu.VMEM), pl.BlockSpec(memory_space=pl.ANY)
    shape = jax.ShapeDtypeStruct
    dma = pltpu.SemaphoreType.DMA
    return pl.pallas_call(
        partial(ffn_kernel, size, tok, micro),
        out_shape=[
            shape((rows, wide), BF),
            shape((rows, 2 * wide), BF),
            shape((size, own, D), BF),
            shape((own, D), F32),
            shape((1, D), F32),
            shape((rows, D), BF),
        ],
        in_specs=[vmem] * 7,
        out_specs=[vmem] * 5 + [hbm],
        scratch_shapes=[
            pltpu.VMEM((size, own, D), BF),
            pltpu.VMEM((size - 1, own, D), BF),
            pltpu.VMEM((own, D), BF),
            dma((size - 1,)),
            dma((size - 1,)),
            dma((micro,)),
            dma((micro * (size - 1),)),
            dma((micro * (size - 1),)),
        ],
        compiler_params=pltpu.CompilerParams(
            collective_id=collective_id, has_side_effects=True, vmem_limit_bytes=VMEM_BYTES
        ),
        name="ffn_rows",
    )(ffn, cot, hidden, cot_own, gain, w_gu, w_down)


def attention_kernel(most, at_k, opened_ref, position_ref, context, probs, sums):
    s, size = lax.axis_index("seq"), lax.axis_size("seq")
    first = (HEADS * s + size - 1) // size
    last = (HEADS * (s + 1) + size - 1) // size
    pack = position_ref.shape[0]
    at = 4 * HEAD
    in_ref = opened_ref.at[:, at_k : at_k + (4 + most) * HEAD]
    rows = lax.broadcasted_iota(jnp.int32, (pack, pack), 0)
    columns = lax.broadcasted_iota(jnp.int32, (pack, pack), 1)
    visible = (columns <= rows) & (columns >= rows - position_ref[...])
    for h in range(most):
        low = (first + h) // (HEADS // KV_HEADS) <= s
        q = in_ref[:, at + h * HEAD : at + (h + 1) * HEAD]
        key = jnp.where(low, in_ref[:, :HEAD], in_ref[:, HEAD : 2 * HEAD])
        value = jnp.where(low, in_ref[:, 2 * HEAD : 3 * HEAD], in_ref[:, 3 * HEAD : 4 * HEAD])
        masked = jnp.where(visible, dot(q, key, 1, 1) * 0.125, -1e30)
        terms = jnp.exp(masked - jnp.max(masked, axis=1, keepdims=True))
        prob = terms / jnp.sum(terms, axis=1, keepdims=True)
        probs[h] = prob
        out = dot(prob.astype(BF), value, 1, 0)
        context[:, h * HEAD : (h + 1) * HEAD] = jnp.where(first + h < last, out, 0.0)
    held = context[...]
    sums[...] = row_sums(held * held)


def attention(opened, at_k, position, most, micro):
    rows, wide = opened.shape
    pack = rows // micro
    return pl.pallas_call(
        partial(attention_kernel, most, at_k),
        grid=(micro,),
        out_shape=[
            SHAPE((rows, most * HEAD), F32),
            SHAPE((micro, most, pack, pack), F32),
            SHAPE((8, rows), F32),
        ],
        in_specs=[
            pl.BlockSpec((pack, wide), lambda m: (m, 0)),
            pl.BlockSpec((pack, 1), lambda m: (m, 0)),
        ],
        out_specs=[
            pl.BlockSpec((pack, most * HEAD), lambda m: (m, 0)),
            pl.BlockSpec((None, most, pack, pack), lambda m: (m, 0, 0, 0)),
            pl.BlockSpec((8, pack), lambda m: (0, m)),
        ],
        compiler_params=pltpu.CompilerParams(vmem_limit_bytes=VMEM_BYTES),
        name="attention",
    )(opened, position)


def sum_slots(slots, send, recv):
    here, row = lax.axis_index("seq"), lax.axis_index("fsdp")
    copies = [
        remote(slots.at[here], slots.at[here], send.at[k], recv.at[k], peer)
        for k, peer in enumerate(pack_peers(slots.shape[0]))
    ]
    for copy in copies:
        copy.start()
    for copy in copies:
        copy.wait()
    total = slots[0].astype(F32)
    for i in range(1, slots.shape[0]):
        total = total + slots[i].astype(F32)
    return total


def taps_of(inner, position, taps, bias):
    shifted = [inner]
    for k in range(1, CONV):
        shifted.append(jnp.where(position >= k, pltpu.roll(inner, k, axis=0), 0.0))
    conv = bias
    for k in range(CONV):
        conv = conv + taps[k : k + 1] * shifted[k]
    return conv, shifted


def ssm_open_kernel(
    size, micro, opened_ref, position_ref, taps, bias, w_x, w_dt, dt_bias, u_ref, lin_ref, proj_ref, bc_ref, slots, send, recv
):
    meet(pack_peers(size))
    steps = opened_ref.shape[0] // micro
    for m in range(micro):
        rows = pl.ds(m * steps, steps)
        for low, high in spans_of(w_x.shape[1], LANES):
            inner = opened_ref[rows, low:high].astype(F32)
            conv, _ = taps_of(inner, position_ref[rows], taps[:, low:high], bias[:, low:high])
            u_ref[rows, low:high] = conv * sigmoid(conv)
    slots[lax.axis_index("seq")] = dot(w_x[...], u_ref[...].astype(BF), 1, 1).astype(BF)
    proj = sum_slots(slots, send, recv).astype(BF)
    proj_ref[...] = proj
    bc_ref[...] = proj[: 2 * STATE]
    lin_ref[...] = dot(proj[2 * STATE :], w_dt[...], 0, 0) + dt_bias[...]


def ssm_open(opened, position, taps, bias, w_x, w_dt, dt_bias, micro, collective_id):
    size = lax.axis_size("seq")
    rows = opened.shape[0]
    wide, channels = w_x.shape
    dma = pltpu.SemaphoreType.DMA((size - 1,))
    return pl.pallas_call(
        partial(ssm_open_kernel, size, micro),
        out_shape=[
            SHAPE((rows, channels), F32),
            SHAPE((rows, channels), F32),
            SHAPE((wide, rows), BF),
            SHAPE((2 * STATE, rows), BF),
        ],
        in_specs=[VMEM] * 7,
        out_specs=[VMEM] * 4,
        scratch_shapes=[pltpu.VMEM((size, wide, rows), BF), dma, dma],
        compiler_params=pltpu.CompilerParams(
            collective_id=collective_id, has_side_effects=True, vmem_limit_bytes=VMEM_BYTES
        ),
        name="ssm_open",
    )(opened, position, taps, bias, w_x, w_dt, dt_bias)


def ssm_close_kernel(
    size, micro, count, *refs
):
    dlin_ref, db_ref, dc_ref, du_ref, opened_ref, position_ref, taps, bias, w_x, w_dt = refs[:10]
    helds, (dproj_ref, dinner_ref, sums_ref) = refs[10 : 10 + count], refs[10 + count : 13 + count]
    gots = refs[13 + count : 13 + 2 * count]
    slots, total, send, recv, own_sem, held_send, held_recv = refs[13 + 2 * count :]
    meet(pack_peers(size))
    here = lax.axis_index("seq")
    place = lax.broadcasted_iota(jnp.int32, (STATE, STATE), 0)
    eye = (place == lax.broadcasted_iota(jnp.int32, (STATE, STATE), 1)).astype(F32)
    for i, ref in enumerate((db_ref, dc_ref)):
        turned = lax.dot_general(
            eye,
            ref[...],
            (((1,), (1,)), ((), ())),
            precision=lax.Precision.HIGHEST,
            preferred_element_type=F32,
        )
        slots[here, i * STATE : (i + 1) * STATE] = turned.astype(BF)
    slots[here, 2 * STATE :] = dot(w_dt[...], dlin_ref[...], 1, 1).astype(BF)
    dproj = sum_slots(slots, send, recv).astype(BF)
    copies = []
    for i, (held, got) in enumerate(zip(helds, gots)):
        copies += start_deal(
            held, got, size, own_sem.at[i], held_send, held_recv, i * (size - 1)
        )
    dproj_ref[...] = dproj
    steps = opened_ref.shape[0] // micro
    total[...] = du_ref[...] + dot(dproj, w_x[...], 0, 0)
    for low, high in spans_of(w_x.shape[1], LANES):
        lines = [jnp.zeros((1, high - low), F32) for _ in range(CONV + 1)]
        for m in range(micro):
            rows = pl.ds(m * steps, steps)
            inner = opened_ref[rows, low:high].astype(F32)
            position = position_ref[rows]
            tap = taps[:, low:high]
            conv, shifted = taps_of(inner, position, tap, bias[:, low:high])
            sig = sigmoid(conv)
            d_conv = total[rows, low:high] * (sig * (1.0 + conv * (1.0 - sig)))
            d_inner = tap[0:1] * d_conv
            for k in range(CONV):
                lines[k] = lines[k] + jnp.sum(d_conv * shifted[k], axis=0, keepdims=True)
                if k:
                    masked = jnp.where(position >= k, d_conv, 0.0)
                    d_inner = d_inner + tap[k : k + 1] * pltpu.roll(masked, steps - k, axis=0)
            lines[CONV] = lines[CONV] + jnp.sum(d_conv, axis=0, keepdims=True)
            dinner_ref[rows, low:high] = d_inner.astype(BF)
        sums_ref[:, low:high] = jnp.concatenate(
            lines + [jnp.zeros((8 - CONV - 1, high - low), F32)], axis=0
        )
    for copy in copies:
        copy.wait()


def ssm_close(dlin, db, dc, du, opened, position, taps, bias, w_x, w_dt, helds, micro, collective_id):
    size = lax.axis_size("seq")
    rows = opened.shape[0]
    wide, channels = w_x.shape
    dma = pltpu.SemaphoreType.DMA((size - 1,))
    return pl.pallas_call(
        partial(ssm_close_kernel, size, micro, len(helds)),
        out_shape=[
            SHAPE((wide, rows), BF),
            SHAPE((rows, channels), BF),
            SHAPE((8, channels), F32),
        ]
        + [SHAPE(held.shape, held.dtype) for held in helds],
        in_specs=[VMEM] * 10 + [HBM] * len(helds),
        out_specs=[VMEM] * 3 + [HBM] * len(helds),
        scratch_shapes=[
            pltpu.VMEM((size, wide, rows), BF),
            pltpu.VMEM((rows, channels), F32),
            dma,
            dma,
        ]
        + deal_sems(size, max(1, len(helds))),
        compiler_params=pltpu.CompilerParams(
            collective_id=collective_id, has_side_effects=True, vmem_limit_bytes=VMEM_BYTES
        ),
        name="ssm_close",
    )(dlin, db, dc, du, opened, position, taps, bias, w_x, w_dt, *helds)


def branch_back_kernel(size, *refs):
    dmix, w_att, w_ssm, context, ssm_out, core, u, gate_ref = refs[:8]
    scale_att, scale_ssm, gain_att, gain_ssm, live, skip = refs[8:14]
    d_context, d_core, d_gate, d_gain_att, d_gain_ssm, d_skip = refs[14:20]
    t_att, t_ssm, slots, send, recv = refs[20:-1]
    w_att = joined(w_att, refs[-1])
    meet(pack_peers(size))
    place = lax.broadcasted_iota(jnp.int32, (8, LANES), 0)
    kinds = (
        (w_att, context, scale_att, gain_att, d_gain_att, t_att),
        (w_ssm, ssm_out, scale_ssm, gain_ssm, d_gain_ssm, t_ssm),
    )
    sums = []
    for w, value, scale, gain, d_gain, t in kinds:
        total = None
        for low, high in spans_of(w.shape[0], 2 * LANES):
            grad = 0.5 * dot(dmix[...], w[low:high, :], 1, 1)
            held = value[:, low:high]
            d_gain[:, low:high] = jnp.sum(grad * held * scale[:, :1], axis=0, keepdims=True)
            scaled = grad * gain[:, low:high]
            t[:, low:high] = scaled
            term = row_sums(scaled * held)
            total = term if total is None else total + term
        sums.append(total)
    rows8 = lax.broadcasted_iota(jnp.int32, sums[0].shape, 0)
    slots[lax.axis_index("seq")] = jnp.where(rows8 == 0, sums[0], sums[1])
    total = sum_slots(slots, send, recv)
    columns = [
        lax.dot_general(
            total,
            (place == kind).astype(F32),
            (((0,), (0,)), ((), ())),
            precision=lax.Precision.HIGHEST,
            preferred_element_type=F32,
        )
        for kind in range(2)
    ]
    scale = scale_att[:, :1]
    inward = scale * scale * scale * (columns[0][:, :1] / ATT)
    d_context[...] = ((t_att[...] * scale - context[...] * inward) * live[...]).astype(BF)
    scale = scale_ssm[:, :1]
    inward = scale * scale * scale * (columns[1][:, :1] / INNER)
    for low, high in spans_of(w_ssm.shape[0], 2 * LANES):
        at = slice(low, high)
        d_out = t_ssm[:, at] * scale - ssm_out[:, at] * inward
        gate = gate_ref[:, at].astype(F32)
        sig = sigmoid(gate)
        silu = gate * sig
        held = d_out * silu
        d_core[:, at] = held
        d_skip[:, at] = jnp.sum(held * u[:, at], axis=0, keepdims=True)
        mixed = core[:, at] + skip[:, at] * u[:, at]
        d_gate[:, at] = (d_out * mixed * (sig * (1.0 + gate - silu))).astype(BF)


def branch_back(
    dmix, w_att, w_ssm, context, ssm_out, core, u, gate_z, scales, gains, live, skip, collective_id
):
    size = lax.axis_size("seq")
    rows, wide, channels = dmix.shape[0], w_att.shape[1], w_ssm.shape[0]
    dma = pltpu.SemaphoreType.DMA((size - 1,))
    return pl.pallas_call(
        partial(branch_back_kernel, size),
        out_shape=[
            SHAPE((rows, wide), BF),
            SHAPE((rows, channels), F32),
            SHAPE((rows, channels), BF),
            SHAPE((1, wide), F32),
            SHAPE((1, channels), F32),
            SHAPE((1, channels), F32),
        ],
        in_specs=[VMEM] * 14,
        out_specs=[VMEM] * 6,
        scratch_shapes=[
            pltpu.VMEM((rows, wide), F32),
            pltpu.VMEM((rows, channels), F32),
            pltpu.VMEM((size, 8, rows), F32),
            dma,
            dma,
        ]
        + [pltpu.VMEM((wide, D), BF)],
        compiler_params=pltpu.CompilerParams(
            collective_id=collective_id, has_side_effects=True, vmem_limit_bytes=VMEM_BYTES
        ),
        name="branch_back",
    )(dmix, w_att, w_ssm, context, ssm_out, core, u, gate_z, *scales, *gains, live, skip)


def close_kernel(size, tok, micro, rest, d_inner, w, x_ref, gain, d_hidden, dx, d_gain, sent, got, send, recv):
    here, row = lax.axis_index("seq"), lax.axis_index("fsdp")
    meet(pack_peers(size))

    def copy_of(k):
        return remote(
            sent.at[k], got.at[k], send.at[k], recv.at[k], (lax.rem(here + k + 1, size), row)
        )

    def block(k, carry):
        d = lax.rem(here + k + 1, size)
        spots = [block_rows(size, tok, m, d) for m in range(micro)]
        rows = jnp.concatenate([d_inner[spot] for spot in spots])
        held = jnp.concatenate([rest[spot] for spot in spots])
        for low, high in spans_of(D):
            part = held[:, low:high].astype(F32) + dot(rows, w[low:high, :], 1, 1)
            sent[k, :, low:high] = part.astype(BF)

        @pl.when(k < size - 1)
        def _():
            copy_of(k).start()

        return carry

    lax.fori_loop(0, size, block, 0)
    for k in range(size - 1):
        copy_of(k).wait()
    gain_sum = jnp.zeros((1, D), F32)
    for m in range(micro):
        rows = pl.ds(m * tok, tok)
        d_in = sent[size - 1, rows].astype(F32)
        for k in range(size - 1):
            d_in = d_in + got[k, rows].astype(F32)
        whole = x_ref[rows].astype(F32)
        scale = lax.rsqrt(jnp.mean(whole * whole, axis=-1, keepdims=True) + EPS)
        normal = whole * scale
        gain_sum = gain_sum + jnp.sum(d_in * normal, axis=0, keepdims=True)
        scaled = d_in * gain[...]
        inward = jnp.mean(scaled * normal, axis=-1, keepdims=True)
        dx[rows] = (d_hidden[rows] + scale * (scaled - normal * inward)).astype(BF)
    d_gain[...] = gain_sum


def close_rows(rest, d_inner, w, x_own, gain, d_hidden, micro, collective_id):
    size = lax.axis_size("seq")
    own = x_own.shape[0]
    dma = pltpu.SemaphoreType.DMA((size - 1,))
    return pl.pallas_call(
        partial(close_kernel, size, own // micro, micro),
        out_shape=[SHAPE((own, D), BF), SHAPE((1, D), F32)],
        in_specs=[VMEM] * 6,
        out_specs=[VMEM] * 2,
        scratch_shapes=[
            pltpu.VMEM((size, own, D), BF),
            pltpu.VMEM((size - 1, own, D), BF),
            dma,
            dma,
        ],
        compiler_params=pltpu.CompilerParams(
            collective_id=collective_id, has_side_effects=True, vmem_limit_bytes=VMEM_BYTES
        ),
        name="close_rows",
    )(rest, d_inner, w, x_own, gain, d_hidden)


def squares(row_vals):
    return jnp.sum(row_vals * row_vals)


def local(
    tokens,
    cotangent,
    route,
    lengths,
    gain_in,
    w_qkv,
    w_mix_in,
    w_x,
    w_dt,
    w_small,
    gain_att,
    gain_ssm,
    w_out_att,
    w_out_ssm,
    gain_ffn,
    w_gate,
    w_up,
    w_down,
):
    S, N = lax.axis_size("seq"), lax.axis_size("fsdp")
    s = lax.axis_index("seq")
    micro, tok = tokens.shape[:2]
    pack = tok * S
    rows_d = gain_in.shape[0] // N
    ff = w_gate.shape[1]
    ch_piece, ff_piece = INNER // (N * S), ff // (N * S)
    ch = -(-INNER // (S * LANES)) * LANES
    ffs = -(-ff // (S * LANES)) * LANES
    cols = D // S
    groups = HEADS // KV_HEADS
    first_heads = [(HEADS * i + S - 1) // S for i in range(S + 1)]
    head_counts = [first_heads[i + 1] - first_heads[i] for i in range(S)]
    most = max(head_counts)
    width = most * HEAD
    first_head = jnp.array(first_heads, jnp.int32)[s]
    head_live = jnp.arange(most) < jnp.array(head_counts, jnp.int32)[s]
    live = jnp.repeat(head_live, HEAD).astype(F32)[None, :]
    in_low = (first_head + jnp.arange(most)) // groups <= s

    def gather(shard):
        return lax.all_gather(shard, "fsdp", axis=0, tiled=True)

    def scatter(whole):
        rows, wide = whole.shape[0] // N, whole.shape[1]
        fill = -rows % 8
        whole = whole.astype(BF)
        if fill:
            whole = jnp.pad(whole.reshape(N, rows, wide), ((0, 0), (0, fill), (0, 0)))
            whole = whole.reshape(N * (rows + fill), wide)
        whole = lax.psum_scatter(whole, "fsdp", scatter_dimension=0, tiled=True)
        return lax.optimization_barrier(whole)[:rows]

    def part(shard, axis, chunks, wide):
        shape = shard.shape
        piece = shape[axis] // (chunks * S)
        shaped = shard.reshape(shape[:axis] + (chunks, S, piece) + shape[axis + 1 :])
        picked = lax.dynamic_index_in_dim(shaped, s, axis + 1, keepdims=False)
        fill = [(0, 0)] * picked.ndim
        fill[axis + 1] = (0, wide - piece)
        return jnp.pad(picked, fill).reshape(
            shape[:axis] + (chunks * wide,) + shape[axis + 1 :]
        )

    def span(array, axis, start, size):
        return lax.dynamic_slice_in_dim(array, start, size, axis)

    send_hot, land_hot = routing(route, tok)
    x_own = bring(tokens.reshape(micro * tok, D), send_hot, land_hot)
    q_start = first_head * HEAD
    chw, ffw = ch // N, ffs // N
    q_starts = [h * HEAD for h in first_heads[:S]]
    kv_starts = [ATT + HEAD * i for i in range(S)]
    at_k, at_v, at_q = 2 * ch, 2 * ch + 2 * HEAD, 2 * ch + 4 * HEAD
    at_att = at_q + width
    in_wide = at_att + cols
    mix_table = pieces_table(2 * N, INNER // N, ch_piece, chw)
    in_part = regroup(
        [w_mix_in, jnp.pad(w_qkv, ((0, 0), (0, -w_qkv.shape[1] % LANES))), w_out_att],
        [jax.ShapeDtypeStruct((rows_d, in_wide), BF)],
        [
            (0, None, 0, 0, placed(mix_table, 0, in_wide)),
            (1, None, 0, 0, placed(run_table(kv_starts, 2 * HEAD), at_k, in_wide)),
            (1, None, 0, 0, placed(run_table([a + KV_WIDTH for a in kv_starts], 2 * HEAD), at_v, in_wide)),
            (2, None, 0, 0, placed(run_table([cols * i for i in range(S)], cols), at_att, in_wide)),
            (1, None, 0, 0, placed(run_table(q_starts, width), at_q, in_wide)),
        ],
        s,
    )[0]
    small_part = part(
        jnp.concatenate([w_x, w_dt, w_small, jnp.zeros((w_x.shape[0], 1), BF)], axis=1), 0, 1, chw
    )
    small_wide = small_part.shape[1]
    gathered_in = gather(
        jnp.concatenate([in_part, jnp.pad(small_part, ((0, rows_d - chw), (0, 0)))], axis=1)
    )
    cot_own = bring(cotangent.reshape(micro * tok, D), send_hot, land_hot)
    x_rows = gather_rows([x_own], micro, 3)[0]
    cot_own, x_rows = lax.optimization_barrier((cot_own, x_rows))
    cot_rows = gather_rows([cot_own], micro, 6)[0]
    gathered_in, x_rows, cot_rows = lax.optimization_barrier((gathered_in, x_rows, cot_rows))
    out_piece, gathered_in = lax.optimization_barrier((part(w_out_ssm, 0, 1, chw), gathered_in))
    w_out_part = gather(out_piece)
    w_in = gathered_in[:, :at_att]
    w_att_cols = gathered_in[:, at_att:in_wide]
    w_small_part = (
        gathered_in[:, in_wide:].reshape(N, rows_d, small_wide)[:, :chw].reshape(ch, small_wide)
    )
    ff_table = pieces_table(N, ff // N, ff_piece, ffw)
    gu_part = regroup(
        [w_gate, w_up],
        [jax.ShapeDtypeStruct((rows_d, 2 * ffs), BF)],
        [
            (0, None, 0, 0, placed(ff_table, 0, 2 * ffs)),
            (1, None, 0, 0, placed(ff_table, ffs, 2 * ffs)),
        ],
        s,
    )[0]

    w_att_pad = jnp.pad(w_att_cols, ((0, width), (0, 0)))
    w_att_blocks = jnp.stack([w_att_pad[h * HEAD : h * HEAD + width] for h in first_heads[:S]])

    w_x_turned = w_small_part[:, :PROJ].T
    w_x_turned = jnp.pad(
        jnp.concatenate([w_x_turned[DT_RANK:], w_x_turned[:DT_RANK]], axis=0),
        ((0, PROJ_PAD - PROJ), (0, 0)),
    )
    w_dt_turned = jnp.pad(
        w_small_part[:, PROJ : PROJ + DT_RANK].T, ((0, PROJ_PAD - PROJ), (0, 0))
    )
    small_par = w_small_part[:, PROJ + DT_RANK : PROJ + DT_RANK + CONV + 3 + STATE].astype(F32)
    small_lines = small_par.T
    taps = jnp.pad(small_lines[:CONV], ((0, 8 - CONV), (0, 0)))
    conv_b, dt_bias, skip = [small_lines[CONV + i][None] for i in range(3)]
    rates = -jnp.exp(small_lines[CONV + 3 :])
    gain_att_part = span(jnp.pad(gain_att, (0, width)), 0, q_start, width)[None]
    gain_ssm_part = part(gain_ssm, 0, N, ch // N)[None]

    position = jax.vmap(lambda one: seq_layout(one, pack)[1])(lengths[:, 0])
    position = position.reshape(micro * pack, 1)

    normed_low = rms_scale(x_rows.astype(F32), gain_in).astype(BF)
    opened = dot(normed_low, w_in, 1, 0).astype(BF)
    opened, gu_part, down_part = lax.optimization_barrier(
        (opened, gu_part, part(w_down, 0, 1, ffw))
    )
    w_gu, w_down_part = gather(gu_part), gather(down_part)
    gate_z = opened[:, ch : 2 * ch]
    u, lin, projected, bc = ssm_open(
        opened, position, taps, conv_b, w_x_turned, w_dt_turned, dt_bias, micro, 7
    )
    q = opened[:, at_q:].reshape(micro, pack, most, HEAD)
    kv = opened[:, at_k:at_q].reshape(micro, pack, 4, HEAD)
    pick_low = in_low[None, None, :, None]
    keys = jnp.where(pick_low, kv[:, :, 0:1], kv[:, :, 1:2])
    values = jnp.where(pick_low, kv[:, :, 2:3], kv[:, :, 3:4])
    context, probs, att_sums = attention(opened, at_k, position, most, micro)
    bc = jnp.broadcast_to(bc.T[:, :, None], (micro * pack, 2 * STATE, LANES))
    core, ssm_out, ssm_sums, w_att_part = scan_forward(
        u, lin, bc, rates, position, opened, skip, w_att_blocks, micro, 11
    )
    sums = jnp.stack([att_sums[0], ssm_sums[0]])
    att_low, ssm_low, scale_att, scale_ssm, hidden, mixer_out, ffn_low = mixer_rows(
        context,
        ssm_out,
        jnp.pad(sums, ((0, 6), (0, 0))),
        x_own,
        (gain_att_part, gain_ssm_part, gain_ffn[None]),
        w_att_part,
        w_out_part,
        micro,
        4,
    )
    act_low, dgu_low, down_parts, d_hidden, d_gain_ffn, dmix_low = ffn_rows(
        ffn_low, cot_rows, hidden, cot_own, gain_ffn[None], w_gu, w_down_part, micro, 5
    )

    gu_whole = dot(ffn_low, dgu_low, 0, 0).astype(BF)
    act_low, gu_whole = lax.optimization_barrier((act_low, gu_whole))
    r_gu = scatter(gu_whole)
    down_whole = dot(act_low, cot_rows, 0, 0).astype(BF)
    dmix_low, down_whole = lax.optimization_barrier((dmix_low, down_whole))
    r_down = scatter(down_whole)
    d_context, d_core, d_gate_z, d_gain_att, d_gain_ssm, d_skip = branch_back(
        dmix_low,
        w_att_part,
        w_out_part,
        context,
        ssm_out,
        core,
        u,
        gate_z,
        (scale_att, scale_ssm),
        (gain_att_part, gain_ssm_part),
        live,
        skip,
        8,
    )
    ssm_whole = (0.5 * dot(ssm_low, dmix_low, 0, 0)).astype(BF)
    g_att_rows = (0.5 * dot(att_low, dmix_low, 0, 0)).astype(BF)
    att_blocks = g_att_rows.reshape(width, S, cols).transpose(1, 0, 2)
    dctx_low = d_context.reshape(micro, pack, most, HEAD)
    d_values = jnp.einsum(
        "mhtu,mthd->muhd", probs.astype(BF), dctx_low, preferred_element_type=F32
    )
    d_probs = jnp.einsum("mthd,muhd->mhtu", dctx_low, values, preferred_element_type=F32)
    dscore_low = (
        probs * (d_probs - jnp.sum(probs * d_probs, axis=-1, keepdims=True))
    ).astype(BF)
    d_q = jnp.einsum("mhtu,muhd->mthd", dscore_low, keys, preferred_element_type=F32) * 0.125
    d_keys = jnp.einsum("mhtu,mthd->muhd", dscore_low, q, preferred_element_type=F32) * 0.125

    def kv_sum(d_heads):
        return [
            jnp.sum(jnp.where(pick_low, d_heads, 0.0), axis=2),
            jnp.sum(jnp.where(pick_low, 0.0, d_heads), axis=2),
        ]

    d_rest = jnp.concatenate(
        [d_gate_z]
        + [
            one.astype(BF).reshape(micro * pack, -1)
            for one in kv_sum(d_keys) + kv_sum(d_values) + [d_q]
        ],
        axis=1,
    )
    rest_rows = dot(d_rest, gathered_in[:, ch:at_att], 1, 1).astype(BF)
    rest_whole = dot(normed_low, d_rest, 0, 0).astype(BF)
    d_core, r_gu, ssm_whole, rest_whole, rest_rows = lax.optimization_barrier(
        (d_core, r_gu, ssm_whole, rest_whole, rest_rows)
    )
    r_ssm, r_rest = scatter(ssm_whole), scatter(rest_whole)
    per = N // S
    gate_take = np.concatenate([np.arange(ff_piece) + ffw * i for i in range(per)])
    half_wide = -(-per * ff_piece // LANES) * LANES
    moves = []
    for d in range(S):
        for i in range(2):
            table = gate_take[None] + d * per * ffw + i * ffs
            moves.append((0, None, 0, d, placed(table, i * half_wide, 2 * half_wide)))
    (gu_blocks,) = regroup([r_gu], [SHAPE((S, rows_d, 2 * half_wide), BF)], moves, s)
    d_u, d_lin, d_dt_bias, d_rates, d_in_b, d_out_c, (ffn_got, gu_got, g_att_blocks) = (
        scan_backward(
            d_core, u, lin, bc, rates, position, skip, [down_parts, gu_blocks, att_blocks], micro, 0
        )
    )
    ffn_out = jnp.sum(ffn_got.astype(F32), axis=0)
    result = hidden + ffn_out
    outputs = give(result.astype(BF), send_hot, land_hot)
    g_att_whole = jnp.concatenate(
        [g_att_blocks[i, : head_counts[i] * HEAD] for i in range(S)], axis=0
    )
    moves = []
    for d in range(S):
        moves.append((0, None, 0, d, run_table([d * cols], cols)))
        moves.append((1, None, 1, d, run_table([d * cols], cols)))
    row_blocks = regroup(
        [r_ssm, r_down],
        [SHAPE((S, r_ssm.shape[0], cols), BF), SHAPE((S, r_down.shape[0], cols), BF)],
        moves,
        s,
    )
    dproj_low, d_inner, conv_sums = ssm_close(
        d_lin,
        d_in_b,
        d_out_c,
        d_u,
        opened,
        position,
        taps,
        conv_b,
        w_x_turned,
        w_dt_turned,
        [],
        micro,
        9,
    )
    g_x = dot(u.astype(BF), dproj_low, 0, 1)
    small_whole = jnp.concatenate(
        [
            g_x[:, 2 * STATE : PROJ],
            g_x[:, : 2 * STATE],
            dot(d_lin, projected[2 * STATE : PROJ], 0, 1),
            conv_sums[: CONV + 1].T,
            d_dt_bias[:, None],
            d_skip[0][:, None],
            (d_rates * rates).T,
            jnp.zeros((ch, 1), F32),
        ],
        axis=1,
    ).astype(BF)
    small_whole = jnp.pad(
        small_whole.reshape(N, chw, small_wide), ((0, 0), (0, rows_d - chw), (0, 0))
    ).reshape(N * rows_d, small_wide)
    last_whole = jnp.concatenate(
        [dot(normed_low, d_inner, 0, 0).astype(BF), g_att_whole, small_whole], axis=1
    )
    d_inner, last_whole, r_rest = lax.optimization_barrier((d_inner, last_whole, r_rest))
    r_last = scatter(last_whole)
    dx, d_gain_in = close_rows(
        rest_rows, d_inner, gathered_in[:, :ch], x_own, gain_in[None], d_hidden, micro, 10
    )

    att_at = lax.dynamic_update_slice_in_dim(
        jnp.zeros((ATT + width,), F32), d_gain_att[0] * live[0], q_start, 0
    )[:ATT]
    ssm_at = lax.dynamic_update_index_in_dim(
        jnp.zeros((N, S, ch_piece), F32), d_gain_ssm[0].reshape(N, -1)[:, :ch_piece], s, 1
    ).reshape(INNER)
    stats = jnp.stack(
        [
            squares(x_own.astype(F32)),
            jnp.sum(sums[0]),
            jnp.sum(sums[1]),
            squares(mixer_out),
            squares(ffn_out),
            squares(result),
        ]
    )
    ends = np.cumsum([0, D, ATT, INNER, D, 6])
    line = jnp.concatenate([d_gain_in[0], att_at, ssm_at, d_gain_ffn[0], stats])
    line = jnp.pad(line, (0, -line.shape[0] % 1024)).reshape(-1, LANES)
    row_blocks, dx = lax.optimization_barrier((list(row_blocks), dx))
    ssm_got, down_got = deal(row_blocks, 1)
    input_grads = give(dx, send_hot, land_hot)
    ssm_got, r_last = lax.optimization_barrier((ssm_got, r_last))
    out_ssm = ssm_got[:, :ch_piece].reshape(S * ch_piece, cols).astype(F32)
    out_down = down_got[:, :ff_piece].reshape(S * ff_piece, cols).astype(F32)
    ff_mine, mix_mine = ff // S, 2 * INNER // S
    moves = []
    at = np.arange(ff_mine)
    for source in range(S):
        chunk, inside = at // (S * ff_piece), at % (S * ff_piece)
        table = np.where(
            inside // ff_piece == source, chunk * ff_piece + inside % ff_piece, -1
        )[None].astype(np.int32)
        moves.append((0, source, 0, 0, table))
        moves.append((0, source, 1, 0, np.where(table >= 0, table + half_wide, -1)))
    out_gate, out_up = regroup(
        [gu_got], [jax.ShapeDtypeStruct((rows_d, ff_mine), F32)] * 2, moves, s
    )

    qkv_wide = (ATT + 2 * KV_WIDTH) // S
    mix_slot = -(-mix_mine // S // LANES) * LANES
    at = np.arange(mix_mine // S)
    moves = []
    starts = np.array(q_starts)[:, None]
    counts = np.array(head_counts)[:, None] * HEAD
    for d in range(S):
        chunk = at // ch_piece + d * (2 * N // S)
        table = chunk * chw + at % ch_piece
        wide = mix_slot + qkv_wide
        inner_part = np.where(chunk < N, table, -1)[None].astype(np.int32)
        gate_part = np.where(chunk >= N, table - ch, -1)[None].astype(np.int32)
        moves.append((0, None, 0, d, placed(inner_part, 0, wide)))
        moves.append((1, None, 0, d, placed(gate_part, 0, wide)))
        column = np.arange(qkv_wide)[None] + d * qkv_wide
        from_q = np.where(
            (column >= starts) & (column < starts + counts), column - starts + at_q - ch, -1
        )
        base = np.array(kv_starts)[:, None]
        from_k = np.where(
            (column >= base) & (column < base + 2 * HEAD), column - base + at_k - ch, -1
        )
        base = base + KV_WIDTH
        from_v = np.where(
            (column >= base) & (column < base + 2 * HEAD), column - base + at_v - ch, -1
        )
        table = np.maximum(np.maximum(from_q, from_k), from_v).astype(np.int32)
        moves.append((1, None, 0, d, placed(table, mix_slot, wide)))
    in_blocks = regroup(
        [r_last, r_rest], [jax.ShapeDtypeStruct((S, rows_d, wide), BF)], moves, s
    )[0]
    r_small = r_last[:chw, ch + cols :]
    in_got, small_got, sums_all = last_exchange(
        [in_blocks, jnp.broadcast_to(r_small, (S,) + r_small.shape)], line, 2
    )
    moves = []
    at = np.arange(mix_mine)
    for source in range(S):
        chunk, inside = at // (S * ch_piece), at % (S * ch_piece)
        table = np.where(
            inside // ch_piece == source, chunk * ch_piece + inside % ch_piece, -1
        )[None].astype(np.int32)
        moves.append((0, source, 0, 0, table))
        moves.append((0, source, 1, 0, run_table([mix_slot], qkv_wide)))
    out_mix, out_qkv = regroup(
        [in_got],
        [
            jax.ShapeDtypeStruct((rows_d, mix_mine), F32),
            jax.ShapeDtypeStruct((rows_d, qkv_wide), F32),
        ],
        moves,
        s,
    )
    g_att = r_last[:, ch : ch + cols].astype(F32)
    small_all = small_got[:, :ch_piece].reshape(S * ch_piece, small_wide).astype(F32)
    out_x = span(small_all[:, :PROJ], 1, s * (PROJ // S), PROJ // S)
    out_dt = span(small_all[:, PROJ : PROJ + DT_RANK], 1, s * (DT_RANK // S), DT_RANK // S)
    out_small = small_all[:, PROJ + DT_RANK : PROJ + DT_RANK + CONV + 3 + STATE]

    sums = sums_all.reshape(-1)
    g_gain_in, g_gain_att, g_gain_ssm, g_gain_ffn, stat_sum = [
        sums[a:b] for a, b in zip(ends[:-1], ends[1:])
    ]
    widths = jnp.array([D, ATT, INNER, D, D, D], F32)
    rms = jnp.sqrt(stat_sum / (widths * (micro * pack * N)))
    return (
        outputs.reshape(tokens.shape),
        input_grads.reshape(tokens.shape),
        g_gain_in,
        out_qkv,
        out_mix,
        out_x,
        out_dt,
        out_small,
        out_small[:, CONV + 1],
        g_gain_att,
        g_gain_ssm,
        g_att,
        out_ssm,
        g_gain_ffn,
        out_gate,
        out_up,
        out_down,
        rms,
    )


def solution(mesh):
    rows = P(None, ("seq", "fsdp"), None)
    shard = P("fsdp", None)
    both = P("fsdp", "seq")
    placed = (rows, rows, P(None, "seq"), P(None, "fsdp", None), P())
    placed += (shard,) * 5 + (P(), P(), shard, shard, P(), shard, shard, shard)
    return jax.shard_map(
        local,
        mesh=mesh,
        in_specs=placed,
        out_specs=(
            rows,
            rows,
            P(),
            both,
            both,
            both,
            both,
            shard,
            P("fsdp"),
            P(),
            P(),
            both,
            both,
            P(),
            both,
            both,
            both,
            P(),
        ),
        check_vma=False,
    )
```

```python
from functools import partial

import jax
import jax.numpy as jnp
import numpy as np
from jax import lax
from jax.experimental import pallas as pl
from jax.experimental.pallas import tpu as pltpu
from jax.sharding import PartitionSpec as P

D = 1600
HEADS = 25
KV_HEADS = 5
HEAD = 64
INNER = 3200
STATE = 16
CONV = 4
DT_RANK = 100
MICRO = 2
ATT = 1600
KV_WIDTH = 320
PROJ = DT_RANK + 2 * STATE
PROJ_PAD = 144
LANES = 128
EPS = 1e-05
BF = jnp.bfloat16
F32 = jnp.float32


def dot(left_op, right_op, left_dim, right_dim):
    return lax.dot_general(
        left_op, right_op, (((left_dim,), (right_dim,)), ((), ())), preferred_element_type=F32
    )


def rms_scale(row_vals, gain_vec):
    return (
        row_vals * lax.rsqrt(jnp.mean(row_vals * row_vals, axis=-1, keepdims=True) + EPS) * gain_vec
    )


def seq_layout(seq_lens, span_len):
    places = jnp.arange(span_len, dtype=jnp.int32)
    seq_ends = jnp.cumsum(seq_lens)
    segment = jnp.sum((places[:, None] >= seq_ends[None, :]).astype(jnp.int32), axis=1)
    starts = seq_ends - seq_lens
    picked = (segment[:, None] == jnp.arange(seq_lens.shape[0], dtype=jnp.int32)[None, :]).astype(
        jnp.int32
    )
    position = places - jnp.sum(picked * starts[None, :], axis=1)
    return (segment, position)


def swap(array, k):
    size = lax.axis_size("seq")
    return lax.ppermute(array, "seq", [(i, i ^ k) for i in range(size)])


def pick(blocks, at):
    return lax.dynamic_index_in_dim(blocks, at, 0, keepdims=False)


def seq_deal(blocks):
    size, here = lax.axis_size("seq"), lax.axis_index("seq")
    out = blocks
    for k in range(1, size):
        there = here ^ k
        out = lax.dynamic_update_index_in_dim(out, swap(pick(blocks, there), k), there, 0)
    return out


def seq_gather(block):
    size, here = lax.axis_size("seq"), lax.axis_index("seq")
    out = lax.dynamic_update_index_in_dim(
        jnp.zeros((size,) + block.shape, block.dtype), block, here, 0
    )
    for k in range(1, size):
        out = lax.dynamic_update_index_in_dim(out, swap(block, k), here ^ k, 0)
    return out


def seq_scatter(blocks):
    size, here = lax.axis_size("seq"), lax.axis_index("seq")
    total = pick(blocks, here).astype(F32)
    for k in range(1, size):
        total = total + swap(pick(blocks, here ^ k).astype(BF), k).astype(F32)
    return total


def seq_sum(array):
    return jnp.sum(seq_gather(array).astype(F32), axis=0)


def routing(route_rows, tok_rows):
    fsdp_count, fsdp_rank = lax.axis_size("fsdp"), lax.axis_index("fsdp")
    micro = route_rows.shape[0]
    per_peer = tok_rows // fsdp_count
    target_dev = (route_rows // tok_rows).reshape(micro, fsdp_count, tok_rows)
    target_slot = (route_rows % tok_rows).reshape(micro, fsdp_count, tok_rows)
    steps = jnp.arange(tok_rows, dtype=jnp.int32)
    same = target_dev[:, :, :, None] == target_dev[:, :, None, :]
    earlier = steps[None, :] < steps[:, None]
    rank = jnp.sum((same & earlier).astype(jnp.int32), axis=3)
    my_dev = lax.dynamic_index_in_dim(target_dev, fsdp_rank, 1, keepdims=False)
    my_rank = lax.dynamic_index_in_dim(rank, fsdp_rank, 1, keepdims=False)
    micros = jnp.arange(micro, dtype=jnp.int32)
    send_at = (my_dev * micro + micros[:, None]) * per_peer + my_rank
    ranks = jnp.arange(per_peer, dtype=jnp.int32)
    mine = (target_dev == fsdp_rank)[:, :, None, :] & (rank[:, :, None, :] == ranks[:, None])
    slot = jnp.sum(mine.astype(jnp.int32) * target_slot[:, :, None, :], axis=3)
    land_at = (micros[:, None, None] * tok_rows + slot).transpose(1, 0, 2).reshape(-1)
    rows = jnp.arange(micro * tok_rows, dtype=jnp.int32)
    send_hot = (rows[:, None] == send_at.reshape(-1)[None, :]).astype(BF)
    land_hot = (rows[:, None] == land_at[None, :]).astype(BF)
    return send_hot, land_hot


def exchange(rows):
    return lax.all_to_all(rows, "fsdp", split_axis=0, concat_axis=0, tiled=True)


def bring(rows, send_hot, land_hot):
    sent = dot(send_hot, rows, 1, 0).astype(BF)
    return dot(land_hot, exchange(sent), 1, 0).astype(BF)


def give(rows, send_hot, land_hot):
    sent = dot(land_hot, rows, 0, 0).astype(BF)
    return dot(send_hot, exchange(sent), 0, 0).astype(BF)


def meet(peers):
    barrier = pltpu.get_barrier_semaphore()
    for peer in peers:
        pl.semaphore_signal(barrier, inc=1, device_id=peer, device_id_type=pl.DeviceIdType.MESH)
    pl.semaphore_wait(barrier, len(peers))


def remote(source, target, send, recv, device):
    return pltpu.make_async_remote_copy(
        src_ref=source,
        dst_ref=target,
        send_sem=send,
        recv_sem=recv,
        device_id=device,
        device_id_type=pl.DeviceIdType.MESH,
    )


def pack_peers(size):
    here, row = lax.axis_index("seq"), lax.axis_index("fsdp")
    return [(lax.rem(here + k, size), row) for k in range(1, size)]


def block_rows(size, tok, m, d):
    return pl.ds(pl.multiple_of((m * size + d) * tok, tok), tok)


def flip(place, k):
    return (place // 2 + k // 2) % 2 * 2 + (place % 2 + k % 2) % 2


def crossing():
    here, row = lax.axis_index("seq"), lax.axis_index("fsdp")
    return here, (flip(here, 1), row), (flip(here, 2), row)


class Relay:
    def __init__(self, tok, own, whole, own_sem, send, recv):
        here, one, two = crossing()
        self.whole, self.tok, self.one, self.two = whole, tok, one, two
        spots = [self.spot(m, here) for m in range(2)]
        first, second = own.at[pl.ds(0, tok)], own.at[pl.ds(tok, tok)]
        self.near = [
            remote(first, spots[0], send.at[0], recv.at[0], one),
            remote(second, spots[1], send.at[1], recv.at[1], two),
            remote(second, spots[1], send.at[2], recv.at[2], one),
            remote(first, spots[0], send.at[3], recv.at[3], two),
        ]
        self.far = [
            remote(self.spot(0, one[0]), self.spot(0, one[0]), send.at[4], recv.at[4], two),
            remote(self.spot(1, two[0]), self.spot(1, two[0]), send.at[5], recv.at[5], one),
        ]
        self.kept = [
            pltpu.make_async_copy(source, spot, own_sem.at[m])
            for m, (source, spot) in enumerate(zip((first, second), spots))
        ]

    def spot(self, m, d):
        return self.whole.at[block_rows(4, self.tok, m, d)]

    def start(self):
        for copy in self.near + self.kept:
            copy.start()

    def pass_on(self):
        for near, far in zip(self.near, self.far):
            near.wait_recv()
            far.start()

    def finish(self):
        for copy in self.near[:2]:
            copy.wait_send()
        for copy in self.near[2:] + self.far + self.kept:
            copy.wait()


class Gathering:
    def __init__(self, tok, sent, got, send, recv):
        here, one, two = crossing()
        self.here, self.tok, self.sent, self.got = here, tok, sent, got
        ways = [(0, 0, one), (0, 1, two), (1, 1, two), (2, 0, one), (1, 0, two), (2, 1, one)]
        self.copies = [
            remote(sent.at[k, pl.ds(m * tok, tok)], got.at[i], send.at[i], recv.at[i], way)
            for i, (k, m, way) in enumerate(ways)
        ]

    def device(self, k):
        return flip(self.here, 3 - k)

    def send(self, k):
        for i, block in enumerate((0, 0, 1, 2)):

            @pl.when(k == block)
            def _(i=i):
                self.copies[i].start()

    def add(self, k):
        @pl.when(k == 3)
        def _():
            for i, (block, m) in enumerate(((1, 0), (2, 1))):
                self.copies[i].wait_recv()
                rows = pl.ds(m * self.tok, self.tok)
                total = self.sent[block, rows].astype(F32) + self.got[i].astype(F32)
                self.sent[block, rows] = total.astype(BF)
                self.copies[4 + i].start()

    def finish(self):
        for copy in self.copies[:2]:
            copy.wait_send()
        for copy in self.copies[2:]:
            copy.wait()

    def total(self, m, own):
        pair = (3, 4) if m == 0 else (2, 5)
        return own + self.got[pair[0]].astype(F32) + self.got[pair[1]].astype(F32)


def crossing_sems():
    return [pltpu.SemaphoreType.DMA((6,))] * 2


def start_deal(source, out, size, own_sem, send_sem, recv_sem, first=0, start=True):
    here, row = lax.axis_index("seq"), lax.axis_index("fsdp")
    copies = [pltpu.make_async_copy(source.at[here], out.at[here], own_sem)]
    for k in range(1, size):
        there = lax.rem(here + k, size)
        copies.append(
            remote(
                source.at[there],
                out.at[here],
                send_sem.at[first + k - 1],
                recv_sem.at[first + k - 1],
                (there, row),
            )
        )
    if start:
        for copy in copies:
            copy.start()
    return copies


def start_half(source, out, size, first, own_sem, send_sem, recv_sem):
    here, row = lax.axis_index("seq"), lax.axis_index("fsdp")
    half = size // 2
    own = pltpu.make_async_copy(source.at[lax.rem(here, half)], out.at[here], own_sem)
    mine = (here >= first) & (here < first + half)

    def copy_to(j):
        return remote(
            source.at[j], out.at[here], send_sem.at[j], recv_sem.at[here], (first + j, row)
        )

    pl.when(mine)(own.start)
    for j in range(half):
        pl.when(here != first + j)(lambda j=j: copy_to(j).start())

    def wait():
        pl.when(mine)(own.wait)
        for j in range(half):
            pl.when(here != first + j)(lambda j=j: copy_to(j).wait_send())

        @pl.when(mine)
        def _():
            for k in range(1, size):
                there = lax.rem(here + k, size)
                remote(
                    source.at[0], out.at[there], send_sem.at[0], recv_sem.at[there], (there, row)
                ).wait_recv()

    return wait


def half_sems(size):
    return [pltpu.SemaphoreType.DMA((n,)) for n in (1, size // 2, size)]


def deal_sems(size, count=1):
    links = pltpu.SemaphoreType.DMA((count * (size - 1),))
    return [pltpu.SemaphoreType.DMA((count,)), links, links]


VMEM_BYTES = 60 * 2**20
VMEM = pl.BlockSpec(memory_space=pltpu.VMEM)
HBM = pl.BlockSpec(memory_space=pl.ANY)
SHAPE = jax.ShapeDtypeStruct


def lane_groups(channels, most=4):
    tiles, out, first = channels // LANES, [], 0
    while first < tiles:
        count = min(most, tiles - first)
        out.append((first, count))
        first += count
    return out


def sigmoid(v):
    return 1.0 / (1.0 + jnp.exp(-v))


def softplus(v):
    return jnp.maximum(v, 0.0) + jnp.log1p(jnp.exp(-jnp.abs(v)))


def steps_of(lin_ref, u_ref, position_ref, dtm, dtu):
    step = softplus(lin_ref[...])
    dtu[...] = step * u_ref[...]
    dtm[...] = jnp.where(position_ref[...] > 0, step, 1e30)


def both_of(ref, t):
    row = ref[t].astype(F32)
    return row[:STATE], row[STATE:]


def scan_kernel(size, groups, *refs):
    u_ref, lin_ref, bc_ref, a_ref, position_ref, gate_ref, skip_ref, held = refs[:8]
    core, out, sums, got, dtm, dtu, own_sem, held_send, held_recv = refs[8:]
    steps = u_ref.shape[0]

    def copies(start):
        return start_deal(held, got, size, own_sem.at[0], held_send, held_recv, start=start)

    @pl.when(pl.program_id(0) == 0)
    def _():
        meet(pack_peers(size))
        copies(True)

    steps_of(lin_ref, u_ref, position_ref, dtm, dtu)
    place = lax.broadcasted_iota(jnp.int32, (8, LANES), 0)
    for first, count in groups:
        spans = [pl.ds((first + i) * LANES, LANES) for i in range(count)]
        rates = [a_ref[:, span] for span in spans]

        def block(k, held):
            held = list(held)
            rows = pl.ds(pl.multiple_of(k * 8, 8), 8)
            dts = [dtm[rows, span] for span in spans]
            dus = [dtu[rows, span] for span in spans]
            ys = [jnp.zeros((8, LANES), F32)] * count
            for j in range(8):
                b_now, c_now = both_of(bc_ref, k * 8 + j)
                for i in range(count):
                    decay = jnp.exp(dts[i][j : j + 1] * rates[i])
                    held[i] = decay * held[i] + dus[i][j : j + 1] * b_now
                    y = jnp.sum(held[i] * c_now, axis=0, keepdims=True)
                    ys[i] = jnp.where(place == j, y, ys[i])
            for i, span in enumerate(spans):
                core[rows, span] = ys[i]
            return tuple(held)

        zero = jnp.zeros((STATE, LANES), F32)
        lax.fori_loop(0, steps // 8, block, (zero,) * count)
    gate = gate_ref[...].astype(F32)
    result = (core[...] + skip_ref[...] * u_ref[...]) * (gate * sigmoid(gate))
    out[...] = result
    sums[...] = row_sums(result * result)

    @pl.when(pl.program_id(0) == pl.num_programs(0) - 1)
    def _():
        for copy in copies(False):
            copy.wait()


def row_sums(values):
    return lax.dot_general(
        jnp.ones((8, values.shape[1]), F32),
        values,
        (((1,), (1,)), ((), ())),
        precision=lax.Precision.HIGHEST,
        preferred_element_type=F32,
    )


def scan_forward(u, lin, bc, rates, position, opened, skip, held, micro, collective_id):
    size = lax.axis_size("seq")
    rows, channels = u.shape
    steps = rows // micro
    block = pl.BlockSpec((steps, channels), lambda m: (m, 0))
    lane = pl.BlockSpec((8, steps), lambda m: (0, m))
    return pl.pallas_call(
        partial(scan_kernel, size, lane_groups(channels)),
        grid=(micro,),
        out_shape=[SHAPE((rows, channels), F32)] * 2
        + [SHAPE((8, rows), F32), SHAPE(held.shape, held.dtype)],
        in_specs=[
            block,
            block,
            pl.BlockSpec((steps, 2 * STATE, LANES), lambda m: (m, 0, 0)),
            pl.BlockSpec(rates.shape, lambda m: (0, 0)),
            pl.BlockSpec((steps, 1), lambda m: (m, 0)),
            pl.BlockSpec((steps, channels), lambda m: (m, 1)),
            pl.BlockSpec((1, channels), lambda m: (0, 0)),
            HBM,
        ],
        out_specs=[block, block, lane, HBM],
        scratch_shapes=[pltpu.VMEM((steps, channels), F32)] * 2 + deal_sems(size),
        compiler_params=pltpu.CompilerParams(
            collective_id=collective_id, has_side_effects=True, vmem_limit_bytes=VMEM_BYTES
        ),
        name="scan_forward",
    )(u, lin, bc, rates, position, opened, skip, held)


def scan_back_kernel(size, count, groups, *refs):
    dcore_ref, u_ref, lin_ref, bc_ref, a_ref, position_ref, skip_ref = refs[:7]
    helds, refs = refs[7 : 7 + count], refs[7 + count :]
    du_ref, dlin_ref, bias_ref, da_ref, db_ref, dc_ref = refs[:6]
    gots, refs = refs[6 : 6 + count], refs[6 + count :]
    dtm, dtu, ddtu, ddt, hs, acc_b, acc_c, own_sem, held_send, held_recv = refs
    steps = u_ref.shape[0]

    def copies():
        out = []
        for i, (held, got) in enumerate(zip(helds, gots)):
            out += start_deal(
                held, got, size, own_sem.at[i], held_send, held_recv, i * (size - 1), start=False
            )
        return out

    @pl.when(pl.program_id(0) == 0)
    def _():
        meet(pack_peers(size))
        for copy in copies():
            copy.start()

    steps_of(lin_ref, u_ref, position_ref, dtm, dtu)
    place = lax.broadcasted_iota(jnp.int32, (8, LANES), 0)
    zero = jnp.zeros((STATE, LANES), F32)
    for at, (first, count) in enumerate(groups):
        spans = [pl.ds((first + i) * LANES, LANES) for i in range(count)]
        slots = [pl.ds(i * LANES, LANES) for i in range(count)]
        rates = [a_ref[:, span] for span in spans]
        for slot in slots:
            hs[0, :, slot] = zero

        def block(k, held):
            held = list(held)
            base = pl.multiple_of(k * 8, 8)
            rows = pl.ds(base, 8)
            dts = [dtm[rows, span] for span in spans]
            dus = [dtu[rows, span] for span in spans]
            for j in range(8):
                b_now, _ = both_of(bc_ref, base + j)
                for i in range(count):
                    decay = jnp.exp(dts[i][j : j + 1] * rates[i])
                    held[i] = decay * held[i] + dus[i][j : j + 1] * b_now
                    hs[base + j + 1, :, slots[i]] = held[i]
            return tuple(held)

        lax.fori_loop(0, steps // 8, block, (zero,) * count)

        def back(k, carry):
            carry = list(carry)
            block_at = steps // 8 - 1 - k
            base = pl.multiple_of(block_at * 8, 8)
            rows = pl.ds(base, 8)
            dts = [dtm[rows, span] for span in spans]
            dus = [dtu[rows, span] for span in spans]
            dys = [dcore_ref[rows, span] for span in spans]
            out_u = [jnp.zeros((8, LANES), F32)] * count
            out_t = [jnp.zeros((8, LANES), F32)] * count
            for j in reversed(range(8)):
                t = base + j
                b_now, c_now = both_of(bc_ref, t)
                sum_b = sum_c = zero
                for i in range(count):
                    later, rate_sum = carry[i]
                    dt, du, dy = dts[i][j : j + 1], dus[i][j : j + 1], dys[i][j : j + 1]
                    g = later + dy * c_now
                    sum_c = sum_c + hs[t + 1, :, slots[i]] * dy
                    sum_b = sum_b + g * du
                    through = g * jnp.exp(dt * rates[i])
                    moved = through * hs[t, :, slots[i]]
                    to_u = jnp.sum(g * b_now, axis=0, keepdims=True)
                    to_t = jnp.sum(moved * rates[i], axis=0, keepdims=True)
                    out_u[i] = jnp.where(place == j, to_u, out_u[i])
                    out_t[i] = jnp.where(place == j, to_t, out_t[i])
                    carry[i] = (through, rate_sum + moved * dt)
                if at == 0:
                    acc_b[t] = sum_b
                    acc_c[t] = sum_c
                else:
                    acc_b[t] = acc_b[t] + sum_b
                    acc_c[t] = acc_c[t] + sum_c
            for i, span in enumerate(spans):
                ddtu[rows, span] = out_u[i]
                ddt[rows, span] = out_t[i]
            return tuple(carry)

        ends = lax.fori_loop(0, steps // 8, back, ((zero, zero),) * count)
        for i, span in enumerate(spans):
            da_ref[:, span] = ends[i][1]
    for acc, out in ((acc_b, db_ref), (acc_c, dc_ref)):
        out[...] = row_sums(acc[...].reshape(steps * STATE, LANES))
    lin = lin_ref[...]
    to_step = ddtu[...]
    du_ref[...] = dcore_ref[...] * skip_ref[...] + to_step * softplus(lin)
    d_lin = (ddt[...] + to_step * u_ref[...]) * sigmoid(lin)
    dlin_ref[...] = d_lin.astype(BF)
    bias_ref[...] = jnp.sum(d_lin, axis=0, keepdims=True)

    @pl.when(pl.program_id(0) == pl.num_programs(0) - 1)
    def _():
        for copy in copies():
            copy.wait()


def scan_backward(dcore, u, lin, bc, rates, position, skip, helds, micro, collective_id):
    size = lax.axis_size("seq")
    rows, channels = u.shape
    steps = rows // micro
    groups = lane_groups(channels)
    block = pl.BlockSpec((steps, channels), lambda m: (m, 0))
    rate = pl.BlockSpec(rates.shape, lambda m: (0, 0))
    line = pl.BlockSpec((1, channels), lambda m: (0, 0))
    flat = pl.BlockSpec((None, 8, steps * STATE), lambda m: (m, 0, 0))
    wide = pltpu.VMEM((steps, channels), F32)
    du, dlin, bias, da, db, dc, *gots = pl.pallas_call(
        partial(scan_back_kernel, size, len(helds), groups),
        grid=(micro,),
        out_shape=[
            SHAPE((rows, channels), F32),
            SHAPE((rows, channels), BF),
            SHAPE((micro, 1, channels), F32),
            SHAPE((micro, STATE, channels), F32),
            SHAPE((micro, 8, steps * STATE), F32),
            SHAPE((micro, 8, steps * STATE), F32),
        ]
        + [SHAPE(held.shape, held.dtype) for held in helds],
        in_specs=[
            block,
            block,
            block,
            pl.BlockSpec((steps, 2 * STATE, LANES), lambda m: (m, 0, 0)),
            rate,
            pl.BlockSpec((steps, 1), lambda m: (m, 0)),
            line,
        ]
        + [HBM] * len(helds),
        out_specs=[
            block,
            block,
            pl.BlockSpec((None, 1, channels), lambda m: (m, 0, 0)),
            pl.BlockSpec((None, STATE, channels), lambda m: (m, 0, 0)),
            flat,
            flat,
        ]
        + [HBM] * len(helds),
        scratch_shapes=[wide] * 4
        + [
            pltpu.VMEM((steps + 1, STATE, groups[0][1] * LANES), F32),
            pltpu.VMEM((steps, STATE, LANES), F32),
            pltpu.VMEM((steps, STATE, LANES), F32),
        ]
        + deal_sems(size, len(helds)),
        compiler_params=pltpu.CompilerParams(
            collective_id=collective_id, has_side_effects=True, vmem_limit_bytes=VMEM_BYTES
        ),
        name="scan_backward",
    )(dcore, u, lin, bc, rates, position, skip, *helds)
    return (
        du,
        dlin,
        jnp.sum(bias[:, 0], axis=0),
        jnp.sum(da, axis=0),
        db[:, 0].reshape(rows, STATE),
        dc[:, 0].reshape(rows, STATE),
        gots,
    )


def regroup_kernel(plan, source_count, out_count, *refs):
    here = lax.axis_index("seq")
    sources = refs[:source_count]
    maps = refs[source_count : len(refs) - out_count]
    outs = refs[len(refs) - out_count :]
    for out, block, tile, wide, terms in plan:
        at = pl.ds(tile * LANES, wide)
        total = None
        for source, which, low, high in terms:
            held = sources[source]
            held = held[..., low:high] if len(held.shape) == 2 else held[which[1], :, low:high]
            table = maps[which[0]]
            wanted = table[0:1, at]
            for i in range(1, table.shape[0]):
                wanted = jnp.where(here == i, table[i : i + 1, at], wanted)
            wanted = wanted - low
            places = lax.broadcasted_iota(jnp.int32, (high - low, wide), 0)
            hot = (places == wanted).astype(F32).astype(BF)
            term = dot(held, hot, 1, 0)
            total = term if total is None else total + term
        ref = outs[out]
        if total is None:
            total = jnp.zeros((ref.shape[-2], wide), F32)
        if len(ref.shape) == 2:
            ref[:, at] = total.astype(ref.dtype)
        else:
            ref[block, :, at] = total.astype(ref.dtype)


def regroup(sources, outs, moves):
    plan, maps = [], []
    tables = []
    for source, from_block, out, block, table in moves:
        maps.append(jnp.asarray(table))
        tables.append((source, from_block, out, block, table))
    for out, shape in enumerate(outs):
        for block in range(shape.shape[0] if len(shape.shape) == 3 else 1):
            for tile in range(-(-shape.shape[-1] // LANES)):
                wide = min(LANES, shape.shape[-1] - tile * LANES)
                terms = []
                for which, (source, from_block, to, to_block, table) in enumerate(tables):
                    used = table[:, tile * LANES : tile * LANES + wide]
                    if (to, to_block) != (out, block) or not (used >= 0).any():
                        continue
                    low = int(used[used >= 0].min()) // LANES * LANES
                    high = min(-(-(int(used.max()) + 1) // LANES) * LANES, sources[source].shape[-1])
                    terms.append((source, (which, from_block), low, high))
                plan.append((out, block, tile, wide, tuple(terms)))
    vmem = pl.BlockSpec(memory_space=pltpu.VMEM)
    return pl.pallas_call(
        partial(regroup_kernel, plan, len(sources), len(outs)),
        out_shape=list(outs),
        in_specs=[vmem] * (len(sources) + len(maps)),
        out_specs=[vmem] * len(outs),
        compiler_params=pltpu.CompilerParams(vmem_limit_bytes=VMEM_BYTES),
        name="regroup",
    )(*sources, *maps)


def pieces_table(chunks, size, piece, wide, start=0):
    at = np.arange(chunks * wide)
    chunk, place = at // wide, at % wide
    count = size // piece
    table = start + chunk * size + place + piece * np.arange(count)[:, None]
    return np.where(place < piece, table, -1).astype(np.int32)


def run_table(starts, count):
    return (np.asarray(starts)[:, None] + np.arange(count)).astype(np.int32)


def placed(table, at, width):
    out = np.full((table.shape[0], width), -1, np.int32)
    out[:, at : at + table.shape[1]] = table
    return out


def deal_kernel(count, size, first, *refs):
    sources, half_source = refs[:count], refs[count]
    outs, half_out = refs[count + 1 : 2 * count + 1], refs[2 * count + 1]
    own_sem, send_sem, recv_sem, half_own, half_send, half_recv = refs[2 * count + 2 :]
    meet(pack_peers(size))
    wait = start_half(half_source, half_out, size, first, half_own.at[0], half_send, half_recv)
    copies = []
    for i, (source, out) in enumerate(zip(sources, outs)):
        copies += start_deal(
            source, out, size, own_sem.at[i], send_sem, recv_sem, i * (size - 1)
        )
    for copy in copies:
        copy.wait()
    wait()


def deal(arrays, halves, first, collective_id):
    size, count = lax.axis_size("seq"), len(arrays)
    return pl.pallas_call(
        partial(deal_kernel, count, size, first),
        out_shape=[SHAPE(a.shape, a.dtype) for a in arrays]
        + [SHAPE((size,) + halves.shape[1:], halves.dtype)],
        in_specs=[HBM] * (count + 1),
        out_specs=[HBM] * (count + 1),
        scratch_shapes=deal_sems(size, count) + half_sems(size),
        compiler_params=pltpu.CompilerParams(collective_id=collective_id, has_side_effects=True),
        cost_estimate=pl.CostEstimate(flops=0, bytes_accessed=1024, transcendentals=0),
        name="deal",
    )(*arrays, halves)


def spread(slots, me, devices, send, recv):
    copies = []
    for k, device in enumerate(devices):
        copies.append(remote(slots.at[me], slots.at[me], send.at[k], recv.at[k], device))
        copies[-1].start()
    for copy in copies:
        copy.wait()
    total = slots[0]
    for i in range(1, slots.shape[0]):
        total = total + slots[i]
    return total


def last_kernel(sizes, count, *refs):
    sources, half_source, in_ref = refs[:count], refs[count], refs[count + 1]
    outs, half_out, out_ref = refs[count + 2 : 2 * count + 2], *refs[2 * count + 2 : 2 * count + 4]
    refs = refs[2 * count + 4 :]
    one, two, send_one, recv_one, send_two, recv_two, own_sem, send_sem, recv_sem = refs[:9]
    half_own, half_send, half_recv = refs[9:]
    seq, fsdp = lax.axis_index("seq"), lax.axis_index("fsdp")
    across = [(lax.rem(seq + k, sizes[0]), fsdp) for k in range(1, sizes[0])]
    along = [(seq, lax.rem(fsdp + k, sizes[1])) for k in range(1, sizes[1])]
    meet(across + along)
    one[seq] = in_ref[...]
    two[fsdp] = spread(one, seq, across, send_one, recv_one)
    wait = start_half(half_source, half_out, sizes[0], 0, half_own.at[0], half_send, half_recv)
    copies = []
    for i, (source, out) in enumerate(zip(sources, outs)):
        copies += start_deal(
            source, out, sizes[0], own_sem.at[i], send_sem, recv_sem, i * (sizes[0] - 1)
        )
    out_ref[...] = spread(two, fsdp, along, send_two, recv_two)
    for copy in copies:
        copy.wait()
    wait()


def last_exchange(arrays, halves, block, collective_id):
    sizes, count = (lax.axis_size("seq"), lax.axis_size("fsdp")), len(arrays)
    return pl.pallas_call(
        partial(last_kernel, sizes, count),
        out_shape=[SHAPE(a.shape, a.dtype) for a in arrays]
        + [SHAPE((sizes[0],) + halves.shape[1:], halves.dtype), SHAPE(block.shape, block.dtype)],
        in_specs=[HBM] * (count + 1) + [VMEM],
        out_specs=[HBM] * (count + 1) + [VMEM],
        scratch_shapes=[pltpu.VMEM((n,) + block.shape, F32) for n in sizes]
        + [pltpu.SemaphoreType.DMA((n - 1,)) for n in sizes for _ in range(2)]
        + deal_sems(sizes[0], count)
        + half_sems(sizes[0]),
        compiler_params=pltpu.CompilerParams(collective_id=collective_id, has_side_effects=True),
        cost_estimate=pl.CostEstimate(flops=0, bytes_accessed=1024, transcendentals=0),
        name="last_exchange",
    )(*arrays, halves, block)


def gather_kernel(size, tok, own, whole, own_sem, send, recv):
    meet(pack_peers(size))
    relay = Relay(tok, own, whole, own_sem, send, recv)
    relay.start()
    relay.pass_on()
    relay.finish()


def gather_rows(own, micro, collective_id):
    size, rows = lax.axis_size("seq"), own.shape[0]
    return pl.pallas_call(
        partial(gather_kernel, size, rows // micro),
        out_shape=SHAPE((rows * size, own.shape[1]), own.dtype),
        in_specs=[HBM],
        out_specs=HBM,
        scratch_shapes=[pltpu.SemaphoreType.DMA((micro,))] + crossing_sems(),
        compiler_params=pltpu.CompilerParams(collective_id=collective_id, has_side_effects=True),
        name="gather_rows",
    )(own)


def spans_of(width, most=512):
    return [(low, min(low + most, width)) for low in range(0, width, most)]


def joined(blocks, out):
    wide = blocks.shape[2]
    for i in range(blocks.shape[0]):
        out[:, i * wide : (i + 1) * wide] = blocks[i]
    return out


def mixer_kernel(size, tok, micro, *refs):
    context, ssm_out, sums_ref, x_ref, gain_att, gain_ssm, gain_ffn, w_att, w_ssm = refs[:9]
    att, ssm, scale_att, scale_ssm, hidden, mixer, ffn = refs[9:16]
    sums, sent, got, ffn_own, sums_send, sums_recv, send, recv, own_sem, ffn_send, ffn_recv = refs[
        16:-1
    ]
    w_att = joined(w_att, refs[-1])
    here, row = lax.axis_index("seq"), lax.axis_index("fsdp")
    peers = pack_peers(size)
    meet(peers)
    sums[here] = sums_ref[...]
    copies = [
        remote(sums.at[here], sums.at[here], sums_send.at[k], sums_recv.at[k], peer)
        for k, peer in enumerate(peers)
    ]
    for copy in copies:
        copy.start()
    for copy in copies:
        copy.wait()
    total = sums[0]
    for i in range(1, size):
        total = total + sums[i]
    place = lax.broadcasted_iota(jnp.int32, (8, LANES), 0)
    for kind, scale, width in ((0, scale_att, ATT), (1, scale_ssm, INNER)):
        column = lax.dot_general(
            total,
            (place == kind).astype(F32),
            (((0,), (0,)), ((), ())),
            precision=lax.Precision.HIGHEST,
            preferred_element_type=F32,
        )
        scale[...] = lax.rsqrt(column / width + EPS)
    att[...] = (context[...] * scale_att[:, :1] * gain_att[...]).astype(BF)
    ssm[...] = (ssm_out[...] * scale_ssm[:, :1] * gain_ssm[...]).astype(BF)

    def product(d, low, high):
        left = [jnp.concatenate([ref[block_rows(size, tok, m, d)] for m in range(micro)]) for ref in (att, ssm)]
        return 0.5 * (
            dot(left[0], w_att[:, low:high], 1, 0) + dot(left[1], w_ssm[:, low:high], 1, 0)
        )

    gathering = Gathering(tok, sent, got, send, recv)
    for k in range(3):
        for low, high in spans_of(D):
            sent[k, :, low:high] = product(gathering.device(k), low, high).astype(BF)
        gathering.send(k)
    gathering.add(3)
    for low, high in spans_of(D):
        mixer[:, low:high] = product(here, low, high)
    gathering.finish()
    for m in range(micro):
        rows = pl.ds(m * tok, tok)
        out = gathering.total(m, mixer[rows])
        mixer[rows] = out
        whole = x_ref[rows].astype(F32) + out
        hidden[rows] = whole
        scale = lax.rsqrt(jnp.mean(whole * whole, axis=-1, keepdims=True) + EPS)
        ffn_own[rows] = (whole * scale * gain_ffn[...]).astype(BF)
    relay = Relay(tok, ffn_own, ffn, own_sem, ffn_send, ffn_recv)
    relay.start()
    relay.pass_on()
    relay.finish()


def mixer_rows(context, ssm_out, sums, x_own, gains, w_att, w_ssm, micro, collective_id):
    size = lax.axis_size("seq")
    own = x_own.shape[0]
    rows, tok = own * size, own // micro
    vmem, hbm = pl.BlockSpec(memory_space=pltpu.VMEM), pl.BlockSpec(memory_space=pl.ANY)
    shape = jax.ShapeDtypeStruct
    dma = pltpu.SemaphoreType.DMA
    return pl.pallas_call(
        partial(mixer_kernel, size, tok, micro),
        out_shape=[
            shape((rows, w_att.shape[1]), BF),
            shape((rows, w_ssm.shape[0]), BF),
            shape((rows, LANES), F32),
            shape((rows, LANES), F32),
            shape((own, D), F32),
            shape((own, D), F32),
            shape((rows, D), BF),
        ],
        in_specs=[vmem] * 9,
        out_specs=[vmem] * 6 + [hbm],
        scratch_shapes=[
            pltpu.VMEM((size,) + sums.shape, F32),
            pltpu.VMEM((size - 1, own, D), BF),
            pltpu.VMEM((6, tok, D), BF),
            pltpu.VMEM((own, D), BF),
            dma((size - 1,)),
            dma((size - 1,)),
            *crossing_sems(),
            dma((micro,)),
            *crossing_sems(),
            pltpu.VMEM((w_att.shape[1], D), BF),
        ],
        compiler_params=pltpu.CompilerParams(
            collective_id=collective_id, has_side_effects=True, vmem_limit_bytes=VMEM_BYTES
        ),
        name="mixer_rows",
    )(context, ssm_out, sums, x_own, *gains, w_att, w_ssm)


def ffn_kernel(size, tok, micro, *refs):
    ffn, cot, hidden, cot_own, gain, w_gu, w_down = refs[:7]
    act, dgu, down, d_hidden, d_gain, dmix = refs[7:13]
    sent, got, dmix_own, send, recv, own_sem, dmix_send, dmix_recv = refs[13:]
    here, row = lax.axis_index("seq"), lax.axis_index("fsdp")
    wide = w_down.shape[0]
    meet(pack_peers(size))

    gathering = Gathering(tok, sent, got, send, recv)

    def block(k, carry):
        d = gathering.device(k)
        spots = [block_rows(size, tok, m, d) for m in range(micro)]
        gathering.add(k)
        rows_in = jnp.concatenate([ffn[spot] for spot in spots])
        cots = jnp.concatenate([cot[spot] for spot in spots])
        for low, high in spans_of(wide):
            gate = dot(rows_in, w_gu[:, low:high], 1, 0)
            up = dot(rows_in, w_gu[:, wide + low : wide + high], 1, 0)
            d_act = dot(cots, w_down[low:high, :], 1, 1)
            sig = 1.0 / (1.0 + jnp.exp(-gate))
            silu = gate * sig
            pieces = (
                (act, low, silu * up),
                (dgu, low, d_act * up * (sig * (1.0 + gate - silu))),
                (dgu, wide + low, d_act * silu),
            )
            for ref, at, values in pieces:
                values = values.astype(BF)
                for m, spot in enumerate(spots):
                    ref[spot, at : at + high - low] = values[m * tok : (m + 1) * tok]
        d_all = jnp.concatenate([dgu[spot] for spot in spots])
        for low, high in spans_of(D):
            sent[k, :, low:high] = dot(d_all, w_gu[low:high, :], 1, 1).astype(BF)
        gathering.send(k)
        acts = jnp.concatenate([act[spot] for spot in spots])
        for low, high in spans_of(D):
            down[d, :, low:high] = dot(acts, w_down[:, low:high], 1, 0).astype(BF)
        return carry

    lax.fori_loop(0, size, block, 0)
    gathering.finish()
    gain_sum = jnp.zeros((1, D), F32)
    for m in range(micro):
        rows = pl.ds(m * tok, tok)
        d_in = gathering.total(m, sent[size - 1, rows].astype(F32))
        whole = hidden[rows]
        scale = lax.rsqrt(jnp.mean(whole * whole, axis=-1, keepdims=True) + EPS)
        normal = whole * scale
        gain_sum = gain_sum + jnp.sum(d_in * normal, axis=0, keepdims=True)
        scaled = d_in * gain[...]
        inward = jnp.mean(scaled * normal, axis=-1, keepdims=True)
        out = cot_own[rows].astype(F32) + scale * (scaled - normal * inward)
        d_hidden[rows] = out
        dmix_own[rows] = out.astype(BF)
    d_gain[...] = gain_sum
    relay = Relay(tok, dmix_own, dmix, own_sem, dmix_send, dmix_recv)
    relay.start()
    relay.pass_on()
    relay.finish()


def ffn_rows(ffn, cot, hidden, cot_own, gain, w_gu, w_down, micro, collective_id):
    size = lax.axis_size("seq")
    own, rows = hidden.shape[0], ffn.shape[0]
    wide = w_down.shape[0]
    tok = own // micro
    vmem, hbm = pl.BlockSpec(memory_space=pltpu.VMEM), pl.BlockSpec(memory_space=pl.ANY)
    shape = jax.ShapeDtypeStruct
    dma = pltpu.SemaphoreType.DMA
    return pl.pallas_call(
        partial(ffn_kernel, size, tok, micro),
        out_shape=[
            shape((rows, wide), BF),
            shape((rows, 2 * wide), BF),
            shape((size, own, D), BF),
            shape((own, D), F32),
            shape((1, D), F32),
            shape((rows, D), BF),
        ],
        in_specs=[vmem] * 7,
        out_specs=[vmem] * 5 + [hbm],
        scratch_shapes=[
            pltpu.VMEM((size, own, D), BF),
            pltpu.VMEM((6, tok, D), BF),
            pltpu.VMEM((own, D), BF),
            *crossing_sems(),
            dma((micro,)),
            *crossing_sems(),
        ],
        compiler_params=pltpu.CompilerParams(
            collective_id=collective_id, has_side_effects=True, vmem_limit_bytes=VMEM_BYTES
        ),
        name="ffn_rows",
    )(ffn, cot, hidden, cot_own, gain, w_gu, w_down)


def attention_kernel(most, at_k, opened_ref, position_ref, context, probs, sums):
    s, size = lax.axis_index("seq"), lax.axis_size("seq")
    first = (HEADS * s + size - 1) // size
    last = (HEADS * (s + 1) + size - 1) // size
    pack = position_ref.shape[0]
    at = 4 * HEAD
    in_ref = opened_ref.at[:, at_k : at_k + (4 + most) * HEAD]
    rows = lax.broadcasted_iota(jnp.int32, (pack, pack), 0)
    columns = lax.broadcasted_iota(jnp.int32, (pack, pack), 1)
    visible = (columns <= rows) & (columns >= rows - position_ref[...])
    for h in range(most):
        low = (first + h) // (HEADS // KV_HEADS) <= s
        q = in_ref[:, at + h * HEAD : at + (h + 1) * HEAD]
        key = jnp.where(low, in_ref[:, :HEAD], in_ref[:, HEAD : 2 * HEAD])
        value = jnp.where(low, in_ref[:, 2 * HEAD : 3 * HEAD], in_ref[:, 3 * HEAD : 4 * HEAD])
        masked = jnp.where(visible, dot(q, key, 1, 1) * 0.125, -1e30)
        terms = jnp.exp(masked - jnp.max(masked, axis=1, keepdims=True))
        prob = terms / jnp.sum(terms, axis=1, keepdims=True)
        probs[h] = prob
        out = dot(prob.astype(BF), value, 1, 0)
        context[:, h * HEAD : (h + 1) * HEAD] = jnp.where(first + h < last, out, 0.0)
    held = context[...]
    sums[...] = row_sums(held * held)


def attention(opened, at_k, position, most, micro):
    rows, wide = opened.shape
    pack = rows // micro
    return pl.pallas_call(
        partial(attention_kernel, most, at_k),
        grid=(micro,),
        out_shape=[
            SHAPE((rows, most * HEAD), F32),
            SHAPE((micro, most, pack, pack), F32),
            SHAPE((8, rows), F32),
        ],
        in_specs=[
            pl.BlockSpec((pack, wide), lambda m: (m, 0)),
            pl.BlockSpec((pack, 1), lambda m: (m, 0)),
        ],
        out_specs=[
            pl.BlockSpec((pack, most * HEAD), lambda m: (m, 0)),
            pl.BlockSpec((None, most, pack, pack), lambda m: (m, 0, 0, 0)),
            pl.BlockSpec((8, pack), lambda m: (0, m)),
        ],
        compiler_params=pltpu.CompilerParams(vmem_limit_bytes=VMEM_BYTES),
        name="attention",
    )(opened, position)


def sum_slots(slots, send, recv):
    here, row = lax.axis_index("seq"), lax.axis_index("fsdp")
    copies = [
        remote(slots.at[here], slots.at[here], send.at[k], recv.at[k], peer)
        for k, peer in enumerate(pack_peers(slots.shape[0]))
    ]
    for copy in copies:
        copy.start()
    for copy in copies:
        copy.wait()
    total = slots[0].astype(F32)
    for i in range(1, slots.shape[0]):
        total = total + slots[i].astype(F32)
    return total


def taps_of(inner, position, taps, bias):
    shifted = [inner]
    for k in range(1, CONV):
        shifted.append(jnp.where(position >= k, pltpu.roll(inner, k, axis=0), 0.0))
    conv = bias
    for k in range(CONV):
        conv = conv + taps[k : k + 1] * shifted[k]
    return conv, shifted


def ssm_open_kernel(
    size, micro, opened_ref, position_ref, taps, bias, w_x, w_dt, dt_bias, u_ref, lin_ref, proj_ref, bc_ref, slots, send, recv
):
    meet(pack_peers(size))
    steps = opened_ref.shape[0] // micro
    for m in range(micro):
        rows = pl.ds(m * steps, steps)
        for low, high in spans_of(w_x.shape[1], LANES):
            inner = opened_ref[rows, low:high].astype(F32)
            conv, _ = taps_of(inner, position_ref[rows], taps[:, low:high], bias[:, low:high])
            u_ref[rows, low:high] = conv * sigmoid(conv)
    slots[lax.axis_index("seq")] = dot(w_x[...], u_ref[...].astype(BF), 1, 1).astype(BF)
    proj = sum_slots(slots, send, recv).astype(BF)
    proj_ref[...] = proj
    bc_ref[...] = proj[: 2 * STATE]
    lin_ref[...] = dot(proj[2 * STATE :], w_dt[...], 0, 0) + dt_bias[...]


def ssm_open(opened, position, taps, bias, w_x, w_dt, dt_bias, micro, collective_id):
    size = lax.axis_size("seq")
    rows = opened.shape[0]
    wide, channels = w_x.shape
    dma = pltpu.SemaphoreType.DMA((size - 1,))
    return pl.pallas_call(
        partial(ssm_open_kernel, size, micro),
        out_shape=[
            SHAPE((rows, channels), F32),
            SHAPE((rows, channels), F32),
            SHAPE((wide, rows), BF),
            SHAPE((2 * STATE, rows), BF),
        ],
        in_specs=[VMEM] * 7,
        out_specs=[VMEM] * 4,
        scratch_shapes=[pltpu.VMEM((size, wide, rows), BF), dma, dma],
        compiler_params=pltpu.CompilerParams(
            collective_id=collective_id, has_side_effects=True, vmem_limit_bytes=VMEM_BYTES
        ),
        name="ssm_open",
    )(opened, position, taps, bias, w_x, w_dt, dt_bias)


def ssm_close_kernel(
    size, micro, count, *refs
):
    dlin_ref, db_ref, dc_ref, du_ref, opened_ref, position_ref, taps, bias, w_x, w_dt = refs[:10]
    helds, (dproj_ref, dinner_ref, sums_ref) = refs[10 : 10 + count], refs[10 + count : 13 + count]
    gots = refs[13 + count : 13 + 2 * count]
    slots, total, send, recv, own_sem, held_send, held_recv = refs[13 + 2 * count :]
    meet(pack_peers(size))
    here = lax.axis_index("seq")
    place = lax.broadcasted_iota(jnp.int32, (STATE, STATE), 0)
    eye = (place == lax.broadcasted_iota(jnp.int32, (STATE, STATE), 1)).astype(F32)
    for i, ref in enumerate((db_ref, dc_ref)):
        turned = lax.dot_general(
            eye,
            ref[...],
            (((1,), (1,)), ((), ())),
            precision=lax.Precision.HIGHEST,
            preferred_element_type=F32,
        )
        slots[here, i * STATE : (i + 1) * STATE] = turned.astype(BF)
    slots[here, 2 * STATE :] = dot(w_dt[...], dlin_ref[...], 1, 1).astype(BF)
    dproj = sum_slots(slots, send, recv).astype(BF)
    copies = []
    for i, (held, got) in enumerate(zip(helds, gots)):
        copies += start_deal(
            held, got, size, own_sem.at[i], held_send, held_recv, i * (size - 1)
        )
    dproj_ref[...] = dproj
    steps = opened_ref.shape[0] // micro
    total[...] = du_ref[...] + dot(dproj, w_x[...], 0, 0)
    for low, high in spans_of(w_x.shape[1], LANES):
        lines = [jnp.zeros((1, high - low), F32) for _ in range(CONV + 1)]
        for m in range(micro):
            rows = pl.ds(m * steps, steps)
            inner = opened_ref[rows, low:high].astype(F32)
            position = position_ref[rows]
            tap = taps[:, low:high]
            conv, shifted = taps_of(inner, position, tap, bias[:, low:high])
            sig = sigmoid(conv)
            d_conv = total[rows, low:high] * (sig * (1.0 + conv * (1.0 - sig)))
            d_inner = tap[0:1] * d_conv
            for k in range(CONV):
                lines[k] = lines[k] + jnp.sum(d_conv * shifted[k], axis=0, keepdims=True)
                if k:
                    masked = jnp.where(position >= k, d_conv, 0.0)
                    d_inner = d_inner + tap[k : k + 1] * pltpu.roll(masked, steps - k, axis=0)
            lines[CONV] = lines[CONV] + jnp.sum(d_conv, axis=0, keepdims=True)
            dinner_ref[rows, low:high] = d_inner.astype(BF)
        sums_ref[:, low:high] = jnp.concatenate(
            lines + [jnp.zeros((8 - CONV - 1, high - low), F32)], axis=0
        )
    for copy in copies:
        copy.wait()


def ssm_close(dlin, db, dc, du, opened, position, taps, bias, w_x, w_dt, helds, micro, collective_id):
    size = lax.axis_size("seq")
    rows = opened.shape[0]
    wide, channels = w_x.shape
    dma = pltpu.SemaphoreType.DMA((size - 1,))
    return pl.pallas_call(
        partial(ssm_close_kernel, size, micro, len(helds)),
        out_shape=[
            SHAPE((wide, rows), BF),
            SHAPE((rows, channels), BF),
            SHAPE((8, channels), F32),
        ]
        + [SHAPE(held.shape, held.dtype) for held in helds],
        in_specs=[VMEM] * 10 + [HBM] * len(helds),
        out_specs=[VMEM] * 3 + [HBM] * len(helds),
        scratch_shapes=[
            pltpu.VMEM((size, wide, rows), BF),
            pltpu.VMEM((rows, channels), F32),
            dma,
            dma,
        ]
        + deal_sems(size, max(1, len(helds))),
        compiler_params=pltpu.CompilerParams(
            collective_id=collective_id, has_side_effects=True, vmem_limit_bytes=VMEM_BYTES
        ),
        name="ssm_close",
    )(dlin, db, dc, du, opened, position, taps, bias, w_x, w_dt, *helds)


def branch_back_kernel(size, *refs):
    dmix, w_att, w_ssm, context, ssm_out, core, u, gate_ref = refs[:8]
    scale_att, scale_ssm, gain_att, gain_ssm, live, skip = refs[8:14]
    d_context, d_core, d_gate, d_gain_att, d_gain_ssm, d_skip = refs[14:20]
    t_att, t_ssm, slots, send, recv = refs[20:-1]
    w_att = joined(w_att, refs[-1])
    meet(pack_peers(size))
    place = lax.broadcasted_iota(jnp.int32, (8, LANES), 0)
    kinds = (
        (w_att, context, scale_att, gain_att, d_gain_att, t_att),
        (w_ssm, ssm_out, scale_ssm, gain_ssm, d_gain_ssm, t_ssm),
    )
    sums = []
    for w, value, scale, gain, d_gain, t in kinds:
        total = None
        for low, high in spans_of(w.shape[0], 2 * LANES):
            grad = 0.5 * dot(dmix[...], w[low:high, :], 1, 1)
            held = value[:, low:high]
            d_gain[:, low:high] = jnp.sum(grad * held * scale[:, :1], axis=0, keepdims=True)
            scaled = grad * gain[:, low:high]
            t[:, low:high] = scaled
            term = row_sums(scaled * held)
            total = term if total is None else total + term
        sums.append(total)
    rows8 = lax.broadcasted_iota(jnp.int32, sums[0].shape, 0)
    slots[lax.axis_index("seq")] = jnp.where(rows8 == 0, sums[0], sums[1])
    total = sum_slots(slots, send, recv)
    columns = [
        lax.dot_general(
            total,
            (place == kind).astype(F32),
            (((0,), (0,)), ((), ())),
            precision=lax.Precision.HIGHEST,
            preferred_element_type=F32,
        )
        for kind in range(2)
    ]
    scale = scale_att[:, :1]
    inward = scale * scale * scale * (columns[0][:, :1] / ATT)
    d_context[...] = ((t_att[...] * scale - context[...] * inward) * live[...]).astype(BF)
    scale = scale_ssm[:, :1]
    inward = scale * scale * scale * (columns[1][:, :1] / INNER)
    for low, high in spans_of(w_ssm.shape[0], 2 * LANES):
        at = slice(low, high)
        d_out = t_ssm[:, at] * scale - ssm_out[:, at] * inward
        gate = gate_ref[:, at].astype(F32)
        sig = sigmoid(gate)
        silu = gate * sig
        held = d_out * silu
        d_core[:, at] = held
        d_skip[:, at] = jnp.sum(held * u[:, at], axis=0, keepdims=True)
        mixed = core[:, at] + skip[:, at] * u[:, at]
        d_gate[:, at] = (d_out * mixed * (sig * (1.0 + gate - silu))).astype(BF)


def branch_back(
    dmix, w_att, w_ssm, context, ssm_out, core, u, gate_z, scales, gains, live, skip, collective_id
):
    size = lax.axis_size("seq")
    rows, wide, channels = dmix.shape[0], w_att.shape[1], w_ssm.shape[0]
    dma = pltpu.SemaphoreType.DMA((size - 1,))
    return pl.pallas_call(
        partial(branch_back_kernel, size),
        out_shape=[
            SHAPE((rows, wide), BF),
            SHAPE((rows, channels), F32),
            SHAPE((rows, channels), BF),
            SHAPE((1, wide), F32),
            SHAPE((1, channels), F32),
            SHAPE((1, channels), F32),
        ],
        in_specs=[VMEM] * 14,
        out_specs=[VMEM] * 6,
        scratch_shapes=[
            pltpu.VMEM((rows, wide), F32),
            pltpu.VMEM((rows, channels), F32),
            pltpu.VMEM((size, 8, rows), F32),
            dma,
            dma,
        ]
        + [pltpu.VMEM((wide, D), BF)],
        compiler_params=pltpu.CompilerParams(
            collective_id=collective_id, has_side_effects=True, vmem_limit_bytes=VMEM_BYTES
        ),
        name="branch_back",
    )(dmix, w_att, w_ssm, context, ssm_out, core, u, gate_z, *scales, *gains, live, skip)


def close_kernel(size, tok, micro, rest, d_inner, w, x_ref, gain, d_hidden, dx, d_gain, sent, got, send, recv):
    here, row = lax.axis_index("seq"), lax.axis_index("fsdp")
    meet(pack_peers(size))

    gathering = Gathering(tok, sent, got, send, recv)

    def block(k, carry):
        d = gathering.device(k)
        spots = [block_rows(size, tok, m, d) for m in range(micro)]
        gathering.add(k)
        rows = jnp.concatenate([d_inner[spot] for spot in spots])
        held = jnp.concatenate([rest[spot] for spot in spots])
        for low, high in spans_of(D):
            part = held[:, low:high].astype(F32) + dot(rows, w[low:high, :], 1, 1)
            sent[k, :, low:high] = part.astype(BF)
        gathering.send(k)
        return carry

    lax.fori_loop(0, size, block, 0)
    gathering.finish()
    gain_sum = jnp.zeros((1, D), F32)
    for m in range(micro):
        rows = pl.ds(m * tok, tok)
        d_in = gathering.total(m, sent[size - 1, rows].astype(F32))
        whole = x_ref[rows].astype(F32)
        scale = lax.rsqrt(jnp.mean(whole * whole, axis=-1, keepdims=True) + EPS)
        normal = whole * scale
        gain_sum = gain_sum + jnp.sum(d_in * normal, axis=0, keepdims=True)
        scaled = d_in * gain[...]
        inward = jnp.mean(scaled * normal, axis=-1, keepdims=True)
        dx[rows] = (d_hidden[rows] + scale * (scaled - normal * inward)).astype(BF)
    d_gain[...] = gain_sum


def close_rows(rest, d_inner, w, x_own, gain, d_hidden, micro, collective_id):
    size = lax.axis_size("seq")
    own = x_own.shape[0]
    dma = pltpu.SemaphoreType.DMA((size - 1,))
    return pl.pallas_call(
        partial(close_kernel, size, own // micro, micro),
        out_shape=[SHAPE((own, D), BF), SHAPE((1, D), F32)],
        in_specs=[VMEM] * 6,
        out_specs=[VMEM] * 2,
        scratch_shapes=[
            pltpu.VMEM((size, own, D), BF),
            pltpu.VMEM((6, own // micro, D), BF),
            *crossing_sems(),
        ],
        compiler_params=pltpu.CompilerParams(
            collective_id=collective_id, has_side_effects=True, vmem_limit_bytes=VMEM_BYTES
        ),
        name="close_rows",
    )(rest, d_inner, w, x_own, gain, d_hidden)


def squares(row_vals):
    return jnp.sum(row_vals * row_vals)


def local(
    tokens,
    cotangent,
    route,
    lengths,
    gain_in,
    w_qkv,
    w_mix_in,
    w_x,
    w_dt,
    w_small,
    gain_att,
    gain_ssm,
    w_out_att,
    w_out_ssm,
    gain_ffn,
    w_gate,
    w_up,
    w_down,
):
    S, N = lax.axis_size("seq"), lax.axis_size("fsdp")
    s = lax.axis_index("seq")
    micro, tok = tokens.shape[:2]
    pack = tok * S
    rows_d = gain_in.shape[0] // N
    ff = w_gate.shape[1]
    ch_piece, ff_piece = INNER // (N * S), ff // (N * S)
    ch = -(-INNER // (S * LANES)) * LANES
    ffs = -(-ff // (S * LANES)) * LANES
    cols = D // S
    groups = HEADS // KV_HEADS
    first_heads = [(HEADS * i + S - 1) // S for i in range(S + 1)]
    head_counts = [first_heads[i + 1] - first_heads[i] for i in range(S)]
    most = max(head_counts)
    width = most * HEAD
    first_head = jnp.array(first_heads, jnp.int32)[s]
    head_live = jnp.arange(most) < jnp.array(head_counts, jnp.int32)[s]
    live = jnp.repeat(head_live, HEAD).astype(F32)[None, :]
    in_low = (first_head + jnp.arange(most)) // groups <= s

    def gather(shard):
        return lax.all_gather(shard, "fsdp", axis=0, tiled=True)

    def scatter(whole):
        rows, wide = whole.shape[0] // N, whole.shape[1]
        fill = -rows % 8
        whole = whole.astype(BF)
        if fill:
            whole = jnp.pad(whole.reshape(N, rows, wide), ((0, 0), (0, fill), (0, 0)))
            whole = whole.reshape(N * (rows + fill), wide)
        whole = lax.psum_scatter(whole, "fsdp", scatter_dimension=0, tiled=True)
        return lax.optimization_barrier(whole)[:rows]

    def part(shard, axis, chunks, wide):
        shape = shard.shape
        piece = shape[axis] // (chunks * S)
        shaped = shard.reshape(shape[:axis] + (chunks, S, piece) + shape[axis + 1 :])
        picked = lax.dynamic_index_in_dim(shaped, s, axis + 1, keepdims=False)
        fill = [(0, 0)] * picked.ndim
        fill[axis + 1] = (0, wide - piece)
        return jnp.pad(picked, fill).reshape(
            shape[:axis] + (chunks * wide,) + shape[axis + 1 :]
        )

    def span(array, axis, start, size):
        return lax.dynamic_slice_in_dim(array, start, size, axis)

    send_hot, land_hot = routing(route, tok)
    x_own = bring(tokens.reshape(micro * tok, D), send_hot, land_hot)
    q_start = first_head * HEAD
    chw, ffw = ch // N, ffs // N
    q_starts = [h * HEAD for h in first_heads[:S]]
    kv_starts = [ATT + HEAD * i for i in range(S)]
    at_k, at_v, at_q = 2 * ch, 2 * ch + 2 * HEAD, 2 * ch + 4 * HEAD
    at_att = at_q + width
    in_wide = at_att + cols
    mix_table = pieces_table(2 * N, INNER // N, ch_piece, chw)
    in_part = regroup(
        [w_mix_in, w_qkv, w_out_att],
        [jax.ShapeDtypeStruct((rows_d, in_wide), BF)],
        [
            (0, None, 0, 0, placed(mix_table, 0, in_wide)),
            (1, None, 0, 0, placed(run_table(kv_starts, 2 * HEAD), at_k, in_wide)),
            (1, None, 0, 0, placed(run_table([a + KV_WIDTH for a in kv_starts], 2 * HEAD), at_v, in_wide)),
            (2, None, 0, 0, placed(run_table([cols * i for i in range(S)], cols), at_att, in_wide)),
            (1, None, 0, 0, placed(run_table(q_starts, width), at_q, in_wide)),
        ],
    )[0]
    small_part = part(
        jnp.concatenate([w_x, w_dt, w_small, jnp.zeros((w_x.shape[0], 1), BF)], axis=1), 0, 1, chw
    )
    small_wide = small_part.shape[1]
    gathered_in = gather(
        jnp.concatenate([in_part, jnp.pad(small_part, ((0, rows_d - chw), (0, 0)))], axis=1)
    )
    cot_own = bring(cotangent.reshape(micro * tok, D), send_hot, land_hot)
    x_rows = gather_rows(x_own, micro, 3)
    cot_own, x_rows = lax.optimization_barrier((cot_own, x_rows))
    cot_rows = gather_rows(cot_own, micro, 6)
    gathered_in, x_rows, cot_rows = lax.optimization_barrier((gathered_in, x_rows, cot_rows))
    out_piece, gathered_in = lax.optimization_barrier((part(w_out_ssm, 0, 1, chw), gathered_in))
    w_out_part = gather(out_piece)
    w_in = gathered_in[:, :at_att]
    w_att_cols = gathered_in[:, at_att:in_wide]
    w_small_part = (
        gathered_in[:, in_wide:].reshape(N, rows_d, small_wide)[:, :chw].reshape(ch, small_wide)
    )
    ff_table = pieces_table(N, ff // N, ff_piece, ffw)
    gu_part = regroup(
        [w_gate, w_up],
        [jax.ShapeDtypeStruct((rows_d, 2 * ffs), BF)],
        [
            (0, None, 0, 0, placed(ff_table, 0, 2 * ffs)),
            (1, None, 0, 0, placed(ff_table, ffs, 2 * ffs)),
        ],
    )[0]

    w_att_pad = jnp.pad(w_att_cols, ((0, width), (0, 0)))
    w_att_blocks = jnp.stack([w_att_pad[h * HEAD : h * HEAD + width] for h in first_heads[:S]])

    w_x_turned = w_small_part[:, :PROJ].T
    w_x_turned = jnp.pad(
        jnp.concatenate([w_x_turned[DT_RANK:], w_x_turned[:DT_RANK]], axis=0),
        ((0, PROJ_PAD - PROJ), (0, 0)),
    )
    w_dt_turned = jnp.pad(
        w_small_part[:, PROJ : PROJ + DT_RANK].T, ((0, PROJ_PAD - PROJ), (0, 0))
    )
    small_par = w_small_part[:, PROJ + DT_RANK : PROJ + DT_RANK + CONV + 3 + STATE].astype(F32)
    small_lines = small_par.T
    taps = jnp.pad(small_lines[:CONV], ((0, 8 - CONV), (0, 0)))
    conv_b, dt_bias, skip = [small_lines[CONV + i][None] for i in range(3)]
    rates = -jnp.exp(small_lines[CONV + 3 :])
    gain_att_part = span(jnp.pad(gain_att, (0, width)), 0, q_start, width)[None]
    gain_ssm_part = part(gain_ssm, 0, N, ch // N)[None]

    position = jax.vmap(lambda one: seq_layout(one, pack)[1])(lengths[:, 0])
    position = position.reshape(micro * pack, 1)

    normed_low = rms_scale(x_rows.astype(F32), gain_in).astype(BF)
    opened = dot(normed_low, w_in, 1, 0).astype(BF)
    opened, gu_part, down_part = lax.optimization_barrier(
        (opened, gu_part, part(w_down, 0, 1, ffw))
    )
    w_gu, w_down_part = gather(gu_part), gather(down_part)
    gate_z = opened[:, ch : 2 * ch]
    u, lin, projected, bc = ssm_open(
        opened, position, taps, conv_b, w_x_turned, w_dt_turned, dt_bias, micro, 7
    )
    q = opened[:, at_q:].reshape(micro, pack, most, HEAD)
    kv = opened[:, at_k:at_q].reshape(micro, pack, 4, HEAD)
    pick_low = in_low[None, None, :, None]
    keys = jnp.where(pick_low, kv[:, :, 0:1], kv[:, :, 1:2])
    values = jnp.where(pick_low, kv[:, :, 2:3], kv[:, :, 3:4])
    context, probs, att_sums = attention(opened, at_k, position, most, micro)
    bc = jnp.broadcast_to(bc.T[:, :, None], (micro * pack, 2 * STATE, LANES))
    core, ssm_out, ssm_sums, w_att_part = scan_forward(
        u, lin, bc, rates, position, opened, skip, w_att_blocks, micro, 11
    )
    sums = jnp.stack([att_sums[0], ssm_sums[0]])
    att_low, ssm_low, scale_att, scale_ssm, hidden, mixer_out, ffn_low = mixer_rows(
        context,
        ssm_out,
        jnp.pad(sums, ((0, 6), (0, 0))),
        x_own,
        (gain_att_part, gain_ssm_part, gain_ffn[None]),
        w_att_part,
        w_out_part,
        micro,
        4,
    )
    act_low, dgu_low, down_parts, d_hidden, d_gain_ffn, dmix_low = ffn_rows(
        ffn_low, cot_rows, hidden, cot_own, gain_ffn[None], w_gu, w_down_part, micro, 5
    )

    gu_whole = dot(ffn_low, dgu_low, 0, 0).astype(BF)
    act_low, gu_whole = lax.optimization_barrier((act_low, gu_whole))
    r_gu = scatter(gu_whole)
    down_whole = dot(act_low, cot_rows, 0, 0).astype(BF)
    dmix_low, down_whole = lax.optimization_barrier((dmix_low, down_whole))
    r_down = scatter(down_whole)
    d_context, d_core, d_gate_z, d_gain_att, d_gain_ssm, d_skip = branch_back(
        dmix_low,
        w_att_part,
        w_out_part,
        context,
        ssm_out,
        core,
        u,
        gate_z,
        (scale_att, scale_ssm),
        (gain_att_part, gain_ssm_part),
        live,
        skip,
        8,
    )
    ssm_whole = (0.5 * dot(ssm_low, dmix_low, 0, 0)).astype(BF)
    g_att_rows = (0.5 * dot(att_low, dmix_low, 0, 0)).astype(BF)
    att_blocks = g_att_rows.reshape(width, S, cols).transpose(1, 0, 2)
    dctx_low = d_context.reshape(micro, pack, most, HEAD)
    d_values = jnp.einsum(
        "mhtu,mthd->muhd", probs.astype(BF), dctx_low, preferred_element_type=F32
    )
    d_probs = jnp.einsum("mthd,muhd->mhtu", dctx_low, values, preferred_element_type=F32)
    dscore_low = (
        probs * (d_probs - jnp.sum(probs * d_probs, axis=-1, keepdims=True))
    ).astype(BF)
    d_q = jnp.einsum("mhtu,muhd->mthd", dscore_low, keys, preferred_element_type=F32) * 0.125
    d_keys = jnp.einsum("mhtu,mthd->muhd", dscore_low, q, preferred_element_type=F32) * 0.125

    def kv_sum(d_heads):
        return [
            jnp.sum(jnp.where(pick_low, d_heads, 0.0), axis=2),
            jnp.sum(jnp.where(pick_low, 0.0, d_heads), axis=2),
        ]

    d_rest = jnp.concatenate(
        [d_gate_z]
        + [
            one.astype(BF).reshape(micro * pack, -1)
            for one in kv_sum(d_keys) + kv_sum(d_values) + [d_q]
        ],
        axis=1,
    )
    rest_rows = dot(d_rest, gathered_in[:, ch:at_att], 1, 1).astype(BF)
    rest_whole = dot(normed_low, d_rest, 0, 0).astype(BF)
    d_core, r_gu, ssm_whole, rest_whole, rest_rows = lax.optimization_barrier(
        (d_core, r_gu, ssm_whole, rest_whole, rest_rows)
    )
    r_ssm, r_rest = scatter(ssm_whole), scatter(rest_whole)
    per = N // S
    gate_take = np.concatenate([np.arange(ff_piece) + ffw * i for i in range(per)])
    half_wide = -(-per * ff_piece // LANES) * LANES
    moves = []
    for d in range(S):
        for i in range(2):
            table = gate_take[None] + d * per * ffw + i * ffs
            moves.append((0, None, 0, d, placed(table, i * half_wide, 2 * half_wide)))
    (gu_blocks,) = regroup([r_gu], [SHAPE((S, rows_d, 2 * half_wide), BF)], moves)
    d_u, d_lin, d_dt_bias, d_rates, d_in_b, d_out_c, (ffn_got, gu_got, g_att_blocks) = (
        scan_backward(
            d_core, u, lin, bc, rates, position, skip, [down_parts, gu_blocks, att_blocks], micro, 0
        )
    )
    ffn_out = jnp.sum(ffn_got.astype(F32), axis=0)
    result = hidden + ffn_out
    outputs = give(result.astype(BF), send_hot, land_hot)
    g_att_whole = jnp.concatenate(
        [g_att_blocks[i, : head_counts[i] * HEAD] for i in range(S)], axis=0
    )
    dproj_low, d_inner, conv_sums = ssm_close(
        d_lin,
        d_in_b,
        d_out_c,
        d_u,
        opened,
        position,
        taps,
        conv_b,
        w_x_turned,
        w_dt_turned,
        [],
        micro,
        9,
    )
    g_x = dot(u.astype(BF), dproj_low, 0, 1)
    small_whole = jnp.concatenate(
        [
            g_x[:, 2 * STATE : PROJ],
            g_x[:, : 2 * STATE],
            dot(d_lin, projected[2 * STATE : PROJ], 0, 1),
            conv_sums[: CONV + 1].T,
            d_dt_bias[:, None],
            d_skip[0][:, None],
            (d_rates * rates).T,
            jnp.zeros((ch, 1), F32),
        ],
        axis=1,
    ).astype(BF)
    small_whole = jnp.pad(
        small_whole.reshape(N, chw, small_wide), ((0, 0), (0, rows_d - chw), (0, 0))
    ).reshape(N * rows_d, small_wide)
    last_whole = jnp.concatenate(
        [dot(normed_low, d_inner, 0, 0).astype(BF), g_att_whole, small_whole], axis=1
    )
    d_inner, last_whole, r_rest = lax.optimization_barrier((d_inner, last_whole, r_rest))
    r_last = scatter(last_whole)
    dx, d_gain_in = close_rows(
        rest_rows, d_inner, gathered_in[:, :ch], x_own, gain_in[None], d_hidden, micro, 10
    )

    att_at = lax.dynamic_update_slice_in_dim(
        jnp.zeros((ATT + width,), F32), d_gain_att[0] * live[0], q_start, 0
    )[:ATT]
    ssm_at = lax.dynamic_update_index_in_dim(
        jnp.zeros((N, S, ch_piece), F32), d_gain_ssm[0].reshape(N, -1)[:, :ch_piece], s, 1
    ).reshape(INNER)
    stats = jnp.stack(
        [
            squares(x_own.astype(F32)),
            jnp.sum(sums[0]),
            jnp.sum(sums[1]),
            squares(mixer_out),
            squares(ffn_out),
            squares(result),
        ]
    )
    ends = np.cumsum([0, D, ATT, INNER, D, 6])
    line = jnp.concatenate([d_gain_in[0], att_at, ssm_at, d_gain_ffn[0], stats])
    line = jnp.pad(line, (0, -line.shape[0] % 1024)).reshape(-1, LANES)
    moves = []
    for d in range(S):
        moves.append((0, None, 0, d, run_table([d * cols], cols)))
        moves.append((1, None, 1, d, run_table([d * cols], cols)))
    qkv_wide = (ATT + 2 * KV_WIDTH) // S
    starts = np.array(q_starts)[:, None]
    counts = np.array(head_counts)[:, None] * HEAD
    base = np.array(kv_starts)[:, None]
    for d in range(S):
        column = np.arange(qkv_wide)[None] + d * qkv_wide
        table = np.full((S, qkv_wide), -1)
        for low, count, source in (
            (starts, counts, at_q),
            (base, 2 * HEAD, at_k),
            (base + KV_WIDTH, 2 * HEAD, at_v),
        ):
            inside = (column >= low) & (column < low + count)
            table = np.where(inside, column - low + source - ch, table)
        moves.append((2, None, 2, d, table.astype(np.int32)))
    mix_mine = 2 * INNER // S
    at = np.arange(mix_mine // S)
    mix_tables = [
        ((at // ch_piece + j * (2 * N // S)) * chw + at % ch_piece)[None].astype(np.int32)
        for j in range(S // 2)
    ]
    for j in range(S // 2):
        moves.append((2, None, 3, j, mix_tables[j]))
    (*row_blocks, gate_blocks) = regroup(
        [r_ssm, r_down, r_rest],
        [
            SHAPE((S, r_ssm.shape[0], cols), BF),
            SHAPE((S, r_down.shape[0], cols), BF),
            SHAPE((S, rows_d, qkv_wide), BF),
            SHAPE((S // 2, rows_d, mix_mine // S), BF),
        ],
        moves,
    )
    row_blocks, gate_blocks, dx = lax.optimization_barrier((row_blocks, gate_blocks, dx))
    ssm_got, down_got, qkv_got, gate_got = deal(row_blocks, gate_blocks, S // 2, 1)
    input_grads = give(dx, send_hot, land_hot)
    ssm_got, r_last = lax.optimization_barrier((ssm_got, r_last))
    out_ssm = ssm_got[:, :ch_piece].reshape(S * ch_piece, cols).astype(F32)
    out_down = down_got[:, :ff_piece].reshape(S * ff_piece, cols).astype(F32)
    ff_mine = ff // S
    moves = []
    at = np.arange(ff_mine)
    for source in range(S):
        chunk, inside = at // (S * ff_piece), at % (S * ff_piece)
        table = np.where(
            inside // ff_piece == source, chunk * ff_piece + inside % ff_piece, -1
        )[None].astype(np.int32)
        moves.append((0, source, 0, 0, table))
        moves.append((0, source, 1, 0, np.where(table >= 0, table + half_wide, -1)))
    out_gate, out_up = regroup(
        [gu_got], [jax.ShapeDtypeStruct((rows_d, ff_mine), F32)] * 2, moves
    )

    (inner_blocks,) = regroup(
        [r_last],
        [SHAPE((S // 2, rows_d, mix_mine // S), BF)],
        [(0, None, 0, j, mix_tables[j]) for j in range(S // 2)],
    )
    r_small = r_last[:chw, ch + cols :]
    small_got, inner_got, sums_all = last_exchange(
        [jnp.broadcast_to(r_small, (S,) + r_small.shape)], inner_blocks, line, 2
    )
    out_qkv = jnp.sum(qkv_got.astype(F32), axis=0)
    moves = []
    at = np.arange(mix_mine)
    for source in range(S):
        chunk, inside = at // (S * ch_piece), at % (S * ch_piece)
        table = np.where(
            inside // ch_piece == source, chunk * ch_piece + inside % ch_piece, -1
        )[None].astype(np.int32)
        moves.append((0, source, 0, 0, table))
    (out_mix,) = regroup(
        [jnp.where(s < S // 2, inner_got, gate_got)], [SHAPE((rows_d, mix_mine), F32)], moves
    )
    g_att = r_last[:, ch : ch + cols].astype(F32)
    small_all = small_got[:, :ch_piece].reshape(S * ch_piece, small_wide).astype(F32)
    out_x = span(small_all[:, :PROJ], 1, s * (PROJ // S), PROJ // S)
    out_dt = span(small_all[:, PROJ : PROJ + DT_RANK], 1, s * (DT_RANK // S), DT_RANK // S)
    out_small = small_all[:, PROJ + DT_RANK : PROJ + DT_RANK + CONV + 3 + STATE]

    sums = sums_all.reshape(-1)
    g_gain_in, g_gain_att, g_gain_ssm, g_gain_ffn, stat_sum = [
        sums[a:b] for a, b in zip(ends[:-1], ends[1:])
    ]
    widths = jnp.array([D, ATT, INNER, D, D, D], F32)
    rms = jnp.sqrt(stat_sum / (widths * (micro * pack * N)))
    return (
        outputs.reshape(tokens.shape),
        input_grads.reshape(tokens.shape),
        g_gain_in,
        out_qkv,
        out_mix,
        out_x,
        out_dt,
        out_small,
        out_small[:, CONV + 1],
        g_gain_att,
        g_gain_ssm,
        g_att,
        out_ssm,
        g_gain_ffn,
        out_gate,
        out_up,
        out_down,
        rms,
    )


def solution(mesh):
    rows = P(None, ("seq", "fsdp"), None)
    shard = P("fsdp", None)
    both = P("fsdp", "seq")
    placed = (rows, rows, P(None, "seq"), P(None, "fsdp", None), P())
    placed += (shard,) * 5 + (P(), P(), shard, shard, P(), shard, shard, shard)
    return jax.shard_map(
        local,
        mesh=mesh,
        in_specs=placed,
        out_specs=(
            rows,
            rows,
            P(),
            both,
            both,
            both,
            both,
            shard,
            P("fsdp"),
            P(),
            P(),
            both,
            both,
            P(),
            both,
            both,
            both,
            P(),
        ),
        check_vma=False,
    )
```

```python
from functools import partial

import jax
import jax.numpy as jnp
import numpy as np
from jax import lax
from jax.experimental import pallas as pl
from jax.experimental.pallas import tpu as pltpu
from jax.sharding import PartitionSpec as P

D = 1600
HEADS = 25
KV_HEADS = 5
HEAD = 64
INNER = 3200
STATE = 16
CONV = 4
DT_RANK = 100
MICRO = 2
ATT = 1600
KV_WIDTH = 320
PROJ = DT_RANK + 2 * STATE
PROJ_PAD = 144
LANES = 128
EPS = 1e-05
BF = jnp.bfloat16
F32 = jnp.float32


def dot(left_op, right_op, left_dim, right_dim):
    return lax.dot_general(
        left_op, right_op, (((left_dim,), (right_dim,)), ((), ())), preferred_element_type=F32
    )


def rms_scale(row_vals, gain_vec):
    return (
        row_vals * lax.rsqrt(jnp.mean(row_vals * row_vals, axis=-1, keepdims=True) + EPS) * gain_vec
    )


def seq_layout(seq_lens, span_len):
    places = jnp.arange(span_len, dtype=jnp.int32)
    seq_ends = jnp.cumsum(seq_lens)
    segment = jnp.sum((places[:, None] >= seq_ends[None, :]).astype(jnp.int32), axis=1)
    starts = seq_ends - seq_lens
    picked = (segment[:, None] == jnp.arange(seq_lens.shape[0], dtype=jnp.int32)[None, :]).astype(
        jnp.int32
    )
    position = places - jnp.sum(picked * starts[None, :], axis=1)
    return (segment, position)


def swap(array, k):
    size = lax.axis_size("seq")
    return lax.ppermute(array, "seq", [(i, i ^ k) for i in range(size)])


def pick(blocks, at):
    return lax.dynamic_index_in_dim(blocks, at, 0, keepdims=False)


def seq_deal(blocks):
    size, here = lax.axis_size("seq"), lax.axis_index("seq")
    out = blocks
    for k in range(1, size):
        there = here ^ k
        out = lax.dynamic_update_index_in_dim(out, swap(pick(blocks, there), k), there, 0)
    return out


def seq_gather(block):
    size, here = lax.axis_size("seq"), lax.axis_index("seq")
    out = lax.dynamic_update_index_in_dim(
        jnp.zeros((size,) + block.shape, block.dtype), block, here, 0
    )
    for k in range(1, size):
        out = lax.dynamic_update_index_in_dim(out, swap(block, k), here ^ k, 0)
    return out


def seq_scatter(blocks):
    size, here = lax.axis_size("seq"), lax.axis_index("seq")
    total = pick(blocks, here).astype(F32)
    for k in range(1, size):
        total = total + swap(pick(blocks, here ^ k).astype(BF), k).astype(F32)
    return total


def seq_sum(array):
    return jnp.sum(seq_gather(array).astype(F32), axis=0)


def routing(route_rows, tok_rows):
    fsdp_count, fsdp_rank = lax.axis_size("fsdp"), lax.axis_index("fsdp")
    micro = route_rows.shape[0]
    per_peer = tok_rows // fsdp_count
    target_dev = (route_rows // tok_rows).reshape(micro, fsdp_count, tok_rows)
    target_slot = (route_rows % tok_rows).reshape(micro, fsdp_count, tok_rows)
    steps = jnp.arange(tok_rows, dtype=jnp.int32)
    same = target_dev[:, :, :, None] == target_dev[:, :, None, :]
    earlier = steps[None, :] < steps[:, None]
    rank = jnp.sum((same & earlier).astype(jnp.int32), axis=3)
    my_dev = lax.dynamic_index_in_dim(target_dev, fsdp_rank, 1, keepdims=False)
    my_rank = lax.dynamic_index_in_dim(rank, fsdp_rank, 1, keepdims=False)
    micros = jnp.arange(micro, dtype=jnp.int32)
    send_at = (my_dev * micro + micros[:, None]) * per_peer + my_rank
    ranks = jnp.arange(per_peer, dtype=jnp.int32)
    mine = (target_dev == fsdp_rank)[:, :, None, :] & (rank[:, :, None, :] == ranks[:, None])
    slot = jnp.sum(mine.astype(jnp.int32) * target_slot[:, :, None, :], axis=3)
    land_at = (micros[:, None, None] * tok_rows + slot).transpose(1, 0, 2).reshape(-1)
    rows = jnp.arange(micro * tok_rows, dtype=jnp.int32)
    send_hot = (rows[:, None] == send_at.reshape(-1)[None, :]).astype(BF)
    land_hot = (rows[:, None] == land_at[None, :]).astype(BF)
    return send_hot, land_hot


def exchange(rows):
    return lax.all_to_all(rows, "fsdp", split_axis=0, concat_axis=0, tiled=True)


def bring(rows, send_hot, land_hot):
    sent = dot(send_hot, rows, 1, 0).astype(BF)
    return dot(land_hot, exchange(sent), 1, 0).astype(BF)


def give(rows, send_hot, land_hot):
    sent = dot(land_hot, rows, 0, 0).astype(BF)
    return dot(send_hot, exchange(sent), 0, 0).astype(BF)


def meet(peers):
    barrier = pltpu.get_barrier_semaphore()
    for peer in peers:
        pl.semaphore_signal(barrier, inc=1, device_id=peer, device_id_type=pl.DeviceIdType.MESH)
    pl.semaphore_wait(barrier, len(peers))


def remote(source, target, send, recv, device):
    return pltpu.make_async_remote_copy(
        src_ref=source,
        dst_ref=target,
        send_sem=send,
        recv_sem=recv,
        device_id=device,
        device_id_type=pl.DeviceIdType.MESH,
    )


def pack_peers(size):
    here, row = lax.axis_index("seq"), lax.axis_index("fsdp")
    return [(lax.rem(here + k, size), row) for k in range(1, size)]


def block_rows(size, tok, m, d):
    return pl.ds(pl.multiple_of((m * size + d) * tok, tok), tok)


def flip(place, k):
    return (place // 2 + k // 2) % 2 * 2 + (place % 2 + k % 2) % 2


def crossing():
    here, row = lax.axis_index("seq"), lax.axis_index("fsdp")
    return here, (flip(here, 1), row), (flip(here, 2), row)


class Relay:
    def __init__(self, tok, own, whole, own_sem, send, recv):
        here, one, two = crossing()
        self.whole, self.tok, self.one, self.two = whole, tok, one, two
        spots = [self.spot(m, here) for m in range(2)]
        first, second = own.at[pl.ds(0, tok)], own.at[pl.ds(tok, tok)]
        self.near = [
            remote(first, spots[0], send.at[0], recv.at[0], one),
            remote(second, spots[1], send.at[1], recv.at[1], two),
            remote(second, spots[1], send.at[2], recv.at[2], one),
            remote(first, spots[0], send.at[3], recv.at[3], two),
        ]
        self.far = [
            remote(self.spot(0, one[0]), self.spot(0, one[0]), send.at[4], recv.at[4], two),
            remote(self.spot(1, two[0]), self.spot(1, two[0]), send.at[5], recv.at[5], one),
        ]
        self.kept = [
            pltpu.make_async_copy(source, spot, own_sem.at[m])
            for m, (source, spot) in enumerate(zip((first, second), spots))
        ]

    def spot(self, m, d):
        return self.whole.at[block_rows(4, self.tok, m, d)]

    def start(self):
        for copy in self.near + self.kept:
            copy.start()

    def pass_on(self):
        for near, far in zip(self.near, self.far):
            near.wait_recv()
            far.start()

    def finish(self):
        for copy in self.near[:2]:
            copy.wait_send()
        for copy in self.near[2:] + self.far + self.kept:
            copy.wait()


class Gathering:
    def __init__(self, tok, sent, got, send, recv):
        here, one, two = crossing()
        self.here, self.tok, self.sent, self.got = here, tok, sent, got
        ways = [(0, 0, one), (0, 1, two), (1, 1, two), (2, 0, one), (1, 0, two), (2, 1, one)]
        self.copies = [
            remote(sent.at[k, pl.ds(m * tok, tok)], got.at[i], send.at[i], recv.at[i], way)
            for i, (k, m, way) in enumerate(ways)
        ]

    def device(self, k):
        return flip(self.here, 3 - k)

    def send(self, k):
        for i, block in enumerate((0, 0, 1, 2)):

            @pl.when(k == block)
            def _(i=i):
                self.copies[i].start()

    def add(self, k):
        @pl.when(k == 3)
        def _():
            for i, (block, m) in enumerate(((1, 0), (2, 1))):
                self.copies[i].wait_recv()
                rows = pl.ds(m * self.tok, self.tok)
                total = self.sent[block, rows].astype(F32) + self.got[i].astype(F32)
                self.sent[block, rows] = total.astype(BF)
                self.copies[4 + i].start()

    def finish(self):
        for copy in self.copies[:2]:
            copy.wait_send()
        for copy in self.copies[2:]:
            copy.wait()

    def total(self, m, own):
        pair = (3, 4) if m == 0 else (2, 5)
        return own + self.got[pair[0]].astype(F32) + self.got[pair[1]].astype(F32)


def crossing_sems():
    return [pltpu.SemaphoreType.DMA((6,))] * 2


def start_deal(source, out, size, own_sem, send_sem, recv_sem, first=0, start=True):
    here, row = lax.axis_index("seq"), lax.axis_index("fsdp")
    copies = [pltpu.make_async_copy(source.at[here], out.at[here], own_sem)]
    for k in range(1, size):
        there = lax.rem(here + k, size)
        copies.append(
            remote(
                source.at[there],
                out.at[here],
                send_sem.at[first + k - 1],
                recv_sem.at[first + k - 1],
                (there, row),
            )
        )
    if start:
        for copy in copies:
            copy.start()
    return copies


def start_half(source, out, size, first, own_sem, send_sem, recv_sem):
    here, row = lax.axis_index("seq"), lax.axis_index("fsdp")
    half = size // 2
    own = pltpu.make_async_copy(source.at[lax.rem(here, half)], out.at[here], own_sem)
    mine = (here >= first) & (here < first + half)

    def copy_to(j):
        return remote(
            source.at[j], out.at[here], send_sem.at[j], recv_sem.at[here], (first + j, row)
        )

    pl.when(mine)(own.start)
    for j in range(half):
        pl.when(here != first + j)(lambda j=j: copy_to(j).start())

    def wait():
        pl.when(mine)(own.wait)
        for j in range(half):
            pl.when(here != first + j)(lambda j=j: copy_to(j).wait_send())

        @pl.when(mine)
        def _():
            for k in range(1, size):
                there = lax.rem(here + k, size)
                remote(
                    source.at[0], out.at[there], send_sem.at[0], recv_sem.at[there], (there, row)
                ).wait_recv()

    return wait


def half_sems(size):
    return [pltpu.SemaphoreType.DMA((n,)) for n in (1, size // 2, size)]


def deal_sems(size, count=1):
    links = pltpu.SemaphoreType.DMA((count * (size - 1),))
    return [pltpu.SemaphoreType.DMA((count,)), links, links]


VMEM_BYTES = 60 * 2**20
VMEM = pl.BlockSpec(memory_space=pltpu.VMEM)
HBM = pl.BlockSpec(memory_space=pl.ANY)
SHAPE = jax.ShapeDtypeStruct


def lane_groups(channels, most=4):
    tiles, out, first = channels // LANES, [], 0
    while first < tiles:
        count = min(most, tiles - first)
        out.append((first, count))
        first += count
    return out


def sigmoid(v):
    return 1.0 / (1.0 + jnp.exp(-v))


def softplus(v):
    return jnp.maximum(v, 0.0) + jnp.log1p(jnp.exp(-jnp.abs(v)))


def steps_of(lin_ref, u_ref, position_ref, dtm, dtu):
    step = softplus(lin_ref[...])
    dtu[...] = step * u_ref[...]
    dtm[...] = jnp.where(position_ref[...] > 0, step, 1e30)


def both_of(ref, t):
    row = ref[t].astype(F32)
    return row[:STATE], row[STATE:]


def scan_kernel(size, groups, *refs):
    u_ref, lin_ref, bc_ref, a_ref, position_ref, gate_ref, skip_ref, held = refs[:8]
    core, out, sums, got, dtm, dtu, own_sem, held_send, held_recv = refs[8:]
    steps = u_ref.shape[0]

    def copies(start):
        return start_deal(held, got, size, own_sem.at[0], held_send, held_recv, start=start)

    @pl.when(pl.program_id(0) == 0)
    def _():
        meet(pack_peers(size))
        copies(True)

    steps_of(lin_ref, u_ref, position_ref, dtm, dtu)
    place = lax.broadcasted_iota(jnp.int32, (8, LANES), 0)
    for first, count in groups:
        spans = [pl.ds((first + i) * LANES, LANES) for i in range(count)]
        rates = [a_ref[:, span] for span in spans]

        def block(k, held):
            held = list(held)
            rows = pl.ds(pl.multiple_of(k * 8, 8), 8)
            dts = [dtm[rows, span] for span in spans]
            dus = [dtu[rows, span] for span in spans]
            ys = [jnp.zeros((8, LANES), F32)] * count
            for j in range(8):
                b_now, c_now = both_of(bc_ref, k * 8 + j)
                for i in range(count):
                    decay = jnp.exp(dts[i][j : j + 1] * rates[i])
                    held[i] = decay * held[i] + dus[i][j : j + 1] * b_now
                    y = jnp.sum(held[i] * c_now, axis=0, keepdims=True)
                    ys[i] = jnp.where(place == j, y, ys[i])
            for i, span in enumerate(spans):
                core[rows, span] = ys[i]
            return tuple(held)

        zero = jnp.zeros((STATE, LANES), F32)
        lax.fori_loop(0, steps // 8, block, (zero,) * count)
    gate = gate_ref[...].astype(F32)
    result = (core[...] + skip_ref[...] * u_ref[...]) * (gate * sigmoid(gate))
    out[...] = result
    sums[...] = row_sums(result * result)

    @pl.when(pl.program_id(0) == pl.num_programs(0) - 1)
    def _():
        for copy in copies(False):
            copy.wait()


def row_sums(values):
    return lax.dot_general(
        jnp.ones((8, values.shape[1]), F32),
        values,
        (((1,), (1,)), ((), ())),
        precision=lax.Precision.HIGHEST,
        preferred_element_type=F32,
    )


def scan_forward(u, lin, bc, rates, position, opened, skip, held, micro, collective_id):
    size = lax.axis_size("seq")
    rows, channels = u.shape
    steps = rows // micro
    block = pl.BlockSpec((steps, channels), lambda m: (m, 0))
    lane = pl.BlockSpec((8, steps), lambda m: (0, m))
    return pl.pallas_call(
        partial(scan_kernel, size, lane_groups(channels)),
        grid=(micro,),
        out_shape=[SHAPE((rows, channels), F32)] * 2
        + [SHAPE((8, rows), F32), SHAPE(held.shape, held.dtype)],
        in_specs=[
            block,
            block,
            pl.BlockSpec((steps, 2 * STATE, LANES), lambda m: (m, 0, 0)),
            pl.BlockSpec(rates.shape, lambda m: (0, 0)),
            pl.BlockSpec((steps, 1), lambda m: (m, 0)),
            pl.BlockSpec((steps, channels), lambda m: (m, 1)),
            pl.BlockSpec((1, channels), lambda m: (0, 0)),
            HBM,
        ],
        out_specs=[block, block, lane, HBM],
        scratch_shapes=[pltpu.VMEM((steps, channels), F32)] * 2 + deal_sems(size),
        compiler_params=pltpu.CompilerParams(
            collective_id=collective_id, has_side_effects=True, vmem_limit_bytes=VMEM_BYTES
        ),
        name="scan_forward",
    )(u, lin, bc, rates, position, opened, skip, held)


def scan_back_kernel(size, count, groups, *refs):
    dcore_ref, u_ref, lin_ref, bc_ref, a_ref, position_ref, skip_ref = refs[:7]
    helds, refs = refs[7 : 7 + count], refs[7 + count :]
    du_ref, dlin_ref, bias_ref, da_ref, db_ref, dc_ref = refs[:6]
    gots, refs = refs[6 : 6 + count], refs[6 + count :]
    dtm, dtu, ddtu, ddt, hs, acc_b, acc_c, own_sem, held_send, held_recv = refs
    steps = u_ref.shape[0]

    def copies():
        out = []
        for i, (held, got) in enumerate(zip(helds, gots)):
            out += start_deal(
                held, got, size, own_sem.at[i], held_send, held_recv, i * (size - 1), start=False
            )
        return out

    @pl.when(pl.program_id(0) == 0)
    def _():
        meet(pack_peers(size))
        for copy in copies():
            copy.start()

    steps_of(lin_ref, u_ref, position_ref, dtm, dtu)
    place = lax.broadcasted_iota(jnp.int32, (8, LANES), 0)
    zero = jnp.zeros((STATE, LANES), F32)
    for at, (first, count) in enumerate(groups):
        spans = [pl.ds((first + i) * LANES, LANES) for i in range(count)]
        slots = [pl.ds(i * LANES, LANES) for i in range(count)]
        rates = [a_ref[:, span] for span in spans]
        for slot in slots:
            hs[0, :, slot] = zero

        def block(k, held):
            held = list(held)
            base = pl.multiple_of(k * 8, 8)
            rows = pl.ds(base, 8)
            dts = [dtm[rows, span] for span in spans]
            dus = [dtu[rows, span] for span in spans]
            for j in range(8):
                b_now, _ = both_of(bc_ref, base + j)
                for i in range(count):
                    decay = jnp.exp(dts[i][j : j + 1] * rates[i])
                    held[i] = decay * held[i] + dus[i][j : j + 1] * b_now
                    hs[base + j + 1, :, slots[i]] = held[i]
            return tuple(held)

        lax.fori_loop(0, steps // 8, block, (zero,) * count)

        def back(k, carry):
            carry = list(carry)
            block_at = steps // 8 - 1 - k
            base = pl.multiple_of(block_at * 8, 8)
            rows = pl.ds(base, 8)
            dts = [dtm[rows, span] for span in spans]
            dus = [dtu[rows, span] for span in spans]
            dys = [dcore_ref[rows, span] for span in spans]
            out_u = [jnp.zeros((8, LANES), F32)] * count
            out_t = [jnp.zeros((8, LANES), F32)] * count
            for j in reversed(range(8)):
                t = base + j
                b_now, c_now = both_of(bc_ref, t)
                sum_b = sum_c = zero
                for i in range(count):
                    later, rate_sum = carry[i]
                    dt, du, dy = dts[i][j : j + 1], dus[i][j : j + 1], dys[i][j : j + 1]
                    g = later + dy * c_now
                    sum_c = sum_c + hs[t + 1, :, slots[i]] * dy
                    sum_b = sum_b + g * du
                    through = g * jnp.exp(dt * rates[i])
                    moved = through * hs[t, :, slots[i]]
                    to_u = jnp.sum(g * b_now, axis=0, keepdims=True)
                    to_t = jnp.sum(moved * rates[i], axis=0, keepdims=True)
                    out_u[i] = jnp.where(place == j, to_u, out_u[i])
                    out_t[i] = jnp.where(place == j, to_t, out_t[i])
                    carry[i] = (through, rate_sum + moved * dt)
                if at == 0:
                    acc_b[t] = sum_b
                    acc_c[t] = sum_c
                else:
                    acc_b[t] = acc_b[t] + sum_b
                    acc_c[t] = acc_c[t] + sum_c
            for i, span in enumerate(spans):
                ddtu[rows, span] = out_u[i]
                ddt[rows, span] = out_t[i]
            return tuple(carry)

        ends = lax.fori_loop(0, steps // 8, back, ((zero, zero),) * count)
        for i, span in enumerate(spans):
            da_ref[:, span] = ends[i][1]
    for acc, out in ((acc_b, db_ref), (acc_c, dc_ref)):
        out[...] = row_sums(acc[...].reshape(steps * STATE, LANES))
    lin = lin_ref[...]
    to_step = ddtu[...]
    du_ref[...] = dcore_ref[...] * skip_ref[...] + to_step * softplus(lin)
    d_lin = (ddt[...] + to_step * u_ref[...]) * sigmoid(lin)
    dlin_ref[...] = d_lin.astype(BF)
    bias_ref[...] = jnp.sum(d_lin, axis=0, keepdims=True)

    @pl.when(pl.program_id(0) == pl.num_programs(0) - 1)
    def _():
        for copy in copies():
            copy.wait()


def scan_backward(dcore, u, lin, bc, rates, position, skip, helds, micro, collective_id):
    size = lax.axis_size("seq")
    rows, channels = u.shape
    steps = rows // micro
    groups = lane_groups(channels)
    block = pl.BlockSpec((steps, channels), lambda m: (m, 0))
    rate = pl.BlockSpec(rates.shape, lambda m: (0, 0))
    line = pl.BlockSpec((1, channels), lambda m: (0, 0))
    flat = pl.BlockSpec((None, 8, steps * STATE), lambda m: (m, 0, 0))
    wide = pltpu.VMEM((steps, channels), F32)
    du, dlin, bias, da, db, dc, *gots = pl.pallas_call(
        partial(scan_back_kernel, size, len(helds), groups),
        grid=(micro,),
        out_shape=[
            SHAPE((rows, channels), F32),
            SHAPE((rows, channels), BF),
            SHAPE((micro, 1, channels), F32),
            SHAPE((micro, STATE, channels), F32),
            SHAPE((micro, 8, steps * STATE), F32),
            SHAPE((micro, 8, steps * STATE), F32),
        ]
        + [SHAPE(held.shape, held.dtype) for held in helds],
        in_specs=[
            block,
            block,
            block,
            pl.BlockSpec((steps, 2 * STATE, LANES), lambda m: (m, 0, 0)),
            rate,
            pl.BlockSpec((steps, 1), lambda m: (m, 0)),
            line,
        ]
        + [HBM] * len(helds),
        out_specs=[
            block,
            block,
            pl.BlockSpec((None, 1, channels), lambda m: (m, 0, 0)),
            pl.BlockSpec((None, STATE, channels), lambda m: (m, 0, 0)),
            flat,
            flat,
        ]
        + [HBM] * len(helds),
        scratch_shapes=[wide] * 4
        + [
            pltpu.VMEM((steps + 1, STATE, groups[0][1] * LANES), F32),
            pltpu.VMEM((steps, STATE, LANES), F32),
            pltpu.VMEM((steps, STATE, LANES), F32),
        ]
        + deal_sems(size, len(helds)),
        compiler_params=pltpu.CompilerParams(
            collective_id=collective_id, has_side_effects=True, vmem_limit_bytes=VMEM_BYTES
        ),
        name="scan_backward",
    )(dcore, u, lin, bc, rates, position, skip, *helds)
    return (
        du,
        dlin,
        jnp.sum(bias[:, 0], axis=0),
        jnp.sum(da, axis=0),
        db[:, 0].reshape(rows, STATE),
        dc[:, 0].reshape(rows, STATE),
        gots,
    )


def regroup_kernel(plan, source_count, out_count, *refs):
    here = lax.axis_index("seq")
    sources = refs[:source_count]
    maps = refs[source_count : len(refs) - out_count]
    outs = refs[len(refs) - out_count :]
    for out, block, tile, wide, terms in plan:
        at = pl.ds(tile * LANES, wide)
        total = None
        for source, which, low, high in terms:
            held = sources[source]
            held = held[..., low:high] if len(held.shape) == 2 else held[which[1], :, low:high]
            table = maps[which[0]]
            wanted = table[0:1, at]
            for i in range(1, table.shape[0]):
                wanted = jnp.where(here == i, table[i : i + 1, at], wanted)
            wanted = wanted - low
            places = lax.broadcasted_iota(jnp.int32, (high - low, wide), 0)
            hot = (places == wanted).astype(F32).astype(BF)
            term = dot(held, hot, 1, 0)
            total = term if total is None else total + term
        ref = outs[out]
        if total is None:
            total = jnp.zeros((ref.shape[-2], wide), F32)
        if len(ref.shape) == 2:
            ref[:, at] = total.astype(ref.dtype)
        else:
            ref[block, :, at] = total.astype(ref.dtype)


def regroup(sources, outs, moves):
    plan, maps = [], []
    tables = []
    for source, from_block, out, block, table in moves:
        maps.append(jnp.asarray(table))
        tables.append((source, from_block, out, block, table))
    for out, shape in enumerate(outs):
        for block in range(shape.shape[0] if len(shape.shape) == 3 else 1):
            for tile in range(-(-shape.shape[-1] // LANES)):
                wide = min(LANES, shape.shape[-1] - tile * LANES)
                terms = []
                for which, (source, from_block, to, to_block, table) in enumerate(tables):
                    used = table[:, tile * LANES : tile * LANES + wide]
                    if (to, to_block) != (out, block) or not (used >= 0).any():
                        continue
                    low = int(used[used >= 0].min()) // LANES * LANES
                    high = min(-(-(int(used.max()) + 1) // LANES) * LANES, sources[source].shape[-1])
                    terms.append((source, (which, from_block), low, high))
                plan.append((out, block, tile, wide, tuple(terms)))
    vmem = pl.BlockSpec(memory_space=pltpu.VMEM)
    return pl.pallas_call(
        partial(regroup_kernel, plan, len(sources), len(outs)),
        out_shape=list(outs),
        in_specs=[vmem] * (len(sources) + len(maps)),
        out_specs=[vmem] * len(outs),
        compiler_params=pltpu.CompilerParams(vmem_limit_bytes=VMEM_BYTES),
        name="regroup",
    )(*sources, *maps)


def pieces_table(chunks, size, piece, wide, start=0):
    at = np.arange(chunks * wide)
    chunk, place = at // wide, at % wide
    count = size // piece
    table = start + chunk * size + place + piece * np.arange(count)[:, None]
    return np.where(place < piece, table, -1).astype(np.int32)


def run_table(starts, count):
    return (np.asarray(starts)[:, None] + np.arange(count)).astype(np.int32)


def placed(table, at, width):
    out = np.full((table.shape[0], width), -1, np.int32)
    out[:, at : at + table.shape[1]] = table
    return out


def deal_kernel(count, size, first, *refs):
    sources, half_source = refs[:count], refs[count]
    outs, half_out = refs[count + 1 : 2 * count + 1], refs[2 * count + 1]
    own_sem, send_sem, recv_sem, half_own, half_send, half_recv = refs[2 * count + 2 :]
    meet(pack_peers(size))
    wait = start_half(half_source, half_out, size, first, half_own.at[0], half_send, half_recv)
    copies = []
    for i, (source, out) in enumerate(zip(sources, outs)):
        copies += start_deal(
            source, out, size, own_sem.at[i], send_sem, recv_sem, i * (size - 1)
        )
    for copy in copies:
        copy.wait()
    wait()


def deal(arrays, halves, first, collective_id):
    size, count = lax.axis_size("seq"), len(arrays)
    return pl.pallas_call(
        partial(deal_kernel, count, size, first),
        out_shape=[SHAPE(a.shape, a.dtype) for a in arrays]
        + [SHAPE((size,) + halves.shape[1:], halves.dtype)],
        in_specs=[HBM] * (count + 1),
        out_specs=[HBM] * (count + 1),
        scratch_shapes=deal_sems(size, count) + half_sems(size),
        compiler_params=pltpu.CompilerParams(collective_id=collective_id, has_side_effects=True),
        cost_estimate=pl.CostEstimate(flops=0, bytes_accessed=1024, transcendentals=0),
        name="deal",
    )(*arrays, halves)


def spread(slots, me, devices, send, recv):
    copies = []
    for k, device in enumerate(devices):
        copies.append(remote(slots.at[me], slots.at[me], send.at[k], recv.at[k], device))
        copies[-1].start()
    for copy in copies:
        copy.wait()
    total = slots[0]
    for i in range(1, slots.shape[0]):
        total = total + slots[i]
    return total


def last_kernel(sizes, count, *refs):
    sources, half_source, in_ref = refs[:count], refs[count], refs[count + 1]
    outs, half_out, out_ref = refs[count + 2 : 2 * count + 2], *refs[2 * count + 2 : 2 * count + 4]
    refs = refs[2 * count + 4 :]
    one, two, send_one, recv_one, send_two, recv_two, own_sem, send_sem, recv_sem = refs[:9]
    half_own, half_send, half_recv = refs[9:]
    seq, fsdp = lax.axis_index("seq"), lax.axis_index("fsdp")
    across = [(lax.rem(seq + k, sizes[0]), fsdp) for k in range(1, sizes[0])]
    along = [(seq, lax.rem(fsdp + k, sizes[1])) for k in range(1, sizes[1])]
    meet(across + along)
    one[seq] = in_ref[...]
    two[fsdp] = spread(one, seq, across, send_one, recv_one)
    wait = start_half(half_source, half_out, sizes[0], 0, half_own.at[0], half_send, half_recv)
    copies = []
    for i, (source, out) in enumerate(zip(sources, outs)):
        copies += start_deal(
            source, out, sizes[0], own_sem.at[i], send_sem, recv_sem, i * (sizes[0] - 1)
        )
    out_ref[...] = spread(two, fsdp, along, send_two, recv_two)
    for copy in copies:
        copy.wait()
    wait()


def last_exchange(arrays, halves, block, collective_id):
    sizes, count = (lax.axis_size("seq"), lax.axis_size("fsdp")), len(arrays)
    return pl.pallas_call(
        partial(last_kernel, sizes, count),
        out_shape=[SHAPE(a.shape, a.dtype) for a in arrays]
        + [SHAPE((sizes[0],) + halves.shape[1:], halves.dtype), SHAPE(block.shape, block.dtype)],
        in_specs=[HBM] * (count + 1) + [VMEM],
        out_specs=[HBM] * (count + 1) + [VMEM],
        scratch_shapes=[pltpu.VMEM((n,) + block.shape, F32) for n in sizes]
        + [pltpu.SemaphoreType.DMA((n - 1,)) for n in sizes for _ in range(2)]
        + deal_sems(sizes[0], count)
        + half_sems(sizes[0]),
        compiler_params=pltpu.CompilerParams(collective_id=collective_id, has_side_effects=True),
        cost_estimate=pl.CostEstimate(flops=0, bytes_accessed=1024, transcendentals=0),
        name="last_exchange",
    )(*arrays, halves, block)


def gather_kernel(size, tok, own, whole, own_sem, send, recv):
    meet(pack_peers(size))
    relay = Relay(tok, own, whole, own_sem, send, recv)
    relay.start()
    relay.pass_on()
    relay.finish()


def gather_rows(own, micro, collective_id):
    size, rows = lax.axis_size("seq"), own.shape[0]
    return pl.pallas_call(
        partial(gather_kernel, size, rows // micro),
        out_shape=SHAPE((rows * size, own.shape[1]), own.dtype),
        in_specs=[HBM],
        out_specs=HBM,
        scratch_shapes=[pltpu.SemaphoreType.DMA((micro,))] + crossing_sems(),
        compiler_params=pltpu.CompilerParams(collective_id=collective_id, has_side_effects=True),
        name="gather_rows",
    )(own)


def spans_of(width, most=512):
    return [(low, min(low + most, width)) for low in range(0, width, most)]


def joined(blocks, out):
    wide = blocks.shape[2]
    for i in range(blocks.shape[0]):
        out[:, i * wide : (i + 1) * wide] = blocks[i]
    return out


def mixer_kernel(size, tok, micro, *refs):
    context, ssm_out, sums_ref, x_ref, gain_att, gain_ssm, gain_ffn, w_att, w_ssm = refs[:9]
    att, ssm, scale_att, scale_ssm, hidden, mixer, ffn = refs[9:16]
    sums, sent, got, ffn_own, sums_send, sums_recv, send, recv, own_sem, ffn_send, ffn_recv = refs[
        16:-1
    ]
    w_att = joined(w_att, refs[-1])
    here, row = lax.axis_index("seq"), lax.axis_index("fsdp")
    peers = pack_peers(size)
    meet(peers)
    sums[here] = sums_ref[...]
    copies = [
        remote(sums.at[here], sums.at[here], sums_send.at[k], sums_recv.at[k], peer)
        for k, peer in enumerate(peers)
    ]
    for copy in copies:
        copy.start()
    for copy in copies:
        copy.wait()
    total = sums[0]
    for i in range(1, size):
        total = total + sums[i]
    place = lax.broadcasted_iota(jnp.int32, (8, LANES), 0)
    for kind, scale, width in ((0, scale_att, ATT), (1, scale_ssm, INNER)):
        column = lax.dot_general(
            total,
            (place == kind).astype(F32),
            (((0,), (0,)), ((), ())),
            precision=lax.Precision.HIGHEST,
            preferred_element_type=F32,
        )
        scale[...] = lax.rsqrt(column / width + EPS)
    att[...] = (context[...] * scale_att[:, :1] * gain_att[...]).astype(BF)
    ssm[...] = (ssm_out[...] * scale_ssm[:, :1] * gain_ssm[...]).astype(BF)

    def product(d, low, high):
        left = [jnp.concatenate([ref[block_rows(size, tok, m, d)] for m in range(micro)]) for ref in (att, ssm)]
        return 0.5 * (
            dot(left[0], w_att[:, low:high], 1, 0) + dot(left[1], w_ssm[:, low:high], 1, 0)
        )

    gathering = Gathering(tok, sent, got, send, recv)
    for k in range(3):
        for low, high in spans_of(D):
            sent[k, :, low:high] = product(gathering.device(k), low, high).astype(BF)
        gathering.send(k)
    gathering.add(3)
    for low, high in spans_of(D):
        mixer[:, low:high] = product(here, low, high)
    gathering.finish()
    for m in range(micro):
        rows = pl.ds(m * tok, tok)
        out = gathering.total(m, mixer[rows])
        mixer[rows] = out
        whole = x_ref[rows].astype(F32) + out
        hidden[rows] = whole
        scale = lax.rsqrt(jnp.mean(whole * whole, axis=-1, keepdims=True) + EPS)
        ffn_own[rows] = (whole * scale * gain_ffn[...]).astype(BF)
    relay = Relay(tok, ffn_own, ffn, own_sem, ffn_send, ffn_recv)
    relay.start()
    relay.pass_on()
    relay.finish()


def mixer_rows(context, ssm_out, sums, x_own, gains, w_att, w_ssm, micro, collective_id):
    size = lax.axis_size("seq")
    own = x_own.shape[0]
    rows, tok = own * size, own // micro
    vmem, hbm = pl.BlockSpec(memory_space=pltpu.VMEM), pl.BlockSpec(memory_space=pl.ANY)
    shape = jax.ShapeDtypeStruct
    dma = pltpu.SemaphoreType.DMA
    return pl.pallas_call(
        partial(mixer_kernel, size, tok, micro),
        out_shape=[
            shape((rows, w_att.shape[1]), BF),
            shape((rows, w_ssm.shape[0]), BF),
            shape((rows, LANES), F32),
            shape((rows, LANES), F32),
            shape((own, D), F32),
            shape((own, D), F32),
            shape((rows, D), BF),
        ],
        in_specs=[vmem] * 9,
        out_specs=[vmem] * 6 + [hbm],
        scratch_shapes=[
            pltpu.VMEM((size,) + sums.shape, F32),
            pltpu.VMEM((size - 1, own, D), BF),
            pltpu.VMEM((6, tok, D), BF),
            pltpu.VMEM((own, D), BF),
            dma((size - 1,)),
            dma((size - 1,)),
            *crossing_sems(),
            dma((micro,)),
            *crossing_sems(),
            pltpu.VMEM((w_att.shape[1], D), BF),
        ],
        compiler_params=pltpu.CompilerParams(
            collective_id=collective_id, has_side_effects=True, vmem_limit_bytes=VMEM_BYTES
        ),
        name="mixer_rows",
    )(context, ssm_out, sums, x_own, *gains, w_att, w_ssm)


def ffn_kernel(size, tok, micro, *refs):
    ffn, cot, hidden, cot_own, gain, w_gu, w_down = refs[:7]
    act, dgu, down, d_hidden, d_gain, dmix, grad = refs[7:14]
    sent, got, dmix_own, send, recv, own_sem, dmix_send, dmix_recv, turned = refs[14:]
    here, row = lax.axis_index("seq"), lax.axis_index("fsdp")
    wide = w_down.shape[0]
    meet(pack_peers(size))

    gathering = Gathering(tok, sent, got, send, recv)

    def block(k, carry):
        d = gathering.device(k)
        spots = [block_rows(size, tok, m, d) for m in range(micro)]
        gathering.add(k)
        rows_in = jnp.concatenate([ffn[spot] for spot in spots])
        cots = jnp.concatenate([cot[spot] for spot in spots])
        for low, high in spans_of(wide):
            gate = dot(rows_in, w_gu[:, low:high], 1, 0)
            up = dot(rows_in, w_gu[:, wide + low : wide + high], 1, 0)
            d_act = dot(cots, w_down[low:high, :], 1, 1)
            sig = 1.0 / (1.0 + jnp.exp(-gate))
            silu = gate * sig
            pieces = (
                (act, low, silu * up),
                (dgu, low, d_act * up * (sig * (1.0 + gate - silu))),
                (dgu, wide + low, d_act * silu),
            )
            for ref, at, values in pieces:
                values = values.astype(BF)
                for m, spot in enumerate(spots):
                    ref[spot, at : at + high - low] = values[m * tok : (m + 1) * tok]
        d_all = jnp.concatenate([dgu[spot] for spot in spots])
        for low, high in spans_of(D):
            sent[k, :, low:high] = dot(d_all, w_gu[low:high, :], 1, 1).astype(BF)
        gathering.send(k)
        acts = jnp.concatenate([act[spot] for spot in spots])
        for low, high in spans_of(D):
            down[d, :, low:high] = dot(acts, w_down[:, low:high], 1, 0).astype(BF)
        return carry

    lax.fori_loop(0, size, block, 0)
    gathering.finish()
    gain_sum = jnp.zeros((1, D), F32)
    for m in range(micro):
        rows = pl.ds(m * tok, tok)
        d_in = gathering.total(m, sent[size - 1, rows].astype(F32))
        whole = hidden[rows]
        scale = lax.rsqrt(jnp.mean(whole * whole, axis=-1, keepdims=True) + EPS)
        normal = whole * scale
        gain_sum = gain_sum + jnp.sum(d_in * normal, axis=0, keepdims=True)
        scaled = d_in * gain[...]
        inward = jnp.mean(scaled * normal, axis=-1, keepdims=True)
        out = cot_own[rows].astype(F32) + scale * (scaled - normal * inward)
        d_hidden[rows] = out
        dmix_own[rows] = out.astype(BF)
    d_gain[...] = gain_sum
    relay = Relay(tok, dmix_own, dmix, own_sem, dmix_send, dmix_recv)
    relay.start()
    for low, high in spans_of(D, 2 * LANES):
        turned[low:high, :] = ffn[:, low:high].T

    def columns(j, carry):
        span = pl.ds(pl.multiple_of(j * 2 * LANES, 2 * LANES), 2 * LANES)
        for low, high in spans_of(D):
            grad[low:high, span] = dot(turned[low:high, :], dgu[:, span], 1, 0).astype(BF)
        return carry

    pieces = 2 * wide // (2 * LANES)
    lax.fori_loop(0, pieces // 4, columns, 0)
    relay.pass_on()
    lax.fori_loop(pieces // 4, pieces, columns, 0)
    relay.finish()


def ffn_rows(ffn, cot, hidden, cot_own, gain, w_gu, w_down, micro, collective_id):
    size = lax.axis_size("seq")
    own, rows = hidden.shape[0], ffn.shape[0]
    wide = w_down.shape[0]
    tok = own // micro
    vmem, hbm = pl.BlockSpec(memory_space=pltpu.VMEM), pl.BlockSpec(memory_space=pl.ANY)
    shape = jax.ShapeDtypeStruct
    dma = pltpu.SemaphoreType.DMA
    return pl.pallas_call(
        partial(ffn_kernel, size, tok, micro),
        out_shape=[
            shape((rows, wide), BF),
            shape((rows, 2 * wide), BF),
            shape((size, own, D), BF),
            shape((own, D), F32),
            shape((1, D), F32),
            shape((rows, D), BF),
            shape((D, 2 * wide), BF),
        ],
        in_specs=[vmem] * 7,
        out_specs=[vmem] * 5 + [hbm, vmem],
        scratch_shapes=[
            pltpu.VMEM((size, own, D), BF),
            pltpu.VMEM((6, tok, D), BF),
            pltpu.VMEM((own, D), BF),
            *crossing_sems(),
            dma((micro,)),
            *crossing_sems(),
            pltpu.VMEM((D, rows), BF),
        ],
        compiler_params=pltpu.CompilerParams(
            collective_id=collective_id, has_side_effects=True, vmem_limit_bytes=VMEM_BYTES
        ),
        name="ffn_rows",
    )(ffn, cot, hidden, cot_own, gain, w_gu, w_down)


def attention_kernel(most, at_k, opened_ref, position_ref, context, probs, sums):
    s, size = lax.axis_index("seq"), lax.axis_size("seq")
    first = (HEADS * s + size - 1) // size
    last = (HEADS * (s + 1) + size - 1) // size
    pack = position_ref.shape[0]
    at = 4 * HEAD
    in_ref = opened_ref.at[:, at_k : at_k + (4 + most) * HEAD]
    rows = lax.broadcasted_iota(jnp.int32, (pack, pack), 0)
    columns = lax.broadcasted_iota(jnp.int32, (pack, pack), 1)
    visible = (columns <= rows) & (columns >= rows - position_ref[...])
    for h in range(most):
        low = (first + h) // (HEADS // KV_HEADS) <= s
        q = in_ref[:, at + h * HEAD : at + (h + 1) * HEAD]
        key = jnp.where(low, in_ref[:, :HEAD], in_ref[:, HEAD : 2 * HEAD])
        value = jnp.where(low, in_ref[:, 2 * HEAD : 3 * HEAD], in_ref[:, 3 * HEAD : 4 * HEAD])
        masked = jnp.where(visible, dot(q, key, 1, 1) * 0.125, -1e30)
        terms = jnp.exp(masked - jnp.max(masked, axis=1, keepdims=True))
        prob = terms / jnp.sum(terms, axis=1, keepdims=True)
        probs[h] = prob
        out = dot(prob.astype(BF), value, 1, 0)
        context[:, h * HEAD : (h + 1) * HEAD] = jnp.where(first + h < last, out, 0.0)
    held = context[...]
    sums[...] = row_sums(held * held)


def attention(opened, at_k, position, most, micro):
    rows, wide = opened.shape
    pack = rows // micro
    return pl.pallas_call(
        partial(attention_kernel, most, at_k),
        grid=(micro,),
        out_shape=[
            SHAPE((rows, most * HEAD), F32),
            SHAPE((micro, most, pack, pack), F32),
            SHAPE((8, rows), F32),
        ],
        in_specs=[
            pl.BlockSpec((pack, wide), lambda m: (m, 0)),
            pl.BlockSpec((pack, 1), lambda m: (m, 0)),
        ],
        out_specs=[
            pl.BlockSpec((pack, most * HEAD), lambda m: (m, 0)),
            pl.BlockSpec((None, most, pack, pack), lambda m: (m, 0, 0, 0)),
            pl.BlockSpec((8, pack), lambda m: (0, m)),
        ],
        compiler_params=pltpu.CompilerParams(vmem_limit_bytes=VMEM_BYTES),
        name="attention",
    )(opened, position)


def sum_slots(slots, send, recv):
    here, row = lax.axis_index("seq"), lax.axis_index("fsdp")
    copies = [
        remote(slots.at[here], slots.at[here], send.at[k], recv.at[k], peer)
        for k, peer in enumerate(pack_peers(slots.shape[0]))
    ]
    for copy in copies:
        copy.start()
    for copy in copies:
        copy.wait()
    total = slots[0].astype(F32)
    for i in range(1, slots.shape[0]):
        total = total + slots[i].astype(F32)
    return total


def taps_of(inner, position, taps, bias):
    shifted = [inner]
    for k in range(1, CONV):
        shifted.append(jnp.where(position >= k, pltpu.roll(inner, k, axis=0), 0.0))
    conv = bias
    for k in range(CONV):
        conv = conv + taps[k : k + 1] * shifted[k]
    return conv, shifted


def ssm_open_kernel(
    size, micro, opened_ref, position_ref, taps, bias, w_x, w_dt, dt_bias, u_ref, lin_ref, proj_ref, bc_ref, slots, send, recv
):
    meet(pack_peers(size))
    steps = opened_ref.shape[0] // micro
    for m in range(micro):
        rows = pl.ds(m * steps, steps)
        for low, high in spans_of(w_x.shape[1], LANES):
            inner = opened_ref[rows, low:high].astype(F32)
            conv, _ = taps_of(inner, position_ref[rows], taps[:, low:high], bias[:, low:high])
            u_ref[rows, low:high] = conv * sigmoid(conv)
    slots[lax.axis_index("seq")] = dot(w_x[...], u_ref[...].astype(BF), 1, 1).astype(BF)
    proj = sum_slots(slots, send, recv).astype(BF)
    proj_ref[...] = proj
    bc_ref[...] = proj[: 2 * STATE]
    lin_ref[...] = dot(proj[2 * STATE :], w_dt[...], 0, 0) + dt_bias[...]


def ssm_open(opened, position, taps, bias, w_x, w_dt, dt_bias, micro, collective_id):
    size = lax.axis_size("seq")
    rows = opened.shape[0]
    wide, channels = w_x.shape
    dma = pltpu.SemaphoreType.DMA((size - 1,))
    return pl.pallas_call(
        partial(ssm_open_kernel, size, micro),
        out_shape=[
            SHAPE((rows, channels), F32),
            SHAPE((rows, channels), F32),
            SHAPE((wide, rows), BF),
            SHAPE((2 * STATE, rows), BF),
        ],
        in_specs=[VMEM] * 7,
        out_specs=[VMEM] * 4,
        scratch_shapes=[pltpu.VMEM((size, wide, rows), BF), dma, dma],
        compiler_params=pltpu.CompilerParams(
            collective_id=collective_id, has_side_effects=True, vmem_limit_bytes=VMEM_BYTES
        ),
        name="ssm_open",
    )(opened, position, taps, bias, w_x, w_dt, dt_bias)


def ssm_close_kernel(
    size, micro, count, *refs
):
    dlin_ref, db_ref, dc_ref, du_ref, opened_ref, position_ref, taps, bias, w_x, w_dt = refs[:10]
    helds, (dproj_ref, dinner_ref, sums_ref) = refs[10 : 10 + count], refs[10 + count : 13 + count]
    gots = refs[13 + count : 13 + 2 * count]
    slots, total, send, recv, own_sem, held_send, held_recv = refs[13 + 2 * count :]
    meet(pack_peers(size))
    here = lax.axis_index("seq")
    place = lax.broadcasted_iota(jnp.int32, (STATE, STATE), 0)
    eye = (place == lax.broadcasted_iota(jnp.int32, (STATE, STATE), 1)).astype(F32)
    for i, ref in enumerate((db_ref, dc_ref)):
        turned = lax.dot_general(
            eye,
            ref[...],
            (((1,), (1,)), ((), ())),
            precision=lax.Precision.HIGHEST,
            preferred_element_type=F32,
        )
        slots[here, i * STATE : (i + 1) * STATE] = turned.astype(BF)
    slots[here, 2 * STATE :] = dot(w_dt[...], dlin_ref[...], 1, 1).astype(BF)
    dproj = sum_slots(slots, send, recv).astype(BF)
    copies = []
    for i, (held, got) in enumerate(zip(helds, gots)):
        copies += start_deal(
            held, got, size, own_sem.at[i], held_send, held_recv, i * (size - 1)
        )
    dproj_ref[...] = dproj
    steps = opened_ref.shape[0] // micro
    total[...] = du_ref[...] + dot(dproj, w_x[...], 0, 0)
    for low, high in spans_of(w_x.shape[1], LANES):
        lines = [jnp.zeros((1, high - low), F32) for _ in range(CONV + 1)]
        for m in range(micro):
            rows = pl.ds(m * steps, steps)
            inner = opened_ref[rows, low:high].astype(F32)
            position = position_ref[rows]
            tap = taps[:, low:high]
            conv, shifted = taps_of(inner, position, tap, bias[:, low:high])
            sig = sigmoid(conv)
            d_conv = total[rows, low:high] * (sig * (1.0 + conv * (1.0 - sig)))
            d_inner = tap[0:1] * d_conv
            for k in range(CONV):
                lines[k] = lines[k] + jnp.sum(d_conv * shifted[k], axis=0, keepdims=True)
                if k:
                    masked = jnp.where(position >= k, d_conv, 0.0)
                    d_inner = d_inner + tap[k : k + 1] * pltpu.roll(masked, steps - k, axis=0)
            lines[CONV] = lines[CONV] + jnp.sum(d_conv, axis=0, keepdims=True)
            dinner_ref[rows, low:high] = d_inner.astype(BF)
        sums_ref[:, low:high] = jnp.concatenate(
            lines + [jnp.zeros((8 - CONV - 1, high - low), F32)], axis=0
        )
    for copy in copies:
        copy.wait()


def ssm_close(dlin, db, dc, du, opened, position, taps, bias, w_x, w_dt, helds, micro, collective_id):
    size = lax.axis_size("seq")
    rows = opened.shape[0]
    wide, channels = w_x.shape
    dma = pltpu.SemaphoreType.DMA((size - 1,))
    return pl.pallas_call(
        partial(ssm_close_kernel, size, micro, len(helds)),
        out_shape=[
            SHAPE((wide, rows), BF),
            SHAPE((rows, channels), BF),
            SHAPE((8, channels), F32),
        ]
        + [SHAPE(held.shape, held.dtype) for held in helds],
        in_specs=[VMEM] * 10 + [HBM] * len(helds),
        out_specs=[VMEM] * 3 + [HBM] * len(helds),
        scratch_shapes=[
            pltpu.VMEM((size, wide, rows), BF),
            pltpu.VMEM((rows, channels), F32),
            dma,
            dma,
        ]
        + deal_sems(size, max(1, len(helds))),
        compiler_params=pltpu.CompilerParams(
            collective_id=collective_id, has_side_effects=True, vmem_limit_bytes=VMEM_BYTES
        ),
        name="ssm_close",
    )(dlin, db, dc, du, opened, position, taps, bias, w_x, w_dt, *helds)


def branch_back_kernel(size, *refs):
    dmix, w_att, w_ssm, context, ssm_out, core, u, opened = refs[:8]
    scale_att, scale_ssm, gain_att, gain_ssm, live, skip = refs[8:14]
    d_context, d_core, d_gate, d_gain_att, d_gain_ssm, d_skip = refs[14:20]
    t_att, t_ssm, slots, send, recv, w_whole, gate_ref, gate_sem = refs[20:]
    channels = gate_ref.shape[1]
    fetch = pltpu.make_async_copy(
        opened.at[:, pl.ds(channels, channels)], gate_ref, gate_sem.at[0]
    )
    fetch.start()
    w_att = joined(w_att, w_whole)
    meet(pack_peers(size))
    place = lax.broadcasted_iota(jnp.int32, (8, LANES), 0)
    kinds = (
        (w_att, context, scale_att, gain_att, d_gain_att, t_att),
        (w_ssm, ssm_out, scale_ssm, gain_ssm, d_gain_ssm, t_ssm),
    )
    sums = []
    for w, value, scale, gain, d_gain, t in kinds:
        total = None
        for low, high in spans_of(w.shape[0], 2 * LANES):
            grad = 0.5 * dot(dmix[...], w[low:high, :], 1, 1)
            held = value[:, low:high]
            d_gain[:, low:high] = jnp.sum(grad * held * scale[:, :1], axis=0, keepdims=True)
            scaled = grad * gain[:, low:high]
            t[:, low:high] = scaled
            term = row_sums(scaled * held)
            total = term if total is None else total + term
        sums.append(total)
    rows8 = lax.broadcasted_iota(jnp.int32, sums[0].shape, 0)
    slots[lax.axis_index("seq")] = jnp.where(rows8 == 0, sums[0], sums[1])
    total = sum_slots(slots, send, recv)
    fetch.wait()
    columns = [
        lax.dot_general(
            total,
            (place == kind).astype(F32),
            (((0,), (0,)), ((), ())),
            precision=lax.Precision.HIGHEST,
            preferred_element_type=F32,
        )
        for kind in range(2)
    ]
    scale = scale_att[:, :1]
    inward = scale * scale * scale * (columns[0][:, :1] / ATT)
    d_context[...] = ((t_att[...] * scale - context[...] * inward) * live[...]).astype(BF)
    scale = scale_ssm[:, :1]
    inward = scale * scale * scale * (columns[1][:, :1] / INNER)
    for low, high in spans_of(w_ssm.shape[0], 2 * LANES):
        at = slice(low, high)
        d_out = t_ssm[:, at] * scale - ssm_out[:, at] * inward
        gate = gate_ref[:, at].astype(F32)
        sig = sigmoid(gate)
        silu = gate * sig
        held = d_out * silu
        d_core[:, at] = held
        d_skip[:, at] = jnp.sum(held * u[:, at], axis=0, keepdims=True)
        mixed = core[:, at] + skip[:, at] * u[:, at]
        d_gate[:, at] = (d_out * mixed * (sig * (1.0 + gate - silu))).astype(BF)


def branch_back(
    dmix, w_att, w_ssm, context, ssm_out, core, u, opened, scales, gains, live, skip, collective_id
):
    size = lax.axis_size("seq")
    rows, wide, channels = dmix.shape[0], w_att.shape[1], w_ssm.shape[0]
    dma = pltpu.SemaphoreType.DMA((size - 1,))
    return pl.pallas_call(
        partial(branch_back_kernel, size),
        out_shape=[
            SHAPE((rows, wide), BF),
            SHAPE((rows, channels), F32),
            SHAPE((rows, channels), BF),
            SHAPE((1, wide), F32),
            SHAPE((1, channels), F32),
            SHAPE((1, channels), F32),
        ],
        in_specs=[VMEM] * 7 + [HBM] + [VMEM] * 6,
        out_specs=[VMEM] * 6,
        scratch_shapes=[
            pltpu.VMEM((rows, wide), F32),
            pltpu.VMEM((rows, channels), F32),
            pltpu.VMEM((size, 8, rows), F32),
            dma,
            dma,
        ]
        + [
            pltpu.VMEM((wide, D), BF),
            pltpu.VMEM((rows, channels), BF),
            pltpu.SemaphoreType.DMA((1,)),
        ],
        compiler_params=pltpu.CompilerParams(
            collective_id=collective_id, has_side_effects=True, vmem_limit_bytes=VMEM_BYTES
        ),
        name="branch_back",
    )(dmix, w_att, w_ssm, context, ssm_out, core, u, opened, *scales, *gains, live, skip)


def close_kernel(
    size, tok, micro, rest, d_inner, whole_w, x_ref, gain, d_hidden, dx, d_gain, sent, got, send, recv, w, w_sem
):
    fetch = pltpu.make_async_copy(whole_w.at[:, pl.ds(0, w.shape[1])], w, w_sem.at[0])
    fetch.start()
    here, row = lax.axis_index("seq"), lax.axis_index("fsdp")
    meet(pack_peers(size))

    fetch.wait()
    gathering = Gathering(tok, sent, got, send, recv)

    def block(k, carry):
        d = gathering.device(k)
        spots = [block_rows(size, tok, m, d) for m in range(micro)]
        gathering.add(k)
        rows = jnp.concatenate([d_inner[spot] for spot in spots])
        held = jnp.concatenate([rest[spot] for spot in spots])
        for low, high in spans_of(D):
            part = held[:, low:high].astype(F32) + dot(rows, w[low:high, :], 1, 1)
            sent[k, :, low:high] = part.astype(BF)
        gathering.send(k)
        return carry

    lax.fori_loop(0, size, block, 0)
    gathering.finish()
    gain_sum = jnp.zeros((1, D), F32)
    for m in range(micro):
        rows = pl.ds(m * tok, tok)
        d_in = gathering.total(m, sent[size - 1, rows].astype(F32))
        whole = x_ref[rows].astype(F32)
        scale = lax.rsqrt(jnp.mean(whole * whole, axis=-1, keepdims=True) + EPS)
        normal = whole * scale
        gain_sum = gain_sum + jnp.sum(d_in * normal, axis=0, keepdims=True)
        scaled = d_in * gain[...]
        inward = jnp.mean(scaled * normal, axis=-1, keepdims=True)
        dx[rows] = (d_hidden[rows] + scale * (scaled - normal * inward)).astype(BF)
    d_gain[...] = gain_sum


def close_rows(rest, d_inner, w, x_own, gain, d_hidden, micro, collective_id):
    size = lax.axis_size("seq")
    own = x_own.shape[0]
    dma = pltpu.SemaphoreType.DMA((size - 1,))
    return pl.pallas_call(
        partial(close_kernel, size, own // micro, micro),
        out_shape=[SHAPE((own, D), BF), SHAPE((1, D), F32)],
        in_specs=[VMEM] * 2 + [HBM] + [VMEM] * 3,
        out_specs=[VMEM] * 2,
        scratch_shapes=[
            pltpu.VMEM((size, own, D), BF),
            pltpu.VMEM((6, own // micro, D), BF),
            *crossing_sems(),
            pltpu.VMEM((w.shape[0], d_inner.shape[1]), BF),
            pltpu.SemaphoreType.DMA((1,)),
        ],
        compiler_params=pltpu.CompilerParams(
            collective_id=collective_id, has_side_effects=True, vmem_limit_bytes=VMEM_BYTES
        ),
        name="close_rows",
    )(rest, d_inner, w, x_own, gain, d_hidden)


def squares(row_vals):
    return jnp.sum(row_vals * row_vals)


def local(
    tokens,
    cotangent,
    route,
    lengths,
    gain_in,
    w_qkv,
    w_mix_in,
    w_x,
    w_dt,
    w_small,
    gain_att,
    gain_ssm,
    w_out_att,
    w_out_ssm,
    gain_ffn,
    w_gate,
    w_up,
    w_down,
):
    S, N = lax.axis_size("seq"), lax.axis_size("fsdp")
    s = lax.axis_index("seq")
    micro, tok = tokens.shape[:2]
    pack = tok * S
    rows_d = gain_in.shape[0] // N
    ff = w_gate.shape[1]
    ch_piece, ff_piece = INNER // (N * S), ff // (N * S)
    ch = -(-INNER // (S * LANES)) * LANES
    ffs = -(-ff // (S * LANES)) * LANES
    cols = D // S
    groups = HEADS // KV_HEADS
    first_heads = [(HEADS * i + S - 1) // S for i in range(S + 1)]
    head_counts = [first_heads[i + 1] - first_heads[i] for i in range(S)]
    most = max(head_counts)
    width = most * HEAD
    first_head = jnp.array(first_heads, jnp.int32)[s]
    head_live = jnp.arange(most) < jnp.array(head_counts, jnp.int32)[s]
    live = jnp.repeat(head_live, HEAD).astype(F32)[None, :]
    in_low = (first_head + jnp.arange(most)) // groups <= s

    def gather(shard):
        return lax.all_gather(shard, "fsdp", axis=0, tiled=True)

    def scatter(whole):
        rows, wide = whole.shape[0] // N, whole.shape[1]
        fill = -rows % 8
        whole = whole.astype(BF)
        if fill:
            whole = jnp.pad(whole.reshape(N, rows, wide), ((0, 0), (0, fill), (0, 0)))
            whole = whole.reshape(N * (rows + fill), wide)
        whole = lax.psum_scatter(whole, "fsdp", scatter_dimension=0, tiled=True)
        return lax.optimization_barrier(whole)[:rows]

    def part(shard, axis, chunks, wide):
        shape = shard.shape
        piece = shape[axis] // (chunks * S)
        shaped = shard.reshape(shape[:axis] + (chunks, S, piece) + shape[axis + 1 :])
        picked = lax.dynamic_index_in_dim(shaped, s, axis + 1, keepdims=False)
        fill = [(0, 0)] * picked.ndim
        fill[axis + 1] = (0, wide - piece)
        return jnp.pad(picked, fill).reshape(
            shape[:axis] + (chunks * wide,) + shape[axis + 1 :]
        )

    def span(array, axis, start, size):
        return lax.dynamic_slice_in_dim(array, start, size, axis)

    send_hot, land_hot = routing(route, tok)
    x_own = bring(tokens.reshape(micro * tok, D), send_hot, land_hot)
    q_start = first_head * HEAD
    chw, ffw = ch // N, ffs // N
    q_starts = [h * HEAD for h in first_heads[:S]]
    kv_starts = [ATT + HEAD * i for i in range(S)]
    at_k, at_v, at_q = 2 * ch, 2 * ch + 2 * HEAD, 2 * ch + 4 * HEAD
    at_att = at_q + width
    in_wide = at_att + cols
    mix_table = pieces_table(2 * N, INNER // N, ch_piece, chw)
    in_part = regroup(
        [w_mix_in, w_qkv, w_out_att],
        [jax.ShapeDtypeStruct((rows_d, in_wide), BF)],
        [
            (0, None, 0, 0, placed(mix_table, 0, in_wide)),
            (1, None, 0, 0, placed(run_table(kv_starts, 2 * HEAD), at_k, in_wide)),
            (1, None, 0, 0, placed(run_table([a + KV_WIDTH for a in kv_starts], 2 * HEAD), at_v, in_wide)),
            (2, None, 0, 0, placed(run_table([cols * i for i in range(S)], cols), at_att, in_wide)),
            (1, None, 0, 0, placed(run_table(q_starts, width), at_q, in_wide)),
        ],
    )[0]
    small_part = part(
        jnp.concatenate([w_x, w_dt, w_small, jnp.zeros((w_x.shape[0], 1), BF)], axis=1), 0, 1, chw
    )
    small_wide = small_part.shape[1]
    gathered_in = gather(
        jnp.concatenate([in_part, jnp.pad(small_part, ((0, rows_d - chw), (0, 0)))], axis=1)
    )
    cot_own = bring(cotangent.reshape(micro * tok, D), send_hot, land_hot)
    x_rows = gather_rows(x_own, micro, 3)
    cot_own, x_rows = lax.optimization_barrier((cot_own, x_rows))
    cot_rows = gather_rows(cot_own, micro, 6)
    gathered_in, x_rows, cot_rows = lax.optimization_barrier((gathered_in, x_rows, cot_rows))
    out_piece, gathered_in = lax.optimization_barrier((part(w_out_ssm, 0, 1, chw), gathered_in))
    w_out_part = gather(out_piece)
    w_in = gathered_in[:, :at_att]
    w_att_cols = gathered_in[:, at_att:in_wide]
    w_small_part = (
        gathered_in[:, in_wide:].reshape(N, rows_d, small_wide)[:, :chw].reshape(ch, small_wide)
    )
    ff_table = pieces_table(N, ff // N, ff_piece, ffw)
    gu_part = regroup(
        [w_gate, w_up],
        [jax.ShapeDtypeStruct((rows_d, 2 * ffs), BF)],
        [
            (0, None, 0, 0, placed(ff_table, 0, 2 * ffs)),
            (1, None, 0, 0, placed(ff_table, ffs, 2 * ffs)),
        ],
    )[0]

    w_att_pad = jnp.pad(w_att_cols, ((0, width), (0, 0)))
    w_att_blocks = jnp.stack([w_att_pad[h * HEAD : h * HEAD + width] for h in first_heads[:S]])

    w_x_turned = w_small_part[:, :PROJ].T
    w_x_turned = jnp.pad(
        jnp.concatenate([w_x_turned[DT_RANK:], w_x_turned[:DT_RANK]], axis=0),
        ((0, PROJ_PAD - PROJ), (0, 0)),
    )
    w_dt_turned = jnp.pad(
        w_small_part[:, PROJ : PROJ + DT_RANK].T, ((0, PROJ_PAD - PROJ), (0, 0))
    )
    small_par = w_small_part[:, PROJ + DT_RANK : PROJ + DT_RANK + CONV + 3 + STATE].astype(F32)
    small_lines = small_par.T
    taps = jnp.pad(small_lines[:CONV], ((0, 8 - CONV), (0, 0)))
    conv_b, dt_bias, skip = [small_lines[CONV + i][None] for i in range(3)]
    rates = -jnp.exp(small_lines[CONV + 3 :])
    gain_att_part = span(jnp.pad(gain_att, (0, width)), 0, q_start, width)[None]
    gain_ssm_part = part(gain_ssm, 0, N, ch // N)[None]

    position = jax.vmap(lambda one: seq_layout(one, pack)[1])(lengths[:, 0])
    position = position.reshape(micro * pack, 1)

    normed_low = rms_scale(x_rows.astype(F32), gain_in).astype(BF)
    opened = dot(normed_low, w_in, 1, 0).astype(BF)
    opened, gu_part, down_part = lax.optimization_barrier(
        (opened, gu_part, part(w_down, 0, 1, ffw))
    )
    w_gu, w_down_part = gather(gu_part), gather(down_part)
    u, lin, projected, bc = ssm_open(
        opened, position, taps, conv_b, w_x_turned, w_dt_turned, dt_bias, micro, 7
    )
    q = opened[:, at_q:].reshape(micro, pack, most, HEAD)
    kv = opened[:, at_k:at_q].reshape(micro, pack, 4, HEAD)
    pick_low = in_low[None, None, :, None]
    keys = jnp.where(pick_low, kv[:, :, 0:1], kv[:, :, 1:2])
    values = jnp.where(pick_low, kv[:, :, 2:3], kv[:, :, 3:4])
    context, probs, att_sums = attention(opened, at_k, position, most, micro)
    bc = jnp.broadcast_to(bc.T[:, :, None], (micro * pack, 2 * STATE, LANES))
    core, ssm_out, ssm_sums, w_att_part = scan_forward(
        u, lin, bc, rates, position, opened, skip, w_att_blocks, micro, 11
    )
    sums = jnp.stack([att_sums[0], ssm_sums[0]])
    att_low, ssm_low, scale_att, scale_ssm, hidden, mixer_out, ffn_low = mixer_rows(
        context,
        ssm_out,
        jnp.pad(sums, ((0, 6), (0, 0))),
        x_own,
        (gain_att_part, gain_ssm_part, gain_ffn[None]),
        w_att_part,
        w_out_part,
        micro,
        4,
    )
    act_low, _, down_parts, d_hidden, d_gain_ffn, dmix_low, gu_whole = ffn_rows(
        ffn_low, cot_rows, hidden, cot_own, gain_ffn[None], w_gu, w_down_part, micro, 5
    )

    r_gu = scatter(gu_whole)
    down_whole = dot(act_low, cot_rows, 0, 0).astype(BF)
    dmix_low, down_whole = lax.optimization_barrier((dmix_low, down_whole))
    r_down = scatter(down_whole)
    d_context, d_core, d_gate_z, d_gain_att, d_gain_ssm, d_skip = branch_back(
        dmix_low,
        w_att_part,
        w_out_part,
        context,
        ssm_out,
        core,
        u,
        opened,
        (scale_att, scale_ssm),
        (gain_att_part, gain_ssm_part),
        live,
        skip,
        8,
    )
    ssm_whole = (0.5 * dot(ssm_low, dmix_low, 0, 0)).astype(BF)
    g_att_rows = (0.5 * dot(att_low, dmix_low, 0, 0)).astype(BF)
    att_blocks = g_att_rows.reshape(width, S, cols).transpose(1, 0, 2)
    dctx_low = d_context.reshape(micro, pack, most, HEAD)
    d_values = jnp.einsum(
        "mhtu,mthd->muhd", probs.astype(BF), dctx_low, preferred_element_type=F32
    )
    d_probs = jnp.einsum("mthd,muhd->mhtu", dctx_low, values, preferred_element_type=F32)
    dscore_low = (
        probs * (d_probs - jnp.sum(probs * d_probs, axis=-1, keepdims=True))
    ).astype(BF)
    d_q = jnp.einsum("mhtu,muhd->mthd", dscore_low, keys, preferred_element_type=F32) * 0.125
    d_keys = jnp.einsum("mhtu,mthd->muhd", dscore_low, q, preferred_element_type=F32) * 0.125

    def kv_sum(d_heads):
        return [
            jnp.sum(jnp.where(pick_low, d_heads, 0.0), axis=2),
            jnp.sum(jnp.where(pick_low, 0.0, d_heads), axis=2),
        ]

    d_rest = jnp.concatenate(
        [d_gate_z]
        + [
            one.astype(BF).reshape(micro * pack, -1)
            for one in kv_sum(d_keys) + kv_sum(d_values) + [d_q]
        ],
        axis=1,
    )
    rest_whole = dot(normed_low, d_rest, 0, 0).astype(BF)
    d_rest, rest_whole = lax.optimization_barrier((d_rest, rest_whole))
    rest_rows = dot(d_rest, gathered_in[:, ch:at_att], 1, 1).astype(BF)
    d_core, r_gu, ssm_whole, rest_whole, rest_rows = lax.optimization_barrier(
        (d_core, r_gu, ssm_whole, rest_whole, rest_rows)
    )
    r_ssm, r_rest = scatter(ssm_whole), scatter(rest_whole)
    per = N // S
    gate_take = np.concatenate([np.arange(ff_piece) + ffw * i for i in range(per)])
    half_wide = -(-per * ff_piece // LANES) * LANES
    moves = []
    for d in range(S):
        for i in range(2):
            table = gate_take[None] + d * per * ffw + i * ffs
            moves.append((0, None, 0, d, placed(table, i * half_wide, 2 * half_wide)))
    (gu_blocks,) = regroup([r_gu], [SHAPE((S, rows_d, 2 * half_wide), BF)], moves)
    d_u, d_lin, d_dt_bias, d_rates, d_in_b, d_out_c, (ffn_got, gu_got, g_att_blocks) = (
        scan_backward(
            d_core, u, lin, bc, rates, position, skip, [down_parts, gu_blocks, att_blocks], micro, 0
        )
    )
    ffn_out = jnp.sum(ffn_got.astype(F32), axis=0)
    result = hidden + ffn_out
    outputs = give(result.astype(BF), send_hot, land_hot)
    g_att_whole = jnp.concatenate(
        [g_att_blocks[i, : head_counts[i] * HEAD] for i in range(S)], axis=0
    )
    dproj_low, d_inner, conv_sums = ssm_close(
        d_lin,
        d_in_b,
        d_out_c,
        d_u,
        opened,
        position,
        taps,
        conv_b,
        w_x_turned,
        w_dt_turned,
        [],
        micro,
        9,
    )
    g_x = dot(u.astype(BF), dproj_low, 0, 1)
    small_whole = jnp.concatenate(
        [
            g_x[:, 2 * STATE : PROJ],
            g_x[:, : 2 * STATE],
            dot(d_lin, projected[2 * STATE : PROJ], 0, 1),
            conv_sums[: CONV + 1].T,
            d_dt_bias[:, None],
            d_skip[0][:, None],
            (d_rates * rates).T,
            jnp.zeros((ch, 1), F32),
        ],
        axis=1,
    ).astype(BF)
    small_whole = jnp.pad(
        small_whole.reshape(N, chw, small_wide), ((0, 0), (0, rows_d - chw), (0, 0))
    ).reshape(N * rows_d, small_wide)
    last_whole = jnp.concatenate(
        [dot(normed_low, d_inner, 0, 0).astype(BF), g_att_whole, small_whole], axis=1
    )
    ff_mine = ff // S
    moves = []
    at = np.arange(ff_mine)
    for source in range(S):
        chunk, inside = at // (S * ff_piece), at % (S * ff_piece)
        table = np.where(
            inside // ff_piece == source, chunk * ff_piece + inside % ff_piece, -1
        )[None].astype(np.int32)
        moves.append((0, source, 0, 0, table))
        moves.append((0, source, 1, 0, np.where(table >= 0, table + half_wide, -1)))
    out_gate, out_up = regroup(
        [gu_got], [jax.ShapeDtypeStruct((rows_d, ff_mine), F32)] * 2, moves
    )

    d_inner, last_whole, r_rest, out_gate, out_up = lax.optimization_barrier(
        (d_inner, last_whole, r_rest, out_gate, out_up)
    )
    r_last = scatter(last_whole)
    dx, d_gain_in = close_rows(
        rest_rows, d_inner, gathered_in, x_own, gain_in[None], d_hidden, micro, 10
    )

    att_at = lax.dynamic_update_slice_in_dim(
        jnp.zeros((ATT + width,), F32), d_gain_att[0] * live[0], q_start, 0
    )[:ATT]
    ssm_at = lax.dynamic_update_index_in_dim(
        jnp.zeros((N, S, ch_piece), F32), d_gain_ssm[0].reshape(N, -1)[:, :ch_piece], s, 1
    ).reshape(INNER)
    stats = jnp.stack(
        [
            squares(x_own.astype(F32)),
            jnp.sum(sums[0]),
            jnp.sum(sums[1]),
            squares(mixer_out),
            squares(ffn_out),
            squares(result),
        ]
    )
    ends = np.cumsum([0, D, ATT, INNER, D, 6])
    line = jnp.concatenate([jnp.zeros((D,), F32), att_at, ssm_at, d_gain_ffn[0], stats])
    line = jnp.pad(line, (0, -line.shape[0] % 1024))
    line, d_gain_in = lax.optimization_barrier((line, d_gain_in))
    line = lax.dynamic_update_slice(line, d_gain_in[0], (0,)).reshape(-1, LANES)
    moves = []
    for d in range(S):
        moves.append((0, None, 0, d, run_table([d * cols], cols)))
        moves.append((1, None, 1, d, run_table([d * cols], cols)))
    qkv_wide = (ATT + 2 * KV_WIDTH) // S
    starts = np.array(q_starts)[:, None]
    counts = np.array(head_counts)[:, None] * HEAD
    base = np.array(kv_starts)[:, None]
    for d in range(S):
        column = np.arange(qkv_wide)[None] + d * qkv_wide
        table = np.full((S, qkv_wide), -1)
        for low, count, source in (
            (starts, counts, at_q),
            (base, 2 * HEAD, at_k),
            (base + KV_WIDTH, 2 * HEAD, at_v),
        ):
            inside = (column >= low) & (column < low + count)
            table = np.where(inside, column - low + source - ch, table)
        moves.append((2, None, 2, d, table.astype(np.int32)))
    mix_mine = 2 * INNER // S
    at = np.arange(mix_mine // S)
    mix_tables = [
        ((at // ch_piece + j * (2 * N // S)) * chw + at % ch_piece)[None].astype(np.int32)
        for j in range(S // 2)
    ]
    for j in range(S // 2):
        moves.append((2, None, 3, j, mix_tables[j]))
    dx, r_ssm, r_down, r_rest = lax.optimization_barrier((dx, r_ssm, r_down, r_rest))
    (*row_blocks, gate_blocks) = regroup(
        [r_ssm, r_down, r_rest],
        [
            SHAPE((S, r_ssm.shape[0], cols), BF),
            SHAPE((S, r_down.shape[0], cols), BF),
            SHAPE((S, rows_d, qkv_wide), BF),
            SHAPE((S // 2, rows_d, mix_mine // S), BF),
        ],
        moves,
    )
    row_blocks, gate_blocks, dx = lax.optimization_barrier((row_blocks, gate_blocks, dx))
    ssm_got, down_got, qkv_got, gate_got = deal(row_blocks, gate_blocks, S // 2, 1)
    input_grads = give(dx, send_hot, land_hot)
    ssm_got, r_last = lax.optimization_barrier((ssm_got, r_last))
    out_ssm = ssm_got[:, :ch_piece].reshape(S * ch_piece, cols).astype(F32)
    out_down = down_got[:, :ff_piece].reshape(S * ff_piece, cols).astype(F32)
    (inner_blocks,) = regroup(
        [r_last],
        [SHAPE((S // 2, rows_d, mix_mine // S), BF)],
        [(0, None, 0, j, mix_tables[j]) for j in range(S // 2)],
    )
    r_small = r_last[:chw, ch + cols :]
    small_got, inner_got, sums_all = last_exchange(
        [jnp.broadcast_to(r_small, (S,) + r_small.shape)], inner_blocks, line, 2
    )
    out_qkv = jnp.sum(qkv_got.astype(F32), axis=0)
    moves = []
    at = np.arange(mix_mine)
    for source in range(S):
        chunk, inside = at // (S * ch_piece), at % (S * ch_piece)
        table = np.where(
            inside // ch_piece == source, chunk * ch_piece + inside % ch_piece, -1
        )[None].astype(np.int32)
        moves.append((0, source, 0, 0, table))
    (out_mix,) = regroup(
        [jnp.where(s < S // 2, inner_got, gate_got)], [SHAPE((rows_d, mix_mine), F32)], moves
    )
    g_att = r_last[:, ch : ch + cols].astype(F32)
    small_all = small_got[:, :ch_piece].reshape(S * ch_piece, small_wide).astype(F32)
    out_x = span(small_all[:, :PROJ], 1, s * (PROJ // S), PROJ // S)
    out_dt = span(small_all[:, PROJ : PROJ + DT_RANK], 1, s * (DT_RANK // S), DT_RANK // S)
    out_small = small_all[:, PROJ + DT_RANK : PROJ + DT_RANK + CONV + 3 + STATE]

    sums = sums_all.reshape(-1)
    g_gain_in, g_gain_att, g_gain_ssm, g_gain_ffn, stat_sum = [
        sums[a:b] for a, b in zip(ends[:-1], ends[1:])
    ]
    widths = jnp.array([D, ATT, INNER, D, D, D], F32)
    rms = jnp.sqrt(stat_sum / (widths * (micro * pack * N)))
    return (
        outputs.reshape(tokens.shape),
        input_grads.reshape(tokens.shape),
        g_gain_in,
        out_qkv,
        out_mix,
        out_x,
        out_dt,
        out_small,
        out_small[:, CONV + 1],
        g_gain_att,
        g_gain_ssm,
        g_att,
        out_ssm,
        g_gain_ffn,
        out_gate,
        out_up,
        out_down,
        rms,
    )


def solution(mesh):
    rows = P(None, ("seq", "fsdp"), None)
    shard = P("fsdp", None)
    both = P("fsdp", "seq")
    placed = (rows, rows, P(None, "seq"), P(None, "fsdp", None), P())
    placed += (shard,) * 5 + (P(), P(), shard, shard, P(), shard, shard, shard)
    return jax.shard_map(
        local,
        mesh=mesh,
        in_specs=placed,
        out_specs=(
            rows,
            rows,
            P(),
            both,
            both,
            both,
            both,
            shard,
            P("fsdp"),
            P(),
            P(),
            both,
            both,
            P(),
            both,
            both,
            both,
            P(),
        ),
        check_vma=False,
    )
```

```python
from functools import partial

import jax
import jax.numpy as jnp
import numpy as np
from jax import lax
from jax.experimental import pallas as pl
from jax.experimental.pallas import tpu as pltpu
from jax.sharding import PartitionSpec as P

D = 1600
HEADS = 25
KV_HEADS = 5
HEAD = 64
INNER = 3200
STATE = 16
CONV = 4
DT_RANK = 100
MICRO = 2
ATT = 1600
KV_WIDTH = 320
PROJ = DT_RANK + 2 * STATE
PROJ_PAD = 144
LANES = 128
EPS = 1e-05
BF = jnp.bfloat16
F32 = jnp.float32


def dot(left_op, right_op, left_dim, right_dim):
    return lax.dot_general(
        left_op, right_op, (((left_dim,), (right_dim,)), ((), ())), preferred_element_type=F32
    )


def rms_scale(row_vals, gain_vec):
    return (
        row_vals * lax.rsqrt(jnp.mean(row_vals * row_vals, axis=-1, keepdims=True) + EPS) * gain_vec
    )


def seq_layout(seq_lens, span_len):
    places = jnp.arange(span_len, dtype=jnp.int32)
    seq_ends = jnp.cumsum(seq_lens)
    segment = jnp.sum((places[:, None] >= seq_ends[None, :]).astype(jnp.int32), axis=1)
    starts = seq_ends - seq_lens
    picked = (segment[:, None] == jnp.arange(seq_lens.shape[0], dtype=jnp.int32)[None, :]).astype(
        jnp.int32
    )
    position = places - jnp.sum(picked * starts[None, :], axis=1)
    return (segment, position)


def swap(array, k):
    size = lax.axis_size("seq")
    return lax.ppermute(array, "seq", [(i, i ^ k) for i in range(size)])


def pick(blocks, at):
    return lax.dynamic_index_in_dim(blocks, at, 0, keepdims=False)


def seq_deal(blocks):
    size, here = lax.axis_size("seq"), lax.axis_index("seq")
    out = blocks
    for k in range(1, size):
        there = here ^ k
        out = lax.dynamic_update_index_in_dim(out, swap(pick(blocks, there), k), there, 0)
    return out


def seq_gather(block):
    size, here = lax.axis_size("seq"), lax.axis_index("seq")
    out = lax.dynamic_update_index_in_dim(
        jnp.zeros((size,) + block.shape, block.dtype), block, here, 0
    )
    for k in range(1, size):
        out = lax.dynamic_update_index_in_dim(out, swap(block, k), here ^ k, 0)
    return out


def seq_scatter(blocks):
    size, here = lax.axis_size("seq"), lax.axis_index("seq")
    total = pick(blocks, here).astype(F32)
    for k in range(1, size):
        total = total + swap(pick(blocks, here ^ k).astype(BF), k).astype(F32)
    return total


def seq_sum(array):
    return jnp.sum(seq_gather(array).astype(F32), axis=0)


def routing(route_rows, tok_rows):
    fsdp_count, fsdp_rank = lax.axis_size("fsdp"), lax.axis_index("fsdp")
    micro = route_rows.shape[0]
    per_peer = tok_rows // fsdp_count
    target_dev = (route_rows // tok_rows).reshape(micro, fsdp_count, tok_rows)
    target_slot = (route_rows % tok_rows).reshape(micro, fsdp_count, tok_rows)
    steps = jnp.arange(tok_rows, dtype=jnp.int32)
    same = target_dev[:, :, :, None] == target_dev[:, :, None, :]
    earlier = steps[None, :] < steps[:, None]
    rank = jnp.sum((same & earlier).astype(jnp.int32), axis=3)
    my_dev = lax.dynamic_index_in_dim(target_dev, fsdp_rank, 1, keepdims=False)
    my_rank = lax.dynamic_index_in_dim(rank, fsdp_rank, 1, keepdims=False)
    micros = jnp.arange(micro, dtype=jnp.int32)
    send_at = (my_dev * micro + micros[:, None]) * per_peer + my_rank
    ranks = jnp.arange(per_peer, dtype=jnp.int32)
    mine = (target_dev == fsdp_rank)[:, :, None, :] & (rank[:, :, None, :] == ranks[:, None])
    slot = jnp.sum(mine.astype(jnp.int32) * target_slot[:, :, None, :], axis=3)
    land_at = (micros[:, None, None] * tok_rows + slot).transpose(1, 0, 2).reshape(-1)
    rows = jnp.arange(micro * tok_rows, dtype=jnp.int32)
    send_hot = (rows[:, None] == send_at.reshape(-1)[None, :]).astype(BF)
    land_hot = (rows[:, None] == land_at[None, :]).astype(BF)
    return send_hot, land_hot


def exchange(rows):
    return lax.all_to_all(rows, "fsdp", split_axis=0, concat_axis=0, tiled=True)


def bring(rows, send_hot, land_hot):
    sent = dot(send_hot, rows, 1, 0).astype(BF)
    return dot(land_hot, exchange(sent), 1, 0).astype(BF)


def give(rows, send_hot, land_hot):
    sent = dot(land_hot, rows, 0, 0).astype(BF)
    return dot(send_hot, exchange(sent), 0, 0).astype(BF)


def meet(peers):
    barrier = pltpu.get_barrier_semaphore()
    for peer in peers:
        pl.semaphore_signal(barrier, inc=1, device_id=peer, device_id_type=pl.DeviceIdType.MESH)
    pl.semaphore_wait(barrier, len(peers))


def remote(source, target, send, recv, device):
    return pltpu.make_async_remote_copy(
        src_ref=source,
        dst_ref=target,
        send_sem=send,
        recv_sem=recv,
        device_id=device,
        device_id_type=pl.DeviceIdType.MESH,
    )


def pack_peers(size):
    here, row = lax.axis_index("seq"), lax.axis_index("fsdp")
    return [(lax.rem(here + k, size), row) for k in range(1, size)]


def block_rows(size, tok, m, d):
    return pl.ds(pl.multiple_of((m * size + d) * tok, tok), tok)


def flip(place, k):
    return (place // 2 + k // 2) % 2 * 2 + (place % 2 + k % 2) % 2


def crossing():
    here, row = lax.axis_index("seq"), lax.axis_index("fsdp")
    return here, (flip(here, 1), row), (flip(here, 2), row)


class Relay:
    def __init__(self, tok, own, whole, own_sem, send, recv):
        here, one, two = crossing()
        self.whole, self.tok, self.one, self.two = whole, tok, one, two
        spots = [self.spot(m, here) for m in range(2)]
        first, second = own.at[pl.ds(0, tok)], own.at[pl.ds(tok, tok)]
        self.near = [
            remote(first, spots[0], send.at[0], recv.at[0], one),
            remote(second, spots[1], send.at[1], recv.at[1], two),
            remote(second, spots[1], send.at[2], recv.at[2], one),
            remote(first, spots[0], send.at[3], recv.at[3], two),
        ]
        self.far = [
            remote(self.spot(0, one[0]), self.spot(0, one[0]), send.at[4], recv.at[4], two),
            remote(self.spot(1, two[0]), self.spot(1, two[0]), send.at[5], recv.at[5], one),
        ]
        self.kept = [
            pltpu.make_async_copy(source, spot, own_sem.at[m])
            for m, (source, spot) in enumerate(zip((first, second), spots))
        ]

    def spot(self, m, d):
        return self.whole.at[block_rows(4, self.tok, m, d)]

    def start(self):
        for copy in self.near + self.kept:
            copy.start()

    def pass_on(self):
        for near, far in zip(self.near, self.far):
            near.wait_recv()
            far.start()

    def finish(self):
        for copy in self.near[:2]:
            copy.wait_send()
        for copy in self.near[2:] + self.far + self.kept:
            copy.wait()


class Gathering:
    def __init__(self, tok, sent, got, send, recv):
        here, one, two = crossing()
        self.here, self.tok, self.sent, self.got = here, tok, sent, got
        ways = [(0, 0, one), (0, 1, two), (1, 1, two), (2, 0, one), (1, 0, two), (2, 1, one)]
        self.copies = [
            remote(sent.at[k, pl.ds(m * tok, tok)], got.at[i], send.at[i], recv.at[i], way)
            for i, (k, m, way) in enumerate(ways)
        ]

    def device(self, k):
        return flip(self.here, 3 - k)

    def send(self, k):
        for i, block in enumerate((0, 0, 1, 2)):

            @pl.when(k == block)
            def _(i=i):
                self.copies[i].start()

    def add(self, k):
        @pl.when(k == 3)
        def _():
            for i, (block, m) in enumerate(((1, 0), (2, 1))):
                self.copies[i].wait_recv()
                rows = pl.ds(m * self.tok, self.tok)
                total = self.sent[block, rows].astype(F32) + self.got[i].astype(F32)
                self.sent[block, rows] = total.astype(BF)
                self.copies[4 + i].start()

    def finish(self):
        for copy in self.copies[:2]:
            copy.wait_send()
        for copy in self.copies[2:]:
            copy.wait()

    def total(self, m, own):
        pair = (3, 4) if m == 0 else (2, 5)
        return own + self.got[pair[0]].astype(F32) + self.got[pair[1]].astype(F32)


def crossing_sems():
    return [pltpu.SemaphoreType.DMA((6,))] * 2


def start_deal(source, out, size, own_sem, send_sem, recv_sem, first=0, start=True):
    here, row = lax.axis_index("seq"), lax.axis_index("fsdp")
    copies = [pltpu.make_async_copy(source.at[here], out.at[here], own_sem)]
    for k in range(1, size):
        there = lax.rem(here + k, size)
        copies.append(
            remote(
                source.at[there],
                out.at[here],
                send_sem.at[first + k - 1],
                recv_sem.at[first + k - 1],
                (there, row),
            )
        )
    if start:
        for copy in copies:
            copy.start()
    return copies


def start_half(source, out, size, first, own_sem, send_sem, recv_sem):
    here, row = lax.axis_index("seq"), lax.axis_index("fsdp")
    half = size // 2
    own = pltpu.make_async_copy(source.at[lax.rem(here, half)], out.at[here], own_sem)
    mine = (here >= first) & (here < first + half)

    def copy_to(j):
        return remote(
            source.at[j], out.at[here], send_sem.at[j], recv_sem.at[here], (first + j, row)
        )

    pl.when(mine)(own.start)
    for j in range(half):
        pl.when(here != first + j)(lambda j=j: copy_to(j).start())

    def wait():
        pl.when(mine)(own.wait)
        for j in range(half):
            pl.when(here != first + j)(lambda j=j: copy_to(j).wait_send())

        @pl.when(mine)
        def _():
            for k in range(1, size):
                there = lax.rem(here + k, size)
                remote(
                    source.at[0], out.at[there], send_sem.at[0], recv_sem.at[there], (there, row)
                ).wait_recv()

    return wait


def half_sems(size):
    return [pltpu.SemaphoreType.DMA((n,)) for n in (1, size // 2, size)]


def deal_sems(size, count=1):
    links = pltpu.SemaphoreType.DMA((count * (size - 1),))
    return [pltpu.SemaphoreType.DMA((count,)), links, links]


VMEM_BYTES = 60 * 2**20
VMEM = pl.BlockSpec(memory_space=pltpu.VMEM)
HBM = pl.BlockSpec(memory_space=pl.ANY)
SHAPE = jax.ShapeDtypeStruct


def lane_groups(channels, most=4):
    tiles, out, first = channels // LANES, [], 0
    while first < tiles:
        count = min(most, tiles - first)
        out.append((first, count))
        first += count
    return out


def sigmoid(v):
    return 1.0 / (1.0 + jnp.exp(-v))


def softplus(v):
    return jnp.maximum(v, 0.0) + jnp.log1p(jnp.exp(-jnp.abs(v)))


def steps_of(lin_ref, u_ref, position_ref, dtm, dtu):
    step = softplus(lin_ref[...])
    dtu[...] = step * u_ref[...]
    dtm[...] = jnp.where(position_ref[...] > 0, step, 1e30)


def both_of(ref, t):
    row = ref[t].astype(F32)
    return row[:STATE], row[STATE:]


def scan_kernel(size, groups, *refs):
    u_ref, lin_ref, bc_ref, a_ref, position_ref, gate_ref, skip_ref, held = refs[:8]
    core, out, sums, got, dtm, dtu, own_sem, held_send, held_recv = refs[8:]
    steps = u_ref.shape[0]

    def copies(start):
        return start_deal(held, got, size, own_sem.at[0], held_send, held_recv, start=start)

    @pl.when(pl.program_id(0) == 0)
    def _():
        meet(pack_peers(size))
        copies(True)

    steps_of(lin_ref, u_ref, position_ref, dtm, dtu)
    place = lax.broadcasted_iota(jnp.int32, (8, LANES), 0)
    for first, count in groups:
        spans = [pl.ds((first + i) * LANES, LANES) for i in range(count)]
        rates = [a_ref[:, span] for span in spans]

        def block(k, held):
            held = list(held)
            rows = pl.ds(pl.multiple_of(k * 8, 8), 8)
            dts = [dtm[rows, span] for span in spans]
            dus = [dtu[rows, span] for span in spans]
            ys = [jnp.zeros((8, LANES), F32)] * count
            for j in range(8):
                b_now, c_now = both_of(bc_ref, k * 8 + j)
                for i in range(count):
                    decay = jnp.exp(dts[i][j : j + 1] * rates[i])
                    held[i] = decay * held[i] + dus[i][j : j + 1] * b_now
                    y = jnp.sum(held[i] * c_now, axis=0, keepdims=True)
                    ys[i] = jnp.where(place == j, y, ys[i])
            for i, span in enumerate(spans):
                core[rows, span] = ys[i]
            return tuple(held)

        zero = jnp.zeros((STATE, LANES), F32)
        lax.fori_loop(0, steps // 8, block, (zero,) * count)
    gate = gate_ref[...].astype(F32)
    result = (core[...] + skip_ref[...] * u_ref[...]) * (gate * sigmoid(gate))
    out[...] = result
    sums[...] = row_sums(result * result)

    @pl.when(pl.program_id(0) == pl.num_programs(0) - 1)
    def _():
        for copy in copies(False):
            copy.wait()


def row_sums(values):
    return lax.dot_general(
        jnp.ones((8, values.shape[1]), F32),
        values,
        (((1,), (1,)), ((), ())),
        precision=lax.Precision.HIGHEST,
        preferred_element_type=F32,
    )


def scan_forward(u, lin, bc, rates, position, opened, skip, held, micro, collective_id):
    size = lax.axis_size("seq")
    rows, channels = u.shape
    steps = rows // micro
    block = pl.BlockSpec((steps, channels), lambda m: (m, 0))
    lane = pl.BlockSpec((8, steps), lambda m: (0, m))
    return pl.pallas_call(
        partial(scan_kernel, size, lane_groups(channels)),
        grid=(micro,),
        out_shape=[SHAPE((rows, channels), F32)] * 2
        + [SHAPE((8, rows), F32), SHAPE(held.shape, held.dtype)],
        in_specs=[
            block,
            block,
            pl.BlockSpec((steps, 2 * STATE, LANES), lambda m: (m, 0, 0)),
            pl.BlockSpec(rates.shape, lambda m: (0, 0)),
            pl.BlockSpec((steps, 1), lambda m: (m, 0)),
            pl.BlockSpec((steps, channels), lambda m: (m, 1)),
            pl.BlockSpec((1, channels), lambda m: (0, 0)),
            HBM,
        ],
        out_specs=[block, block, lane, HBM],
        scratch_shapes=[pltpu.VMEM((steps, channels), F32)] * 2 + deal_sems(size),
        compiler_params=pltpu.CompilerParams(
            collective_id=collective_id, has_side_effects=True, vmem_limit_bytes=VMEM_BYTES
        ),
        name="scan_forward",
    )(u, lin, bc, rates, position, opened, skip, held)


def scan_back_kernel(size, count, groups, *refs):
    dcore_ref, u_ref, lin_ref, bc_ref, a_ref, position_ref, skip_ref = refs[:7]
    helds, refs = refs[7 : 7 + count], refs[7 + count :]
    du_ref, dlin_ref, bias_ref, da_ref, db_ref, dc_ref = refs[:6]
    gots, refs = refs[6 : 6 + count], refs[6 + count :]
    dtm, dtu, ddtu, ddt, hs, acc_b, acc_c, own_sem, held_send, held_recv = refs
    steps = u_ref.shape[0]

    def copies():
        out = []
        for i, (held, got) in enumerate(zip(helds, gots)):
            out += start_deal(
                held, got, size, own_sem.at[i], held_send, held_recv, i * (size - 1), start=False
            )
        return out

    @pl.when(pl.program_id(0) == 0)
    def _():
        meet(pack_peers(size))
        for copy in copies():
            copy.start()

    steps_of(lin_ref, u_ref, position_ref, dtm, dtu)
    place = lax.broadcasted_iota(jnp.int32, (8, LANES), 0)
    zero = jnp.zeros((STATE, LANES), F32)
    for at, (first, count) in enumerate(groups):
        spans = [pl.ds((first + i) * LANES, LANES) for i in range(count)]
        slots = [pl.ds(i * LANES, LANES) for i in range(count)]
        rates = [a_ref[:, span] for span in spans]
        for slot in slots:
            hs[0, :, slot] = zero

        def block(k, held):
            held = list(held)
            base = pl.multiple_of(k * 8, 8)
            rows = pl.ds(base, 8)
            dts = [dtm[rows, span] for span in spans]
            dus = [dtu[rows, span] for span in spans]
            for j in range(8):
                b_now, _ = both_of(bc_ref, base + j)
                for i in range(count):
                    decay = jnp.exp(dts[i][j : j + 1] * rates[i])
                    held[i] = decay * held[i] + dus[i][j : j + 1] * b_now
                    hs[base + j + 1, :, slots[i]] = held[i]
            return tuple(held)

        lax.fori_loop(0, steps // 8, block, (zero,) * count)

        def back(k, carry):
            carry = list(carry)
            block_at = steps // 8 - 1 - k
            base = pl.multiple_of(block_at * 8, 8)
            rows = pl.ds(base, 8)
            dts = [dtm[rows, span] for span in spans]
            dus = [dtu[rows, span] for span in spans]
            dys = [dcore_ref[rows, span] for span in spans]
            out_u = [jnp.zeros((8, LANES), F32)] * count
            out_t = [jnp.zeros((8, LANES), F32)] * count
            for j in reversed(range(8)):
                t = base + j
                b_now, c_now = both_of(bc_ref, t)
                sum_b = sum_c = zero
                for i in range(count):
                    later, rate_sum = carry[i]
                    dt, du, dy = dts[i][j : j + 1], dus[i][j : j + 1], dys[i][j : j + 1]
                    g = later + dy * c_now
                    sum_c = sum_c + hs[t + 1, :, slots[i]] * dy
                    sum_b = sum_b + g * du
                    through = g * jnp.exp(dt * rates[i])
                    moved = through * hs[t, :, slots[i]]
                    to_u = jnp.sum(g * b_now, axis=0, keepdims=True)
                    to_t = jnp.sum(moved * rates[i], axis=0, keepdims=True)
                    out_u[i] = jnp.where(place == j, to_u, out_u[i])
                    out_t[i] = jnp.where(place == j, to_t, out_t[i])
                    carry[i] = (through, rate_sum + moved * dt)
                if at == 0:
                    acc_b[t] = sum_b
                    acc_c[t] = sum_c
                else:
                    acc_b[t] = acc_b[t] + sum_b
                    acc_c[t] = acc_c[t] + sum_c
            for i, span in enumerate(spans):
                ddtu[rows, span] = out_u[i]
                ddt[rows, span] = out_t[i]
            return tuple(carry)

        ends = lax.fori_loop(0, steps // 8, back, ((zero, zero),) * count)
        for i, span in enumerate(spans):
            da_ref[:, span] = ends[i][1]
    for acc, out in ((acc_b, db_ref), (acc_c, dc_ref)):
        out[...] = row_sums(acc[...].reshape(steps * STATE, LANES))
    lin = lin_ref[...]
    to_step = ddtu[...]
    du_ref[...] = dcore_ref[...] * skip_ref[...] + to_step * softplus(lin)
    d_lin = (ddt[...] + to_step * u_ref[...]) * sigmoid(lin)
    dlin_ref[...] = d_lin.astype(BF)
    bias_ref[...] = jnp.sum(d_lin, axis=0, keepdims=True)

    @pl.when(pl.program_id(0) == pl.num_programs(0) - 1)
    def _():
        for copy in copies():
            copy.wait()


def scan_backward(dcore, u, lin, bc, rates, position, skip, helds, micro, collective_id):
    size = lax.axis_size("seq")
    rows, channels = u.shape
    steps = rows // micro
    groups = lane_groups(channels)
    block = pl.BlockSpec((steps, channels), lambda m: (m, 0))
    rate = pl.BlockSpec(rates.shape, lambda m: (0, 0))
    line = pl.BlockSpec((1, channels), lambda m: (0, 0))
    flat = pl.BlockSpec((None, 8, steps * STATE), lambda m: (m, 0, 0))
    wide = pltpu.VMEM((steps, channels), F32)
    du, dlin, bias, da, db, dc, *gots = pl.pallas_call(
        partial(scan_back_kernel, size, len(helds), groups),
        grid=(micro,),
        out_shape=[
            SHAPE((rows, channels), F32),
            SHAPE((rows, channels), BF),
            SHAPE((micro, 1, channels), F32),
            SHAPE((micro, STATE, channels), F32),
            SHAPE((micro, 8, steps * STATE), F32),
            SHAPE((micro, 8, steps * STATE), F32),
        ]
        + [SHAPE(held.shape, held.dtype) for held in helds],
        in_specs=[
            block,
            block,
            block,
            pl.BlockSpec((steps, 2 * STATE, LANES), lambda m: (m, 0, 0)),
            rate,
            pl.BlockSpec((steps, 1), lambda m: (m, 0)),
            line,
        ]
        + [HBM] * len(helds),
        out_specs=[
            block,
            block,
            pl.BlockSpec((None, 1, channels), lambda m: (m, 0, 0)),
            pl.BlockSpec((None, STATE, channels), lambda m: (m, 0, 0)),
            flat,
            flat,
        ]
        + [HBM] * len(helds),
        scratch_shapes=[wide] * 4
        + [
            pltpu.VMEM((steps + 1, STATE, groups[0][1] * LANES), F32),
            pltpu.VMEM((steps, STATE, LANES), F32),
            pltpu.VMEM((steps, STATE, LANES), F32),
        ]
        + deal_sems(size, len(helds)),
        compiler_params=pltpu.CompilerParams(
            collective_id=collective_id, has_side_effects=True, vmem_limit_bytes=VMEM_BYTES
        ),
        name="scan_backward",
    )(dcore, u, lin, bc, rates, position, skip, *helds)
    return (
        du,
        dlin,
        jnp.sum(bias[:, 0], axis=0),
        jnp.sum(da, axis=0),
        db[:, 0].reshape(rows, STATE),
        dc[:, 0].reshape(rows, STATE),
        gots,
    )


def regroup_kernel(plan, source_count, out_count, *refs):
    here = lax.axis_index("seq")
    sources = refs[:source_count]
    maps = refs[source_count : len(refs) - out_count]
    outs = refs[len(refs) - out_count :]
    for out, block, tile, wide, terms in plan:
        at = pl.ds(tile * LANES, wide)
        total = None
        for source, which, low, high in terms:
            held = sources[source]
            held = held[..., low:high] if len(held.shape) == 2 else held[which[1], :, low:high]
            table = maps[which[0]]
            wanted = table[0:1, at]
            for i in range(1, table.shape[0]):
                wanted = jnp.where(here == i, table[i : i + 1, at], wanted)
            wanted = wanted - low
            places = lax.broadcasted_iota(jnp.int32, (high - low, wide), 0)
            hot = (places == wanted).astype(F32).astype(BF)
            term = dot(held, hot, 1, 0)
            total = term if total is None else total + term
        ref = outs[out]
        if total is None:
            total = jnp.zeros((ref.shape[-2], wide), F32)
        if len(ref.shape) == 2:
            ref[:, at] = total.astype(ref.dtype)
        else:
            ref[block, :, at] = total.astype(ref.dtype)


def regroup(sources, outs, moves):
    plan, maps = [], []
    tables = []
    for source, from_block, out, block, table in moves:
        maps.append(jnp.asarray(table))
        tables.append((source, from_block, out, block, table))
    for out, shape in enumerate(outs):
        for block in range(shape.shape[0] if len(shape.shape) == 3 else 1):
            for tile in range(-(-shape.shape[-1] // LANES)):
                wide = min(LANES, shape.shape[-1] - tile * LANES)
                terms = []
                for which, (source, from_block, to, to_block, table) in enumerate(tables):
                    used = table[:, tile * LANES : tile * LANES + wide]
                    if (to, to_block) != (out, block) or not (used >= 0).any():
                        continue
                    low = int(used[used >= 0].min()) // LANES * LANES
                    high = min(-(-(int(used.max()) + 1) // LANES) * LANES, sources[source].shape[-1])
                    terms.append((source, (which, from_block), low, high))
                plan.append((out, block, tile, wide, tuple(terms)))
    vmem = pl.BlockSpec(memory_space=pltpu.VMEM)
    return pl.pallas_call(
        partial(regroup_kernel, plan, len(sources), len(outs)),
        out_shape=list(outs),
        in_specs=[vmem] * (len(sources) + len(maps)),
        out_specs=[vmem] * len(outs),
        compiler_params=pltpu.CompilerParams(vmem_limit_bytes=VMEM_BYTES),
        name="regroup",
    )(*sources, *maps)


def pieces_table(chunks, size, piece, wide, start=0):
    at = np.arange(chunks * wide)
    chunk, place = at // wide, at % wide
    count = size // piece
    table = start + chunk * size + place + piece * np.arange(count)[:, None]
    return np.where(place < piece, table, -1).astype(np.int32)


def run_table(starts, count):
    return (np.asarray(starts)[:, None] + np.arange(count)).astype(np.int32)


def placed(table, at, width):
    out = np.full((table.shape[0], width), -1, np.int32)
    out[:, at : at + table.shape[1]] = table
    return out


def deal_kernel(count, size, first, *refs):
    sources, half_source = refs[:count], refs[count]
    outs, half_out = refs[count + 1 : 2 * count + 1], refs[2 * count + 1]
    own_sem, send_sem, recv_sem, half_own, half_send, half_recv = refs[2 * count + 2 :]
    meet(pack_peers(size))
    wait = start_half(half_source, half_out, size, first, half_own.at[0], half_send, half_recv)
    copies = []
    for i, (source, out) in enumerate(zip(sources, outs)):
        copies += start_deal(
            source, out, size, own_sem.at[i], send_sem, recv_sem, i * (size - 1)
        )
    for copy in copies:
        copy.wait()
    wait()


def deal(arrays, halves, first, collective_id):
    size, count = lax.axis_size("seq"), len(arrays)
    return pl.pallas_call(
        partial(deal_kernel, count, size, first),
        out_shape=[SHAPE(a.shape, a.dtype) for a in arrays]
        + [SHAPE((size,) + halves.shape[1:], halves.dtype)],
        in_specs=[HBM] * (count + 1),
        out_specs=[HBM] * (count + 1),
        scratch_shapes=deal_sems(size, count) + half_sems(size),
        compiler_params=pltpu.CompilerParams(collective_id=collective_id, has_side_effects=True),
        cost_estimate=pl.CostEstimate(flops=0, bytes_accessed=1024, transcendentals=0),
        name="deal",
    )(*arrays, halves)


def spread(slots, me, devices, send, recv):
    copies = []
    for k, device in enumerate(devices):
        copies.append(remote(slots.at[me], slots.at[me], send.at[k], recv.at[k], device))
        copies[-1].start()
    for copy in copies:
        copy.wait()
    total = slots[0]
    for i in range(1, slots.shape[0]):
        total = total + slots[i]
    return total


def last_kernel(sizes, count, *refs):
    sources, half_source, in_ref = refs[:count], refs[count], refs[count + 1]
    outs, half_out, out_ref = refs[count + 2 : 2 * count + 2], *refs[2 * count + 2 : 2 * count + 4]
    refs = refs[2 * count + 4 :]
    one, two, send_one, recv_one, send_two, recv_two, own_sem, send_sem, recv_sem = refs[:9]
    half_own, half_send, half_recv = refs[9:]
    seq, fsdp = lax.axis_index("seq"), lax.axis_index("fsdp")
    across = [(lax.rem(seq + k, sizes[0]), fsdp) for k in range(1, sizes[0])]
    along = [(seq, lax.rem(fsdp + k, sizes[1])) for k in range(1, sizes[1])]
    meet(across + along)
    one[seq] = in_ref[...]
    two[fsdp] = spread(one, seq, across, send_one, recv_one)
    wait = start_half(half_source, half_out, sizes[0], 0, half_own.at[0], half_send, half_recv)
    copies = []
    for i, (source, out) in enumerate(zip(sources, outs)):
        copies += start_deal(
            source, out, sizes[0], own_sem.at[i], send_sem, recv_sem, i * (sizes[0] - 1)
        )
    out_ref[...] = spread(two, fsdp, along, send_two, recv_two)
    for copy in copies:
        copy.wait()
    wait()


def last_exchange(arrays, halves, block, collective_id):
    sizes, count = (lax.axis_size("seq"), lax.axis_size("fsdp")), len(arrays)
    return pl.pallas_call(
        partial(last_kernel, sizes, count),
        out_shape=[SHAPE(a.shape, a.dtype) for a in arrays]
        + [SHAPE((sizes[0],) + halves.shape[1:], halves.dtype), SHAPE(block.shape, block.dtype)],
        in_specs=[HBM] * (count + 1) + [VMEM],
        out_specs=[HBM] * (count + 1) + [VMEM],
        scratch_shapes=[pltpu.VMEM((n,) + block.shape, F32) for n in sizes]
        + [pltpu.SemaphoreType.DMA((n - 1,)) for n in sizes for _ in range(2)]
        + deal_sems(sizes[0], count)
        + half_sems(sizes[0]),
        compiler_params=pltpu.CompilerParams(collective_id=collective_id, has_side_effects=True),
        cost_estimate=pl.CostEstimate(flops=0, bytes_accessed=1024, transcendentals=0),
        name="last_exchange",
    )(*arrays, halves, block)


def gather_kernel(size, tok, own, whole, own_sem, send, recv):
    meet(pack_peers(size))
    relay = Relay(tok, own, whole, own_sem, send, recv)
    relay.start()
    relay.pass_on()
    relay.finish()


def gather_rows(own, micro, collective_id):
    size, rows = lax.axis_size("seq"), own.shape[0]
    return pl.pallas_call(
        partial(gather_kernel, size, rows // micro),
        out_shape=SHAPE((rows * size, own.shape[1]), own.dtype),
        in_specs=[HBM],
        out_specs=HBM,
        scratch_shapes=[pltpu.SemaphoreType.DMA((micro,))] + crossing_sems(),
        compiler_params=pltpu.CompilerParams(collective_id=collective_id, has_side_effects=True),
        name="gather_rows",
    )(own)


def spans_of(width, most=512):
    return [(low, min(low + most, width)) for low in range(0, width, most)]


def joined(blocks, out):
    wide = blocks.shape[2]
    for i in range(blocks.shape[0]):
        out[:, i * wide : (i + 1) * wide] = blocks[i]
    return out


def mixer_kernel(size, tok, micro, *refs):
    context, ssm_out, sums_ref, x_ref, gain_att, gain_ssm, gain_ffn, w_att, w_ssm = refs[:9]
    att, ssm, scale_att, scale_ssm, hidden, mixer, ffn = refs[9:16]
    sums, sent, got, ffn_own, sums_send, sums_recv, send, recv, own_sem, ffn_send, ffn_recv = refs[
        16:-1
    ]
    w_att = joined(w_att, refs[-1])
    here, row = lax.axis_index("seq"), lax.axis_index("fsdp")
    peers = pack_peers(size)
    meet(peers)
    sums[here] = sums_ref[...]
    copies = [
        remote(sums.at[here], sums.at[here], sums_send.at[k], sums_recv.at[k], peer)
        for k, peer in enumerate(peers)
    ]
    for copy in copies:
        copy.start()
    for copy in copies:
        copy.wait()
    total = sums[0]
    for i in range(1, size):
        total = total + sums[i]
    place = lax.broadcasted_iota(jnp.int32, (8, LANES), 0)
    for kind, scale, width in ((0, scale_att, ATT), (1, scale_ssm, INNER)):
        column = lax.dot_general(
            total,
            (place == kind).astype(F32),
            (((0,), (0,)), ((), ())),
            precision=lax.Precision.HIGHEST,
            preferred_element_type=F32,
        )
        scale[...] = lax.rsqrt(column / width + EPS)
    att[...] = (context[...] * scale_att[:, :1] * gain_att[...]).astype(BF)
    ssm[...] = (ssm_out[...] * scale_ssm[:, :1] * gain_ssm[...]).astype(BF)

    def product(d, low, high):
        left = [jnp.concatenate([ref[block_rows(size, tok, m, d)] for m in range(micro)]) for ref in (att, ssm)]
        return 0.5 * (
            dot(left[0], w_att[:, low:high], 1, 0) + dot(left[1], w_ssm[:, low:high], 1, 0)
        )

    gathering = Gathering(tok, sent, got, send, recv)
    for k in range(3):
        for low, high in spans_of(D):
            sent[k, :, low:high] = product(gathering.device(k), low, high).astype(BF)
        gathering.send(k)
    gathering.add(3)
    for low, high in spans_of(D):
        mixer[:, low:high] = product(here, low, high)
    gathering.finish()
    for m in range(micro):
        rows = pl.ds(m * tok, tok)
        out = gathering.total(m, mixer[rows])
        mixer[rows] = out
        whole = x_ref[rows].astype(F32) + out
        hidden[rows] = whole
        scale = lax.rsqrt(jnp.mean(whole * whole, axis=-1, keepdims=True) + EPS)
        ffn_own[rows] = (whole * scale * gain_ffn[...]).astype(BF)
    relay = Relay(tok, ffn_own, ffn, own_sem, ffn_send, ffn_recv)
    relay.start()
    relay.pass_on()
    relay.finish()


def mixer_rows(context, ssm_out, sums, x_own, gains, w_att, w_ssm, micro, collective_id):
    size = lax.axis_size("seq")
    own = x_own.shape[0]
    rows, tok = own * size, own // micro
    vmem, hbm = pl.BlockSpec(memory_space=pltpu.VMEM), pl.BlockSpec(memory_space=pl.ANY)
    shape = jax.ShapeDtypeStruct
    dma = pltpu.SemaphoreType.DMA
    return pl.pallas_call(
        partial(mixer_kernel, size, tok, micro),
        out_shape=[
            shape((rows, w_att.shape[1]), BF),
            shape((rows, w_ssm.shape[0]), BF),
            shape((rows, LANES), F32),
            shape((rows, LANES), F32),
            shape((own, D), F32),
            shape((own, D), F32),
            shape((rows, D), BF),
        ],
        in_specs=[vmem] * 9,
        out_specs=[vmem] * 6 + [hbm],
        scratch_shapes=[
            pltpu.VMEM((size,) + sums.shape, F32),
            pltpu.VMEM((size - 1, own, D), BF),
            pltpu.VMEM((6, tok, D), BF),
            pltpu.VMEM((own, D), BF),
            dma((size - 1,)),
            dma((size - 1,)),
            *crossing_sems(),
            dma((micro,)),
            *crossing_sems(),
            pltpu.VMEM((w_att.shape[1], D), BF),
        ],
        compiler_params=pltpu.CompilerParams(
            collective_id=collective_id, has_side_effects=True, vmem_limit_bytes=VMEM_BYTES
        ),
        name="mixer_rows",
    )(context, ssm_out, sums, x_own, *gains, w_att, w_ssm)


def ffn_kernel(size, tok, micro, *refs):
    ffn, cot, hidden, cot_own, gain, w_gu, w_down = refs[:7]
    act, dgu, down, d_hidden, d_gain, dmix, grad, grad_down = refs[7:15]
    sent, got, dmix_own, send, recv, own_sem, dmix_send, dmix_recv, turned, turned_act = refs[15:]
    here, row = lax.axis_index("seq"), lax.axis_index("fsdp")
    wide = w_down.shape[0]
    meet(pack_peers(size))

    gathering = Gathering(tok, sent, got, send, recv)

    def block(k, carry):
        d = gathering.device(k)
        spots = [block_rows(size, tok, m, d) for m in range(micro)]
        gathering.add(k)
        rows_in = jnp.concatenate([ffn[spot] for spot in spots])
        cots = jnp.concatenate([cot[spot] for spot in spots])
        for low, high in spans_of(wide):
            gate = dot(rows_in, w_gu[:, low:high], 1, 0)
            up = dot(rows_in, w_gu[:, wide + low : wide + high], 1, 0)
            d_act = dot(cots, w_down[low:high, :], 1, 1)
            sig = 1.0 / (1.0 + jnp.exp(-gate))
            silu = gate * sig
            pieces = (
                (act, low, silu * up),
                (dgu, low, d_act * up * (sig * (1.0 + gate - silu))),
                (dgu, wide + low, d_act * silu),
            )
            for ref, at, values in pieces:
                values = values.astype(BF)
                for m, spot in enumerate(spots):
                    ref[spot, at : at + high - low] = values[m * tok : (m + 1) * tok]
        d_all = jnp.concatenate([dgu[spot] for spot in spots])
        for low, high in spans_of(D):
            sent[k, :, low:high] = dot(d_all, w_gu[low:high, :], 1, 1).astype(BF)
        gathering.send(k)
        acts = jnp.concatenate([act[spot] for spot in spots])
        for low, high in spans_of(D):
            down[d, :, low:high] = dot(acts, w_down[:, low:high], 1, 0).astype(BF)
        return carry

    lax.fori_loop(0, size, block, 0)
    gathering.finish()
    gain_sum = jnp.zeros((1, D), F32)
    for m in range(micro):
        rows = pl.ds(m * tok, tok)
        d_in = gathering.total(m, sent[size - 1, rows].astype(F32))
        whole = hidden[rows]
        scale = lax.rsqrt(jnp.mean(whole * whole, axis=-1, keepdims=True) + EPS)
        normal = whole * scale
        gain_sum = gain_sum + jnp.sum(d_in * normal, axis=0, keepdims=True)
        scaled = d_in * gain[...]
        inward = jnp.mean(scaled * normal, axis=-1, keepdims=True)
        out = cot_own[rows].astype(F32) + scale * (scaled - normal * inward)
        d_hidden[rows] = out
        dmix_own[rows] = out.astype(BF)
    d_gain[...] = gain_sum
    relay = Relay(tok, dmix_own, dmix, own_sem, dmix_send, dmix_recv)
    relay.start()
    for low, high in spans_of(D, 2 * LANES):
        turned[low:high, :] = ffn[:, low:high].T

    def columns(j, carry):
        span = pl.ds(pl.multiple_of(j * 2 * LANES, 2 * LANES), 2 * LANES)
        for low, high in spans_of(D):
            grad[low:high, span] = dot(turned[low:high, :], dgu[:, span], 1, 0).astype(BF)
        return carry

    pieces = 2 * wide // (2 * LANES)
    lax.fori_loop(0, pieces // 4, columns, 0)
    relay.pass_on()
    lax.fori_loop(pieces // 4, pieces, columns, 0)
    for low, high in spans_of(wide, 2 * LANES):
        turned_act[low:high, :] = act[:, low:high].T
    for first, last in spans_of(D):
        for low, high in spans_of(wide):
            part = dot(turned_act[low:high, :], cot[:, first:last], 1, 0)
            grad_down[low:high, first:last] = part.astype(BF)
    relay.finish()


def ffn_rows(ffn, cot, hidden, cot_own, gain, w_gu, w_down, micro, collective_id):
    size = lax.axis_size("seq")
    own, rows = hidden.shape[0], ffn.shape[0]
    wide = w_down.shape[0]
    tok = own // micro
    vmem, hbm = pl.BlockSpec(memory_space=pltpu.VMEM), pl.BlockSpec(memory_space=pl.ANY)
    shape = jax.ShapeDtypeStruct
    dma = pltpu.SemaphoreType.DMA
    return pl.pallas_call(
        partial(ffn_kernel, size, tok, micro),
        out_shape=[
            shape((rows, wide), BF),
            shape((rows, 2 * wide), BF),
            shape((size, own, D), BF),
            shape((own, D), F32),
            shape((1, D), F32),
            shape((rows, D), BF),
            shape((D, 2 * wide), BF),
            shape((wide, D), BF),
        ],
        in_specs=[vmem] * 7,
        out_specs=[vmem] * 5 + [hbm, vmem, vmem],
        scratch_shapes=[
            pltpu.VMEM((size, own, D), BF),
            pltpu.VMEM((6, tok, D), BF),
            pltpu.VMEM((own, D), BF),
            *crossing_sems(),
            dma((micro,)),
            *crossing_sems(),
            pltpu.VMEM((D, rows), BF),
            pltpu.VMEM((wide, rows), BF),
        ],
        compiler_params=pltpu.CompilerParams(
            collective_id=collective_id, has_side_effects=True, vmem_limit_bytes=VMEM_BYTES
        ),
        name="ffn_rows",
    )(ffn, cot, hidden, cot_own, gain, w_gu, w_down)


def attention_kernel(most, at_k, opened_ref, position_ref, context, probs, sums):
    s, size = lax.axis_index("seq"), lax.axis_size("seq")
    first = (HEADS * s + size - 1) // size
    last = (HEADS * (s + 1) + size - 1) // size
    pack = position_ref.shape[0]
    at = 4 * HEAD
    in_ref = opened_ref.at[:, at_k : at_k + (4 + most) * HEAD]
    rows = lax.broadcasted_iota(jnp.int32, (pack, pack), 0)
    columns = lax.broadcasted_iota(jnp.int32, (pack, pack), 1)
    visible = (columns <= rows) & (columns >= rows - position_ref[...])
    for h in range(most):
        low = (first + h) // (HEADS // KV_HEADS) <= s
        q = in_ref[:, at + h * HEAD : at + (h + 1) * HEAD]
        key = jnp.where(low, in_ref[:, :HEAD], in_ref[:, HEAD : 2 * HEAD])
        value = jnp.where(low, in_ref[:, 2 * HEAD : 3 * HEAD], in_ref[:, 3 * HEAD : 4 * HEAD])
        masked = jnp.where(visible, dot(q, key, 1, 1) * 0.125, -1e30)
        terms = jnp.exp(masked - jnp.max(masked, axis=1, keepdims=True))
        prob = terms / jnp.sum(terms, axis=1, keepdims=True)
        probs[h] = prob
        out = dot(prob.astype(BF), value, 1, 0)
        context[:, h * HEAD : (h + 1) * HEAD] = jnp.where(first + h < last, out, 0.0)
    held = context[...]
    sums[...] = row_sums(held * held)


def attention(opened, at_k, position, most, micro):
    rows, wide = opened.shape
    pack = rows // micro
    return pl.pallas_call(
        partial(attention_kernel, most, at_k),
        grid=(micro,),
        out_shape=[
            SHAPE((rows, most * HEAD), F32),
            SHAPE((micro, most, pack, pack), F32),
            SHAPE((8, rows), F32),
        ],
        in_specs=[
            pl.BlockSpec((pack, wide), lambda m: (m, 0)),
            pl.BlockSpec((pack, 1), lambda m: (m, 0)),
        ],
        out_specs=[
            pl.BlockSpec((pack, most * HEAD), lambda m: (m, 0)),
            pl.BlockSpec((None, most, pack, pack), lambda m: (m, 0, 0, 0)),
            pl.BlockSpec((8, pack), lambda m: (0, m)),
        ],
        compiler_params=pltpu.CompilerParams(vmem_limit_bytes=VMEM_BYTES),
        name="attention",
    )(opened, position)


def sum_slots(slots, send, recv):
    here, row = lax.axis_index("seq"), lax.axis_index("fsdp")
    copies = [
        remote(slots.at[here], slots.at[here], send.at[k], recv.at[k], peer)
        for k, peer in enumerate(pack_peers(slots.shape[0]))
    ]
    for copy in copies:
        copy.start()
    for copy in copies:
        copy.wait()
    total = slots[0].astype(F32)
    for i in range(1, slots.shape[0]):
        total = total + slots[i].astype(F32)
    return total


def taps_of(inner, position, taps, bias):
    shifted = [inner]
    for k in range(1, CONV):
        shifted.append(jnp.where(position >= k, pltpu.roll(inner, k, axis=0), 0.0))
    conv = bias
    for k in range(CONV):
        conv = conv + taps[k : k + 1] * shifted[k]
    return conv, shifted


def ssm_open_kernel(
    size, micro, opened_ref, position_ref, taps, bias, w_x, w_dt, dt_bias, u_ref, lin_ref, proj_ref, bc_ref, slots, send, recv
):
    meet(pack_peers(size))
    steps = opened_ref.shape[0] // micro
    for m in range(micro):
        rows = pl.ds(m * steps, steps)
        for low, high in spans_of(w_x.shape[1], LANES):
            inner = opened_ref[rows, low:high].astype(F32)
            conv, _ = taps_of(inner, position_ref[rows], taps[:, low:high], bias[:, low:high])
            u_ref[rows, low:high] = conv * sigmoid(conv)
    slots[lax.axis_index("seq")] = dot(w_x[...], u_ref[...].astype(BF), 1, 1).astype(BF)
    proj = sum_slots(slots, send, recv).astype(BF)
    proj_ref[...] = proj
    bc_ref[...] = proj[: 2 * STATE]
    lin_ref[...] = dot(proj[2 * STATE :], w_dt[...], 0, 0) + dt_bias[...]


def ssm_open(opened, position, taps, bias, w_x, w_dt, dt_bias, micro, collective_id):
    size = lax.axis_size("seq")
    rows = opened.shape[0]
    wide, channels = w_x.shape
    dma = pltpu.SemaphoreType.DMA((size - 1,))
    return pl.pallas_call(
        partial(ssm_open_kernel, size, micro),
        out_shape=[
            SHAPE((rows, channels), F32),
            SHAPE((rows, channels), F32),
            SHAPE((wide, rows), BF),
            SHAPE((2 * STATE, rows), BF),
        ],
        in_specs=[VMEM] * 7,
        out_specs=[VMEM] * 4,
        scratch_shapes=[pltpu.VMEM((size, wide, rows), BF), dma, dma],
        compiler_params=pltpu.CompilerParams(
            collective_id=collective_id, has_side_effects=True, vmem_limit_bytes=VMEM_BYTES
        ),
        name="ssm_open",
    )(opened, position, taps, bias, w_x, w_dt, dt_bias)


def ssm_close_kernel(
    size, micro, count, *refs
):
    dlin_ref, db_ref, dc_ref, du_ref, opened_ref, position_ref, taps, bias, w_x, w_dt = refs[:10]
    helds, (dproj_ref, dinner_ref, sums_ref) = refs[10 : 10 + count], refs[10 + count : 13 + count]
    gots = refs[13 + count : 13 + 2 * count]
    slots, total, send, recv, own_sem, held_send, held_recv = refs[13 + 2 * count :]
    meet(pack_peers(size))
    here = lax.axis_index("seq")
    place = lax.broadcasted_iota(jnp.int32, (STATE, STATE), 0)
    eye = (place == lax.broadcasted_iota(jnp.int32, (STATE, STATE), 1)).astype(F32)
    for i, ref in enumerate((db_ref, dc_ref)):
        turned = lax.dot_general(
            eye,
            ref[...],
            (((1,), (1,)), ((), ())),
            precision=lax.Precision.HIGHEST,
            preferred_element_type=F32,
        )
        slots[here, i * STATE : (i + 1) * STATE] = turned.astype(BF)
    slots[here, 2 * STATE :] = dot(w_dt[...], dlin_ref[...], 1, 1).astype(BF)
    dproj = sum_slots(slots, send, recv).astype(BF)
    copies = []
    for i, (held, got) in enumerate(zip(helds, gots)):
        copies += start_deal(
            held, got, size, own_sem.at[i], held_send, held_recv, i * (size - 1)
        )
    dproj_ref[...] = dproj
    steps = opened_ref.shape[0] // micro
    total[...] = du_ref[...] + dot(dproj, w_x[...], 0, 0)
    for low, high in spans_of(w_x.shape[1], LANES):
        lines = [jnp.zeros((1, high - low), F32) for _ in range(CONV + 1)]
        for m in range(micro):
            rows = pl.ds(m * steps, steps)
            inner = opened_ref[rows, low:high].astype(F32)
            position = position_ref[rows]
            tap = taps[:, low:high]
            conv, shifted = taps_of(inner, position, tap, bias[:, low:high])
            sig = sigmoid(conv)
            d_conv = total[rows, low:high] * (sig * (1.0 + conv * (1.0 - sig)))
            d_inner = tap[0:1] * d_conv
            for k in range(CONV):
                lines[k] = lines[k] + jnp.sum(d_conv * shifted[k], axis=0, keepdims=True)
                if k:
                    masked = jnp.where(position >= k, d_conv, 0.0)
                    d_inner = d_inner + tap[k : k + 1] * pltpu.roll(masked, steps - k, axis=0)
            lines[CONV] = lines[CONV] + jnp.sum(d_conv, axis=0, keepdims=True)
            dinner_ref[rows, low:high] = d_inner.astype(BF)
        sums_ref[:, low:high] = jnp.concatenate(
            lines + [jnp.zeros((8 - CONV - 1, high - low), F32)], axis=0
        )
    for copy in copies:
        copy.wait()


def ssm_close(dlin, db, dc, du, opened, position, taps, bias, w_x, w_dt, helds, micro, collective_id):
    size = lax.axis_size("seq")
    rows = opened.shape[0]
    wide, channels = w_x.shape
    dma = pltpu.SemaphoreType.DMA((size - 1,))
    return pl.pallas_call(
        partial(ssm_close_kernel, size, micro, len(helds)),
        out_shape=[
            SHAPE((wide, rows), BF),
            SHAPE((rows, channels), BF),
            SHAPE((8, channels), F32),
        ]
        + [SHAPE(held.shape, held.dtype) for held in helds],
        in_specs=[VMEM] * 10 + [HBM] * len(helds),
        out_specs=[VMEM] * 3 + [HBM] * len(helds),
        scratch_shapes=[
            pltpu.VMEM((size, wide, rows), BF),
            pltpu.VMEM((rows, channels), F32),
            dma,
            dma,
        ]
        + deal_sems(size, max(1, len(helds))),
        compiler_params=pltpu.CompilerParams(
            collective_id=collective_id, has_side_effects=True, vmem_limit_bytes=VMEM_BYTES
        ),
        name="ssm_close",
    )(dlin, db, dc, du, opened, position, taps, bias, w_x, w_dt, *helds)


def branch_back_kernel(size, *refs):
    dmix, w_att, w_ssm, context, ssm_out, core, u, opened = refs[:8]
    scale_att, scale_ssm, gain_att, gain_ssm, live, skip = refs[8:14]
    d_context, d_core, d_gate, d_gain_att, d_gain_ssm, d_skip = refs[14:20]
    t_att, t_ssm, slots, send, recv, w_whole, gate_ref, gate_sem = refs[20:]
    channels = gate_ref.shape[1]
    fetch = pltpu.make_async_copy(
        opened.at[:, pl.ds(channels, channels)], gate_ref, gate_sem.at[0]
    )
    fetch.start()
    w_att = joined(w_att, w_whole)
    meet(pack_peers(size))
    place = lax.broadcasted_iota(jnp.int32, (8, LANES), 0)
    kinds = (
        (w_att, context, scale_att, gain_att, d_gain_att, t_att),
        (w_ssm, ssm_out, scale_ssm, gain_ssm, d_gain_ssm, t_ssm),
    )
    sums = []
    for w, value, scale, gain, d_gain, t in kinds:
        total = None
        for low, high in spans_of(w.shape[0], 2 * LANES):
            grad = 0.5 * dot(dmix[...], w[low:high, :], 1, 1)
            held = value[:, low:high]
            d_gain[:, low:high] = jnp.sum(grad * held * scale[:, :1], axis=0, keepdims=True)
            scaled = grad * gain[:, low:high]
            t[:, low:high] = scaled
            term = row_sums(scaled * held)
            total = term if total is None else total + term
        sums.append(total)
    rows8 = lax.broadcasted_iota(jnp.int32, sums[0].shape, 0)
    slots[lax.axis_index("seq")] = jnp.where(rows8 == 0, sums[0], sums[1])
    total = sum_slots(slots, send, recv)
    fetch.wait()
    columns = [
        lax.dot_general(
            total,
            (place == kind).astype(F32),
            (((0,), (0,)), ((), ())),
            precision=lax.Precision.HIGHEST,
            preferred_element_type=F32,
        )
        for kind in range(2)
    ]
    scale = scale_att[:, :1]
    inward = scale * scale * scale * (columns[0][:, :1] / ATT)
    d_context[...] = ((t_att[...] * scale - context[...] * inward) * live[...]).astype(BF)
    scale = scale_ssm[:, :1]
    inward = scale * scale * scale * (columns[1][:, :1] / INNER)
    for low, high in spans_of(w_ssm.shape[0], 2 * LANES):
        at = slice(low, high)
        d_out = t_ssm[:, at] * scale - ssm_out[:, at] * inward
        gate = gate_ref[:, at].astype(F32)
        sig = sigmoid(gate)
        silu = gate * sig
        held = d_out * silu
        d_core[:, at] = held
        d_skip[:, at] = jnp.sum(held * u[:, at], axis=0, keepdims=True)
        mixed = core[:, at] + skip[:, at] * u[:, at]
        d_gate[:, at] = (d_out * mixed * (sig * (1.0 + gate - silu))).astype(BF)


def branch_back(
    dmix, w_att, w_ssm, context, ssm_out, core, u, opened, scales, gains, live, skip, collective_id
):
    size = lax.axis_size("seq")
    rows, wide, channels = dmix.shape[0], w_att.shape[1], w_ssm.shape[0]
    dma = pltpu.SemaphoreType.DMA((size - 1,))
    return pl.pallas_call(
        partial(branch_back_kernel, size),
        out_shape=[
            SHAPE((rows, wide), BF),
            SHAPE((rows, channels), F32),
            SHAPE((rows, channels), BF),
            SHAPE((1, wide), F32),
            SHAPE((1, channels), F32),
            SHAPE((1, channels), F32),
        ],
        in_specs=[VMEM] * 7 + [HBM] + [VMEM] * 6,
        out_specs=[VMEM] * 6,
        scratch_shapes=[
            pltpu.VMEM((rows, wide), F32),
            pltpu.VMEM((rows, channels), F32),
            pltpu.VMEM((size, 8, rows), F32),
            dma,
            dma,
        ]
        + [
            pltpu.VMEM((wide, D), BF),
            pltpu.VMEM((rows, channels), BF),
            pltpu.SemaphoreType.DMA((1,)),
        ],
        compiler_params=pltpu.CompilerParams(
            collective_id=collective_id, has_side_effects=True, vmem_limit_bytes=VMEM_BYTES
        ),
        name="branch_back",
    )(dmix, w_att, w_ssm, context, ssm_out, core, u, opened, *scales, *gains, live, skip)


def close_kernel(
    size, tok, micro, rest, d_inner, whole_w, x_ref, gain, d_hidden, dx, d_gain, sent, got, send, recv, w, w_sem
):
    fetch = pltpu.make_async_copy(whole_w.at[:, pl.ds(0, w.shape[1])], w, w_sem.at[0])
    fetch.start()
    here, row = lax.axis_index("seq"), lax.axis_index("fsdp")
    meet(pack_peers(size))

    fetch.wait()
    gathering = Gathering(tok, sent, got, send, recv)

    def block(k, carry):
        d = gathering.device(k)
        spots = [block_rows(size, tok, m, d) for m in range(micro)]
        gathering.add(k)
        rows = jnp.concatenate([d_inner[spot] for spot in spots])
        held = jnp.concatenate([rest[spot] for spot in spots])
        for low, high in spans_of(D):
            part = held[:, low:high].astype(F32) + dot(rows, w[low:high, :], 1, 1)
            sent[k, :, low:high] = part.astype(BF)
        gathering.send(k)
        return carry

    lax.fori_loop(0, size, block, 0)
    gathering.finish()
    gain_sum = jnp.zeros((1, D), F32)
    for m in range(micro):
        rows = pl.ds(m * tok, tok)
        d_in = gathering.total(m, sent[size - 1, rows].astype(F32))
        whole = x_ref[rows].astype(F32)
        scale = lax.rsqrt(jnp.mean(whole * whole, axis=-1, keepdims=True) + EPS)
        normal = whole * scale
        gain_sum = gain_sum + jnp.sum(d_in * normal, axis=0, keepdims=True)
        scaled = d_in * gain[...]
        inward = jnp.mean(scaled * normal, axis=-1, keepdims=True)
        dx[rows] = (d_hidden[rows] + scale * (scaled - normal * inward)).astype(BF)
    d_gain[...] = gain_sum


def close_rows(rest, d_inner, w, x_own, gain, d_hidden, micro, collective_id):
    size = lax.axis_size("seq")
    own = x_own.shape[0]
    dma = pltpu.SemaphoreType.DMA((size - 1,))
    return pl.pallas_call(
        partial(close_kernel, size, own // micro, micro),
        out_shape=[SHAPE((own, D), BF), SHAPE((1, D), F32)],
        in_specs=[VMEM] * 2 + [HBM] + [VMEM] * 3,
        out_specs=[VMEM] * 2,
        scratch_shapes=[
            pltpu.VMEM((size, own, D), BF),
            pltpu.VMEM((6, own // micro, D), BF),
            *crossing_sems(),
            pltpu.VMEM((w.shape[0], d_inner.shape[1]), BF),
            pltpu.SemaphoreType.DMA((1,)),
        ],
        compiler_params=pltpu.CompilerParams(
            collective_id=collective_id, has_side_effects=True, vmem_limit_bytes=VMEM_BYTES
        ),
        name="close_rows",
    )(rest, d_inner, w, x_own, gain, d_hidden)


def squares(row_vals):
    return jnp.sum(row_vals * row_vals)


def local(
    tokens,
    cotangent,
    route,
    lengths,
    gain_in,
    w_qkv,
    w_mix_in,
    w_x,
    w_dt,
    w_small,
    gain_att,
    gain_ssm,
    w_out_att,
    w_out_ssm,
    gain_ffn,
    w_gate,
    w_up,
    w_down,
):
    S, N = lax.axis_size("seq"), lax.axis_size("fsdp")
    s = lax.axis_index("seq")
    micro, tok = tokens.shape[:2]
    pack = tok * S
    rows_d = gain_in.shape[0] // N
    ff = w_gate.shape[1]
    ch_piece, ff_piece = INNER // (N * S), ff // (N * S)
    ch = -(-INNER // (S * LANES)) * LANES
    ffs = -(-ff // (S * LANES)) * LANES
    cols = D // S
    groups = HEADS // KV_HEADS
    first_heads = [(HEADS * i + S - 1) // S for i in range(S + 1)]
    head_counts = [first_heads[i + 1] - first_heads[i] for i in range(S)]
    most = max(head_counts)
    width = most * HEAD
    first_head = jnp.array(first_heads, jnp.int32)[s]
    head_live = jnp.arange(most) < jnp.array(head_counts, jnp.int32)[s]
    live = jnp.repeat(head_live, HEAD).astype(F32)[None, :]
    in_low = (first_head + jnp.arange(most)) // groups <= s

    def gather(shard):
        return lax.all_gather(shard, "fsdp", axis=0, tiled=True)

    def scatter(whole):
        rows, wide = whole.shape[0] // N, whole.shape[1]
        fill = -rows % 8
        whole = whole.astype(BF)
        if fill:
            whole = jnp.pad(whole.reshape(N, rows, wide), ((0, 0), (0, fill), (0, 0)))
            whole = whole.reshape(N * (rows + fill), wide)
        whole = lax.psum_scatter(whole, "fsdp", scatter_dimension=0, tiled=True)
        return lax.optimization_barrier(whole)[:rows]

    def part(shard, axis, chunks, wide):
        shape = shard.shape
        piece = shape[axis] // (chunks * S)
        shaped = shard.reshape(shape[:axis] + (chunks, S, piece) + shape[axis + 1 :])
        picked = lax.dynamic_index_in_dim(shaped, s, axis + 1, keepdims=False)
        fill = [(0, 0)] * picked.ndim
        fill[axis + 1] = (0, wide - piece)
        return jnp.pad(picked, fill).reshape(
            shape[:axis] + (chunks * wide,) + shape[axis + 1 :]
        )

    def span(array, axis, start, size):
        return lax.dynamic_slice_in_dim(array, start, size, axis)

    send_hot, land_hot = routing(route, tok)
    x_own = bring(tokens.reshape(micro * tok, D), send_hot, land_hot)
    q_start = first_head * HEAD
    chw, ffw = ch // N, ffs // N
    q_starts = [h * HEAD for h in first_heads[:S]]
    kv_starts = [ATT + HEAD * i for i in range(S)]
    at_k, at_v, at_q = 2 * ch, 2 * ch + 2 * HEAD, 2 * ch + 4 * HEAD
    at_att = at_q + width
    in_wide = at_att + cols
    mix_table = pieces_table(2 * N, INNER // N, ch_piece, chw)
    in_part = regroup(
        [w_mix_in, w_qkv, w_out_att],
        [jax.ShapeDtypeStruct((rows_d, in_wide), BF)],
        [
            (0, None, 0, 0, placed(mix_table, 0, in_wide)),
            (1, None, 0, 0, placed(run_table(kv_starts, 2 * HEAD), at_k, in_wide)),
            (1, None, 0, 0, placed(run_table([a + KV_WIDTH for a in kv_starts], 2 * HEAD), at_v, in_wide)),
            (2, None, 0, 0, placed(run_table([cols * i for i in range(S)], cols), at_att, in_wide)),
            (1, None, 0, 0, placed(run_table(q_starts, width), at_q, in_wide)),
        ],
    )[0]
    small_part = part(
        jnp.concatenate([w_x, w_dt, w_small, jnp.zeros((w_x.shape[0], 1), BF)], axis=1), 0, 1, chw
    )
    small_wide = small_part.shape[1]
    gathered_in = gather(
        jnp.concatenate([in_part, jnp.pad(small_part, ((0, rows_d - chw), (0, 0)))], axis=1)
    )
    cot_own = bring(cotangent.reshape(micro * tok, D), send_hot, land_hot)
    x_rows = gather_rows(x_own, micro, 3)
    cot_own, x_rows = lax.optimization_barrier((cot_own, x_rows))
    cot_rows = gather_rows(cot_own, micro, 6)
    gathered_in, x_rows, cot_rows = lax.optimization_barrier((gathered_in, x_rows, cot_rows))
    out_piece, gathered_in = lax.optimization_barrier((part(w_out_ssm, 0, 1, chw), gathered_in))
    w_out_part = gather(out_piece)
    w_in = gathered_in[:, :at_att]
    w_att_cols = gathered_in[:, at_att:in_wide]
    w_small_part = (
        gathered_in[:, in_wide:].reshape(N, rows_d, small_wide)[:, :chw].reshape(ch, small_wide)
    )
    ff_table = pieces_table(N, ff // N, ff_piece, ffw)
    gu_part = regroup(
        [w_gate, w_up],
        [jax.ShapeDtypeStruct((rows_d, 2 * ffs), BF)],
        [
            (0, None, 0, 0, placed(ff_table, 0, 2 * ffs)),
            (1, None, 0, 0, placed(ff_table, ffs, 2 * ffs)),
        ],
    )[0]

    w_att_pad = jnp.pad(w_att_cols, ((0, width), (0, 0)))
    w_att_blocks = jnp.stack([w_att_pad[h * HEAD : h * HEAD + width] for h in first_heads[:S]])

    w_x_turned = w_small_part[:, :PROJ].T
    w_x_turned = jnp.pad(
        jnp.concatenate([w_x_turned[DT_RANK:], w_x_turned[:DT_RANK]], axis=0),
        ((0, PROJ_PAD - PROJ), (0, 0)),
    )
    w_dt_turned = jnp.pad(
        w_small_part[:, PROJ : PROJ + DT_RANK].T, ((0, PROJ_PAD - PROJ), (0, 0))
    )
    small_par = w_small_part[:, PROJ + DT_RANK : PROJ + DT_RANK + CONV + 3 + STATE].astype(F32)
    small_lines = small_par.T
    taps = jnp.pad(small_lines[:CONV], ((0, 8 - CONV), (0, 0)))
    conv_b, dt_bias, skip = [small_lines[CONV + i][None] for i in range(3)]
    rates = -jnp.exp(small_lines[CONV + 3 :])
    gain_att_part = span(jnp.pad(gain_att, (0, width)), 0, q_start, width)[None]
    gain_ssm_part = part(gain_ssm, 0, N, ch // N)[None]

    position = jax.vmap(lambda one: seq_layout(one, pack)[1])(lengths[:, 0])
    position = position.reshape(micro * pack, 1)

    normed_low = rms_scale(x_rows.astype(F32), gain_in).astype(BF)
    opened = dot(normed_low, w_in, 1, 0).astype(BF)
    opened, gu_part, down_part = lax.optimization_barrier(
        (opened, gu_part, part(w_down, 0, 1, ffw))
    )
    w_gu, w_down_part = gather(gu_part), gather(down_part)
    u, lin, projected, bc = ssm_open(
        opened, position, taps, conv_b, w_x_turned, w_dt_turned, dt_bias, micro, 7
    )
    q = opened[:, at_q:].reshape(micro, pack, most, HEAD)
    kv = opened[:, at_k:at_q].reshape(micro, pack, 4, HEAD)
    pick_low = in_low[None, None, :, None]
    keys = jnp.where(pick_low, kv[:, :, 0:1], kv[:, :, 1:2])
    values = jnp.where(pick_low, kv[:, :, 2:3], kv[:, :, 3:4])
    context, probs, att_sums = attention(opened, at_k, position, most, micro)
    bc = jnp.broadcast_to(bc.T[:, :, None], (micro * pack, 2 * STATE, LANES))
    core, ssm_out, ssm_sums, w_att_part = scan_forward(
        u, lin, bc, rates, position, opened, skip, w_att_blocks, micro, 11
    )
    sums = jnp.stack([att_sums[0], ssm_sums[0]])
    att_low, ssm_low, scale_att, scale_ssm, hidden, mixer_out, ffn_low = mixer_rows(
        context,
        ssm_out,
        jnp.pad(sums, ((0, 6), (0, 0))),
        x_own,
        (gain_att_part, gain_ssm_part, gain_ffn[None]),
        w_att_part,
        w_out_part,
        micro,
        4,
    )
    _, _, down_parts, d_hidden, d_gain_ffn, dmix_low, gu_whole, down_whole = ffn_rows(
        ffn_low, cot_rows, hidden, cot_own, gain_ffn[None], w_gu, w_down_part, micro, 5
    )

    r_gu = scatter(gu_whole)
    r_down = scatter(down_whole)
    d_context, d_core, d_gate_z, d_gain_att, d_gain_ssm, d_skip = branch_back(
        dmix_low,
        w_att_part,
        w_out_part,
        context,
        ssm_out,
        core,
        u,
        opened,
        (scale_att, scale_ssm),
        (gain_att_part, gain_ssm_part),
        live,
        skip,
        8,
    )
    ssm_whole = (0.5 * dot(ssm_low, dmix_low, 0, 0)).astype(BF)
    g_att_rows = (0.5 * dot(att_low, dmix_low, 0, 0)).astype(BF)
    att_blocks = g_att_rows.reshape(width, S, cols).transpose(1, 0, 2)
    dctx_low = d_context.reshape(micro, pack, most, HEAD)
    d_values = jnp.einsum(
        "mhtu,mthd->muhd", probs.astype(BF), dctx_low, preferred_element_type=F32
    )
    d_probs = jnp.einsum("mthd,muhd->mhtu", dctx_low, values, preferred_element_type=F32)
    dscore_low = (
        probs * (d_probs - jnp.sum(probs * d_probs, axis=-1, keepdims=True))
    ).astype(BF)
    d_q = jnp.einsum("mhtu,muhd->mthd", dscore_low, keys, preferred_element_type=F32) * 0.125
    d_keys = jnp.einsum("mhtu,mthd->muhd", dscore_low, q, preferred_element_type=F32) * 0.125

    def kv_sum(d_heads):
        return [
            jnp.sum(jnp.where(pick_low, d_heads, 0.0), axis=2),
            jnp.sum(jnp.where(pick_low, 0.0, d_heads), axis=2),
        ]

    d_rest = jnp.concatenate(
        [d_gate_z]
        + [
            one.astype(BF).reshape(micro * pack, -1)
            for one in kv_sum(d_keys) + kv_sum(d_values) + [d_q]
        ],
        axis=1,
    )
    rest_whole = dot(normed_low, d_rest, 0, 0).astype(BF)
    d_rest, rest_whole = lax.optimization_barrier((d_rest, rest_whole))
    rest_rows = dot(d_rest, gathered_in[:, ch:at_att], 1, 1).astype(BF)
    d_core, r_gu, ssm_whole, rest_whole, rest_rows = lax.optimization_barrier(
        (d_core, r_gu, ssm_whole, rest_whole, rest_rows)
    )
    r_ssm, r_rest = scatter(ssm_whole), scatter(rest_whole)
    per = N // S
    gate_take = np.concatenate([np.arange(ff_piece) + ffw * i for i in range(per)])
    half_wide = -(-per * ff_piece // LANES) * LANES
    moves = []
    for d in range(S):
        for i in range(2):
            table = gate_take[None] + d * per * ffw + i * ffs
            moves.append((0, None, 0, d, placed(table, i * half_wide, 2 * half_wide)))
    (gu_blocks,) = regroup([r_gu], [SHAPE((S, rows_d, 2 * half_wide), BF)], moves)
    d_u, d_lin, d_dt_bias, d_rates, d_in_b, d_out_c, (ffn_got, gu_got, g_att_blocks) = (
        scan_backward(
            d_core, u, lin, bc, rates, position, skip, [down_parts, gu_blocks, att_blocks], micro, 0
        )
    )
    ffn_out = jnp.sum(ffn_got.astype(F32), axis=0)
    result = hidden + ffn_out
    outputs = give(result.astype(BF), send_hot, land_hot)
    g_att_whole = jnp.concatenate(
        [g_att_blocks[i, : head_counts[i] * HEAD] for i in range(S)], axis=0
    )
    dproj_low, d_inner, conv_sums = ssm_close(
        d_lin,
        d_in_b,
        d_out_c,
        d_u,
        opened,
        position,
        taps,
        conv_b,
        w_x_turned,
        w_dt_turned,
        [],
        micro,
        9,
    )
    g_x = dot(u.astype(BF), dproj_low, 0, 1)
    small_whole = jnp.concatenate(
        [
            g_x[:, 2 * STATE : PROJ],
            g_x[:, : 2 * STATE],
            dot(d_lin, projected[2 * STATE : PROJ], 0, 1),
            conv_sums[: CONV + 1].T,
            d_dt_bias[:, None],
            d_skip[0][:, None],
            (d_rates * rates).T,
            jnp.zeros((ch, 1), F32),
        ],
        axis=1,
    ).astype(BF)
    small_whole = jnp.pad(
        small_whole.reshape(N, chw, small_wide), ((0, 0), (0, rows_d - chw), (0, 0))
    ).reshape(N * rows_d, small_wide)
    last_whole = jnp.concatenate(
        [dot(normed_low, d_inner, 0, 0).astype(BF), g_att_whole, small_whole], axis=1
    )
    ff_mine = ff // S
    moves = []
    at = np.arange(ff_mine)
    for source in range(S):
        chunk, inside = at // (S * ff_piece), at % (S * ff_piece)
        table = np.where(
            inside // ff_piece == source, chunk * ff_piece + inside % ff_piece, -1
        )[None].astype(np.int32)
        moves.append((0, source, 0, 0, table))
        moves.append((0, source, 1, 0, np.where(table >= 0, table + half_wide, -1)))
    out_gate, out_up = regroup(
        [gu_got], [jax.ShapeDtypeStruct((rows_d, ff_mine), F32)] * 2, moves
    )

    d_inner, last_whole, r_rest, out_gate, out_up = lax.optimization_barrier(
        (d_inner, last_whole, r_rest, out_gate, out_up)
    )
    r_last = scatter(last_whole)
    dx, d_gain_in = close_rows(
        rest_rows, d_inner, gathered_in, x_own, gain_in[None], d_hidden, micro, 10
    )

    att_at = lax.dynamic_update_slice_in_dim(
        jnp.zeros((ATT + width,), F32), d_gain_att[0] * live[0], q_start, 0
    )[:ATT]
    ssm_at = lax.dynamic_update_index_in_dim(
        jnp.zeros((N, S, ch_piece), F32), d_gain_ssm[0].reshape(N, -1)[:, :ch_piece], s, 1
    ).reshape(INNER)
    stats = jnp.stack(
        [
            squares(x_own.astype(F32)),
            jnp.sum(sums[0]),
            jnp.sum(sums[1]),
            squares(mixer_out),
            squares(ffn_out),
            squares(result),
        ]
    )
    ends = np.cumsum([0, D, ATT, INNER, D, 6])
    line = jnp.concatenate([jnp.zeros((D,), F32), att_at, ssm_at, d_gain_ffn[0], stats])
    line = jnp.pad(line, (0, -line.shape[0] % 1024))
    line, d_gain_in = lax.optimization_barrier((line, d_gain_in))
    line = lax.dynamic_update_slice(line, d_gain_in[0], (0,)).reshape(-1, LANES)
    moves = []
    for d in range(S):
        moves.append((0, None, 0, d, run_table([d * cols], cols)))
        moves.append((1, None, 1, d, run_table([d * cols], cols)))
    qkv_wide = (ATT + 2 * KV_WIDTH) // S
    starts = np.array(q_starts)[:, None]
    counts = np.array(head_counts)[:, None] * HEAD
    base = np.array(kv_starts)[:, None]
    for d in range(S):
        column = np.arange(qkv_wide)[None] + d * qkv_wide
        table = np.full((S, qkv_wide), -1)
        for low, count, source in (
            (starts, counts, at_q),
            (base, 2 * HEAD, at_k),
            (base + KV_WIDTH, 2 * HEAD, at_v),
        ):
            inside = (column >= low) & (column < low + count)
            table = np.where(inside, column - low + source - ch, table)
        moves.append((2, None, 2, d, table.astype(np.int32)))
    mix_mine = 2 * INNER // S
    at = np.arange(mix_mine // S)
    mix_tables = [
        ((at // ch_piece + j * (2 * N // S)) * chw + at % ch_piece)[None].astype(np.int32)
        for j in range(S // 2)
    ]
    for j in range(S // 2):
        moves.append((2, None, 3, j, mix_tables[j]))
    dx, r_ssm, r_down, r_rest = lax.optimization_barrier((dx, r_ssm, r_down, r_rest))
    (*row_blocks, gate_blocks) = regroup(
        [r_ssm, r_down, r_rest],
        [
            SHAPE((S, r_ssm.shape[0], cols), BF),
            SHAPE((S, r_down.shape[0], cols), BF),
            SHAPE((S, rows_d, qkv_wide), BF),
            SHAPE((S // 2, rows_d, mix_mine // S), BF),
        ],
        moves,
    )
    row_blocks, gate_blocks, dx = lax.optimization_barrier((row_blocks, gate_blocks, dx))
    ssm_got, down_got, qkv_got, gate_got = deal(row_blocks, gate_blocks, S // 2, 1)
    input_grads = give(dx, send_hot, land_hot)
    ssm_got, r_last = lax.optimization_barrier((ssm_got, r_last))
    out_ssm = ssm_got[:, :ch_piece].reshape(S * ch_piece, cols).astype(F32)
    out_down = down_got[:, :ff_piece].reshape(S * ff_piece, cols).astype(F32)
    (inner_blocks,) = regroup(
        [r_last],
        [SHAPE((S // 2, rows_d, mix_mine // S), BF)],
        [(0, None, 0, j, mix_tables[j]) for j in range(S // 2)],
    )
    r_small = r_last[:chw, ch + cols :]
    small_got, inner_got, sums_all = last_exchange(
        [jnp.broadcast_to(r_small, (S,) + r_small.shape)], inner_blocks, line, 2
    )
    out_qkv = jnp.sum(qkv_got.astype(F32), axis=0)
    moves = []
    at = np.arange(mix_mine)
    for source in range(S):
        chunk, inside = at // (S * ch_piece), at % (S * ch_piece)
        table = np.where(
            inside // ch_piece == source, chunk * ch_piece + inside % ch_piece, -1
        )[None].astype(np.int32)
        moves.append((0, source, 0, 0, table))
    (out_mix,) = regroup(
        [jnp.where(s < S // 2, inner_got, gate_got)], [SHAPE((rows_d, mix_mine), F32)], moves
    )
    g_att = r_last[:, ch : ch + cols].astype(F32)
    small_all = small_got[:, :ch_piece].reshape(S * ch_piece, small_wide).astype(F32)
    out_x = span(small_all[:, :PROJ], 1, s * (PROJ // S), PROJ // S)
    out_dt = span(small_all[:, PROJ : PROJ + DT_RANK], 1, s * (DT_RANK // S), DT_RANK // S)
    out_small = small_all[:, PROJ + DT_RANK : PROJ + DT_RANK + CONV + 3 + STATE]

    sums = sums_all.reshape(-1)
    g_gain_in, g_gain_att, g_gain_ssm, g_gain_ffn, stat_sum = [
        sums[a:b] for a, b in zip(ends[:-1], ends[1:])
    ]
    widths = jnp.array([D, ATT, INNER, D, D, D], F32)
    rms = jnp.sqrt(stat_sum / (widths * (micro * pack * N)))
    return (
        outputs.reshape(tokens.shape),
        input_grads.reshape(tokens.shape),
        g_gain_in,
        out_qkv,
        out_mix,
        out_x,
        out_dt,
        out_small,
        out_small[:, CONV + 1],
        g_gain_att,
        g_gain_ssm,
        g_att,
        out_ssm,
        g_gain_ffn,
        out_gate,
        out_up,
        out_down,
        rms,
    )


def solution(mesh):
    rows = P(None, ("seq", "fsdp"), None)
    shard = P("fsdp", None)
    both = P("fsdp", "seq")
    placed = (rows, rows, P(None, "seq"), P(None, "fsdp", None), P())
    placed += (shard,) * 5 + (P(), P(), shard, shard, P(), shard, shard, shard)
    return jax.shard_map(
        local,
        mesh=mesh,
        in_specs=placed,
        out_specs=(
            rows,
            rows,
            P(),
            both,
            both,
            both,
            both,
            shard,
            P("fsdp"),
            P(),
            P(),
            both,
            both,
            P(),
            both,
            both,
            both,
            P(),
        ),
        check_vma=False,
    )
```
